32 devices in a mesh: exp: 16 (over z, y, x), hid: 2 (over core).
Axes of the slice: x: 2, y: 2, z: 4, core: 2. Of those that a mesh axis runs over, the one named last changes fastest.
Arguments:
- tokens: bfloat16 [8192, 1280], P(('exp', 'hid')), may hold values from -6 to 6
- norm_one: float32 [1280], replicated, may hold values from 0.5 to 1.5
- w_query: bfloat16 [1280, 1280], P('hid'), may hold values from -0.15625 to 0.15625
- w_key: bfloat16 [1280, 1280], P('hid'), may hold values from -0.15625 to 0.15625
- w_value: bfloat16 [1280, 1280], P('hid'), may hold values from -0.15625 to 0.15625
- w_out: bfloat16 [1280, 1280], P('hid'), may hold values from -0.625 to 0.625
- norm_two: float32 [1280], replicated, may hold values from 0.5 to 1.5
- r_gate: bfloat16 [16, 1280, 896], P('exp', None, 'hid'), may hold values from -0.15625 to 0.15625
- r_up: bfloat16 [16, 1280, 896], P('exp', None, 'hid'), may hold values from -0.15625 to 0.15625
- r_down: bfloat16 [16, 896, 1280], P('exp', 'hid'), may hold values from -0.375 to 0.375
- s_gate: bfloat16 [1280, 896], P(None, 'hid'), may hold values from -0.15625 to 0.15625
- s_up: bfloat16 [1280, 896], P(None, 'hid'), may hold values from -0.15625 to 0.15625
- s_down: bfloat16 [896, 1280], P('hid'), may hold values from -0.375 to 0.375
- logits: float32 [8192, 7], P(('exp', 'hid')), may hold values from -3 to 3
- routes: int32 [8192, 7], P(('exp', 'hid')), may hold values from 0 to 14, all different within a row; in each aligned block of 256 rows (0 to 255, 256 to 511, ...) at most 216 rows name the same one
- lengths: int32 [32], P(('exp', 'hid')), may hold values from 64 to 256, as said below
- cotangent: bfloat16 [8192, 1280], P(('exp', 'hid')), may hold values from -6 to 6
Outputs:
- mixed_out: bfloat16 [8192, 1280], P(('exp', 'hid'))
- grad_tokens: bfloat16 [8192, 1280], P(('exp', 'hid'))
- grad_norm_one: float32 [1280], replicated
- grad_query: float32 [1280, 1280], P('hid')
- grad_key: float32 [1280, 1280], P('hid')
- grad_value: float32 [1280, 1280], P('hid')
- grad_wout: float32 [1280, 1280], P('hid')
- grad_norm_two: float32 [1280], replicated
- grad_rgate: float32 [16, 1280, 896], P('exp', None, 'hid')
- grad_rup: float32 [16, 1280, 896], P('exp', None, 'hid')
- grad_rdown: float32 [16, 896, 1280], P('exp', 'hid')
- grad_sgate: float32 [1280, 896], P(None, 'hid')
- grad_sup: float32 [1280, 896], P(None, 'hid')
- grad_sdown: float32 [896, 1280], P('hid')
- grad_logits: float32 [8192, 7], P(('exp', 'hid'))
- counts: int32 [16], replicated
The draws below stay inside these ranges and needn't reach their ends.
Inputs may be any that keep to these rules, and one draw needn't show every extreme that they name: `routes`: each row names 7 different routed experts; among the rows of one device no expert is named more than 216 times. `lengths`: some sequence is used to its full length.
All inputs are finite; a program needn't handle non-finite values.
Results may differ from the reference program's by a relative error of at most 0.02.
Values may be sent and summed in bfloat16 or wider, within the bound.
A program may use at most 384 MiB of HBM per device.

```python
import math
import jax
import jax.numpy as jnp
import numpy as np
from jax import lax

D = 1280
HEADS = 10
HD = 128
FF = 896
TOP = 7
TOK_DEV = 256
SLOTS = 16
ROUTED = 15
CAP = 216
SEQS = 32
TOKENS = 8192
DEVICES = 32


def draw_lengths(key, part):
    key = jax.random.fold_in(key, 11)
    first_key, second_key = jax.random.split(key)
    drawn = jax.random.randint(first_key, (SEQS,), TOK_DEV // 4, TOK_DEV + 1)
    longest = jax.random.randint(second_key, (), 0, SEQS)
    return drawn.at[longest].set(TOK_DEV).astype(jnp.int32)


def shard_levels(key, extent, cuts, smallest, largest):
    gain = 1.0
    for axis_at, blocks in cuts:
        steps = jax.random.uniform(jax.random.fold_in(jax.random.fold_in(key, 6), axis_at), (blocks,), jnp.float32, smallest / len(cuts), largest / len(cuts))
        gain = gain * jnp.repeat(jnp.exp(steps), extent[axis_at] // blocks).reshape((-1,) + (1,) * (len(extent) - 1 - axis_at))
    return gain


def routed_block(stream_key, own, number, rows, number_of, top, limit, lean):
    order = jax.random.permutation(stream_key, number_of)
    crowded, common = load_shares(number_of, rows * top, limit, lean, True), load_shares(number_of, rows * top, limit, lean, False)
    places = jnp.arange(number_of)

    def named(tallies, offset_by):
        used = int((tallies > 0).sum())
        fixed = max(1, used // 4)
        moved = fixed + (places - fixed + offset_by * (used - fixed)) % max(1, number_of - fixed)
        return jnp.zeros((number_of,), jnp.int32).at[order[jnp.where(places < fixed, places, moved)]].set(jnp.asarray(tallies, jnp.int32))

    tallies = jnp.where(number % 4 == 0, named(crowded, number // 4), named(common, number - number // 4 - 1))
    mixed = jax.random.permutation(jax.random.fold_in(own, 3), number_of)
    source_of, taker = mixed[0:number_of // 2 * 2:2], mixed[1:number_of // 2 * 2:2]
    slack = jnp.minimum(tallies[source_of] - 1, limit - tallies[taker]) // 2
    slack = jnp.where((source_of == order[0]) | (taker == order[0]) | (tallies[taker] == 0), 0, jnp.maximum(slack, 0))
    moved = jax.random.randint(jax.random.fold_in(own, 4), (number_of // 2,), 0, 1 << 20) % (slack + 1)
    tallies = tallies.at[source_of].add(-moved).at[taker].add(moved)
    labels = jnp.searchsorted(jnp.cumsum(tallies), jnp.arange(rows * top), side="right").astype(jnp.int32)
    listing = labels.reshape(top, rows).T
    listing = listing[jax.random.permutation(jax.random.fold_in(own, 1), rows)]
    offset_by = jax.random.randint(jax.random.fold_in(own, 2), (rows, 1), 0, top)
    return jnp.take_along_axis(listing, (jnp.arange(top)[None, :] + offset_by) % top, axis=1)


def load_shares(count, total, reach, lean, full):
    loads = [(1 << 20) // math.isqrt(rank ** lean) + 1 for rank in range(1, count + 1)]
    largest = reach if full else min(reach, max(-(-total // count), total * loads[0] // sum(loads)))
    least = 1 if total - largest >= count - 1 else 0
    given, spare = [largest] + [least] * (count - 1), total - largest - least * (count - 1)
    while spare > 0:
        free = [i for i in range(1, count) if given[i] < largest] or [i for i in range(1, count) if given[i] < reach]
        mass, remaining = sum([loads[i] for i in free]), spare
        for i in free:
            addition = min(reach - given[i], max(1, remaining * loads[i] // mass), spare)
            given[i] = given[i] + addition
            spare = spare - addition
    return np.array(given)


def gaussian(stream_key, shape, scale, reach, pieces=(), held_as=jnp.bfloat16):
    values = scale * jax.random.normal(stream_key, shape, jnp.float32)
    if pieces:
        values = values * shard_levels(stream_key, shape, pieces, -0.22, 0.18)
    return jnp.clip(values, -reach, reach).astype(held_as)


def setup_inputs(seed: int = 0) -> dict:
    seeds = jax.random.split(jax.random.key(seed), 18)
    tokens = gaussian(seeds[0], (TOKENS, D), 1.0, 6.0, ((0, 32),))
    norm_one = jnp.clip(1.0 + 0.1 * jax.random.normal(seeds[1], (D,), jnp.float32), 0.5, 1.5)
    w_query = gaussian(seeds[2], (D, D), D ** -0.5, 0.15625, ((0, 2),))
    w_key = gaussian(seeds[3], (D, D), D ** -0.5, 0.15625, ((0, 2),))
    w_value = gaussian(seeds[4], (D, D), D ** -0.5, 0.15625, ((0, 2),))
    w_out = gaussian(seeds[5], (D, D), (D // 16) ** -0.5, 0.625, ((0, 2),))
    norm_two = jnp.clip(1.0 + 0.1 * jax.random.normal(seeds[6], (D,), jnp.float32), 0.5, 1.5)
    r_gate = gaussian(seeds[7], (SLOTS, D, FF), D ** -0.5, 0.15625, ((0, 16), (2, 2)))
    r_up = gaussian(seeds[8], (SLOTS, D, FF), D ** -0.5, 0.15625, ((0, 16), (2, 2)))
    r_down = gaussian(seeds[9], (SLOTS, FF, D), (FF // 4) ** -0.5, 0.375, ((0, 16), (1, 2)))
    s_gate = gaussian(seeds[10], (D, FF), D ** -0.5, 0.15625, ((1, 2),))
    s_up = gaussian(seeds[11], (D, FF), D ** -0.5, 0.15625, ((1, 2),))
    s_down = gaussian(seeds[12], (FF, D), (FF // 4) ** -0.5, 0.375, ((0, 2),))
    logits = gaussian(seeds[13], (TOKENS, TOP), 0.5, 3.0, ((0, 32),), jnp.float32)
    routes_keys = jax.random.split(jax.random.fold_in(seeds[14], 1), TOKENS // TOK_DEV)
    routes_turns = jax.random.permutation(jax.random.fold_in(seeds[14], 3), TOKENS // TOK_DEV)
    routes = jax.vmap(lambda own, number: routed_block(jax.random.fold_in(seeds[14], 2), own, number, TOK_DEV, ROUTED, TOP, CAP, 1))(routes_keys, routes_turns).reshape((TOKENS, TOP))
    lengths = draw_lengths(jax.random.fold_in(seeds[17], 71), 0)
    cotangent = gaussian(seeds[16], (TOKENS, D), 1.0, 6.0, ((0, 32),))
    return {"tokens": tokens, "norm_one": norm_one, "w_query": w_query, "w_key": w_key, "w_value": w_value, "w_out": w_out, "norm_two": norm_two, "r_gate": r_gate, "r_up": r_up, "r_down": r_down, "s_gate": s_gate, "s_up": s_up, "s_down": s_down, "logits": logits, "routes": routes, "lengths": lengths, "cotangent": cotangent}


norm_eps = 1e-06
rotary_base = 10000.0

@jax.custom_vjp
def low(v):
    return lax.optimization_barrier(v.astype(jnp.bfloat16)).astype(jnp.float32)

@jax.custom_vjp
def low_back(v):
    return v

def low_keep(v):
    return (low(v), None)

def low_pass(kept, grad):
    return (grad,)

def back_keep(v):
    return (v, None)

def back_low(kept, grad):
    return (low(grad),)
low.defvjp(low_keep, low_pass)
low_back.defvjp(back_keep, back_low)

def product(left_side, right_side):
    return jnp.dot(left_side, right_side, precision=lax.Precision.HIGHEST, preferred_element_type=jnp.float32)

def rms_norm(values, norm_gain):
    return values * lax.rsqrt(lax.optimization_barrier(jnp.mean(values * values, axis=-1, keepdims=True)) + norm_eps) * norm_gain

def rotary_tables(seq_len):
    position = jnp.arange(seq_len).astype(jnp.float32)
    inverse_freq = rotary_base ** (-2.0 * jnp.arange(HD // 2).astype(jnp.float32) / HD)
    angle_grid = position[:, None] * inverse_freq[None, :]
    return (jnp.cos(angle_grid)[:, None, :], jnp.sin(angle_grid)[:, None, :])

def rotate(values, cosine_table, sine_table):
    half_width = values.shape[-1] // 2
    first_half = values[..., :half_width]
    second_half = values[..., half_width:]
    return jnp.concatenate([first_half * cosine_table - second_half * sine_table, second_half * cosine_table + first_half * sine_table], axis=-1)

def sequence_attention(queries, keys_all, values_all, seq_length):
    row_count = queries.shape[0]
    scores = jnp.einsum('qhd,khd->hqk', queries, keys_all, precision=lax.Precision.HIGHEST) * HD ** (-0.5)
    scores = low_back(scores)
    row_pos = jnp.arange(row_count)[:, None]
    col_pos = jnp.arange(row_count)[None, :]
    allowed = (col_pos <= row_pos) & (col_pos < seq_length)
    scores = jnp.where(allowed[None], scores, -1e+30)
    top_val = lax.optimization_barrier(jnp.max(scores, axis=-1, keepdims=True))
    raised = jnp.exp(scores - top_val)
    attn_prob = low(raised / lax.optimization_barrier(jnp.sum(raised, axis=-1, keepdims=True)))
    return jnp.einsum('hqk,khd->qhd', attn_prob, values_all, precision=lax.Precision.HIGHEST)

def attention_all(queries, keys_all, values_all, lengths):
    group_size = math.gcd(SEQS, max(1, 4096 // TOK_DEV))
    group_shape = (SEQS // group_size, group_size, TOK_DEV, HEADS, HD)

    def one_group(group_items):
        return jax.vmap(sequence_attention)(group_items[0], group_items[1], group_items[2], group_items[3])
    outputs = lax.map(jax.checkpoint(one_group), (queries.reshape(group_shape), keys_all.reshape(group_shape), values_all.reshape(group_shape), lengths.reshape(SEQS // group_size, group_size)))
    return outputs.reshape(TOKENS, D)

def routing_tables(routes):
    flat_routes = routes.reshape(DEVICES, TOK_DEV * TOP)

    def one_device(device_routes):
        onehot = (device_routes[:, None] == jnp.arange(SLOTS)[None, :]).astype(jnp.int32)
        earlier = jnp.cumsum(onehot, axis=0).astype(jnp.int32) - onehot
        return lax.optimization_barrier(jnp.sum(earlier * onehot, axis=1)).astype(jnp.int32)
    places = jax.vmap(one_device)(flat_routes)
    device_ids = jnp.arange(DEVICES).astype(jnp.int32)[:, None]
    row_index = flat_routes * (DEVICES * CAP) + device_ids * CAP + places
    return row_index.reshape(TOKENS, TOP).astype(jnp.int32)

def swiglu_expert(expert_items):
    expert_in, gate_w, up_w, down_w = expert_items
    gate_val = low_back(product(expert_in, gate_w))
    up_val = low_back(product(expert_in, up_w))
    active = low(jax.nn.silu(gate_val) * up_val)
    return low(low_back(product(active, down_w)))

def layer(tokens, norm_one, w_query, w_key, w_value, w_out, norm_two, r_gate, r_up, r_down, s_gate, s_up, s_down, logits, lengths, row_index, source_rows, token_valid):
    normed = low(rms_norm(tokens, norm_one))
    cosine_table, sine_table = rotary_tables(TOK_DEV)
    heads_shape = (SEQS, TOK_DEV, HEADS, HD)
    queries = low(rotate(low_back(product(normed, w_query)).reshape(heads_shape), cosine_table, sine_table))
    keys_all = low(rotate(low_back(product(normed, w_key)).reshape(heads_shape), cosine_table, sine_table))
    values_all = low(low_back(product(normed, w_value)).reshape(heads_shape))
    attended = low(low_back(attention_all(queries, keys_all, values_all, lengths)))
    mixed = tokens + low_back(product(attended, w_out))
    hidden_in = low(rms_norm(mixed, norm_two))
    shared_gate = low_back(product(hidden_in, s_gate))
    shared_up = low_back(product(hidden_in, s_up))
    shared_act = low(jax.nn.silu(shared_gate) * shared_up)
    shared_out = low_back(product(shared_act, s_down))
    padded = jnp.concatenate([hidden_in, jnp.zeros((1, D), hidden_in.dtype)], axis=0)
    expert_rows = low_back(padded[source_rows]).reshape(SLOTS, DEVICES * CAP, D)
    expert_out = lax.map(jax.checkpoint(swiglu_expert), (expert_rows, r_gate, r_up, r_down)).reshape(-1, D)
    picked = expert_out[row_index]
    gate_share = jax.nn.softmax(logits, axis=-1) * token_valid[:, None]
    routed = jnp.einsum('tk,tkd->td', gate_share, picked, precision=lax.Precision.HIGHEST)
    return mixed + shared_out + routed

def reference(tokens, norm_one, w_query, w_key, w_value, w_out, norm_two, r_gate, r_up, r_down, s_gate, s_up, s_down, logits, routes, lengths, cotangent):
    row_index = routing_tables(routes)
    token_ids = (jnp.arange(TOKENS * TOP) // TOP).astype(jnp.int32)
    source_rows = jnp.full((SLOTS * DEVICES * CAP,), TOKENS, jnp.int32).at[row_index.reshape(-1)].set(token_ids)
    position = jnp.arange(TOKENS) % TOK_DEV
    valid_int = (position < jnp.repeat(lengths, TOK_DEV)).astype(jnp.int32)
    token_valid = valid_int.astype(jnp.float32)
    floats = [item_array.astype(jnp.float32) for item_array in (tokens, norm_one, w_query, w_key, w_value, w_out, norm_two, r_gate, r_up, r_down, s_gate, s_up, s_down, logits)]

    def forward(*params):
        return layer(*params, lengths, row_index, source_rows, token_valid)
    output, pullback = jax.vjp(forward, *floats)
    gradients = pullback(cotangent.astype(jnp.float32))
    chosen = (routes[:, :, None] == jnp.arange(SLOTS)[None, None, :]).astype(jnp.int32)
    counts = lax.optimization_barrier(jnp.sum(chosen * valid_int[:, None, None], axis=(0, 1))).astype(jnp.int32)
    return (output.astype(jnp.bfloat16), gradients[0].astype(jnp.bfloat16), gradients[1], gradients[2], gradients[3], gradients[4], gradients[5], gradients[6], gradients[7], gradients[8], gradients[9], gradients[10], gradients[11], gradients[12], gradients[13], counts)
```

```python
import functools

import jax
import jax.numpy as jnp
from jax import lax
from jax.experimental import pallas as pl
from jax.experimental.pallas import tpu as pltpu
from jax.sharding import PartitionSpec as P

HEADS = 10
HD = 128
MESH = pl.DeviceIdType.MESH


norm_eps = 1e-06
rotary_base = 10000.0
block_rows = 512
contract_rows = (((0,), (0,)), ((), ()))
contract_cols = (((1,), (1,)), ((), ()))


def matmul(left_side, right_side):
    return jnp.dot(left_side, right_side, preferred_element_type=jnp.float32)


def outer_rows(left_side, right_side):
    return lax.dot_general(left_side, right_side, contract_rows, preferred_element_type=jnp.float32)


def inner_cols(left_side, right_side):
    return lax.dot_general(left_side, right_side, contract_cols, preferred_element_type=jnp.float32)


def rms_parts(values):
    inv_rms = lax.rsqrt(jnp.mean(values * values, axis=-1, keepdims=True) + norm_eps)
    return (values * inv_rms, inv_rms)


def rms_back(normed, inv_rms, norm_gain, upstream):
    gain_grad = jnp.sum(upstream * normed, axis=0)
    scaled_up = upstream * norm_gain
    return (
        inv_rms * (scaled_up - normed * jnp.mean(scaled_up * normed, axis=-1, keepdims=True)),
        gain_grad,
    )


def rotary_tables(seq_len, head_size):
    position = jnp.arange(seq_len).astype(jnp.float32)
    inverse_freq = rotary_base ** (
        -2.0 * jnp.arange(head_size // 2).astype(jnp.float32) / head_size
    )
    angle_grid = position[:, None] * inverse_freq[None, :]
    return (jnp.cos(angle_grid)[:, None, :], jnp.sin(angle_grid)[:, None, :])


def rotate(values, cosine_table, sine_table):
    half_width = values.shape[-1] // 2
    first_half = values[..., :half_width]
    second_half = values[..., half_width:]
    return jnp.concatenate(
        [
            first_half * cosine_table - second_half * sine_table,
            second_half * cosine_table + first_half * sine_table,
        ],
        axis=-1,
    )


def masked_scores(query_blk, keys_all, block_start, seq_length, score_scale):
    scores = (
        jnp.einsum("qhd,khd->hqk", query_blk, keys_all, preferred_element_type=jnp.float32)
        * score_scale
    )
    row_pos = block_start + jnp.arange(query_blk.shape[0])[:, None]
    col_pos = jnp.arange(keys_all.shape[0])[None, :]
    allowed = (col_pos <= row_pos) & (col_pos < seq_length)
    return jnp.where(allowed[None], scores, -1e30)


def attend_forward(queries, keys_all, values_all, seq_length):
    total_rows = queries.shape[0]
    step_rows = min(total_rows, block_rows)
    score_scale = queries.shape[-1] ** (-0.5)

    def one_block(block_start):
        scores = masked_scores(queries, keys_all, block_start, seq_length, score_scale)
        top_val = jnp.max(scores, axis=-1, keepdims=True)
        raised = jnp.exp(scores - top_val)
        totals = jnp.sum(raised, axis=-1, keepdims=True)
        attn_prob = (raised / totals).astype(jnp.bfloat16)
        attended = jnp.einsum(
            "hqk,khd->qhd", attn_prob, values_all, preferred_element_type=jnp.float32
        )
        return (attended, (top_val + jnp.log(totals))[..., 0])

    starts = jnp.arange(total_rows // step_rows) * step_rows
    attended, log_total = lax.map(one_block, starts)
    return (attended.reshape(queries.shape), log_total)


def attend_backward(queries, keys_all, values_all, seq_length, log_total, grad_out):
    total_rows = queries.shape[0]
    step_rows = min(total_rows, block_rows)
    score_scale = queries.shape[-1] ** (-0.5)

    def one_block(running, inputs):
        grad_keys, grad_values = running
        block_start, lse_block = inputs
        scores = masked_scores(queries, keys_all, block_start, seq_length, score_scale)
        attn_prob = jnp.exp(scores - lse_block[..., None])
        grad_values = grad_values + jnp.einsum(
            "hqk,qhd->khd",
            attn_prob.astype(jnp.bfloat16),
            grad_out,
            preferred_element_type=jnp.float32,
        )
        grad_prob = jnp.einsum(
            "qhd,khd->hqk", grad_out, values_all, preferred_element_type=jnp.float32
        )
        row_inner = jnp.sum(attn_prob * grad_prob, axis=-1, keepdims=True)
        grad_scores = (attn_prob * (grad_prob - row_inner)).astype(jnp.bfloat16)
        grad_query = (
            jnp.einsum("hqk,khd->qhd", grad_scores, keys_all, preferred_element_type=jnp.float32)
            * score_scale
        )
        grad_keys = (
            grad_keys
            + jnp.einsum("hqk,qhd->khd", grad_scores, queries, preferred_element_type=jnp.float32)
            * score_scale
        )
        return ((grad_keys, grad_values), grad_query)

    zero_grads = jnp.zeros(queries.shape, jnp.float32)
    starts = jnp.arange(total_rows // step_rows) * step_rows
    (grad_keys, grad_values), grad_query = lax.scan(
        one_block, (zero_grads, zero_grads), (starts, log_total)
    )
    return (grad_query.reshape(queries.shape), grad_keys, grad_values)


class Place:
    def __init__(self, n):
        self.nz = 4; self.m = {16: 2, 64: 4}[n]; m = self.m
        self.e = lax.axis_index("exp"); self.c = lax.axis_index("hid"); c = self.c; e = self.e
        self.s1 = m * m; self.s2 = 1 + c * (m - 1); self.s3 = m - c * (m - 1)
        self.c1 = e // self.s1; self.c2 = (e // self.s2) % m; self.c3 = (e // self.s3) % m
    def blk(self, a, b, d): return a * self.s1 + b * self.s2 + d * self.s3
    def o2(self): return [(self.c2 + j) % self.m for j in range(1, self.m)]
    def o3(self): return [(self.c3 + j) % self.m for j in range(1, self.m)]
    def enter(self):
        bar = pltpu.get_barrier_semaphore()
        c1, c2, c3 = self.c1, self.c2, self.c3
        def sig(p): pl.semaphore_signal(bar, inc=1, device_id=(p, self.c), device_id_type=MESH)
        for j in self.o2(): sig(self.blk(c1, j, c3))
        for j in self.o3(): sig(self.blk(c1, c2, j))
        for j in range(1, self.nz): sig(self.blk((c1 + j) % self.nz, c2, c3))
        pl.semaphore_wait(bar, 2 * (self.m - 1) + self.nz - 1)

class Gather:
    def __init__(self, pc, src, dst, ssem, rsem, split, base=0):
        self.pc, self.src, self.dst, self.ssem, self.rsem = pc, src, dst, ssem, rsem
        self.split = split; self.sends = []; self.base = base
    def view(self, ref, part):
        R = self.src.shape[0]
        return ref.at[pl.ds(0, self.split)] if part == 0 else ref.at[pl.ds(self.split, R - self.split)]
    def send(self, part, own, b, to, cond=None):
        i = self.base + len(self.sends)
        src = self.view(self.src if own else self.dst.at[b], part)
        cp = pltpu.make_async_remote_copy(src_ref=src, dst_ref=self.view(self.dst.at[b], part), send_sem=self.ssem.at[i], recv_sem=self.rsem.at[part, b], device_id=(to, self.pc.c), device_id_type=MESH)
        self.sends.append((cond, cp))
        if cond is None: cp.start()
        else: pl.when(cond)(cp.start)
    def wait(self, part, b):
        v = self.view(self.dst.at[b], part)
        pltpu.make_async_copy(v, v, self.rsem.at[part, b]).wait()
    def updown(self, part, own, b):
        pc = self.pc
        self.send(part, own, b, pc.blk(pc.c1 + 1, pc.c2, pc.c3), pc.c1 < pc.nz - 1)
        self.send(part, own, b, pc.blk(pc.c1 - 1, pc.c2, pc.c3), pc.c1 > 0)
    def to2(self, part, own, b):
        pc = self.pc
        for j in pc.o2(): self.send(part, own, b, pc.blk(pc.c1, j, pc.c3))
    def to3(self, part, own, b):
        pc = self.pc
        for j in pc.o3(): self.send(part, own, b, pc.blk(pc.c1, pc.c2, j))
    def start(self):
        e = self.pc.e
        self.to3(0, True, e); self.to2(0, True, e); self.updown(0, True, e)
        if self.split < self.src.shape[0]:
            self.to3(1, True, e); self.to2(1, True, e); self.updown(1, True, e)
    def zarr(self, part, s, up, k2, k3, more):
        pc = self.pc
        a = pc.c1 - s if up else pc.c1 + s
        cond = (pc.c1 >= s) if up else (pc.c1 < pc.nz - s)
        b = pc.blk(a, k2, k3)
        pl.when(cond)(lambda: self.wait(part, b))
        if s < pc.nz - 1:
            if up: self.send(part, False, b, pc.blk(pc.c1 + 1, pc.c2, pc.c3), (pc.c1 >= s) & (pc.c1 < pc.nz - 1))
            else: self.send(part, False, b, pc.blk(pc.c1 - 1, pc.c2, pc.c3), (pc.c1 < pc.nz - s) & (pc.c1 > 0))
        if more:
            for j in pc.o2(): self.send(part, False, b, pc.blk(pc.c1, j, pc.c3), cond)
            for j in pc.o3(): self.send(part, False, b, pc.blk(pc.c1, pc.c2, j), cond)
    def events(self):
        pc = self.pc; ev = []
        def a2(s):
            def go():
                for j in pc.o2():
                    for sg in ((1, -1) if s else (1,)):
                        a = pc.c1 + sg * s
                        cond = None if s == 0 else ((a >= 0) & (a < pc.nz))
                        b = pc.blk(a, j, pc.c3)
                        if cond is None: self.wait(0, b)
                        else: pl.when(cond)(lambda b=b: self.wait(0, b))
                        for k in pc.o3(): self.send(0, False, b, pc.blk(pc.c1, pc.c2, k), cond)
            return go
        def az(s):
            def go():
                self.zarr(0, s, True, pc.c2, pc.c3, True); self.zarr(0, s, False, pc.c2, pc.c3, True)
            return go
        B = self.split < self.src.shape[0]
        def f1():
            for j in pc.o2():
                b = pc.blk(pc.c1, j, pc.c3); self.wait(1, b); self.to3(1, False, b); self.updown(1, False, b)
        def f2():
            for k in pc.o3():
                b = pc.blk(pc.c1, pc.c2, k); self.wait(1, b); self.updown(1, False, b)
        def f3():
            for j in pc.o2():
                for k in pc.o3():
                    b = pc.blk(pc.c1, j, k); self.wait(1, b); self.updown(1, False, b)
        def fz(s):
            def go():
                for k2 in range(pc.m):
                    for k3 in range(pc.m):
                        self.zarr(1, s, True, k2, k3, False); self.zarr(1, s, False, k2, k3, False)
            return go
        ev += [az(1), a2(0)]
        if B: ev += [f1, f2, f3]
        ev += [az(2), a2(1)]
        if B: ev += [fz(1)]
        ev += [az(3), a2(2)]
        if B: ev += [fz(2)]
        ev += [a2(3)]
        if B: ev += [fz(3)]
        def last():
            for a in range(pc.nz):
                for j in range(pc.m):
                    for k in pc.o3(): self.wait(0, pc.blk(a, j, k))
        ev += [last]
        return ev
    def finish(self):
        for cond, cp in self.sends:
            if cond is None: cp.wait_send()
            else: pl.when(cond)(cp.wait_send)


def gather_kernel(n, x_ref, w_ref, ox_ref, ow_ref, ssem, rsem, lsem):
    pc = Place(n)
    pc.enter()
    rows = x_ref.shape[0]
    first = Gather(pc, x_ref, ox_ref, ssem.at[0], rsem.at[0], rows)
    second = Gather(pc, w_ref, ow_ref, ssem.at[1], rsem.at[1], rows)
    first.start()
    second.start()
    own_x = pltpu.make_async_copy(x_ref, ox_ref.at[pc.e], lsem.at[0])
    own_w = pltpu.make_async_copy(w_ref, ow_ref.at[pc.e], lsem.at[1])
    own_x.start()
    own_w.start()
    for event in first.events():
        event()
    for event in second.events():
        event()
    first.finish()
    second.finish()
    own_x.wait()
    own_w.wait()


def gather_both(x, w):
    n = lax.axis_size("exp")
    any_spec = pl.BlockSpec(memory_space=pl.ANY)
    return pl.pallas_call(
        functools.partial(gather_kernel, n),
        out_shape=(jax.ShapeDtypeStruct((n,) + x.shape, x.dtype), jax.ShapeDtypeStruct((n,) + w.shape, w.dtype)),
        in_specs=[any_spec, any_spec],
        out_specs=(any_spec, any_spec),
        scratch_shapes=[
            pltpu.SemaphoreType.DMA((2, 128)),
            pltpu.SemaphoreType.DMA((2, 2, n)),
            pltpu.SemaphoreType.DMA((2,)),
        ],
        compiler_params=pltpu.CompilerParams(collective_id=0, has_side_effects=True),
    )(x, w)


def experts_kernel(
    n, slots,
    h_hbm, dy_hbm, gate_ref, wg, wu, wd,
    s_ref, sums_hbm, gg_hbm, gu_hbm, gd_hbm, pg_hbm, pu_hbm, pd_hbm, r3_hbm, r2_hbm, r1_hbm,
    og, ou, od, ysum, hbuf, dbuf, act, dg, dup, stage, rbuf, xg, xu, xd,
    lsem, ssem, r3sem, r2sem, r1sem, bsem, xssem, xrsem, osem,
):
    pc = Place(n)
    nz, m = pc.nz, pc.m
    c1, c2, c3, e, c = pc.c1, pc.c2, pc.c3, pc.e, pc.c
    barrier = pltpu.get_barrier_semaphore()

    def greet(to, core):
        pl.semaphore_signal(barrier, inc=1, device_id=(to, core), device_id_type=MESH)

    for j in range(1, m):
        greet(pc.blk(c1, c2, (c3 + j) % m), c)
        greet(pc.blk(c1, (c2 + j) % m, c3), c)
    for j in range(1, nz):
        greet(pc.blk((c1 + j) % nz, c2, c3), c)
    greet(e, 1 - c)
    pl.semaphore_wait(barrier, 2 * (m - 1) + nz)

    og[...] = jnp.zeros_like(og)
    ou[...] = jnp.zeros_like(ou)
    od[...] = jnp.zeros_like(od)
    s_ref[...] = jnp.zeros_like(s_ref)
    n3 = (m - 1) * nz * m
    n2 = (m - 1) * nz

    def dest(t):
        return (c1 + t + 1) % nz, (c2 + t // nz + 1) % m, (c3 + t // (nz * m) + 1) % m

    def load(t, i):
        b = pc.blk(*dest(t))
        return (
            pltpu.make_async_copy(h_hbm.at[b], hbuf.at[i], lsem.at[0, i]),
            pltpu.make_async_copy(dy_hbm.at[b], dbuf.at[i], lsem.at[1, i]),
        )

    def partial_copy(i, to, dst, sem):
        return pltpu.make_async_remote_copy(
            src_ref=stage.at[i], dst_ref=dst, send_sem=ssem.at[i], recv_sem=sem,
            device_id=(to, c), device_id_type=MESH,
        )

    def add_received(src, sem):
        pltpu.make_async_remote_copy(
            src_ref=src, dst_ref=src, send_sem=ssem.at[0], recv_sem=sem,
            device_id=(e, 1 - c), device_id_type=MESH,
        ).wait_recv()
        copy = pltpu.make_async_copy(src, rbuf, bsem)
        copy.start()
        copy.wait()
        ysum[...] += rbuf[...].astype(jnp.float32)

    def swaps():
        return [
            pltpu.make_async_remote_copy(
                src_ref=src, dst_ref=dst, send_sem=xssem.at[i], recv_sem=xrsem.at[i],
                device_id=(e, 1 - c), device_id_type=MESH,
            )
            for i, (src, dst) in enumerate(((xg, pg_hbm), (xu, pu_hbm), (xd, pd_hbm)))
        ]

    def own_halves():
        return [
            pltpu.make_async_copy(src.at[c], dst, osem.at[i])
            for i, (src, dst) in enumerate(((og, gg_hbm), (ou, gu_hbm), (od, gd_hbm)))
        ]

    for copy in load(0, 0):
        copy.start()

    def body(t, carry):
        i = t % 2
        slot = t % slots
        a, b2, b3 = dest(t)
        b = pc.blk(a, b2, b3)
        for copy in load(t, i):
            copy.wait()

        @pl.when(t < n - 1)
        def _():
            for copy in load(t + 1, 1 - i):
                copy.start()

        lane = lax.broadcasted_iota(jnp.int32, gate_ref.shape, 1)
        gate = jnp.sum(jnp.where(lane == b, gate_ref[...], 0.0), axis=1, keepdims=True)
        h = hbuf[i]
        dy = dbuf[i].astype(jnp.float32)
        z = (gate * dy).astype(jnp.bfloat16)
        for half in range(2):
            g = matmul(h, wg[half])
            u = matmul(h, wu[half])
            da = inner_cols(z, wd[half])
            sg = jax.nn.sigmoid(g)
            si = g * sg
            act[half] = (si * u).astype(jnp.bfloat16)
            dup[half] = (da * si).astype(jnp.bfloat16)
            dg[half] = (da * u * sg * (1.0 + g * (1.0 - sg))).astype(jnp.bfloat16)
        y = (matmul(act[0], wd[0]) + matmul(act[1], wd[1])).astype(jnp.bfloat16).astype(jnp.float32)
        s = jnp.sum(y * dy, axis=1, keepdims=True)
        s_ref[...] = jnp.where(lane == b, s, s_ref[...])
        ysum[0] = gate * y
        ysum[1] = (
            inner_cols(dg[0], wg[0]) + inner_cols(dg[1], wg[1])
            + inner_cols(dup[0], wu[0]) + inner_cols(dup[1], wu[1])
        ).astype(jnp.bfloat16).astype(jnp.float32)

        @pl.when((t >= slots) & (t - slots < n - 1))
        def _():
            partial_copy(slot, e, r1_hbm.at[0], r1sem.at[0]).wait_send()

        @pl.when(t >= n3)
        def _():
            for j in range(1, m):
                add_received(r3_hbm.at[j - 1, a, b2], r3sem.at[j - 1, a, b2])

        @pl.when(t >= n3 + n2)
        def _():
            for j in range(1, m):
                add_received(r2_hbm.at[j - 1, a], r2sem.at[j - 1, a])

        @pl.when(t < n - 1)
        def _():
            stage[slot] = ysum[...].astype(jnp.bfloat16)

        for j in range(1, m):
            @pl.when((t < n3) & (b3 == (c3 + j) % m))
            def _():
                partial_copy(slot, pc.blk(c1, c2, b3), r3_hbm.at[m - j - 1, a, b2], r3sem.at[m - j - 1, a, b2]).start()

            @pl.when((t >= n3) & (t < n3 + n2) & (b2 == (c2 + j) % m))
            def _():
                partial_copy(slot, pc.blk(c1, b2, c3), r2_hbm.at[m - j - 1, a], r2sem.at[m - j - 1, a]).start()

        for j in range(1, nz):
            @pl.when((t >= n3 + n2) & (t < n - 1) & (a == (c1 + j) % nz))
            def _():
                partial_copy(slot, pc.blk(a, c2, c3), r1_hbm.at[nz - j - 1], r1sem.at[nz - j - 1]).start()

        for half in range(2):
            og[half] += outer_rows(h, dg[half])
            ou[half] += outer_rows(h, dup[half])
            od[half] += outer_rows(act[half], z)
        return carry

    lax.fori_loop(0, n, body, 0)
    xg[...] = og[1 - c].astype(jnp.bfloat16)
    xu[...] = ou[1 - c].astype(jnp.bfloat16)
    xd[...] = od[1 - c].astype(jnp.bfloat16)
    for copy in swaps():
        copy.start()
    for copy in own_halves():
        copy.start()
    for j in range(1, nz):
        add_received(r1_hbm.at[j - 1], r1sem.at[j - 1])
    final = pltpu.make_async_copy(ysum, sums_hbm, bsem)
    final.start()
    final.wait()
    for t in range(max(0, n - slots), n - 1):
        partial_copy(t % slots, e, r1_hbm.at[0], r1sem.at[0]).wait_send()
    for copy in swaps():
        copy.wait()
    for copy in own_halves():
        copy.wait()


def experts(h, dy, gates, wg, wu, wd):
    n, rows, width = h.shape
    hidden = wg.shape[2]
    nz = 4
    m = {16: 2, 64: 4}[n]
    slots = 8
    vmem = pl.BlockSpec(memory_space=pltpu.VMEM)
    hbm = pl.BlockSpec(memory_space=pl.ANY)
    f32, b16 = jnp.float32, jnp.bfloat16
    out = jax.ShapeDtypeStruct
    return pl.pallas_call(
        functools.partial(experts_kernel, n, slots),
        out_shape=(
            out((rows, n), f32), out((2, rows, width), f32),
            out((width, hidden), f32), out((width, hidden), f32), out((hidden, width), f32),
            out((width, hidden), b16), out((width, hidden), b16), out((hidden, width), b16),
            out((m - 1, nz, m, 2, rows, width), b16), out((m - 1, nz, 2, rows, width), b16), out((nz - 1, 2, rows, width), b16),
        ),
        in_specs=[hbm, hbm, vmem, vmem, vmem, vmem],
        out_specs=(vmem,) + (hbm,) * 10,
        scratch_shapes=[
            pltpu.VMEM((2, width, hidden), f32), pltpu.VMEM((2, width, hidden), f32), pltpu.VMEM((2, hidden, width), f32),
            pltpu.VMEM((2, rows, width), f32), pltpu.VMEM((2, rows, width), b16), pltpu.VMEM((2, rows, width), b16),
            pltpu.VMEM((2, rows, hidden), b16), pltpu.VMEM((2, rows, hidden), b16), pltpu.VMEM((2, rows, hidden), b16),
            pltpu.VMEM((slots, 2, rows, width), b16), pltpu.VMEM((2, rows, width), b16),
            pltpu.VMEM((width, hidden), b16), pltpu.VMEM((width, hidden), b16), pltpu.VMEM((hidden, width), b16),
            pltpu.SemaphoreType.DMA((2, 2)), pltpu.SemaphoreType.DMA((slots,)),
            pltpu.SemaphoreType.DMA((m - 1, nz, m)), pltpu.SemaphoreType.DMA((m - 1, nz)), pltpu.SemaphoreType.DMA((nz - 1,)),
            pltpu.SemaphoreType.DMA, pltpu.SemaphoreType.DMA((3,)), pltpu.SemaphoreType.DMA((3,)), pltpu.SemaphoreType.DMA((3,)),
        ],
        compiler_params=pltpu.CompilerParams(collective_id=1, has_side_effects=True, vmem_limit_bytes=60 * 2**20),
    )(h, dy, gates, wg, wu, wd)


def on_device(
    tokens,
    norm_one,
    w_query,
    w_key,
    w_value,
    w_out,
    norm_two,
    r_gate,
    r_up,
    r_down,
    s_gate,
    s_up,
    s_down,
    logits,
    routes,
    lengths,
    cotangent,
):
    seq_len = tokens.shape[0]
    width = tokens.shape[1]
    slot_count = lax.axis_size("exp")
    seq_length = lengths[0]
    inputs_full = tokens.astype(jnp.float32)
    full_query, full_key, full_value, full_out = (
        lax.all_gather(w_query, "hid", axis=0, tiled=True),
        lax.all_gather(w_key, "hid", axis=0, tiled=True),
        lax.all_gather(w_value, "hid", axis=0, tiled=True),
        lax.all_gather(w_out, "hid", axis=0, tiled=True),
    )
    normed_one, scale_one = rms_parts(inputs_full)
    attn_in = (normed_one * norm_one).astype(jnp.bfloat16)
    cosine_table, sine_table = rotary_tables(seq_len, HD)
    heads_shape = (seq_len, HEADS, HD)
    queries = rotate(
        matmul(attn_in, full_query).reshape(heads_shape), cosine_table, sine_table
    ).astype(jnp.bfloat16)
    keys_all = rotate(
        matmul(attn_in, full_key).reshape(heads_shape), cosine_table, sine_table
    ).astype(jnp.bfloat16)
    values_all = matmul(attn_in, full_value).reshape(heads_shape).astype(jnp.bfloat16)
    attended, log_total = attend_forward(queries, keys_all, values_all, seq_length)
    attended_low = attended.reshape(seq_len, width).astype(jnp.bfloat16)
    mixed = inputs_full + matmul(attended_low, full_out)
    normed_two, scale_two = rms_parts(mixed)
    hidden_in = (normed_two * norm_two).astype(jnp.bfloat16)
    onehot = (routes[:, :, None] == jnp.arange(slot_count)[None, None, :]).astype(jnp.float32)
    token_valid = (jnp.arange(seq_len) < seq_length).astype(jnp.float32)
    soft_gates = jax.nn.softmax(logits, axis=-1)
    gate_share = soft_gates * token_valid[:, None]
    local_counts = jnp.sum(onehot * token_valid[:, None, None], axis=(0, 1))
    is_last = jnp.arange(slot_count) == slot_count - 1
    own_gates = jnp.where(is_last[None, :], 1.0, jnp.sum(onehot * gate_share[:, :, None], axis=1))
    gates = lax.all_to_all(own_gates.T, "exp", split_axis=0, concat_axis=0, tiled=True).T
    holds_shared = lax.axis_index("exp") == slot_count - 1
    wg, wu, wd = (
        lax.all_gather(jnp.where(holds_shared, shared, routed[0]), "hid", axis=0)
        for shared, routed in ((s_gate, r_gate), (s_up, r_up), (s_down, r_down))
    )
    all_dy, all_h = gather_both(cotangent, hidden_in)
    scores_e, sums, gg, gu, gd, pg, pu, pd = experts(all_h, all_dy, gates, wg, wu, wd)[:8]
    slot_grads = (gg + pg.astype(jnp.float32), gu + pu.astype(jnp.float32), gd + pd.astype(jnp.float32))
    scores = lax.all_to_all(scores_e.T, "exp", split_axis=0, concat_axis=0, tiled=True).T
    output = mixed + sums[0]
    upstream = cotangent.astype(jnp.float32)
    grad_share = jnp.sum(onehot * scores[:, None, :], axis=-1) * token_valid[:, None]
    grad_logits = soft_gates * (
        grad_share - jnp.sum(soft_gates * grad_share, axis=-1, keepdims=True)
    )
    grad_hidden = sums[1]
    grad_norm_in, grad_two = rms_back(normed_two, scale_two, norm_two, grad_hidden)
    grad_mixed = upstream + grad_norm_in
    grad_mixed_low = grad_mixed.astype(jnp.bfloat16)
    grad_wout = outer_rows(attended_low, grad_mixed_low)
    grad_attended = inner_cols(grad_mixed_low, full_out).astype(jnp.bfloat16).reshape(heads_shape)
    grad_query_rot, grad_key_rot, grad_value_all = attend_backward(
        queries, keys_all, values_all, seq_length, log_total, grad_attended
    )
    grad_query_pre = (
        rotate(grad_query_rot, cosine_table, -sine_table)
        .reshape(seq_len, width)
        .astype(jnp.bfloat16)
    )
    grad_key_pre = (
        rotate(grad_key_rot, cosine_table, -sine_table).reshape(seq_len, width).astype(jnp.bfloat16)
    )
    grad_value_pre = grad_value_all.reshape(seq_len, width).astype(jnp.bfloat16)
    grad_wquery = outer_rows(attn_in, grad_query_pre)
    grad_wkey = outer_rows(attn_in, grad_key_pre)
    grad_wvalue = outer_rows(attn_in, grad_value_pre)
    grad_attn_in = (
        inner_cols(grad_query_pre, full_query)
        + inner_cols(grad_key_pre, full_key)
        + inner_cols(grad_value_pre, full_value)
    )
    grad_in_one, grad_one = rms_back(normed_one, scale_one, norm_one, grad_attn_in)
    grad_tokens = (grad_mixed + grad_in_one).astype(jnp.bfloat16)
    attn_half = (
        lax.psum_scatter(
            grad_wquery.astype(jnp.bfloat16), "hid", scatter_dimension=0, tiled=True
        ),
        lax.psum_scatter(
            grad_wkey.astype(jnp.bfloat16), "hid", scatter_dimension=0, tiled=True
        ),
        lax.psum_scatter(
            grad_wvalue.astype(jnp.bfloat16), "hid", scatter_dimension=0, tiled=True
        ),
        lax.psum_scatter(
            grad_wout.astype(jnp.bfloat16), "hid", scatter_dimension=0, tiled=True
        ),
    )
    shared_grads = tuple(jnp.where(holds_shared, grad, 0.0).astype(jnp.bfloat16) for grad in slot_grads)
    routed_grads = tuple(jnp.where(holds_shared, 0.0, grad)[None] for grad in slot_grads)
    summed = lax.psum(
        (
            attn_half[0],
            attn_half[1],
            attn_half[2],
            attn_half[3],
            shared_grads[0],
            shared_grads[1],
            shared_grads[2],
        ),
        "exp",
    )
    small_sums = lax.psum((grad_one, grad_two, local_counts), ("exp", "hid"))
    counts = small_sums[2].astype(jnp.int32)
    return (
        output.astype(jnp.bfloat16),
        grad_tokens,
        small_sums[0],
        summed[0].astype(jnp.float32),
        summed[1].astype(jnp.float32),
        summed[2].astype(jnp.float32),
        summed[3].astype(jnp.float32),
        small_sums[1],
        routed_grads[0],
        routed_grads[1],
        routed_grads[2],
        summed[4].astype(jnp.float32),
        summed[5].astype(jnp.float32),
        summed[6].astype(jnp.float32),
        grad_logits,
        counts,
    )


def solution(mesh):
    in_specs = (
        P(("exp", "hid"), None),
        P(),
        P("hid", None),
        P("hid", None),
        P("hid", None),
        P("hid", None),
        P(),
        P("exp", None, "hid"),
        P("exp", None, "hid"),
        P("exp", "hid", None),
        P(None, "hid"),
        P(None, "hid"),
        P("hid", None),
        P(("exp", "hid"), None),
        P(("exp", "hid"), None),
        P(("exp", "hid")),
        P(("exp", "hid"), None),
    )
    out_specs = (
        P(("exp", "hid"), None),
        P(("exp", "hid"), None),
        P(),
        P("hid", None),
        P("hid", None),
        P("hid", None),
        P("hid", None),
        P(),
        P("exp", None, "hid"),
        P("exp", None, "hid"),
        P("exp", "hid", None),
        P(None, "hid"),
        P(None, "hid"),
        P("hid", None),
        P(("exp", "hid"), None),
        P(),
    )
    return jax.shard_map(
        on_device, mesh=mesh, in_specs=in_specs, out_specs=out_specs, check_vma=False
    )
```

```python
import functools

import jax
import jax.numpy as jnp
from jax import lax
from jax.experimental import pallas as pl
from jax.experimental.pallas import tpu as pltpu
from jax.sharding import PartitionSpec as P

HEADS = 10
HD = 128
MESH = pl.DeviceIdType.MESH


norm_eps = 1e-06
rotary_base = 10000.0
block_rows = 512
contract_rows = (((0,), (0,)), ((), ()))
contract_cols = (((1,), (1,)), ((), ()))


def matmul(left_side, right_side):
    return jnp.dot(left_side, right_side, preferred_element_type=jnp.float32)


def outer_rows(left_side, right_side):
    return lax.dot_general(left_side, right_side, contract_rows, preferred_element_type=jnp.float32)


def inner_cols(left_side, right_side):
    return lax.dot_general(left_side, right_side, contract_cols, preferred_element_type=jnp.float32)


def rms_parts(values):
    inv_rms = lax.rsqrt(jnp.mean(values * values, axis=-1, keepdims=True) + norm_eps)
    return (values * inv_rms, inv_rms)


def rms_back(normed, inv_rms, norm_gain, upstream):
    gain_grad = jnp.sum(upstream * normed, axis=0)
    scaled_up = upstream * norm_gain
    return (
        inv_rms * (scaled_up - normed * jnp.mean(scaled_up * normed, axis=-1, keepdims=True)),
        gain_grad,
    )


def rotary_tables(seq_len, head_size):
    position = jnp.arange(seq_len).astype(jnp.float32)
    inverse_freq = rotary_base ** (
        -2.0 * jnp.arange(head_size // 2).astype(jnp.float32) / head_size
    )
    angle_grid = position[:, None] * inverse_freq[None, :]
    return (jnp.cos(angle_grid)[:, None, :], jnp.sin(angle_grid)[:, None, :])


def rotate(values, cosine_table, sine_table):
    half_width = values.shape[-1] // 2
    first_half = values[..., :half_width]
    second_half = values[..., half_width:]
    return jnp.concatenate(
        [
            first_half * cosine_table - second_half * sine_table,
            second_half * cosine_table + first_half * sine_table,
        ],
        axis=-1,
    )


def masked_scores(query_blk, keys_all, block_start, seq_length, score_scale):
    scores = (
        jnp.einsum("qhd,khd->hqk", query_blk, keys_all, preferred_element_type=jnp.float32)
        * score_scale
    )
    row_pos = block_start + jnp.arange(query_blk.shape[0])[:, None]
    col_pos = jnp.arange(keys_all.shape[0])[None, :]
    allowed = (col_pos <= row_pos) & (col_pos < seq_length)
    return jnp.where(allowed[None], scores, -1e30)


def attend_forward(queries, keys_all, values_all, seq_length):
    score_scale = queries.shape[-1] ** (-0.5)
    scores = masked_scores(queries, keys_all, 0, seq_length, score_scale)
    top_val = jnp.max(scores, axis=-1, keepdims=True)
    raised = jnp.exp(scores - top_val)
    attn_prob = raised / jnp.sum(raised, axis=-1, keepdims=True)
    attended = jnp.einsum(
        "hqk,khd->qhd", attn_prob.astype(jnp.bfloat16), values_all, preferred_element_type=jnp.float32
    )
    return (attended, attn_prob)


class Place:
    def __init__(self, n):
        self.n = n; self.nz = 4; self.m = {16: 2, 64: 4}[n]; m = self.m
        self.e = lax.axis_index("exp"); self.c = lax.axis_index("hid"); c = self.c; e = self.e
        self.s1 = m * m; self.s2 = 1 + c * (m - 1); self.s3 = m - c * (m - 1)
        self.c1 = e // self.s1; self.c2 = (e // self.s2) % m; self.c3 = (e // self.s3) % m
    def blk(self, a, b, d): return a * self.s1 + b * self.s2 + d * self.s3
    def o2(self): return [(self.c2 + j) % self.m for j in range(1, self.m)]
    def o3(self): return [(self.c3 + j) % self.m for j in range(1, self.m)]
    def enter(self):
        bar = pltpu.get_barrier_semaphore()
        c1, c2, c3 = self.c1, self.c2, self.c3
        def sig(p): pl.semaphore_signal(bar, inc=1, device_id=(p, self.c), device_id_type=MESH)
        for j in self.o2(): sig(self.blk(c1, j, c3))
        for j in self.o3(): sig(self.blk(c1, c2, j))
        for j in range(1, self.nz): sig(self.blk((c1 + j) % self.nz, c2, c3))
        pl.semaphore_wait(bar, 2 * (self.m - 1) + self.nz - 1)

class Gather:
    def __init__(self, pc, src, dst, ssem, rsem, split, base=0):
        self.pc, self.src, self.dst, self.ssem, self.rsem = pc, src, dst, ssem, rsem
        self.split = split; self.sends = []; self.base = base
    def view(self, ref, part):
        R = self.src.shape[0]
        return ref.at[pl.ds(0, self.split)] if part == 0 else ref.at[pl.ds(self.split, R - self.split)]
    def send(self, part, own, b, to, cond=None):
        i = self.base + len(self.sends)
        src = self.view(self.src if own else self.dst.at[b], part)
        cp = pltpu.make_async_remote_copy(src_ref=src, dst_ref=self.view(self.dst.at[b], part), send_sem=self.ssem.at[i], recv_sem=self.rsem.at[part, b], device_id=(to, self.pc.c), device_id_type=MESH)
        self.sends.append((cond, cp))
        if cond is None: cp.start()
        else: pl.when(cond)(cp.start)
    def wait(self, part, b):
        v = self.view(self.dst.at[b], part)
        pltpu.make_async_copy(v, v, self.rsem.at[part, b]).wait()
    def updown(self, part, own, b):
        pc = self.pc
        self.send(part, own, b, pc.blk(pc.c1 + 1, pc.c2, pc.c3), pc.c1 < pc.nz - 1)
        self.send(part, own, b, pc.blk(pc.c1 - 1, pc.c2, pc.c3), pc.c1 > 0)
    def to2(self, part, own, b):
        pc = self.pc
        for j in pc.o2(): self.send(part, own, b, pc.blk(pc.c1, j, pc.c3))
    def to3(self, part, own, b):
        pc = self.pc
        for j in pc.o3(): self.send(part, own, b, pc.blk(pc.c1, pc.c2, j))
    def start(self):
        e = self.pc.e
        self.to3(0, True, e); self.to2(0, True, e); self.updown(0, True, e)
        if self.split < self.src.shape[0]:
            self.to3(1, True, e); self.to2(1, True, e); self.updown(1, True, e)
    def zarr(self, part, s, up, k2, k3, more):
        pc = self.pc
        a = pc.c1 - s if up else pc.c1 + s
        cond = (pc.c1 >= s) if up else (pc.c1 < pc.nz - s)
        b = pc.blk(a, k2, k3)
        pl.when(cond)(lambda: self.wait(part, b))
        if s < pc.nz - 1:
            if up: self.send(part, False, b, pc.blk(pc.c1 + 1, pc.c2, pc.c3), (pc.c1 >= s) & (pc.c1 < pc.nz - 1))
            else: self.send(part, False, b, pc.blk(pc.c1 - 1, pc.c2, pc.c3), (pc.c1 < pc.nz - s) & (pc.c1 > 0))
        if more:
            for j in pc.o2(): self.send(part, False, b, pc.blk(pc.c1, j, pc.c3), cond)
            for j in pc.o3(): self.send(part, False, b, pc.blk(pc.c1, pc.c2, j), cond)
    def events(self):
        pc = self.pc; ev = []
        def a2(s):
            def go():
                for j in pc.o2():
                    for sg in ((1, -1) if s else (1,)):
                        a = pc.c1 + sg * s
                        cond = None if s == 0 else ((a >= 0) & (a < pc.nz))
                        b = pc.blk(a, j, pc.c3)
                        if cond is None: self.wait(0, b)
                        else: pl.when(cond)(lambda b=b: self.wait(0, b))
                        for k in pc.o3(): self.send(0, False, b, pc.blk(pc.c1, pc.c2, k), cond)
            return go
        def az(s):
            def go():
                self.zarr(0, s, True, pc.c2, pc.c3, True); self.zarr(0, s, False, pc.c2, pc.c3, True)
            return go
        B = self.split < self.src.shape[0]
        def f1():
            for j in pc.o2():
                b = pc.blk(pc.c1, j, pc.c3); self.wait(1, b); self.to3(1, False, b); self.updown(1, False, b)
        def f2():
            for k in pc.o3():
                b = pc.blk(pc.c1, pc.c2, k); self.wait(1, b); self.updown(1, False, b)
        def f3():
            for j in pc.o2():
                for k in pc.o3():
                    b = pc.blk(pc.c1, j, k); self.wait(1, b); self.updown(1, False, b)
        def fz(s):
            def go():
                for k2 in range(pc.m):
                    for k3 in range(pc.m):
                        self.zarr(1, s, True, k2, k3, False); self.zarr(1, s, False, k2, k3, False)
            return go
        ev += [az(1), a2(0)]
        if B: ev += [f1, f2, f3]
        ev += [az(2), a2(1)]
        if B: ev += [fz(1)]
        ev += [az(3), a2(2)]
        if B: ev += [fz(2)]
        ev += [a2(3)]
        if B: ev += [fz(3)]
        def last():
            for a in range(pc.nz):
                for j in range(pc.m):
                    for k in pc.o3(): self.wait(0, pc.blk(a, j, k))
        ev += [last]
        return ev
    def finish(self):
        for cond, cp in self.sends:
            if cond is None: cp.wait_send()
            else: pl.when(cond)(cp.wait_send)


def gather_kernel(n, x_ref, w_ref, ox_ref, ow_ref, ssem, rsem, lsem):
    pc = Place(n)
    pc.enter()
    rows = x_ref.shape[0]
    first = Gather(pc, x_ref, ox_ref, ssem.at[0], rsem.at[0], rows)
    second = Gather(pc, w_ref, ow_ref, ssem.at[1], rsem.at[1], rows)
    first.start()
    second.start()
    own_x = pltpu.make_async_copy(x_ref, ox_ref.at[pc.e], lsem.at[0])
    own_w = pltpu.make_async_copy(w_ref, ow_ref.at[pc.e], lsem.at[1])
    own_x.start()
    own_w.start()
    for event in first.events():
        event()
    for event in second.events():
        event()
    first.finish()
    second.finish()
    own_x.wait()
    own_w.wait()


def gather_both(x, w):
    n = lax.axis_size("exp")
    any_spec = pl.BlockSpec(memory_space=pl.ANY)
    return pl.pallas_call(
        functools.partial(gather_kernel, n),
        out_shape=(jax.ShapeDtypeStruct((n,) + x.shape, x.dtype), jax.ShapeDtypeStruct((n,) + w.shape, w.dtype)),
        in_specs=[any_spec, any_spec],
        out_specs=(any_spec, any_spec),
        scratch_shapes=[
            pltpu.SemaphoreType.DMA((2, 128)),
            pltpu.SemaphoreType.DMA((2, 2, n)),
            pltpu.SemaphoreType.DMA((2,)),
        ],
        compiler_params=pltpu.CompilerParams(collective_id=0, has_side_effects=True),
    )(x, w)


def experts_kernel(
    n, slots,
    h_hbm, dy_hbm, gate_ref, wg, wu, wd,
    s_ref, sums_hbm, gg_hbm, gu_hbm, gd_hbm, pg_hbm, pu_hbm, pd_hbm, r3_hbm, r2_hbm, r1_hbm,
    og, ou, od, ysum, hbuf, dbuf, act, dg, dup, stage, rbuf, xg, xu, xd,
    lsem, ssem, r3sem, r2sem, r1sem, bsem, xssem, xrsem, osem,
):
    pc = Place(n)
    nz, m = pc.nz, pc.m
    c1, c2, c3, e, c = pc.c1, pc.c2, pc.c3, pc.e, pc.c
    barrier = pltpu.get_barrier_semaphore()

    def greet(to, core):
        pl.semaphore_signal(barrier, inc=1, device_id=(to, core), device_id_type=MESH)

    for j in range(1, m):
        greet(pc.blk(c1, c2, (c3 + j) % m), c)
        greet(pc.blk(c1, (c2 + j) % m, c3), c)
    for j in range(1, nz):
        greet(pc.blk((c1 + j) % nz, c2, c3), c)
    greet(e, 1 - c)
    pl.semaphore_wait(barrier, 2 * (m - 1) + nz)

    og[...] = jnp.zeros_like(og)
    ou[...] = jnp.zeros_like(ou)
    od[...] = jnp.zeros_like(od)
    s_ref[...] = jnp.zeros_like(s_ref)
    n3 = (m - 1) * nz * m
    n2 = (m - 1) * nz

    def dest(t):
        return (c1 + t + 1) % nz, (c2 + t // nz + 1) % m, (c3 + t // (nz * m) + 1) % m

    def load(t, i):
        b = pc.blk(*dest(t))
        return (
            pltpu.make_async_copy(h_hbm.at[b], hbuf.at[i], lsem.at[0, i]),
            pltpu.make_async_copy(dy_hbm.at[b], dbuf.at[i], lsem.at[1, i]),
        )

    def partial_copy(i, to, dst, sem):
        return pltpu.make_async_remote_copy(
            src_ref=stage.at[i], dst_ref=dst, send_sem=ssem.at[i], recv_sem=sem,
            device_id=(to, c), device_id_type=MESH,
        )

    def add_received(src, sem):
        pltpu.make_async_remote_copy(
            src_ref=src, dst_ref=src, send_sem=ssem.at[0], recv_sem=sem,
            device_id=(e, 1 - c), device_id_type=MESH,
        ).wait_recv()
        copy = pltpu.make_async_copy(src, rbuf, bsem)
        copy.start()
        copy.wait()
        ysum[...] += rbuf[...].astype(jnp.float32)

    def swaps():
        return [
            pltpu.make_async_remote_copy(
                src_ref=src, dst_ref=dst, send_sem=xssem.at[i], recv_sem=xrsem.at[i],
                device_id=(e, 1 - c), device_id_type=MESH,
            )
            for i, (src, dst) in enumerate(((xg, pg_hbm), (xu, pu_hbm), (xd, pd_hbm)))
        ]

    def own_halves():
        return [
            pltpu.make_async_copy(src.at[c], dst, osem.at[i])
            for i, (src, dst) in enumerate(((og, gg_hbm), (ou, gu_hbm), (od, gd_hbm)))
        ]

    for copy in load(0, 0):
        copy.start()

    def body(t, carry):
        i = t % 2
        slot = t % slots
        a, b2, b3 = dest(t)
        b = pc.blk(a, b2, b3)
        for copy in load(t, i):
            copy.wait()

        @pl.when(t < n - 1)
        def _():
            for copy in load(t + 1, 1 - i):
                copy.start()

        lane = lax.broadcasted_iota(jnp.int32, gate_ref.shape, 1)
        gate = jnp.sum(jnp.where(lane == b, gate_ref[...], 0.0), axis=1, keepdims=True)
        h = hbuf[i]
        dy = dbuf[i].astype(jnp.float32)
        z = (gate * dy).astype(jnp.bfloat16)
        for half in range(2):
            g = matmul(h, wg[half])
            u = matmul(h, wu[half])
            da = inner_cols(z, wd[half])
            sg = jax.nn.sigmoid(g)
            si = g * sg
            act[half] = (si * u).astype(jnp.bfloat16)
            dup[half] = (da * si).astype(jnp.bfloat16)
            dg[half] = (da * u * sg * (1.0 + g * (1.0 - sg))).astype(jnp.bfloat16)
        y = (matmul(act[0], wd[0]) + matmul(act[1], wd[1])).astype(jnp.bfloat16).astype(jnp.float32)
        s = jnp.sum(y * dy, axis=1, keepdims=True)
        s_ref[...] = jnp.where(lane == b, s, s_ref[...])
        ysum[0] = gate * y
        ysum[1] = (
            inner_cols(dg[0], wg[0]) + inner_cols(dg[1], wg[1])
            + inner_cols(dup[0], wu[0]) + inner_cols(dup[1], wu[1])
        ).astype(jnp.bfloat16).astype(jnp.float32)

        @pl.when((t >= slots) & (t - slots < n - 1))
        def _():
            partial_copy(slot, e, r1_hbm.at[0], r1sem.at[0]).wait_send()

        @pl.when(t >= n3)
        def _():
            for j in range(1, m):
                add_received(r3_hbm.at[j - 1, a, b2], r3sem.at[j - 1, a, b2])

        @pl.when(t >= n3 + n2)
        def _():
            for j in range(1, m):
                add_received(r2_hbm.at[j - 1, a], r2sem.at[j - 1, a])

        @pl.when(t < n - 1)
        def _():
            stage[slot] = ysum[...].astype(jnp.bfloat16)

        for j in range(1, m):
            @pl.when((t < n3) & (b3 == (c3 + j) % m))
            def _():
                partial_copy(slot, pc.blk(c1, c2, b3), r3_hbm.at[m - j - 1, a, b2], r3sem.at[m - j - 1, a, b2]).start()

            @pl.when((t >= n3) & (t < n3 + n2) & (b2 == (c2 + j) % m))
            def _():
                partial_copy(slot, pc.blk(c1, b2, c3), r2_hbm.at[m - j - 1, a], r2sem.at[m - j - 1, a]).start()

        for j in range(1, nz):
            @pl.when((t >= n3 + n2) & (t < n - 1) & (a == (c1 + j) % nz))
            def _():
                partial_copy(slot, pc.blk(a, c2, c3), r1_hbm.at[nz - j - 1], r1sem.at[nz - j - 1]).start()

        for half in range(2):
            og[half] += outer_rows(h, dg[half])
            ou[half] += outer_rows(h, dup[half])
            od[half] += outer_rows(act[half], z)
        return carry

    lax.fori_loop(0, n, body, 0)
    xg[...] = og[1 - c].astype(jnp.bfloat16)
    xu[...] = ou[1 - c].astype(jnp.bfloat16)
    xd[...] = od[1 - c].astype(jnp.bfloat16)
    for copy in swaps():
        copy.start()
    for copy in own_halves():
        copy.start()
    for j in range(1, nz):
        add_received(r1_hbm.at[j - 1], r1sem.at[j - 1])
    final = pltpu.make_async_copy(ysum, sums_hbm, bsem)
    final.start()
    final.wait()
    for t in range(max(0, n - slots), n - 1):
        partial_copy(t % slots, e, r1_hbm.at[0], r1sem.at[0]).wait_send()
    for copy in swaps():
        copy.wait()
    for copy in own_halves():
        copy.wait()


def experts(h, dy, gates, wg, wu, wd):
    n, rows, width = h.shape
    hidden = wg.shape[2]
    nz = 4
    m = {16: 2, 64: 4}[n]
    slots = 8
    vmem = pl.BlockSpec(memory_space=pltpu.VMEM)
    hbm = pl.BlockSpec(memory_space=pl.ANY)
    f32, b16 = jnp.float32, jnp.bfloat16
    out = jax.ShapeDtypeStruct
    return pl.pallas_call(
        functools.partial(experts_kernel, n, slots),
        out_shape=(
            out((rows, n), f32), out((2, rows, width), f32),
            out((width, hidden), f32), out((width, hidden), f32), out((hidden, width), f32),
            out((width, hidden), b16), out((width, hidden), b16), out((hidden, width), b16),
            out((m - 1, nz, m, 2, rows, width), b16), out((m - 1, nz, 2, rows, width), b16), out((nz - 1, 2, rows, width), b16),
        ),
        in_specs=[hbm, hbm, vmem, vmem, vmem, vmem],
        out_specs=(vmem,) + (hbm,) * 10,
        scratch_shapes=[
            pltpu.VMEM((2, width, hidden), f32), pltpu.VMEM((2, width, hidden), f32), pltpu.VMEM((2, hidden, width), f32),
            pltpu.VMEM((2, rows, width), f32), pltpu.VMEM((2, rows, width), b16), pltpu.VMEM((2, rows, width), b16),
            pltpu.VMEM((2, rows, hidden), b16), pltpu.VMEM((2, rows, hidden), b16), pltpu.VMEM((2, rows, hidden), b16),
            pltpu.VMEM((slots, 2, rows, width), b16), pltpu.VMEM((2, rows, width), b16),
            pltpu.VMEM((width, hidden), b16), pltpu.VMEM((width, hidden), b16), pltpu.VMEM((hidden, width), b16),
            pltpu.SemaphoreType.DMA((2, 2)), pltpu.SemaphoreType.DMA((slots,)),
            pltpu.SemaphoreType.DMA((m - 1, nz, m)), pltpu.SemaphoreType.DMA((m - 1, nz)), pltpu.SemaphoreType.DMA((nz - 1,)),
            pltpu.SemaphoreType.DMA, pltpu.SemaphoreType.DMA((3,)), pltpu.SemaphoreType.DMA((3,)), pltpu.SemaphoreType.DMA((3,)),
        ],
        compiler_params=pltpu.CompilerParams(collective_id=1, has_side_effects=True, vmem_limit_bytes=60 * 2**20),
    )(h, dy, gates, wg, wu, wd)


def swap_halves(values):
    return pltpu.roll(values, HD // 2, axis=1)


class Scatter:
    def __init__(self, pc, stack, r3, r2, r1, sems):
        self.pc, self.stack, self.r3, self.r2, self.r1 = pc, stack, r3, r2, r1
        self.ssem, self.s3, self.s2, self.s1 = sems

    def copy(self, b, dst, sem, to):
        return pltpu.make_async_remote_copy(
            src_ref=self.stack.at[b], dst_ref=dst, send_sem=self.ssem.at[b], recv_sem=sem,
            device_id=(to, self.pc.c), device_id_type=MESH,
        )

    def add(self, total, src, sem):
        self.copy(self.pc.e, src, sem, self.pc.blk(self.pc.c1, self.pc.c2, self.pc.o3()[0])).wait_recv()
        return total + src[...].astype(jnp.float32)

    def places(self):
        pc = self.pc
        far = [pc.c1 + j for j in range(1, pc.nz)] + [pc.c1]
        return [a % pc.nz for a in far]

    def start(self):
        pc = self.pc
        for k in range(1, pc.m):
            for b2 in pc.o2() + [pc.c2]:
                for a in self.places():
                    b3 = (pc.c3 + k) % pc.m
                    self.copy(pc.blk(a, b2, b3), self.r3.at[pc.m - k - 1, a, b2], self.s3.at[pc.m - k - 1, a, b2], pc.blk(pc.c1, pc.c2, b3)).start()

    def collect(self, a, b2, level):
        pc = self.pc
        total = self.stack[pc.blk(a, b2, pc.c3)].astype(jnp.float32)
        for k in range(pc.m - 1):
            total = self.add(total, self.r3.at[k, a, b2], self.s3.at[k, a, b2])
        if level >= 2:
            for k in range(pc.m - 1):
                total = self.add(total, self.r2.at[k, a], self.s2.at[k, a])
        if level >= 3:
            for k in range(pc.nz - 1):
                total = self.add(total, self.r1.at[k], self.s1.at[k])
        self.stack[pc.blk(a, b2, pc.c3)] = total.astype(jnp.bfloat16)

    def second(self):
        pc = self.pc
        for k in range(1, pc.m):
            for a in self.places():
                b2 = (pc.c2 + k) % pc.m
                self.collect(a, b2, 1)
                self.copy(pc.blk(a, b2, pc.c3), self.r2.at[pc.m - k - 1, a], self.s2.at[pc.m - k - 1, a], pc.blk(pc.c1, b2, pc.c3)).start()

    def third(self):
        pc = self.pc
        for k in range(1, pc.nz):
            a = (pc.c1 + k) % pc.nz
            self.collect(a, pc.c2, 2)
            self.copy(pc.blk(a, pc.c2, pc.c3), self.r1.at[pc.nz - k - 1], self.s1.at[pc.nz - k - 1], pc.blk(a, pc.c2, pc.c3)).start()

    def last(self):
        self.collect(self.pc.c1, self.pc.c2, 3)

    def finish(self):
        pc = self.pc
        for j in range(1, pc.n):
            self.copy((pc.e + j) % pc.n, self.r1.at[0], self.s1.at[0], (pc.e + j) % pc.n).wait_send()


def tail_kernel(
    n,
    x_ref, x1_ref, cot_ref, sums_ref, q_ref, k_ref, v_ref, o_ref, p_ref, wq, wk, wv, wo,
    gain1, gain2, cos_ref, sin_ref, cnt_ref, sg_hbm, su_hbm, sd_hbm,
    out_ref, gtok_ref, small_ref, ag0, ag1, agg, agu, agd,
    dx_ref, dq_ref, dk_ref, dv_ref, do_ref, a_ref, give, take, stack0, stack1, r3, r2, r1,
    sm_core, sm_d3, sm_d2, sm_z,
    wbuf, wsem,
    gs, gr, ss, s3, s2, s1, xs, xr, cs, cr, scs, scr, locs,
):
    pc = Place(n)
    c1, c2, c3, e, c, nz, m = pc.c1, pc.c2, pc.c3, pc.e, pc.c, pc.nz, pc.m
    rows, width = x_ref.shape
    half = width // 2
    barrier = pltpu.get_barrier_semaphore()

    def greet(j, carry):
        pl.semaphore_signal(barrier, inc=1, device_id=((e + j) % n, c), device_id_type=MESH)
        return carry

    lax.fori_loop(1, n, greet, 0)
    pl.semaphore_signal(barrier, inc=1, device_id=(e, 1 - c), device_id_type=MESH)
    pl.semaphore_wait(barrier, n)

    shared = ((sg_hbm, agg), (su_hbm, agu), (sd_hbm, agd))

    def deal(i, to):
        src, dst = shared[i]
        return pltpu.make_async_remote_copy(
            src_ref=src.at[to], dst_ref=dst.at[to], send_sem=scs.at[i, to], recv_sem=scr.at[i],
            device_id=(to, c), device_id_type=MESH,
        )

    def keep(i):
        src, dst = shared[i]
        return pltpu.make_async_copy(src.at[n - 1], dst.at[n - 1], scs.at[i, n - 1])

    @pl.when(e == n - 1)
    def _():
        def one(j, carry):
            for i in range(3):
                deal(i, n - 2 - j).start()
            return carry

        lax.fori_loop(0, n - 1, one, 0)
        for i in range(3):
            keep(i).start()

    gathers = [Gather(pc, dst.at[e], dst, gs.at[i], gr.at[i], dst.shape[1]) for i, (src, dst) in enumerate(shared)]

    def shared_start():
        @pl.when(e == n - 1)
        def _():
            for i in range(3):
                keep(i).wait()

        @pl.when(e != n - 1)
        def _():
            for i in range(3):
                src, dst = shared[i]
                pltpu.make_async_remote_copy(
                    src_ref=dst.at[e], dst_ref=dst.at[e], send_sem=scs.at[i, 0], recv_sem=scr.at[i],
                    device_id=(n - 1, c), device_id_type=MESH,
                ).wait_recv()

        for g in gathers:
            g.start()

    def fetch(src, i):
        return pltpu.make_async_copy(src, wbuf.at[i], wsem.at[i])

    fetch(wo, 0).start()
    fetch(wv, 1).start()

    x1 = x1_ref[...]
    up = cot_ref[...].astype(jnp.float32)
    out_ref[...] = (x1 + sums_ref[0]).astype(jnp.bfloat16)
    dh = sums_ref[1]
    r_two = lax.rsqrt(jnp.mean(x1 * x1, axis=-1, keepdims=True) + norm_eps)
    n_two = x1 * r_two
    scaled = dh * gain2[...]
    grad_two = jnp.sum(dh * n_two, axis=0, keepdims=True)
    dx = up + r_two * (scaled - n_two * jnp.mean(scaled * n_two, axis=-1, keepdims=True))
    dx_ref[...] = dx
    dx_low = dx.astype(jnp.bfloat16)

    def columns(ref, which):
        return ref[:, pl.ds(pl.multiple_of(which * half, 128), half)]

    def hand(i):
        return pltpu.make_async_remote_copy(
            src_ref=give.at[i], dst_ref=take.at[i], send_sem=xs.at[i], recv_sem=xr.at[i],
            device_id=(e, 1 - c), device_id_type=MESH,
        )

    def to_partner(i, left, right):
        give[i] = outer_rows(columns(left, 1 - c), right).astype(jnp.bfloat16)
        hand(i).start()

    def own_part(i, left, right, stack, at):
        block = stack.shape[1]
        part = outer_rows(columns(left, c), right)
        hand(i).wait_recv()
        total = (part + take[i].astype(jnp.float32)).astype(jnp.bfloat16)
        stack[pl.ds(at * (half // block), half // block)] = total.reshape(half // block, block, width)

    to_partner(0, o_ref, dx_low)
    fetch(wo, 0).wait()
    do_ref[...] = inner_cols(dx_low, wbuf[0]).astype(jnp.bfloat16)
    fetch(wk, 0).start()
    cosine, sine = cos_ref[...], sin_ref[...]
    scale = HD ** (-0.5)

    def one_head(hd, carry):
        at = pl.ds(pl.multiple_of(hd * HD, HD), HD)
        prob = p_ref[hd]
        d_o, val, que, key = do_ref[:, at], v_ref[:, at], q_ref[:, at], k_ref[:, at]
        dv_ref[:, at] = outer_rows(prob.astype(jnp.bfloat16), d_o).astype(jnp.bfloat16)
        d_prob = inner_cols(d_o, val)
        inner = jnp.sum(prob * d_prob, axis=-1, keepdims=True)
        d_score = (prob * (d_prob - inner)).astype(jnp.bfloat16)
        d_q = matmul(d_score, key) * scale
        d_k = outer_rows(d_score, que) * scale
        dq_ref[:, at] = (d_q * cosine - swap_halves(d_q) * sine).astype(jnp.bfloat16)
        dk_ref[:, at] = (d_k * cosine - swap_halves(d_k) * sine).astype(jnp.bfloat16)
        return carry

    lax.fori_loop(0, HEADS, one_head, 0)
    xv = x_ref[...].astype(jnp.float32)
    r_one = lax.rsqrt(jnp.mean(xv * xv, axis=-1, keepdims=True) + norm_eps)
    n_one = xv * r_one
    a_ref[...] = (n_one * gain1[...]).astype(jnp.bfloat16)
    to_partner(1, a_ref, dv_ref[...])
    to_partner(2, a_ref, dk_ref[...])
    to_partner(3, a_ref, dq_ref[...])
    if n * stack0.shape[1] > 2 * half:
        stack0[...] = jnp.zeros_like(stack0)
        stack1[...] = jnp.zeros_like(stack1)
    own_part(0, o_ref, dx_low, stack0, 0)
    own_part(1, a_ref, dv_ref[...], stack0, 1)
    first = Scatter(pc, stack0, r3.at[0], r2.at[0], r1.at[0], (ss.at[0], s3.at[0], s2.at[0], s1.at[0]))
    second = Scatter(pc, stack1, r3.at[1], r2.at[1], r1.at[1], (ss.at[1], s3.at[1], s2.at[1], s1.at[1]))
    first.start()
    shared_start()
    own_part(2, a_ref, dk_ref[...], stack1, 0)
    own_part(3, a_ref, dq_ref[...], stack1, 1)
    second.start()
    fetch(wv, 1).wait()
    da = inner_cols(dv_ref[...], wbuf[1])
    fetch(wq, 1).start()
    fetch(wk, 0).wait()
    da = da + inner_cols(dk_ref[...], wbuf[0])
    fetch(wq, 1).wait()
    da = da + inner_cols(dq_ref[...], wbuf[1])
    scaled_one = da * gain1[...]
    grad_one = jnp.sum(da * n_one, axis=0, keepdims=True)
    back = r_one * (scaled_one - n_one * jnp.mean(scaled_one * n_one, axis=-1, keepdims=True))
    gtok_ref[...] = (dx_ref[...] + back).astype(jnp.bfloat16)

    def exchange(ref, own, level, peers, value):
        ref[own] = value
        copies = [
            pltpu.make_async_remote_copy(
                src_ref=ref.at[own], dst_ref=ref.at[own], send_sem=cs.at[level, i], recv_sem=cr.at[level, own],
                device_id=to, device_id_type=MESH,
            )
            for i, (to, at) in enumerate(peers)
        ]
        for copy in copies:
            copy.start()

        def done():
            for i, (to, at) in enumerate(peers):
                pltpu.make_async_remote_copy(
                    src_ref=ref.at[own], dst_ref=ref.at[at], send_sem=cs.at[level, i], recv_sem=cr.at[level, at],
                    device_id=to, device_id_type=MESH,
                ).wait_recv()
            for copy in copies:
                copy.wait_send()
            total = ref[0]
            for i in range(1, ref.shape[0]):
                total = total + ref[i]
            return total

        return done

    small = jnp.concatenate([grad_one, grad_two, cnt_ref[...], jnp.zeros((5, width), jnp.float32)], axis=0)
    level0 = exchange(sm_core, c, 0, [((e, 1 - c), 1 - c)], small)
    first.second()
    level1 = exchange(sm_d3, c3, 1, [((pc.blk(c1, c2, j), c), j) for j in pc.o3()], level0())
    second.second()
    level2 = exchange(sm_d2, c2, 2, [((pc.blk(c1, j, c3), c), j) for j in pc.o2()], level1())
    first.third()
    level3 = exchange(sm_z, c1, 3, [((pc.blk((c1 + j) % nz, c2, c3), c), (c1 + j) % nz) for j in range(1, nz)], level2())
    second.third()
    small_ref[...] = level3()

    events = [g.events() for g in gathers]
    for i in range(len(events[0])):
        for ev in events:
            ev[i]()
    first.last()
    g0 = Gather(pc, stack0.at[e], ag0, gs.at[3], gr.at[3], stack0.shape[1])
    g0.start()
    loc0 = pltpu.make_async_copy(stack0.at[e], ag0.at[e], locs.at[0])
    loc0.start()
    second.last()
    g1 = Gather(pc, stack1.at[e], ag1, gs.at[4], gr.at[4], stack1.shape[1])
    g1.start()
    loc1 = pltpu.make_async_copy(stack1.at[e], ag1.at[e], locs.at[1])
    loc1.start()
    ev0, ev1 = g0.events(), g1.events()
    for i in range(len(ev0)):
        ev0[i]()
        ev1[i]()
    for g in gathers + [g0, g1]:
        g.finish()
    first.finish()
    second.finish()
    loc0.wait()
    loc1.wait()
    for i in range(4):
        hand(i).wait_send()

    @pl.when(e == n - 1)
    def _():
        def one(j, carry):
            for i in range(3):
                deal(i, j).wait_send()
            return carry

        lax.fori_loop(0, n - 1, one, 0)


def tail(n, x, x1, cot, sums, q, k, v, o, prob, wq, wk, wv, wo, gain1, gain2, cosine, sine, cnt, sg, su, sd):
    nz = 4
    m = {16: 2, 64: 4}[n]
    rows, width = x.shape
    half = width // 2
    block = blocked(2 * half, n)
    vmem = pl.BlockSpec(memory_space=pltpu.VMEM)
    hbm = pl.BlockSpec(memory_space=pl.ANY)
    f32, b16 = jnp.float32, jnp.bfloat16
    out = jax.ShapeDtypeStruct
    dma = pltpu.SemaphoreType.DMA
    wide = pltpu.VMEM((rows, width), b16)
    return pl.pallas_call(
        functools.partial(tail_kernel, n),
        out_shape=(
            out((rows, width), b16), out((rows, width), b16), out((8, width), f32),
            out((n, block, width), b16), out((n, block, width), b16),
            out(sg.shape, b16), out(su.shape, b16), out(sd.shape, b16),
        ),
        in_specs=[vmem] * 9 + [hbm] * 4 + [vmem] * 5 + [hbm] * 3,
        out_specs=(vmem, vmem, vmem) + (hbm,) * 5,
        scratch_shapes=[
            pltpu.VMEM((rows, width), f32), wide, wide, wide, wide, wide,
            pltpu.VMEM((4, half, width), b16), pltpu.VMEM((4, half, width), b16),
            pltpu.VMEM((n, block, width), b16), pltpu.VMEM((n, block, width), b16),
            pltpu.VMEM((2, m - 1, nz, m, block, width), b16), pltpu.VMEM((2, m - 1, nz, block, width), b16),
            pltpu.VMEM((2, nz - 1, block, width), b16),
            pltpu.VMEM((2, 8, width), f32), pltpu.VMEM((m, 8, width), f32), pltpu.VMEM((m, 8, width), f32), pltpu.VMEM((nz, 8, width), f32),
            pltpu.VMEM((2, width, width), b16), dma((2,)),
            dma((5, 160)), dma((5, 1, n)), dma((2, n)), dma((2, m - 1, nz, m)), dma((2, m - 1, nz)), dma((2, nz - 1)),
            dma((4,)), dma((4,)), dma((4, max(nz, m))), dma((4, max(nz, m, 2))), dma((3, n)), dma((3,)), dma((2,)),
        ],
        compiler_params=pltpu.CompilerParams(collective_id=2, has_side_effects=True, vmem_limit_bytes=62 * 2**20),
    )(x, x1, cot, sums, q, k, v, o, prob, wq, wk, wv, wo, gain1, gain2, cosine, sine, cnt, sg, su, sd)


def blocked(count, n):
    return -(-count // (16 * n)) * 16


def to_blocks(values, n):
    block = blocked(values.shape[0], n)
    padded = jnp.pad(values.astype(jnp.bfloat16), ((0, n * block - values.shape[0]), (0, 0)))
    return padded.reshape(n, block, values.shape[1])


def from_blocks(blocks, count):
    return blocks.reshape(-1, blocks.shape[2])[:count].astype(jnp.float32)


def on_device(
    tokens,
    norm_one,
    w_query,
    w_key,
    w_value,
    w_out,
    norm_two,
    r_gate,
    r_up,
    r_down,
    s_gate,
    s_up,
    s_down,
    logits,
    routes,
    lengths,
    cotangent,
):
    seq_len = tokens.shape[0]
    width = tokens.shape[1]
    slot_count = lax.axis_size("exp")
    seq_length = lengths[0]
    inputs_full = tokens.astype(jnp.float32)
    full_query, full_key, full_value, full_out = (
        lax.all_gather(w_query, "hid", axis=0, tiled=True),
        lax.all_gather(w_key, "hid", axis=0, tiled=True),
        lax.all_gather(w_value, "hid", axis=0, tiled=True),
        lax.all_gather(w_out, "hid", axis=0, tiled=True),
    )
    normed_one, scale_one = rms_parts(inputs_full)
    attn_in = (normed_one * norm_one).astype(jnp.bfloat16)
    cosine_table, sine_table = rotary_tables(seq_len, HD)
    heads_shape = (seq_len, HEADS, HD)
    queries = rotate(
        matmul(attn_in, full_query).reshape(heads_shape), cosine_table, sine_table
    ).astype(jnp.bfloat16)
    keys_all = rotate(
        matmul(attn_in, full_key).reshape(heads_shape), cosine_table, sine_table
    ).astype(jnp.bfloat16)
    values_all = matmul(attn_in, full_value).reshape(heads_shape).astype(jnp.bfloat16)
    attended, attn_prob = attend_forward(queries, keys_all, values_all, seq_length)
    attended_low = attended.reshape(seq_len, width).astype(jnp.bfloat16)
    mixed = inputs_full + matmul(attended_low, full_out)
    normed_two, scale_two = rms_parts(mixed)
    hidden_in = (normed_two * norm_two).astype(jnp.bfloat16)
    onehot = (routes[:, :, None] == jnp.arange(slot_count)[None, None, :]).astype(jnp.float32)
    token_valid = (jnp.arange(seq_len) < seq_length).astype(jnp.float32)
    soft_gates = jax.nn.softmax(logits, axis=-1)
    gate_share = soft_gates * token_valid[:, None]
    local_counts = jnp.sum(onehot * token_valid[:, None, None], axis=(0, 1))
    is_last = jnp.arange(slot_count) == slot_count - 1
    own_gates = jnp.where(is_last[None, :], 1.0, jnp.sum(onehot * gate_share[:, :, None], axis=1))
    gates = lax.all_to_all(own_gates.T, "exp", split_axis=0, concat_axis=0, tiled=True).T
    holds_shared = lax.axis_index("exp") == slot_count - 1
    wg, wu, wd = (
        lax.all_gather(jnp.where(holds_shared, shared, routed[0]), "hid", axis=0)
        for shared, routed in ((s_gate, r_gate), (s_up, r_up), (s_down, r_down))
    )
    all_dy, all_h = gather_both(cotangent, hidden_in)
    scores_e, sums, gg, gu, gd, pg, pu, pd = experts(all_h, all_dy, gates, wg, wu, wd)[:8]
    slot_grads = (gg + pg.astype(jnp.float32), gu + pu.astype(jnp.float32), gd + pd.astype(jnp.float32))
    scores = lax.all_to_all(scores_e.T, "exp", split_axis=0, concat_axis=0, tiled=True).T
    grad_share = jnp.sum(onehot * scores[:, None, :], axis=-1) * token_valid[:, None]
    grad_logits = soft_gates * (
        grad_share - jnp.sum(soft_gates * grad_share, axis=-1, keepdims=True)
    )
    flat = (seq_len, width)
    cosine = jnp.tile(cosine_table[:, 0], (1, 2))
    sine = jnp.concatenate([-sine_table[:, 0], sine_table[:, 0]], axis=1)
    count_row = jnp.pad(local_counts[None], ((0, 0), (0, width - slot_count)))
    output, grad_tokens, small_sums, sum0, sum1, sum_g, sum_u, sum_d = tail(
        slot_count, tokens, mixed, cotangent, sums, queries.reshape(flat), keys_all.reshape(flat),
        values_all.reshape(flat), attended_low, attn_prob, full_query, full_key, full_value, full_out,
        norm_one[None], norm_two[None], cosine, sine, count_row,
        to_blocks(slot_grads[0], slot_count), to_blocks(slot_grads[1], slot_count), to_blocks(slot_grads[2], slot_count),
    )
    half = width // 2
    wout_value = from_blocks(sum0, width)
    key_query = from_blocks(sum1, width)
    hidden = s_gate.shape[1]
    routed_grads = tuple(jnp.where(holds_shared, 0.0, grad)[None] for grad in slot_grads)
    return (
        output,
        grad_tokens,
        small_sums[0],
        key_query[half:],
        key_query[:half],
        wout_value[half:],
        wout_value[:half],
        small_sums[1],
        routed_grads[0],
        routed_grads[1],
        routed_grads[2],
        from_blocks(sum_g, width),
        from_blocks(sum_u, width),
        from_blocks(sum_d, hidden),
        grad_logits,
        small_sums[2, :slot_count].astype(jnp.int32),
    )


def solution(mesh):
    in_specs = (
        P(("exp", "hid"), None),
        P(),
        P("hid", None),
        P("hid", None),
        P("hid", None),
        P("hid", None),
        P(),
        P("exp", None, "hid"),
        P("exp", None, "hid"),
        P("exp", "hid", None),
        P(None, "hid"),
        P(None, "hid"),
        P("hid", None),
        P(("exp", "hid"), None),
        P(("exp", "hid"), None),
        P(("exp", "hid")),
        P(("exp", "hid"), None),
    )
    out_specs = (
        P(("exp", "hid"), None),
        P(("exp", "hid"), None),
        P(),
        P("hid", None),
        P("hid", None),
        P("hid", None),
        P("hid", None),
        P(),
        P("exp", None, "hid"),
        P("exp", None, "hid"),
        P("exp", "hid", None),
        P(None, "hid"),
        P(None, "hid"),
        P("hid", None),
        P(("exp", "hid"), None),
        P(),
    )
    return jax.shard_map(
        on_device, mesh=mesh, in_specs=in_specs, out_specs=out_specs, check_vma=False
    )
```

```python
import functools

import jax
import jax.numpy as jnp
import numpy as np
from jax import lax
from jax.experimental import pallas as pl
from jax.experimental.pallas import tpu as pltpu
from jax.sharding import PartitionSpec as P

HEADS = 10
HD = 128
MESH = pl.DeviceIdType.MESH


norm_eps = 1e-06
rotary_base = 10000.0
contract_rows = (((0,), (0,)), ((), ()))
contract_cols = (((1,), (1,)), ((), ()))


def matmul(left_side, right_side):
    return jnp.dot(left_side, right_side, preferred_element_type=jnp.float32)


def outer_rows(left_side, right_side):
    return lax.dot_general(left_side, right_side, contract_rows, preferred_element_type=jnp.float32)


def inner_cols(left_side, right_side):
    return lax.dot_general(left_side, right_side, contract_cols, preferred_element_type=jnp.float32)


class Place:
    def __init__(self, n):
        self.n = n; self.nz = 4; self.m = {16: 2, 64: 4}[n]; m = self.m
        self.e = lax.axis_index("exp"); self.c = lax.axis_index("hid"); c = self.c; e = self.e
        self.s1 = m * m; self.s2 = 1 + c * (m - 1); self.s3 = m - c * (m - 1)
        self.c1 = e // self.s1; self.c2 = (e // self.s2) % m; self.c3 = (e // self.s3) % m
    def blk(self, a, b, d): return a * self.s1 + b * self.s2 + d * self.s3
    def o2(self): return [(self.c2 + j) % self.m for j in range(1, self.m)]
    def o3(self): return [(self.c3 + j) % self.m for j in range(1, self.m)]
    def greet_all(self):
        barrier = pltpu.get_barrier_semaphore()

        def greet(j, carry):
            pl.semaphore_signal(barrier, inc=1, device_id=((self.e + j) % self.n, self.c), device_id_type=MESH)
            return carry

        lax.fori_loop(1, self.n, greet, 0)
        pl.semaphore_signal(barrier, inc=1, device_id=(self.e, 1 - self.c), device_id_type=MESH)
        pl.semaphore_wait(barrier, self.n)


class Gather:
    def __init__(self, pc, src, dst, ssem, rsem, split, base=0):
        self.pc, self.src, self.dst, self.ssem, self.rsem = pc, src, dst, ssem, rsem
        self.split = split; self.sends = []; self.base = base
    def view(self, ref, part):
        R = self.src.shape[0]
        return ref.at[pl.ds(0, self.split)] if part == 0 else ref.at[pl.ds(self.split, R - self.split)]
    def send(self, part, own, b, to, cond=None):
        i = self.base + len(self.sends)
        src = self.view(self.src if own else self.dst.at[b], part)
        cp = pltpu.make_async_remote_copy(src_ref=src, dst_ref=self.view(self.dst.at[b], part), send_sem=self.ssem.at[i], recv_sem=self.rsem.at[part, b], device_id=(to, self.pc.c), device_id_type=MESH)
        self.sends.append((cond, cp))
        if cond is None: cp.start()
        else: pl.when(cond)(cp.start)
    def wait(self, part, b):
        v = self.view(self.dst.at[b], part)
        to = self.pc.blk(self.pc.c1, self.pc.c2, self.pc.o3()[0])
        pltpu.make_async_remote_copy(src_ref=v, dst_ref=v, send_sem=self.ssem.at[0], recv_sem=self.rsem.at[part, b], device_id=(to, self.pc.c), device_id_type=MESH).wait_recv()
    def updown(self, part, own, b):
        pc = self.pc
        self.send(part, own, b, pc.blk(pc.c1 + 1, pc.c2, pc.c3), pc.c1 < pc.nz - 1)
        self.send(part, own, b, pc.blk(pc.c1 - 1, pc.c2, pc.c3), pc.c1 > 0)
    def to2(self, part, own, b):
        pc = self.pc
        for j in pc.o2(): self.send(part, own, b, pc.blk(pc.c1, j, pc.c3))
    def to3(self, part, own, b):
        pc = self.pc
        for j in pc.o3(): self.send(part, own, b, pc.blk(pc.c1, pc.c2, j))
    def start(self):
        e = self.pc.e
        self.to3(0, True, e); self.to2(0, True, e); self.updown(0, True, e)
        if self.split < self.src.shape[0]:
            self.to3(1, True, e); self.to2(1, True, e); self.updown(1, True, e)
    def zarr(self, part, s, up, k2, k3, more):
        pc = self.pc
        a = pc.c1 - s if up else pc.c1 + s
        cond = (pc.c1 >= s) if up else (pc.c1 < pc.nz - s)
        b = pc.blk(a, k2, k3)
        pl.when(cond)(lambda: self.wait(part, b))
        if s < pc.nz - 1:
            if up: self.send(part, False, b, pc.blk(pc.c1 + 1, pc.c2, pc.c3), (pc.c1 >= s) & (pc.c1 < pc.nz - 1))
            else: self.send(part, False, b, pc.blk(pc.c1 - 1, pc.c2, pc.c3), (pc.c1 < pc.nz - s) & (pc.c1 > 0))
        if more:
            for j in pc.o2(): self.send(part, False, b, pc.blk(pc.c1, j, pc.c3), cond)
            for j in pc.o3(): self.send(part, False, b, pc.blk(pc.c1, pc.c2, j), cond)
    def events(self):
        pc = self.pc; ev = []
        def a2(s):
            def go():
                for j in pc.o2():
                    for sg in ((1, -1) if s else (1,)):
                        a = pc.c1 + sg * s
                        cond = None if s == 0 else ((a >= 0) & (a < pc.nz))
                        b = pc.blk(a, j, pc.c3)
                        if cond is None: self.wait(0, b)
                        else: pl.when(cond)(lambda b=b: self.wait(0, b))
                        for k in pc.o3(): self.send(0, False, b, pc.blk(pc.c1, pc.c2, k), cond)
            return go
        def az(s):
            def go():
                self.zarr(0, s, True, pc.c2, pc.c3, True); self.zarr(0, s, False, pc.c2, pc.c3, True)
            return go
        B = self.split < self.src.shape[0]
        def f1():
            for j in pc.o2():
                b = pc.blk(pc.c1, j, pc.c3); self.wait(1, b); self.to3(1, False, b); self.updown(1, False, b)
        def f2():
            for k in pc.o3():
                b = pc.blk(pc.c1, pc.c2, k); self.wait(1, b); self.updown(1, False, b)
        def f3():
            for j in pc.o2():
                for k in pc.o3():
                    b = pc.blk(pc.c1, j, k); self.wait(1, b); self.updown(1, False, b)
        def fz(s):
            def go():
                for k2 in range(pc.m):
                    for k3 in range(pc.m):
                        self.zarr(1, s, True, k2, k3, False); self.zarr(1, s, False, k2, k3, False)
            return go
        ev += [az(1), a2(0)]
        if B: ev += [f1, f2, f3]
        ev += [az(2), a2(1)]
        if B: ev += [fz(1)]
        ev += [az(3), a2(2)]
        if B: ev += [fz(2)]
        ev += [a2(3)]
        if B: ev += [fz(3)]
        def last():
            for a in range(pc.nz):
                for j in range(pc.m):
                    for k in pc.o3(): self.wait(0, pc.blk(a, j, k))
        ev += [last]
        return ev
    def finish(self):
        for cond, cp in self.sends:
            if cond is None: cp.wait_send()
            else: pl.when(cond)(cp.wait_send)


def run_staggered(first, second, lag):
    for i in range(max(len(first), len(second) + lag)):
        if i < len(first):
            first[i]()
        if lag <= i < len(second) + lag:
            second[i - lag]()


def part_rows(rows):
    return rows


def front_kernel(
    n,
    x_ref, cot_hbm, gain1, gain2, cos_ref, sin_ref, len_ref, logit_ref, route_ref,
    wq, wk, wv, wo, rg, ru, rd, sg, su, sd,
    all_dy, all_h, fq, fk, fv, fo, fg, fu, fd,
    x1_ref, q_ref, k_ref, v_ref, o_ref, p_ref, gates_in, cnt_ref,
    wbuf, h_ref, rows_out,
    gs, gr, ls, ws, wr, wl, es, er, el, gss, grs,
):
    pc = Place(n)
    e, c = pc.e, pc.c
    rows, width = x_ref.shape
    half = width // 2
    pc.greet_all()
    gather_dy = Gather(pc, cot_hbm, all_dy, gs.at[0], gr.at[0], part_rows(rows))
    gather_h = Gather(pc, h_ref, all_h, gs.at[1], gr.at[1], part_rows(rows))
    gather_dy.start()
    own_dy = pltpu.make_async_copy(cot_hbm, all_dy.at[e], ls.at[0])
    own_dy.start()
    partner = (e, 1 - c)
    halves = (wq, wk, wv, wo)
    fulls = (fq, fk, fv, fo)

    def swap(i):
        return pltpu.make_async_remote_copy(
            src_ref=halves[i], dst_ref=wbuf.at[i, c], send_sem=ws.at[i], recv_sem=wr.at[i],
            device_id=partner, device_id_type=MESH,
        )

    def own(i):
        return pltpu.make_async_copy(halves[i], wbuf.at[i, c], wl.at[0, i])

    def keep(i):
        return pltpu.make_async_copy(wbuf.at[i], fulls[i], wl.at[1, i])

    experts_full = (fg, fu, fd)

    def expert_swap(i, src):
        return pltpu.make_async_remote_copy(
            src_ref=src, dst_ref=experts_full[i].at[c], send_sem=es.at[i], recv_sem=er.at[i],
            device_id=partner, device_id_type=MESH,
        )

    def expert_own(i, src):
        return pltpu.make_async_copy(src, experts_full[i].at[c], el.at[i])

    for i in range(4):
        swap(i).start()
        own(i).start()
    for i, (routed, shared) in enumerate(((rg, sg), (ru, su), (rd, sd))):
        @pl.when(e == n - 1)
        def _():
            expert_swap(i, shared).start()
            expert_own(i, shared).start()

        @pl.when(e != n - 1)
        def _():
            expert_swap(i, routed).start()
            expert_own(i, routed).start()

    lane = lax.broadcasted_iota(jnp.int32, (rows, 128), 1)
    row = lax.broadcasted_iota(jnp.int32, (rows, 128), 0)
    valid = (row < len_ref[...]).astype(jnp.float32)
    logits = logit_ref[...]
    raised = jnp.exp(logits - jnp.max(logits, axis=-1, keepdims=True))
    soft = raised / jnp.sum(raised, axis=-1, keepdims=True)
    routes = route_ref[...]
    dense = jnp.zeros((rows, 128), jnp.float32)
    named = jnp.zeros((rows, 128), jnp.float32)
    for i in range(routes.shape[1]):
        hit = lane == routes[:, i : i + 1]
        dense = dense + jnp.where(hit, soft[:, i : i + 1], 0.0)
        named = named + jnp.where(hit, 1.0, 0.0)
    dense = jnp.where(lane == n - 1, 1.0, dense * valid)
    cnt_ref[...] = jnp.zeros_like(cnt_ref)
    cnt_ref[:, 0:128] = jnp.sum(named * valid, axis=0, keepdims=True)
    turned = dense.T
    for i in range(n):
        rows_out[i] = turned[i : i + 1, :]
    gates_in[e] = rows_out[e]

    def gate_send(to):
        return pltpu.make_async_remote_copy(
            src_ref=rows_out.at[to], dst_ref=gates_in.at[e], send_sem=gss.at[to], recv_sem=grs.at[e],
            device_id=(to, c), device_id_type=MESH,
        )

    def gate_start(j, carry):
        gate_send((e + j) % n).start()
        return carry

    lax.fori_loop(1, n, gate_start, 0)

    xv = x_ref[...].astype(jnp.float32)
    a = (xv * lax.rsqrt(jnp.mean(xv * xv, axis=-1, keepdims=True) + norm_eps) * gain1[...]).astype(jnp.bfloat16)
    cosine, sine = cos_ref[...], sin_ref[...]

    def project(values, i):
        own(i).wait()
        swap(i).wait_recv()
        keep(i).start()
        return matmul(values[:, :half], wbuf[i, 0]) + matmul(values[:, half:], wbuf[i, 1])

    for i, ref in ((0, q_ref), (1, k_ref)):
        flat = project(a, i)
        for hd in range(HEADS):
            part = flat[:, hd * HD : (hd + 1) * HD]
            ref[:, hd * HD : (hd + 1) * HD] = (part * cosine + swap_halves(part) * sine).astype(jnp.bfloat16)
    v_ref[...] = project(a, 2).astype(jnp.bfloat16)
    events = gather_dy.events()
    events[0]()
    scale = HD ** (-0.5)
    row_pos = lax.broadcasted_iota(jnp.int32, (rows, rows), 0)
    col_pos = lax.broadcasted_iota(jnp.int32, (rows, rows), 1)
    length = jnp.concatenate([len_ref[...]] * (rows // 128), axis=1)
    allowed = (col_pos <= row_pos) & (col_pos < length)

    def one_head(hd, carry):
        at = pl.ds(pl.multiple_of(hd * HD, HD), HD)
        scores = jnp.where(allowed, inner_cols(q_ref[:, at], k_ref[:, at]) * scale, -1e30)
        up = jnp.exp(scores - jnp.max(scores, axis=-1, keepdims=True))
        prob = up / jnp.sum(up, axis=-1, keepdims=True)
        p_ref[hd] = prob
        o_ref[:, at] = matmul(prob.astype(jnp.bfloat16), v_ref[:, at]).astype(jnp.bfloat16)
        return carry

    lax.fori_loop(0, HEADS, one_head, 0)
    events[1]()
    x1 = xv + project(o_ref[...], 3)
    x1_ref[...] = x1
    h_ref[...] = (x1 * lax.rsqrt(jnp.mean(x1 * x1, axis=-1, keepdims=True) + norm_eps) * gain2[...]).astype(jnp.bfloat16)
    gather_h.start()
    own_h = pltpu.make_async_copy(h_ref, all_h.at[e], ls.at[1])
    own_h.start()
    run_staggered(events[2:], gather_h.events(), 2)

    def gate_wait(j, carry):
        pltpu.make_async_remote_copy(
            src_ref=rows_out.at[0], dst_ref=gates_in.at[(e + j) % n], send_sem=gss.at[0], recv_sem=grs.at[(e + j) % n],
            device_id=((e + j) % n, c), device_id_type=MESH,
        ).wait_recv()
        gate_send((e + j) % n).wait_send()
        return carry

    lax.fori_loop(1, n, gate_wait, 0)
    gather_dy.finish()
    gather_h.finish()
    own_dy.wait()
    own_h.wait()
    for i in range(4):
        swap(i).wait_send()
        keep(i).wait()
    for i, shared in enumerate((sg, su, sd)):
        expert_swap(i, shared).wait()
        expert_own(i, shared).wait()


def front(n, x, cot, gain1, gain2, cosine, sine, length, logits, routes, attn_w, routed_w, shared_w):
    rows, width = x.shape
    hidden = shared_w[0].shape[1]
    vmem = pl.BlockSpec(memory_space=pltpu.VMEM)
    hbm = pl.BlockSpec(memory_space=pl.ANY)
    f32, b16 = jnp.float32, jnp.bfloat16
    out = jax.ShapeDtypeStruct
    dma = pltpu.SemaphoreType.DMA
    wide = out((rows, width), b16)
    full = out((2, width // 2, width), b16)
    return pl.pallas_call(
        functools.partial(front_kernel, n),
        out_shape=(
            out((n, rows, width), b16), out((n, rows, width), b16), full, full, full, full,
            out((2, width, hidden), b16), out((2, width, hidden), b16), out((2, hidden, width), b16),
            out((rows, width), f32), wide, wide, wide, wide, out((HEADS, rows, rows), f32),
            out((n, 1, rows), f32), out((1, width), f32),
        ),
        in_specs=[vmem, hbm] + [vmem] * 7 + [hbm] * 10,
        out_specs=(hbm,) * 9 + (vmem,) * 8,
        scratch_shapes=[
            pltpu.VMEM((4, 2, width // 2, width), b16), pltpu.VMEM((rows, width), b16), pltpu.VMEM((n, 1, rows), f32),
            dma((2, 160)), dma((2, 2, n)), dma((2,)), dma((4,)), dma((4,)), dma((2, 4)), dma((3,)), dma((3,)), dma((3,)),
            dma((n,)), dma((n,)),
        ],
        compiler_params=pltpu.CompilerParams(collective_id=0, has_side_effects=True, vmem_limit_bytes=56 * 2**20),
    )(x, cot, gain1, gain2, cosine, sine, length, logits, routes, *attn_w, *routed_w, *shared_w)


def experts_kernel(
    n, slots,
    h_hbm, dy_hbm, gates_in, wg, wu, wd,
    scores_in, sums_hbm, tg_hbm, tu_hbm, td_hbm, bg_hbm, bu_hbm, bd_hbm, r3_hbm, r2_hbm, r1_hbm,
    og, ou, od, ysum, hbuf, dbuf, act, dg, dup, stage, rbuf, xg, xu, xd, pg, pu, pd, gate_ref, s_ref, turn_ref, rows_out,
    lsem, ssem, r3sem, r2sem, r1sem, bsem, xssem, xrsem, osem, psem, scs, scr,
):
    pc = Place(n)
    nz, m = pc.nz, pc.m
    c1, c2, c3, e, c = pc.c1, pc.c2, pc.c3, pc.e, pc.c
    pc.greet_all()
    turn_ref[...] = jnp.zeros_like(turn_ref)
    for i in range(n):
        turn_ref[i : i + 1, :] = gates_in[i]
    gate_ref[...] = turn_ref[...].T
    og[...] = jnp.zeros_like(og)
    ou[...] = jnp.zeros_like(ou)
    od[...] = jnp.zeros_like(od)
    s_ref[...] = jnp.zeros_like(s_ref)
    n3 = (m - 1) * nz * m
    n2 = (m - 1) * nz

    def dest(t):
        return (c1 + t + 1) % nz, (c2 + t // nz + 1) % m, (c3 + t // (nz * m) + 1) % m

    def load(t, i):
        b = pc.blk(*dest(t))
        return (
            pltpu.make_async_copy(h_hbm.at[b], hbuf.at[i], lsem.at[0, i]),
            pltpu.make_async_copy(dy_hbm.at[b], dbuf.at[i], lsem.at[1, i]),
        )

    def partial_copy(i, to, dst, sem):
        return pltpu.make_async_remote_copy(
            src_ref=stage.at[i], dst_ref=dst, send_sem=ssem.at[i], recv_sem=sem,
            device_id=(to, c), device_id_type=MESH,
        )

    def add_received(src, sem):
        pltpu.make_async_remote_copy(
            src_ref=src, dst_ref=src, send_sem=ssem.at[0], recv_sem=sem,
            device_id=(e, 1 - c), device_id_type=MESH,
        ).wait_recv()
        copy = pltpu.make_async_copy(src, rbuf, bsem)
        copy.start()
        copy.wait()
        ysum[...] += rbuf[...].astype(jnp.float32)

    def swaps():
        return [
            pltpu.make_async_remote_copy(
                src_ref=src, dst_ref=dst, send_sem=xssem.at[i], recv_sem=xrsem.at[i],
                device_id=(e, 1 - c), device_id_type=MESH,
            )
            for i, (src, dst) in enumerate(((xg, pg), (xu, pu), (xd, pd)))
        ]

    def totals():
        return [
            pltpu.make_async_copy(src.at[c], dst, osem.at[i])
            for i, (src, dst) in enumerate(((og, tg_hbm), (ou, tu_hbm), (od, td_hbm)))
        ]

    def payload():
        return [
            pltpu.make_async_copy(src, dst.at[pl.ds(0, src.shape[0])], psem.at[i])
            for i, (src, dst) in enumerate(((xg, bg_hbm), (xu, bu_hbm), (xd, bd_hbm)))
        ]

    def score_send(to):
        return pltpu.make_async_remote_copy(
            src_ref=rows_out.at[to], dst_ref=scores_in.at[e], send_sem=scs.at[to], recv_sem=scr.at[e],
            device_id=(to, c), device_id_type=MESH,
        )

    for copy in load(0, 0):
        copy.start()

    def body(t, carry):
        i = t % 2
        slot = t % slots
        a, b2, b3 = dest(t)
        b = pc.blk(a, b2, b3)
        for copy in load(t, i):
            copy.wait()

        @pl.when(t < n - 1)
        def _():
            for copy in load(t + 1, 1 - i):
                copy.start()

        lane = lax.broadcasted_iota(jnp.int32, gate_ref.shape, 1)
        gate = jnp.sum(jnp.where(lane == b, gate_ref[...], 0.0), axis=1, keepdims=True)
        h = hbuf[i]
        dy = dbuf[i].astype(jnp.float32)
        z = (gate * dy).astype(jnp.bfloat16)
        for half in range(2):
            g = matmul(h, wg[half])
            u = matmul(h, wu[half])
            da = inner_cols(z, wd[half])
            sg = jax.nn.sigmoid(g)
            si = g * sg
            act[half] = (si * u).astype(jnp.bfloat16)
            dup[half] = (da * si).astype(jnp.bfloat16)
            dg[half] = (da * u * sg * (1.0 + g * (1.0 - sg))).astype(jnp.bfloat16)
        y = (matmul(act[0], wd[0]) + matmul(act[1], wd[1])).astype(jnp.bfloat16).astype(jnp.float32)
        s = jnp.sum(y * dy, axis=1, keepdims=True)
        s_ref[...] = jnp.where(lane == b, s, s_ref[...])
        ysum[0] = gate * y
        ysum[1] = (
            inner_cols(dg[0], wg[0]) + inner_cols(dg[1], wg[1])
            + inner_cols(dup[0], wu[0]) + inner_cols(dup[1], wu[1])
        ).astype(jnp.bfloat16).astype(jnp.float32)

        @pl.when((t >= slots) & (t - slots < n - 1))
        def _():
            partial_copy(slot, e, r1_hbm.at[0], r1sem.at[0]).wait_send()

        @pl.when(t >= n3)
        def _():
            for j in range(1, m):
                add_received(r3_hbm.at[j - 1, a, b2], r3sem.at[j - 1, a, b2])

        @pl.when(t >= n3 + n2)
        def _():
            for j in range(1, m):
                add_received(r2_hbm.at[j - 1, a], r2sem.at[j - 1, a])

        @pl.when(t < n - 1)
        def _():
            stage[slot] = ysum[...].astype(jnp.bfloat16)

        for j in range(1, m):
            @pl.when((t < n3) & (b3 == (c3 + j) % m))
            def _():
                partial_copy(slot, pc.blk(c1, c2, b3), r3_hbm.at[m - j - 1, a, b2], r3sem.at[m - j - 1, a, b2]).start()

            @pl.when((t >= n3) & (t < n3 + n2) & (b2 == (c2 + j) % m))
            def _():
                partial_copy(slot, pc.blk(c1, b2, c3), r2_hbm.at[m - j - 1, a], r2sem.at[m - j - 1, a]).start()

        for j in range(1, nz):
            @pl.when((t >= n3 + n2) & (t < n - 1) & (a == (c1 + j) % nz))
            def _():
                partial_copy(slot, pc.blk(a, c2, c3), r1_hbm.at[nz - j - 1], r1sem.at[nz - j - 1]).start()

        for half in range(2):
            og[half] += outer_rows(h, dg[half])
            ou[half] += outer_rows(h, dup[half])
            od[half] += outer_rows(act[half], z)
        return carry

    lax.fori_loop(0, n, body, 0)
    for buf, total in ((xg, og), (xu, ou), (xd, od)):
        buf[...] = total[1 - c].astype(jnp.bfloat16)
    for copy in swaps():
        copy.start()
    turned = s_ref[...].T
    for i in range(n):
        rows_out[i] = turned[i : i + 1, :]
    scores_in[e] = rows_out[e]

    def score_start(j, carry):
        score_send((e + j) % n).start()
        return carry

    lax.fori_loop(1, n, score_start, 0)
    for copy in swaps():
        copy.wait()
    for buf, got, total in ((xg, pg, og), (xu, pu, ou), (xd, pd, od)):
        total[c] += got[...].astype(jnp.float32)
        buf[...] = total[c].astype(jnp.bfloat16)
    for copy in totals() + payload():
        copy.start()
    for j in range(1, nz):
        add_received(r1_hbm.at[j - 1], r1sem.at[j - 1])
    final = pltpu.make_async_copy(ysum, sums_hbm, bsem)
    final.start()
    final.wait()
    for t in range(max(0, n - slots), n - 1):
        partial_copy(t % slots, e, r1_hbm.at[0], r1sem.at[0]).wait_send()

    def score_wait(j, carry):
        pltpu.make_async_remote_copy(
            src_ref=rows_out.at[0], dst_ref=scores_in.at[(e + j) % n], send_sem=scs.at[0], recv_sem=scr.at[(e + j) % n],
            device_id=((e + j) % n, c), device_id_type=MESH,
        ).wait_recv()
        score_send((e + j) % n).wait_send()
        return carry

    lax.fori_loop(1, n, score_wait, 0)
    for copy in totals() + payload():
        copy.wait()


def experts(h, dy, gates, wg, wu, wd):
    n, rows, width = h.shape
    hidden = wg.shape[2]
    nz = 4
    m = {16: 2, 64: 4}[n]
    slots = 8
    vmem = pl.BlockSpec(memory_space=pltpu.VMEM)
    hbm = pl.BlockSpec(memory_space=pl.ANY)
    f32, b16 = jnp.float32, jnp.bfloat16
    out = jax.ShapeDtypeStruct
    dma = pltpu.SemaphoreType.DMA
    up_rows, down_rows = n * blocked(width, n), n * blocked(hidden, n)
    return pl.pallas_call(
        functools.partial(experts_kernel, n, slots),
        out_shape=(
            out((n, 1, rows), f32), out((2, rows, width), f32),
            out((width, hidden), f32), out((width, hidden), f32), out((hidden, width), f32),
            out((up_rows, hidden), b16), out((up_rows, hidden), b16), out((down_rows, width), b16),
            out((m - 1, nz, m, 2, rows, width), b16), out((m - 1, nz, 2, rows, width), b16), out((nz - 1, 2, rows, width), b16),
        ),
        in_specs=[hbm, hbm, vmem, vmem, vmem, vmem],
        out_specs=(vmem,) + (hbm,) * 10,
        scratch_shapes=[
            pltpu.VMEM((2, width, hidden), f32), pltpu.VMEM((2, width, hidden), f32), pltpu.VMEM((2, hidden, width), f32),
            pltpu.VMEM((2, rows, width), f32), pltpu.VMEM((2, rows, width), b16), pltpu.VMEM((2, rows, width), b16),
            pltpu.VMEM((2, rows, hidden), b16), pltpu.VMEM((2, rows, hidden), b16), pltpu.VMEM((2, rows, hidden), b16),
            pltpu.VMEM((slots, 2, rows, width), b16), pltpu.VMEM((2, rows, width), b16),
            pltpu.VMEM((width, hidden), b16), pltpu.VMEM((width, hidden), b16), pltpu.VMEM((hidden, width), b16),
            pltpu.VMEM((width, hidden), b16), pltpu.VMEM((width, hidden), b16), pltpu.VMEM((hidden, width), b16),
            pltpu.VMEM((rows, 128), f32), pltpu.VMEM((rows, 128), f32), pltpu.VMEM((128, rows), f32), pltpu.VMEM((n, 1, rows), f32),
            dma((2, 2)), dma((slots,)), dma((m - 1, nz, m)), dma((m - 1, nz)), dma((nz - 1,)), dma,
            dma((3,)), dma((3,)), dma((3,)), dma((3,)), dma((n,)), dma((n,)),
        ],
        compiler_params=pltpu.CompilerParams(collective_id=1, has_side_effects=True, vmem_limit_bytes=62 * 2**20),
    )(h, dy, gates, wg, wu, wd)


def swap_halves(values):
    return pltpu.roll(values, HD // 2, axis=1)


class Scatter:
    def __init__(self, pc, stack, r3, r2, r1, sems):
        self.pc, self.stack, self.r3, self.r2, self.r1 = pc, stack, r3, r2, r1
        self.ssem, self.s3, self.s2, self.s1 = sems

    def copy(self, b, dst, sem, to):
        return pltpu.make_async_remote_copy(
            src_ref=self.stack.at[b], dst_ref=dst, send_sem=self.ssem.at[b], recv_sem=sem,
            device_id=(to, self.pc.c), device_id_type=MESH,
        )

    def add(self, total, src, sem):
        self.copy(self.pc.e, src, sem, self.pc.blk(self.pc.c1, self.pc.c2, self.pc.o3()[0])).wait_recv()
        return total + src[...].astype(jnp.float32)

    def places(self):
        pc = self.pc
        far = [pc.c1 + j for j in range(1, pc.nz)] + [pc.c1]
        return [a % pc.nz for a in far]

    def start(self):
        pc = self.pc
        for k in range(1, pc.m):
            for b2 in pc.o2() + [pc.c2]:
                for a in self.places():
                    b3 = (pc.c3 + k) % pc.m
                    self.copy(pc.blk(a, b2, b3), self.r3.at[pc.m - k - 1, a, b2], self.s3.at[pc.m - k - 1, a, b2], pc.blk(pc.c1, pc.c2, b3)).start()

    def collect(self, a, b2, level):
        pc = self.pc
        total = self.stack[pc.blk(a, b2, pc.c3)].astype(jnp.float32)
        for k in range(pc.m - 1):
            total = self.add(total, self.r3.at[k, a, b2], self.s3.at[k, a, b2])
        if level >= 2:
            for k in range(pc.m - 1):
                total = self.add(total, self.r2.at[k, a], self.s2.at[k, a])
        if level >= 3:
            for k in range(pc.nz - 1):
                total = self.add(total, self.r1.at[k], self.s1.at[k])
        self.stack[pc.blk(a, b2, pc.c3)] = total.astype(jnp.bfloat16)

    def second(self):
        pc = self.pc
        for k in range(1, pc.m):
            for a in self.places():
                b2 = (pc.c2 + k) % pc.m
                self.collect(a, b2, 1)
                self.copy(pc.blk(a, b2, pc.c3), self.r2.at[pc.m - k - 1, a], self.s2.at[pc.m - k - 1, a], pc.blk(pc.c1, b2, pc.c3)).start()

    def third(self):
        pc = self.pc
        for k in range(1, pc.nz):
            a = (pc.c1 + k) % pc.nz
            self.collect(a, pc.c2, 2)
            self.copy(pc.blk(a, pc.c2, pc.c3), self.r1.at[pc.nz - k - 1], self.s1.at[pc.nz - k - 1], pc.blk(a, pc.c2, pc.c3)).start()

    def last(self):
        self.collect(self.pc.c1, self.pc.c2, 3)

    def finish(self):
        pc = self.pc
        for j in range(1, pc.n):
            self.copy((pc.e + j) % pc.n, self.r1.at[0], self.s1.at[0], (pc.e + j) % pc.n).wait_send()


def tail_kernel(
    n,
    x_ref, x1_ref, cot_ref, sums_ref, q_ref, k_ref, v_ref, o_ref, p_ref, wq, wk, wv, wo,
    gain1, gain2, cos_ref, sin_ref, cnt_ref, len_ref, logit_ref, route_ref, scores_in, sg_hbm, su_hbm, sd_hbm,
    out_ref, gtok_ref, glog_ref, small_ref, ag0, ag1, agg, agu, agd,
    dx_ref, dq_ref, dk_ref, dv_ref, do_ref, a_ref, give, take, stack0, stack1, r3, r2, r1,
    sm_core, sm_d3, sm_d2, sm_z,
    wbuf, wsem, turn_ref,
    gs, gr, ss, s3, s2, s1, xs, xr, cs, cr, scs, scr, locs,
):
    pc = Place(n)
    c1, c2, c3, e, c, nz, m = pc.c1, pc.c2, pc.c3, pc.e, pc.c, pc.nz, pc.m
    rows, width = x_ref.shape
    half = width // 2
    pc.greet_all()

    shared = ((sg_hbm, agg), (su_hbm, agu), (sd_hbm, agd))

    def deal(i, to):
        src, dst = shared[i]
        return pltpu.make_async_remote_copy(
            src_ref=src.at[to], dst_ref=dst.at[to], send_sem=scs.at[i, to], recv_sem=scr.at[i],
            device_id=(to, c), device_id_type=MESH,
        )

    def keep(i):
        src, dst = shared[i]
        return pltpu.make_async_copy(src.at[n - 1], dst.at[n - 1], scs.at[i, n - 1])

    @pl.when(e == n - 1)
    def _():
        def one(j, carry):
            for i in range(3):
                deal(i, n - 2 - j).start()
            return carry

        lax.fori_loop(0, n - 1, one, 0)
        for i in range(3):
            keep(i).start()

    gathers = [Gather(pc, dst.at[e], dst, gs.at[i], gr.at[i], dst.shape[1]) for i, (src, dst) in enumerate(shared)]

    def shared_start():
        @pl.when(e == n - 1)
        def _():
            for i in range(3):
                keep(i).wait()

        @pl.when(e != n - 1)
        def _():
            for i in range(3):
                src, dst = shared[i]
                pltpu.make_async_remote_copy(
                    src_ref=dst.at[e], dst_ref=dst.at[e], send_sem=scs.at[i, 0], recv_sem=scr.at[i],
                    device_id=(n - 1, c), device_id_type=MESH,
                ).wait_recv()

        for g in gathers:
            g.start()

    def fetch(src, i):
        return pltpu.make_async_copy(src, wbuf.at[i], wsem.at[i])

    fetch(wo, 0).start()
    fetch(wv, 1).start()

    x1 = x1_ref[...]
    up = cot_ref[...].astype(jnp.float32)
    out_ref[...] = (x1 + sums_ref[0]).astype(jnp.bfloat16)
    dh = sums_ref[1]
    r_two = lax.rsqrt(jnp.mean(x1 * x1, axis=-1, keepdims=True) + norm_eps)
    n_two = x1 * r_two
    scaled = dh * gain2[...]
    grad_two = jnp.sum(dh * n_two, axis=0, keepdims=True)
    dx = up + r_two * (scaled - n_two * jnp.mean(scaled * n_two, axis=-1, keepdims=True))
    dx_ref[...] = dx
    dx_low = dx.astype(jnp.bfloat16)

    def columns(ref, which):
        return ref[:, pl.ds(pl.multiple_of(which * half, 128), half)]

    def hand(i):
        return pltpu.make_async_remote_copy(
            src_ref=give.at[i], dst_ref=take.at[i], send_sem=xs.at[i], recv_sem=xr.at[i],
            device_id=(e, 1 - c), device_id_type=MESH,
        )

    def to_partner(i, left, right):
        give[i] = outer_rows(columns(left, 1 - c), right).astype(jnp.bfloat16)
        hand(i).start()

    def own_part(i, left, right, stack, at):
        block = stack.shape[1]
        part = outer_rows(columns(left, c), right)
        hand(i).wait_recv()
        total = (part + take[i].astype(jnp.float32)).astype(jnp.bfloat16)
        stack[pl.ds(at * (half // block), half // block)] = total.reshape(half // block, block, width)

    to_partner(0, o_ref, dx_low)
    fetch(wo, 0).wait()
    do_ref[...] = inner_cols(dx_low, wbuf[0]).astype(jnp.bfloat16)
    fetch(wk, 0).start()
    cosine, sine = cos_ref[...], sin_ref[...]
    scale = HD ** (-0.5)

    def one_head(hd, carry):
        at = pl.ds(pl.multiple_of(hd * HD, HD), HD)
        prob = p_ref[hd]
        d_o, val, que, key = do_ref[:, at], v_ref[:, at], q_ref[:, at], k_ref[:, at]
        dv_ref[:, at] = outer_rows(prob.astype(jnp.bfloat16), d_o).astype(jnp.bfloat16)
        d_prob = inner_cols(d_o, val)
        inner = jnp.sum(prob * d_prob, axis=-1, keepdims=True)
        d_score = (prob * (d_prob - inner)).astype(jnp.bfloat16)
        d_q = matmul(d_score, key) * scale
        d_k = outer_rows(d_score, que) * scale
        dq_ref[:, at] = (d_q * cosine - swap_halves(d_q) * sine).astype(jnp.bfloat16)
        dk_ref[:, at] = (d_k * cosine - swap_halves(d_k) * sine).astype(jnp.bfloat16)
        return carry

    lax.fori_loop(0, HEADS, one_head, 0)
    xv = x_ref[...].astype(jnp.float32)
    r_one = lax.rsqrt(jnp.mean(xv * xv, axis=-1, keepdims=True) + norm_eps)
    n_one = xv * r_one
    a_ref[...] = (n_one * gain1[...]).astype(jnp.bfloat16)
    to_partner(1, a_ref, dv_ref[...])
    to_partner(2, a_ref, dk_ref[...])
    to_partner(3, a_ref, dq_ref[...])
    if n * stack0.shape[1] > 2 * half:
        stack0[...] = jnp.zeros_like(stack0)
        stack1[...] = jnp.zeros_like(stack1)
    own_part(0, o_ref, dx_low, stack0, 0)
    own_part(1, a_ref, dv_ref[...], stack0, 1)
    first = Scatter(pc, stack0, r3.at[0], r2.at[0], r1.at[0], (ss.at[0], s3.at[0], s2.at[0], s1.at[0]))
    second = Scatter(pc, stack1, r3.at[1], r2.at[1], r1.at[1], (ss.at[1], s3.at[1], s2.at[1], s1.at[1]))
    first.start()
    shared_start()
    own_part(2, a_ref, dk_ref[...], stack1, 0)
    own_part(3, a_ref, dq_ref[...], stack1, 1)
    second.start()
    fetch(wv, 1).wait()
    da = inner_cols(dv_ref[...], wbuf[1])
    fetch(wq, 1).start()
    fetch(wk, 0).wait()
    da = da + inner_cols(dk_ref[...], wbuf[0])
    fetch(wq, 1).wait()
    da = da + inner_cols(dq_ref[...], wbuf[1])
    scaled_one = da * gain1[...]
    grad_one = jnp.sum(da * n_one, axis=0, keepdims=True)
    back = r_one * (scaled_one - n_one * jnp.mean(scaled_one * n_one, axis=-1, keepdims=True))
    gtok_ref[...] = (dx_ref[...] + back).astype(jnp.bfloat16)

    def exchange(ref, own, level, peers, value):
        ref[own] = value
        copies = [
            pltpu.make_async_remote_copy(
                src_ref=ref.at[own], dst_ref=ref.at[own], send_sem=cs.at[level, i], recv_sem=cr.at[level, own],
                device_id=to, device_id_type=MESH,
            )
            for i, (to, at) in enumerate(peers)
        ]
        for copy in copies:
            copy.start()

        def done():
            for i, (to, at) in enumerate(peers):
                pltpu.make_async_remote_copy(
                    src_ref=ref.at[own], dst_ref=ref.at[at], send_sem=cs.at[level, i], recv_sem=cr.at[level, at],
                    device_id=to, device_id_type=MESH,
                ).wait_recv()
            for copy in copies:
                copy.wait_send()
            total = ref[0]
            for i in range(1, ref.shape[0]):
                total = total + ref[i]
            return total

        return done

    turn_ref[...] = jnp.zeros_like(turn_ref)
    for i in range(n):
        turn_ref[i : i + 1, :] = scores_in[i]
    scores = turn_ref[...].T
    lane = lax.broadcasted_iota(jnp.int32, (rows, 128), 1)
    row = lax.broadcasted_iota(jnp.int32, (rows, 128), 0)
    scores = jnp.where(row < len_ref[...], scores, 0.0)
    logits, routes = logit_ref[...], route_ref[...]
    raised = jnp.exp(logits - jnp.max(logits, axis=-1, keepdims=True))
    soft = raised / jnp.sum(raised, axis=-1, keepdims=True)
    picked = [
        jnp.sum(jnp.where(lane == routes[:, i : i + 1], scores, 0.0), axis=-1, keepdims=True)
        for i in range(routes.shape[1])
    ]
    share = jnp.concatenate(picked, axis=1)
    glog_ref[...] = soft * (share - jnp.sum(soft * share, axis=-1, keepdims=True))

    small = jnp.concatenate([grad_one, grad_two, cnt_ref[...], jnp.zeros((5, width), jnp.float32)], axis=0)
    level0 = exchange(sm_core, c, 0, [((e, 1 - c), 1 - c)], small)
    first.second()
    level1 = exchange(sm_d3, c3, 1, [((pc.blk(c1, c2, j), c), j) for j in pc.o3()], level0())
    second.second()
    level2 = exchange(sm_d2, c2, 2, [((pc.blk(c1, j, c3), c), j) for j in pc.o2()], level1())
    first.third()
    level3 = exchange(sm_z, c1, 3, [((pc.blk((c1 + j) % nz, c2, c3), c), (c1 + j) % nz) for j in range(1, nz)], level2())
    second.third()
    small_ref[...] = level3()

    events = [g.events() for g in gathers]
    for i in range(len(events[0])):
        for ev in events:
            ev[i]()
    first.last()
    g0 = Gather(pc, stack0.at[e], ag0, gs.at[3], gr.at[3], stack0.shape[1])
    g0.start()
    loc0 = pltpu.make_async_copy(stack0.at[e], ag0.at[e], locs.at[0])
    loc0.start()
    second.last()
    g1 = Gather(pc, stack1.at[e], ag1, gs.at[4], gr.at[4], stack1.shape[1])
    g1.start()
    loc1 = pltpu.make_async_copy(stack1.at[e], ag1.at[e], locs.at[1])
    loc1.start()
    ev0, ev1 = g0.events(), g1.events()
    for i in range(len(ev0)):
        ev0[i]()
        ev1[i]()
    for g in gathers + [g0, g1]:
        g.finish()
    first.finish()
    second.finish()
    loc0.wait()
    loc1.wait()
    for i in range(4):
        hand(i).wait_send()

    @pl.when(e == n - 1)
    def _():
        def one(j, carry):
            for i in range(3):
                deal(i, j).wait_send()
            return carry

        lax.fori_loop(0, n - 1, one, 0)


def tail(n, x, x1, cot, sums, q, k, v, o, prob, wq, wk, wv, wo, gain1, gain2, cosine, sine, cnt, length, logits, routes, scores, sg, su, sd):
    nz = 4
    m = {16: 2, 64: 4}[n]
    rows, width = x.shape
    half = width // 2
    block = blocked(2 * half, n)
    vmem = pl.BlockSpec(memory_space=pltpu.VMEM)
    hbm = pl.BlockSpec(memory_space=pl.ANY)
    f32, b16 = jnp.float32, jnp.bfloat16
    out = jax.ShapeDtypeStruct
    dma = pltpu.SemaphoreType.DMA
    wide = pltpu.VMEM((rows, width), b16)
    return pl.pallas_call(
        functools.partial(tail_kernel, n),
        out_shape=(
            out((rows, width), b16), out((rows, width), b16), out(logits.shape, f32), out((8, width), f32),
            out((n, block, width), b16), out((n, block, width), b16),
            out(sg.shape, b16), out(su.shape, b16), out(sd.shape, b16),
        ),
        in_specs=[vmem] * 9 + [hbm] * 4 + [vmem] * 9 + [hbm] * 3,
        out_specs=(vmem,) * 4 + (hbm,) * 5,
        scratch_shapes=[
            pltpu.VMEM((rows, width), f32), wide, wide, wide, wide, wide,
            pltpu.VMEM((4, half, width), b16), pltpu.VMEM((4, half, width), b16),
            pltpu.VMEM((n, block, width), b16), pltpu.VMEM((n, block, width), b16),
            pltpu.VMEM((2, m - 1, nz, m, block, width), b16), pltpu.VMEM((2, m - 1, nz, block, width), b16),
            pltpu.VMEM((2, nz - 1, block, width), b16),
            pltpu.VMEM((2, 8, width), f32), pltpu.VMEM((m, 8, width), f32), pltpu.VMEM((m, 8, width), f32), pltpu.VMEM((nz, 8, width), f32),
            pltpu.VMEM((2, width, width), b16), dma((2,)), pltpu.VMEM((128, rows), f32),
            dma((5, 160)), dma((5, 1, n)), dma((2, n)), dma((2, m - 1, nz, m)), dma((2, m - 1, nz)), dma((2, nz - 1)),
            dma((4,)), dma((4,)), dma((4, max(nz, m))), dma((4, max(nz, m, 2))), dma((3, n)), dma((3,)), dma((2,)),
        ],
        compiler_params=pltpu.CompilerParams(collective_id=2, has_side_effects=True, vmem_limit_bytes=62 * 2**20),
    )(x, x1, cot, sums, q, k, v, o, prob, wq, wk, wv, wo, gain1, gain2, cosine, sine, cnt, length, logits, routes, scores, sg, su, sd)


def blocked(count, n):
    return -(-count // (16 * n)) * 16


def from_blocks(blocks, count):
    return blocks.reshape(-1, blocks.shape[2])[:count].astype(jnp.float32)


def rotary_rows(seq_len):
    position = np.arange(seq_len).astype(np.float32)
    inverse_freq = (rotary_base ** (-2.0 * np.arange(HD // 2).astype(np.float32) / HD)).astype(np.float32)
    angle = position[:, None] * inverse_freq[None, :]
    cosine, sine = np.cos(angle), np.sin(angle)
    return np.concatenate([cosine, cosine], axis=1), np.concatenate([-sine, sine], axis=1)


def on_device(
    tokens, norm_one, w_query, w_key, w_value, w_out, norm_two, r_gate, r_up, r_down, s_gate, s_up, s_down,
    logits, routes, lengths, cotangent,
):
    rows, width = tokens.shape
    n = lax.axis_size("exp")
    hidden = s_gate.shape[1]
    cosine, sine = (jnp.asarray(table) for table in rotary_rows(rows))
    length = jnp.broadcast_to(lengths[:, None], (1, 128))
    gain1, gain2 = norm_one[None], norm_two[None]
    (
        all_dy, all_h, fq, fk, fv, fo, fg, fu, fd, mixed, queries, keys_all, values_all, attended, prob, gates, counts,
    ) = front(
        n, tokens, cotangent, gain1, gain2, cosine, sine, length, logits, routes,
        (w_query, w_key, w_value, w_out), (r_gate[0], r_up[0], r_down[0]), (s_gate, s_up, s_down),
    )
    scores, sums, tg, tu, td, bg, bu, bd = experts(all_h, all_dy, gates, fg, fu, fd)[:8]
    full = (width, width)
    output, grad_tokens, grad_logits, small_sums, sum0, sum1, sum_g, sum_u, sum_d = tail(
        n, tokens, mixed, cotangent, sums, queries, keys_all, values_all, attended, prob,
        fq.reshape(full), fk.reshape(full), fv.reshape(full), fo.reshape(full),
        gain1, gain2, cosine, sine, counts, length, logits, routes, scores,
        bg.reshape(n, -1, hidden), bu.reshape(n, -1, hidden), bd.reshape(n, -1, width),
    )
    half = width // 2
    wout_value = from_blocks(sum0, width)
    key_query = from_blocks(sum1, width)
    holds_shared = lax.axis_index("exp") == n - 1
    routed_grads = tuple(jnp.where(holds_shared, 0.0, grad)[None] for grad in (tg, tu, td))
    return (
        output, grad_tokens, small_sums[0],
        key_query[half:], key_query[:half], wout_value[half:], wout_value[:half],
        small_sums[1], routed_grads[0], routed_grads[1], routed_grads[2],
        from_blocks(sum_g, width), from_blocks(sum_u, width), from_blocks(sum_d, hidden),
        grad_logits, small_sums[2, :n].astype(jnp.int32),
    )


def solution(mesh):
    in_specs = (
        P(("exp", "hid"), None),
        P(),
        P("hid", None),
        P("hid", None),
        P("hid", None),
        P("hid", None),
        P(),
        P("exp", None, "hid"),
        P("exp", None, "hid"),
        P("exp", "hid", None),
        P(None, "hid"),
        P(None, "hid"),
        P("hid", None),
        P(("exp", "hid"), None),
        P(("exp", "hid"), None),
        P(("exp", "hid")),
        P(("exp", "hid"), None),
    )
    out_specs = (
        P(("exp", "hid"), None),
        P(("exp", "hid"), None),
        P(),
        P("hid", None),
        P("hid", None),
        P("hid", None),
        P("hid", None),
        P(),
        P("exp", None, "hid"),
        P("exp", None, "hid"),
        P("exp", "hid", None),
        P(None, "hid"),
        P(None, "hid"),
        P("hid", None),
        P(("exp", "hid"), None),
        P(),
    )
    return jax.shard_map(
        on_device, mesh=mesh, in_specs=in_specs, out_specs=out_specs, check_vma=False
    )
```

```python
import functools

import jax
import jax.numpy as jnp
import numpy as np
from jax import lax
from jax.experimental import pallas as pl
from jax.experimental.pallas import tpu as pltpu
from jax.sharding import PartitionSpec as P

HEADS = 10
HD = 128
MESH = pl.DeviceIdType.MESH


norm_eps = 1e-06
rotary_base = 10000.0
contract_rows = (((0,), (0,)), ((), ()))
contract_cols = (((1,), (1,)), ((), ()))


def matmul(left_side, right_side):
    return jnp.dot(left_side, right_side, preferred_element_type=jnp.float32)


def outer_rows(left_side, right_side):
    return lax.dot_general(left_side, right_side, contract_rows, preferred_element_type=jnp.float32)


def inner_cols(left_side, right_side):
    return lax.dot_general(left_side, right_side, contract_cols, preferred_element_type=jnp.float32)


class Place:
    def __init__(self, n):
        self.n = n; self.nz = 4; self.m = {16: 2, 64: 4}[n]; m = self.m
        self.e = lax.axis_index("exp"); self.c = lax.axis_index("hid"); c = self.c; e = self.e
        self.s1 = m * m; self.s2 = 1 + c * (m - 1); self.s3 = m - c * (m - 1)
        self.c1 = e // self.s1; self.c2 = (e // self.s2) % m; self.c3 = (e // self.s3) % m
    def blk(self, a, b, d): return a * self.s1 + b * self.s2 + d * self.s3
    def o2(self): return [(self.c2 + j) % self.m for j in range(1, self.m)]
    def o3(self): return [(self.c3 + j) % self.m for j in range(1, self.m)]
    def greet_all(self):
        barrier = pltpu.get_barrier_semaphore()

        def greet(j, carry):
            pl.semaphore_signal(barrier, inc=1, device_id=((self.e + j) % self.n, self.c), device_id_type=MESH)
            return carry

        lax.fori_loop(1, self.n, greet, 0)
        pl.semaphore_signal(barrier, inc=1, device_id=(self.e, 1 - self.c), device_id_type=MESH)
        pl.semaphore_wait(barrier, self.n)


class Gather:
    def __init__(self, pc, src, dst, ssem, rsem, split, base=0):
        self.pc, self.src, self.dst, self.ssem, self.rsem = pc, src, dst, ssem, rsem
        self.split = split; self.sends = []; self.base = base
    def view(self, ref, part):
        R = self.src.shape[0]
        return ref.at[pl.ds(0, self.split)] if part == 0 else ref.at[pl.ds(self.split, R - self.split)]
    def send(self, part, own, b, to, cond=None):
        i = self.base + len(self.sends)
        src = self.view(self.src if own else self.dst.at[b], part)
        cp = pltpu.make_async_remote_copy(src_ref=src, dst_ref=self.view(self.dst.at[b], part), send_sem=self.ssem.at[i], recv_sem=self.rsem.at[part, b], device_id=(to, self.pc.c), device_id_type=MESH)
        self.sends.append((cond, cp))
        if cond is None: cp.start()
        else: pl.when(cond)(cp.start)
    def wait(self, part, b):
        v = self.view(self.dst.at[b], part)
        to = self.pc.blk(self.pc.c1, self.pc.c2, self.pc.o3()[0])
        pltpu.make_async_remote_copy(src_ref=v, dst_ref=v, send_sem=self.ssem.at[0], recv_sem=self.rsem.at[part, b], device_id=(to, self.pc.c), device_id_type=MESH).wait_recv()
    def updown(self, part, own, b):
        pc = self.pc
        self.send(part, own, b, pc.blk(pc.c1 + 1, pc.c2, pc.c3), pc.c1 < pc.nz - 1)
        self.send(part, own, b, pc.blk(pc.c1 - 1, pc.c2, pc.c3), pc.c1 > 0)
    def to2(self, part, own, b):
        pc = self.pc
        for j in pc.o2(): self.send(part, own, b, pc.blk(pc.c1, j, pc.c3))
    def to3(self, part, own, b):
        pc = self.pc
        for j in pc.o3(): self.send(part, own, b, pc.blk(pc.c1, pc.c2, j))
    def start(self):
        e = self.pc.e
        self.to3(0, True, e); self.to2(0, True, e); self.updown(0, True, e)
        if self.split < self.src.shape[0]:
            self.to3(1, True, e); self.to2(1, True, e); self.updown(1, True, e)
    def zarr(self, part, s, up, k2, k3, more):
        pc = self.pc
        a = pc.c1 - s if up else pc.c1 + s
        cond = (pc.c1 >= s) if up else (pc.c1 < pc.nz - s)
        b = pc.blk(a, k2, k3)
        pl.when(cond)(lambda: self.wait(part, b))
        if s < pc.nz - 1:
            if up: self.send(part, False, b, pc.blk(pc.c1 + 1, pc.c2, pc.c3), (pc.c1 >= s) & (pc.c1 < pc.nz - 1))
            else: self.send(part, False, b, pc.blk(pc.c1 - 1, pc.c2, pc.c3), (pc.c1 < pc.nz - s) & (pc.c1 > 0))
        if more:
            for j in pc.o2(): self.send(part, False, b, pc.blk(pc.c1, j, pc.c3), cond)
            for j in pc.o3(): self.send(part, False, b, pc.blk(pc.c1, pc.c2, j), cond)
    def events(self):
        pc = self.pc; ev = []
        def a2(s):
            def go():
                for j in pc.o2():
                    for sg in ((1, -1) if s else (1,)):
                        a = pc.c1 + sg * s
                        cond = None if s == 0 else ((a >= 0) & (a < pc.nz))
                        b = pc.blk(a, j, pc.c3)
                        if cond is None: self.wait(0, b)
                        else: pl.when(cond)(lambda b=b: self.wait(0, b))
                        for k in pc.o3(): self.send(0, False, b, pc.blk(pc.c1, pc.c2, k), cond)
            return go
        def az(s):
            def go():
                self.zarr(0, s, True, pc.c2, pc.c3, True); self.zarr(0, s, False, pc.c2, pc.c3, True)
            return go
        B = self.split < self.src.shape[0]
        def f1():
            for j in pc.o2():
                b = pc.blk(pc.c1, j, pc.c3); self.wait(1, b); self.to3(1, False, b); self.updown(1, False, b)
        def f2():
            for k in pc.o3():
                b = pc.blk(pc.c1, pc.c2, k); self.wait(1, b); self.updown(1, False, b)
        def f3():
            for j in pc.o2():
                for k in pc.o3():
                    b = pc.blk(pc.c1, j, k); self.wait(1, b); self.updown(1, False, b)
        def fz(s):
            def go():
                for k2 in range(pc.m):
                    for k3 in range(pc.m):
                        self.zarr(1, s, True, k2, k3, False); self.zarr(1, s, False, k2, k3, False)
            return go
        ev += [az(1), a2(0)]
        if B: ev += [f1, f2, f3]
        ev += [az(2), a2(1)]
        if B: ev += [fz(1)]
        ev += [az(3), a2(2)]
        if B: ev += [fz(2)]
        ev += [a2(3)]
        if B: ev += [fz(3)]
        def last():
            for a in range(pc.nz):
                for j in range(pc.m):
                    for k in pc.o3(): self.wait(0, pc.blk(a, j, k))
        ev += [last]
        return ev
    def finish(self):
        for cond, cp in self.sends:
            if cond is None: cp.wait_send()
            else: pl.when(cond)(cp.wait_send)


def run_staggered(first, second, lag):
    for i in range(max(len(first), len(second) + lag)):
        if i < len(first):
            first[i]()
        if lag <= i < len(second) + lag:
            second[i - lag]()


def part_rows(rows):
    return rows - rows // 80 * 16


def front_kernel(
    n,
    x_ref, cot_ref, gain1, gain2, cos_ref, sin_ref, len_ref, logit_ref, route_ref,
    wq, wk, wv, wo, rg, ru, rd, sg, su, sd,
    all_dy, all_h, fq, fk, fv, fo, fg, fu, fd,
    x1_ref, q_ref, k_ref, v_ref, o_ref, p_ref, gates_in, cnt_ref,
    wbuf, h_ref, rows_out, turn_ref,
    gs, gr, ls, ws, wr, wl, es, er, gss, grs,
):
    pc = Place(n)
    e, c = pc.e, pc.c
    rows, width = x_ref.shape
    half = width // 2
    pc.greet_all()
    gather_dy = Gather(pc, cot_ref, all_dy, gs.at[0], gr.at[0], part_rows(rows))
    gather_h = Gather(pc, h_ref, all_h, gs.at[1], gr.at[1], part_rows(rows))
    gather_dy.start()
    own_dy = pltpu.make_async_copy(cot_ref, all_dy.at[e], ls.at[0])
    own_dy.start()
    partner = (e, 1 - c)
    halves = (wq, wk, wv, wo)
    fulls = (fq, fk, fv, fo)

    def swap(i):
        return pltpu.make_async_remote_copy(
            src_ref=halves[i], dst_ref=wbuf.at[i, c], send_sem=ws.at[i], recv_sem=wr.at[i],
            device_id=partner, device_id_type=MESH,
        )

    def own(i):
        return pltpu.make_async_copy(halves[i], wbuf.at[i, c], wl.at[0, i])

    def keep(i):
        return pltpu.make_async_copy(wbuf.at[i], fulls[i], wl.at[1, i])

    experts_other = (fg, fu, fd)

    def expert_swap(i, src):
        return pltpu.make_async_remote_copy(
            src_ref=src, dst_ref=experts_other[i], send_sem=es.at[i], recv_sem=er.at[i],
            device_id=partner, device_id_type=MESH,
        )

    for i in range(4):
        swap(i).start()
        own(i).start()
    for i, (routed, shared) in enumerate(((rg, sg), (ru, su), (rd, sd))):
        @pl.when(e == n - 1)
        def _():
            expert_swap(i, shared).start()

        @pl.when(e != n - 1)
        def _():
            expert_swap(i, routed).start()

    lane = lax.broadcasted_iota(jnp.int32, (rows, 128), 1)
    row = lax.broadcasted_iota(jnp.int32, (rows, 128), 0)
    valid = (row < len_ref[0]).astype(jnp.float32)
    soft, routes = route_columns(logit_ref, route_ref, turn_ref)
    dense = jnp.zeros((rows, 128), jnp.float32)
    named = jnp.zeros((rows, 128), jnp.float32)
    for i in range(route_ref.shape[0]):
        hit = lane == routes[:, i : i + 1]
        dense = dense + jnp.where(hit, soft[:, i : i + 1], 0.0)
        named = named + jnp.where(hit, 1.0, 0.0)
    dense = jnp.where(lane == n - 1, 1.0, dense * valid)
    cnt_ref[...] = jnp.zeros_like(cnt_ref)
    cnt_ref[:, 0:128] = jnp.sum(named * valid, axis=0, keepdims=True)
    turned = dense.T
    for i in range(n):
        rows_out[i] = turned[i : i + 1, :]
    gates_in[e] = rows_out[e]

    def gate_send(to):
        return pltpu.make_async_remote_copy(
            src_ref=rows_out.at[to], dst_ref=gates_in.at[e], send_sem=gss.at[to], recv_sem=grs.at[e],
            device_id=(to, c), device_id_type=MESH,
        )

    def gate_start(j, carry):
        gate_send((e + j) % n).start()
        return carry

    lax.fori_loop(1, n, gate_start, 0)

    xv = x_ref[...].astype(jnp.float32)
    a = (xv * lax.rsqrt(jnp.mean(xv * xv, axis=-1, keepdims=True) + norm_eps) * gain1[...]).astype(jnp.bfloat16)
    cosine, sine = cos_ref[...], sin_ref[...]

    def project(values, i):
        own(i).wait()
        swap(i).wait_recv()
        keep(i).start()
        return matmul(values[:, :half], wbuf[i, 0]) + matmul(values[:, half:], wbuf[i, 1])

    for i, ref in ((0, q_ref), (1, k_ref)):
        flat = project(a, i)
        for hd in range(HEADS):
            part = flat[:, hd * HD : (hd + 1) * HD]
            ref[:, hd * HD : (hd + 1) * HD] = (part * cosine + swap_halves(part) * sine).astype(jnp.bfloat16)
    v_ref[...] = project(a, 2).astype(jnp.bfloat16)
    events = gather_dy.events()
    events[0]()
    scale = HD ** (-0.5)
    row_pos = lax.broadcasted_iota(jnp.int32, (rows, rows), 0)
    col_pos = lax.broadcasted_iota(jnp.int32, (rows, rows), 1)
    allowed = (col_pos <= row_pos) & (col_pos < len_ref[0])

    def one_head(hd, carry):
        at = pl.ds(pl.multiple_of(hd * HD, HD), HD)
        scores = jnp.where(allowed, inner_cols(q_ref[:, at], k_ref[:, at]) * scale, -1e30)
        up = jnp.exp(scores - jnp.max(scores, axis=-1, keepdims=True))
        prob = up / jnp.sum(up, axis=-1, keepdims=True)
        p_ref[hd] = prob
        o_ref[:, at] = matmul(prob.astype(jnp.bfloat16), v_ref[:, at]).astype(jnp.bfloat16)
        return carry

    lax.fori_loop(0, HEADS, one_head, 0)
    events[1]()
    x1 = xv + project(o_ref[...], 3)
    x1_ref[...] = x1
    h_ref[...] = (x1 * lax.rsqrt(jnp.mean(x1 * x1, axis=-1, keepdims=True) + norm_eps) * gain2[...]).astype(jnp.bfloat16)
    gather_h.start()
    own_h = pltpu.make_async_copy(h_ref, all_h.at[e], ls.at[1])
    own_h.start()
    run_staggered(events[2:], gather_h.events(), 2)

    def gate_wait(j, carry):
        pltpu.make_async_remote_copy(
            src_ref=rows_out.at[0], dst_ref=gates_in.at[(e + j) % n], send_sem=gss.at[0], recv_sem=grs.at[(e + j) % n],
            device_id=((e + j) % n, c), device_id_type=MESH,
        ).wait_recv()
        gate_send((e + j) % n).wait_send()
        return carry

    lax.fori_loop(1, n, gate_wait, 0)
    gather_dy.finish()
    gather_h.finish()
    own_dy.wait()
    own_h.wait()
    for i in range(4):
        swap(i).wait_send()
        keep(i).wait()
    for i, shared in enumerate((sg, su, sd)):
        expert_swap(i, shared).wait()


def front(n, x, cot, gain1, gain2, cosine, sine, length, logits, routes, attn_w, routed_w, shared_w):
    rows, width = x.shape
    hidden = shared_w[0].shape[0]
    vmem = pl.BlockSpec(memory_space=pltpu.VMEM)
    hbm = pl.BlockSpec(memory_space=pl.ANY)
    f32, b16 = jnp.float32, jnp.bfloat16
    out = jax.ShapeDtypeStruct
    dma = pltpu.SemaphoreType.DMA
    wide = out((rows, width), b16)
    full = out((2, width // 2, width), b16)
    return pl.pallas_call(
        functools.partial(front_kernel, n),
        out_shape=(
            out((n, rows, width), b16), out((n, rows, width), b16), full, full, full, full,
            out((hidden, width), b16), out((hidden, width), b16), out((hidden, width), b16),
            out((rows, width), f32), wide, wide, wide, wide, out((HEADS, rows, rows), f32),
            out((n, 1, rows), f32), out((1, width), f32),
        ),
        in_specs=[vmem] * 6 + [pl.BlockSpec(memory_space=pltpu.SMEM)] + [vmem] * 2 + [hbm] * 10,
        out_specs=(hbm,) * 9 + (vmem,) * 8,
        scratch_shapes=[
            pltpu.VMEM((4, 2, width // 2, width), b16), pltpu.VMEM((rows, width), b16), pltpu.VMEM((n, 1, rows), f32), pltpu.VMEM((128, rows), f32),
            dma((2, 160)), dma((2, 2, n)), dma((2,)), dma((4,)), dma((4,)), dma((2, 4)), dma((3,)), dma((3,)),
            dma((n,)), dma((n,)),
        ],
        compiler_params=pltpu.CompilerParams(collective_id=0, has_side_effects=True, vmem_limit_bytes=56 * 2**20),
    )(x, cot, gain1, gain2, cosine, sine, length, logits, routes, *attn_w, *routed_w, *shared_w)


def experts_kernel(
    n, slots,
    h_hbm, dy_hbm, gates_in, rg, ru, rd, shg, shu, shd, xg, xu, xd,
    scores_in, sums_hbm, tg_hbm, tu_hbm, td_hbm, pay_hbm, r3_hbm, r2_hbm, r1_hbm,
    wg, wu, wd, og, ou, od, ysum, hbuf, dbuf, act, dg, dup, stage, rbuf, give, take, gate_ref, s_ref, turn_ref, rows_out,
    lsem, ssem, r3sem, r2sem, r1sem, bsem, xssem, xrsem, osem, psem, scs, scr, wsem,
):
    pc = Place(n)
    nz, m = pc.nz, pc.m
    plane = m * m
    c1, c2, c3, e, c = pc.c1, pc.c2, pc.c3, pc.e, pc.c
    weights = (wg, wu, wd)

    def weight(i, src, which):
        return pltpu.make_async_copy(src, weights[i].at[which], wsem.at[i, which])

    for i, (routed, shared, other) in enumerate(((rg, shg, xg), (ru, shu, xu), (rd, shd, xd))):
        pl.when(e == n - 1)(weight(i, shared, c).start)
        pl.when(e != n - 1)(weight(i, routed, c).start)
        weight(i, other, 1 - c).start()
    pc.greet_all()
    turn_ref[...] = jnp.zeros_like(turn_ref)
    for i in range(n):
        turn_ref[i : i + 1, :] = gates_in[i]
    gate_ref[...] = turn_ref[...].T
    grads = (og, ou, od)
    for total in grads:
        total[...] = jnp.zeros_like(total)
    s_ref[...] = jnp.zeros_like(s_ref)

    def dest(t):
        r = t % plane
        return (c1 + t // plane + 1) % nz, (c2 + r % m + 1) % m, (c3 + r // m + 1) % m

    def load(t, i):
        b = pc.blk(*dest(t))
        return (
            pltpu.make_async_copy(h_hbm.at[b], hbuf.at[i], lsem.at[0, i]),
            pltpu.make_async_copy(dy_hbm.at[b], dbuf.at[i], lsem.at[1, i]),
        )

    def partial_copy(i, to, dst, sem):
        return pltpu.make_async_remote_copy(
            src_ref=stage.at[i], dst_ref=dst, send_sem=ssem.at[i], recv_sem=sem,
            device_id=(to, c), device_id_type=MESH,
        )

    def collect(slot, received):
        def fetch(i):
            return pltpu.make_async_copy(received[i][0], rbuf.at[i % 2], bsem.at[i % 2])

        def begin(i):
            src, sem = received[i]
            partial_copy(slot, e, src, sem).wait_recv()
            fetch(i).start()

        begin(0)
        ysum[...] = stage[slot].astype(jnp.float32)
        for i in range(len(received)):
            if i + 1 < len(received):
                begin(i + 1)
            fetch(i).wait()
            ysum[...] += rbuf[i % 2].astype(jnp.float32)

    def from3(a, b2):
        return [(r3_hbm.at[j, a, b2], r3sem.at[j, a, b2]) for j in range(m - 1)]

    def from2(a):
        return [(r2_hbm.at[j, a], r2sem.at[j, a]) for j in range(m - 1)]

    def from1():
        return [(r1_hbm.at[j], r1sem.at[j]) for j in range(nz - 1)]

    def swaps():
        return [
            pltpu.make_async_remote_copy(
                src_ref=give.at[i], dst_ref=take.at[i], send_sem=xssem.at[i], recv_sem=xrsem.at[i],
                device_id=(e, 1 - c), device_id_type=MESH,
            )
            for i in range(3)
        ]

    def totals():
        return [
            pltpu.make_async_copy(src.at[c], dst, osem.at[i])
            for i, (src, dst) in enumerate(((og, tg_hbm), (ou, tu_hbm), (od, td_hbm)))
        ]

    def payload():
        return [pltpu.make_async_copy(give.at[i], pay_hbm.at[i, pl.ds(0, give.shape[1])], psem.at[i]) for i in range(3)]

    def score_send(to):
        return pltpu.make_async_remote_copy(
            src_ref=rows_out.at[to], dst_ref=scores_in.at[e], send_sem=scs.at[to], recv_sem=scr.at[e],
            device_id=(to, c), device_id_type=MESH,
        )

    for copy in load(0, 0):
        copy.start()
    for i, other in enumerate((xg, xu, xd)):
        for which in range(2):
            weight(i, other, which).wait()

    def body(t, carry):
        i = t % 2
        slot = t % slots
        a, b2, b3 = dest(t)
        b = pc.blk(a, b2, b3)
        for copy in load(t, i):
            copy.wait()

        @pl.when(t < n - 1)
        def _():
            for copy in load(t + 1, 1 - i):
                copy.start()

        lane = lax.broadcasted_iota(jnp.int32, gate_ref.shape, 1)
        gate = jnp.sum(jnp.where(lane == b, gate_ref[...], 0.0), axis=1, keepdims=True)
        h = hbuf[i]
        dy = dbuf[i].astype(jnp.float32)
        z = (gate * dy).astype(jnp.bfloat16)
        for half in range(2):
            g = inner_cols(h, wg[half])
            u = inner_cols(h, wu[half])
            da = inner_cols(z, wd[half])
            sg = jax.nn.sigmoid(g)
            si = g * sg
            act[half] = (si * u).astype(jnp.bfloat16)
            dup[half] = (da * si).astype(jnp.bfloat16)
            dg[half] = (da * u * sg * (1.0 + g * (1.0 - sg))).astype(jnp.bfloat16)

        @pl.when(t >= slots)
        def _():
            partial_copy(slot, e, r1_hbm.at[0], r1sem.at[0]).wait_send()

        y = (matmul(act[0], wd[0]) + matmul(act[1], wd[1])).astype(jnp.bfloat16).astype(jnp.float32)
        s = jnp.sum(y * dy, axis=1, keepdims=True)
        s_ref[...] = jnp.where(lane == b, s, s_ref[...])
        stage[slot, 0] = (gate * y).astype(jnp.bfloat16)
        stage[slot, 1] = (
            matmul(dg[0], wg[0]) + matmul(dg[1], wg[1]) + matmul(dup[0], wu[0]) + matmul(dup[1], wu[1])
        ).astype(jnp.bfloat16)

        for j in range(1, m):
            @pl.when(b3 == (c3 + j) % m)
            def _():
                partial_copy(slot, pc.blk(c1, c2, b3), r3_hbm.at[m - j - 1, a, b2], r3sem.at[m - j - 1, a, b2]).start()

        for half in range(2):
            og[half] += outer_rows(dg[half], h)
            ou[half] += outer_rows(dup[half], h)
            od[half] += outer_rows(act[half], z)

        @pl.when(t % plane == plane - 1)
        def _():
            for j in range(1, m):
                to2 = (c2 + j) % m
                at = (t - m + j) % slots
                collect(at, from3(a, to2))
                stage[at] = ysum[...].astype(jnp.bfloat16)
                partial_copy(at, pc.blk(c1, to2, c3), r2_hbm.at[m - j - 1, a], r2sem.at[m - j - 1, a]).start()

        @pl.when((t % plane == 1) & (t >= plane))
        def _():
            at = (t - 2) % slots
            for j in range(1, nz):
                @pl.when(t // plane == j)
                def _():
                    a1 = (c1 + j) % nz
                    collect(at, from3(a1, c2) + from2(a1))
                    stage[at] = ysum[...].astype(jnp.bfloat16)
                    partial_copy(at, pc.blk(a1, c2, c3), r1_hbm.at[nz - j - 1], r1sem.at[nz - j - 1]).start()

        return carry

    lax.fori_loop(0, n, body, 0)
    for i, total in enumerate(grads):
        give[i] = total[1 - c].astype(jnp.bfloat16)
    for copy in swaps():
        copy.start()
    turned = s_ref[...].T
    for i in range(n):
        rows_out[i] = turned[i : i + 1, :]
    scores_in[e] = rows_out[e]

    def score_start(j, carry):
        score_send((e + j) % n).start()
        return carry

    lax.fori_loop(1, n, score_start, 0)
    for copy in swaps():
        copy.wait()
    for i, total in enumerate(grads):
        total[c] += take[i].astype(jnp.float32)
        give[i] = total[c].astype(jnp.bfloat16)
    for copy in totals() + payload():
        copy.start()
    collect((n - 1) % slots, from3(c1, c2) + from2(c1) + from1())
    final = pltpu.make_async_copy(ysum, sums_hbm, bsem.at[0])
    final.start()
    final.wait()
    for t in range(max(0, n - slots), n - 1):
        partial_copy(t % slots, e, r1_hbm.at[0], r1sem.at[0]).wait_send()

    def score_wait(j, carry):
        pltpu.make_async_remote_copy(
            src_ref=rows_out.at[0], dst_ref=scores_in.at[(e + j) % n], send_sem=scs.at[0], recv_sem=scr.at[(e + j) % n],
            device_id=((e + j) % n, c), device_id_type=MESH,
        ).wait_recv()
        score_send((e + j) % n).wait_send()
        return carry

    lax.fori_loop(1, n, score_wait, 0)
    for copy in totals() + payload():
        copy.wait()


def experts(h, dy, gates, routed_w, shared_w, other_w):
    n, rows, width = h.shape
    hidden = shared_w[0].shape[0]
    nz = 4
    m = {16: 2, 64: 4}[n]
    slots = 8
    vmem = pl.BlockSpec(memory_space=pltpu.VMEM)
    hbm = pl.BlockSpec(memory_space=pl.ANY)
    f32, b16 = jnp.float32, jnp.bfloat16
    out = jax.ShapeDtypeStruct
    dma = pltpu.SemaphoreType.DMA
    grad, both = pltpu.VMEM((2, hidden, width), f32), pltpu.VMEM((2, hidden, width), b16)
    return pl.pallas_call(
        functools.partial(experts_kernel, n, slots),
        out_shape=(
            out((n, 1, rows), f32), out((2, rows, width), f32),
            out((hidden, width), f32), out((hidden, width), f32), out((hidden, width), f32),
            out((3, n * blocked(hidden, n), width), b16),
            out((m - 1, nz, m, 2, rows, width), b16), out((m - 1, nz, 2, rows, width), b16), out((nz - 1, 2, rows, width), b16),
        ),
        in_specs=[hbm, hbm, vmem] + [hbm] * 9,
        out_specs=(vmem,) + (hbm,) * 8,
        scratch_shapes=[
            both, both, both, grad, grad, grad,
            pltpu.VMEM((2, rows, width), f32), pltpu.VMEM((2, rows, width), b16), pltpu.VMEM((2, rows, width), b16),
            pltpu.VMEM((2, rows, hidden), b16), pltpu.VMEM((2, rows, hidden), b16), pltpu.VMEM((2, rows, hidden), b16),
            pltpu.VMEM((slots, 2, rows, width), b16), pltpu.VMEM((2, 2, rows, width), b16),
            pltpu.VMEM((3, hidden, width), b16), pltpu.VMEM((3, hidden, width), b16),
            pltpu.VMEM((rows, 128), f32), pltpu.VMEM((rows, 128), f32), pltpu.VMEM((128, rows), f32), pltpu.VMEM((n, 1, rows), f32),
            dma((2, 2)), dma((slots,)), dma((m - 1, nz, m)), dma((m - 1, nz)), dma((nz - 1,)), dma((2,)),
            dma((3,)), dma((3,)), dma((3,)), dma((3,)), dma((n,)), dma((n,)), dma((3, 2)),
        ],
        compiler_params=pltpu.CompilerParams(collective_id=1, has_side_effects=True, vmem_limit_bytes=62 * 2**20),
    )(h, dy, gates, *routed_w, *shared_w, *other_w)


def swap_halves(values):
    return pltpu.roll(values, HD // 2, axis=1)


def route_columns(logit_ref, route_ref, turn_ref):
    count = logit_ref.shape[0]
    logits = logit_ref[...]
    raised = jnp.exp(logits - jnp.max(logits, axis=0, keepdims=True))
    turn_ref[...] = jnp.zeros_like(turn_ref)
    turn_ref[0:count, :] = raised / jnp.sum(raised, axis=0, keepdims=True)
    soft = turn_ref[...].T
    turn_ref[0:count, :] = route_ref[...].astype(jnp.float32)
    return soft, turn_ref[...].T.astype(jnp.int32)


class Scatter:
    def __init__(self, pc, stack, r3, r2, r1, sems):
        self.pc, self.stack, self.r3, self.r2, self.r1 = pc, stack, r3, r2, r1
        self.ssem, self.s3, self.s2, self.s1 = sems

    def copy(self, b, dst, sem, to):
        return pltpu.make_async_remote_copy(
            src_ref=self.stack.at[b], dst_ref=dst, send_sem=self.ssem.at[b], recv_sem=sem,
            device_id=(to, self.pc.c), device_id_type=MESH,
        )

    def add(self, total, src, sem):
        self.copy(self.pc.e, src, sem, self.pc.blk(self.pc.c1, self.pc.c2, self.pc.o3()[0])).wait_recv()
        return total + src[...].astype(jnp.float32)

    def places(self):
        pc = self.pc
        far = [pc.c1 + j for j in range(1, pc.nz)] + [pc.c1]
        return [a % pc.nz for a in far]

    def start(self):
        pc = self.pc
        for k in range(1, pc.m):
            for b2 in pc.o2() + [pc.c2]:
                for a in self.places():
                    b3 = (pc.c3 + k) % pc.m
                    self.copy(pc.blk(a, b2, b3), self.r3.at[pc.m - k - 1, a, b2], self.s3.at[pc.m - k - 1, a, b2], pc.blk(pc.c1, pc.c2, b3)).start()

    def collect(self, a, b2, level):
        pc = self.pc
        total = self.stack[pc.blk(a, b2, pc.c3)].astype(jnp.float32)
        for k in range(pc.m - 1):
            total = self.add(total, self.r3.at[k, a, b2], self.s3.at[k, a, b2])
        if level >= 2:
            for k in range(pc.m - 1):
                total = self.add(total, self.r2.at[k, a], self.s2.at[k, a])
        if level >= 3:
            for k in range(pc.nz - 1):
                total = self.add(total, self.r1.at[k], self.s1.at[k])
        self.stack[pc.blk(a, b2, pc.c3)] = total.astype(jnp.bfloat16)

    def second(self):
        pc = self.pc
        for k in range(1, pc.m):
            for a in self.places():
                b2 = (pc.c2 + k) % pc.m
                self.collect(a, b2, 1)
                self.copy(pc.blk(a, b2, pc.c3), self.r2.at[pc.m - k - 1, a], self.s2.at[pc.m - k - 1, a], pc.blk(pc.c1, b2, pc.c3)).start()

    def third(self):
        pc = self.pc
        for k in range(1, pc.nz):
            a = (pc.c1 + k) % pc.nz
            self.collect(a, pc.c2, 2)
            self.copy(pc.blk(a, pc.c2, pc.c3), self.r1.at[pc.nz - k - 1], self.s1.at[pc.nz - k - 1], pc.blk(a, pc.c2, pc.c3)).start()

    def last(self):
        self.collect(self.pc.c1, self.pc.c2, 3)

    def finish(self):
        pc = self.pc
        for j in range(1, pc.n):
            self.copy((pc.e + j) % pc.n, self.r1.at[0], self.s1.at[0], (pc.e + j) % pc.n).wait_send()


def tail_kernel(
    n,
    x_ref, x1_ref, cot_ref, sums_ref, q_ref, k_ref, v_ref, o_ref, p_ref, wq, wk, wv, wo,
    gain1, gain2, cos_ref, sin_ref, cnt_ref, len_ref, logit_ref, route_ref, scores_in, pay_hbm,
    out_ref, gtok_ref, glog_ref, small_ref, ag0, ag1, ags,
    dx_ref, dq_ref, dk_ref, dv_ref, do_ref, a_ref, give, take, stack0, stack1, r3, r2, r1,
    sm_core, sm_d3, sm_d2, sm_z,
    wbuf, wsem, turn_ref, own_pay,
    gs, gr, ss, s3, s2, s1, xs, xr, cs, cr, scs, scr, locs,
):
    pc = Place(n)
    c1, c2, c3, e, c, nz, m = pc.c1, pc.c2, pc.c3, pc.e, pc.c, pc.nz, pc.m
    rows, width = x_ref.shape
    half = width // 2
    pc.greet_all()


    def deal(i, to):
        return pltpu.make_async_remote_copy(
            src_ref=pay_hbm.at[i, to], dst_ref=own_pay.at[i], send_sem=scs.at[i, to], recv_sem=scr.at[i],
            device_id=(to, c), device_id_type=MESH,
        )

    def keep(i):
        return pltpu.make_async_copy(pay_hbm.at[i, n - 1], own_pay.at[i], scs.at[i, n - 1])

    @pl.when(e == n - 1)
    def _():
        def one(j, carry):
            for i in range(3):
                deal(i, n - 2 - j).start()
            return carry

        lax.fori_loop(0, n - 1, one, 0)
        for i in range(3):
            keep(i).start()

    gather_s = Gather(pc, own_pay, ags, gs.at[2], gr.at[2], 3)
    loc_s = pltpu.make_async_copy(own_pay, ags.at[e], locs.at[2])

    def shared_start():
        @pl.when(e == n - 1)
        def _():
            for i in range(3):
                keep(i).wait()

        @pl.when(e != n - 1)
        def _():
            for i in range(3):
                pltpu.make_async_remote_copy(
                    src_ref=own_pay.at[i], dst_ref=own_pay.at[i], send_sem=scs.at[i, 0], recv_sem=scr.at[i],
                    device_id=(n - 1, c), device_id_type=MESH,
                ).wait_recv()

        gather_s.start()
        loc_s.start()

    def fetch(src, i):
        return pltpu.make_async_copy(src, wbuf.at[i], wsem.at[i])

    fetch(wo, 0).start()
    fetch(wv, 1).start()

    x1 = x1_ref[...]
    up = cot_ref[...].astype(jnp.float32)
    out_ref[...] = (x1 + sums_ref[0]).astype(jnp.bfloat16)
    dh = sums_ref[1]
    r_two = lax.rsqrt(jnp.mean(x1 * x1, axis=-1, keepdims=True) + norm_eps)
    n_two = x1 * r_two
    scaled = dh * gain2[...]
    grad_two = jnp.sum(dh * n_two, axis=0, keepdims=True)
    dx = up + r_two * (scaled - n_two * jnp.mean(scaled * n_two, axis=-1, keepdims=True))
    dx_ref[...] = dx
    dx_low = dx.astype(jnp.bfloat16)

    def columns(ref, which):
        return ref[:, pl.ds(pl.multiple_of(which * half, 128), half)]

    def hand(i):
        return pltpu.make_async_remote_copy(
            src_ref=give.at[i], dst_ref=take.at[i], send_sem=xs.at[i], recv_sem=xr.at[i],
            device_id=(e, 1 - c), device_id_type=MESH,
        )

    def to_partner(i, left, right):
        give[i] = outer_rows(columns(left, 1 - c), right).astype(jnp.bfloat16)
        hand(i).start()

    def own_part(i, left, right, stack, at):
        block = stack.shape[1]
        part = outer_rows(columns(left, c), right)
        hand(i).wait_recv()
        total = (part + take[i].astype(jnp.float32)).astype(jnp.bfloat16)
        stack[pl.ds(at * (half // block), half // block)] = total.reshape(half // block, block, width)

    to_partner(0, o_ref, dx_low)
    fetch(wo, 0).wait()
    do_ref[...] = inner_cols(dx_low, wbuf[0]).astype(jnp.bfloat16)
    fetch(wk, 0).start()
    cosine, sine = cos_ref[...], sin_ref[...]
    scale = HD ** (-0.5)

    def one_head(hd, carry):
        at = pl.ds(pl.multiple_of(hd * HD, HD), HD)
        prob = p_ref[hd]
        d_o, val, que, key = do_ref[:, at], v_ref[:, at], q_ref[:, at], k_ref[:, at]
        dv_ref[:, at] = outer_rows(prob.astype(jnp.bfloat16), d_o).astype(jnp.bfloat16)
        d_prob = inner_cols(d_o, val)
        inner = jnp.sum(prob * d_prob, axis=-1, keepdims=True)
        d_score = (prob * (d_prob - inner)).astype(jnp.bfloat16)
        d_q = matmul(d_score, key) * scale
        d_k = outer_rows(d_score, que) * scale
        dq_ref[:, at] = (d_q * cosine - swap_halves(d_q) * sine).astype(jnp.bfloat16)
        dk_ref[:, at] = (d_k * cosine - swap_halves(d_k) * sine).astype(jnp.bfloat16)
        return carry

    lax.fori_loop(0, HEADS, one_head, 0)
    xv = x_ref[...].astype(jnp.float32)
    r_one = lax.rsqrt(jnp.mean(xv * xv, axis=-1, keepdims=True) + norm_eps)
    n_one = xv * r_one
    a_ref[...] = (n_one * gain1[...]).astype(jnp.bfloat16)
    to_partner(1, a_ref, dv_ref[...])
    to_partner(2, a_ref, dk_ref[...])
    to_partner(3, a_ref, dq_ref[...])
    if n * stack0.shape[1] > 2 * half:
        stack0[...] = jnp.zeros_like(stack0)
        stack1[...] = jnp.zeros_like(stack1)
    own_part(0, o_ref, dx_low, stack0, 0)
    own_part(1, a_ref, dv_ref[...], stack0, 1)
    first = Scatter(pc, stack0, r3.at[0], r2.at[0], r1.at[0], (ss.at[0], s3.at[0], s2.at[0], s1.at[0]))
    second = Scatter(pc, stack1, r3.at[1], r2.at[1], r1.at[1], (ss.at[1], s3.at[1], s2.at[1], s1.at[1]))
    first.start()
    own_part(2, a_ref, dk_ref[...], stack1, 0)
    own_part(3, a_ref, dq_ref[...], stack1, 1)
    second.start()
    shared_start()
    shared_events = gather_s.events()
    fetch(wv, 1).wait()
    da = inner_cols(dv_ref[...], wbuf[1])
    fetch(wq, 1).start()
    fetch(wk, 0).wait()
    da = da + inner_cols(dk_ref[...], wbuf[0])
    fetch(wq, 1).wait()
    da = da + inner_cols(dq_ref[...], wbuf[1])
    scaled_one = da * gain1[...]
    grad_one = jnp.sum(da * n_one, axis=0, keepdims=True)
    back = r_one * (scaled_one - n_one * jnp.mean(scaled_one * n_one, axis=-1, keepdims=True))
    gtok_ref[...] = (dx_ref[...] + back).astype(jnp.bfloat16)

    def exchange(ref, own, level, peers, value):
        ref[own] = value
        copies = [
            pltpu.make_async_remote_copy(
                src_ref=ref.at[own], dst_ref=ref.at[own], send_sem=cs.at[level, i], recv_sem=cr.at[level, own],
                device_id=to, device_id_type=MESH,
            )
            for i, (to, at) in enumerate(peers)
        ]
        for copy in copies:
            copy.start()

        def done():
            for i, (to, at) in enumerate(peers):
                pltpu.make_async_remote_copy(
                    src_ref=ref.at[own], dst_ref=ref.at[at], send_sem=cs.at[level, i], recv_sem=cr.at[level, at],
                    device_id=to, device_id_type=MESH,
                ).wait_recv()
            for copy in copies:
                copy.wait_send()
            total = ref[0]
            for i in range(1, ref.shape[0]):
                total = total + ref[i]
            return total

        return done

    turn_ref[...] = jnp.zeros_like(turn_ref)
    for i in range(n):
        turn_ref[i : i + 1, :] = scores_in[i]
    scores = turn_ref[...].T
    lane = lax.broadcasted_iota(jnp.int32, (rows, 128), 1)
    row = lax.broadcasted_iota(jnp.int32, (rows, 128), 0)
    scores = jnp.where(row < len_ref[0], scores, 0.0)
    soft, routes = route_columns(logit_ref, route_ref, turn_ref)
    share = jnp.zeros((rows, 128), jnp.float32)
    for i in range(route_ref.shape[0]):
        picked = jnp.sum(jnp.where(lane == routes[:, i : i + 1], scores, 0.0), axis=-1, keepdims=True)
        share = jnp.where(lane == i, picked, share)
    grad_logits = soft * (share - jnp.sum(soft * share, axis=-1, keepdims=True))
    glog_ref[...] = grad_logits.T[0 : route_ref.shape[0], :]

    small = jnp.concatenate([grad_one, grad_two, cnt_ref[...], jnp.zeros((5, width), jnp.float32)], axis=0)
    level0 = exchange(sm_core, c, 0, [((e, 1 - c), 1 - c)], small)
    first.second()
    shared_events[0]()
    level1 = exchange(sm_d3, c3, 1, [((pc.blk(c1, c2, j), c), j) for j in pc.o3()], level0())
    second.second()
    shared_events[1]()
    level2 = exchange(sm_d2, c2, 2, [((pc.blk(c1, j, c3), c), j) for j in pc.o2()], level1())
    first.third()
    level3 = exchange(sm_z, c1, 3, [((pc.blk((c1 + j) % nz, c2, c3), c), (c1 + j) % nz) for j in range(1, nz)], level2())
    shared_events[2]()
    second.third()
    shared_events[3]()
    small_ref[...] = level3()
    first.last()
    g0 = Gather(pc, stack0.at[e], ag0, gs.at[0], gr.at[0], stack0.shape[1])
    g0.start()
    loc0 = pltpu.make_async_copy(stack0.at[e], ag0.at[e], locs.at[0])
    loc0.start()
    shared_events[4]()
    second.last()
    g1 = Gather(pc, stack1.at[e], ag1, gs.at[1], gr.at[1], stack1.shape[1])
    g1.start()
    loc1 = pltpu.make_async_copy(stack1.at[e], ag1.at[e], locs.at[1])
    loc1.start()
    for event in shared_events[5:-1]:
        event()
    run_staggered(g0.events(), g1.events(), 1)
    shared_events[-1]()
    for g in (gather_s, g0, g1):
        g.finish()
    first.finish()
    second.finish()
    loc_s.wait()
    loc0.wait()
    loc1.wait()
    for i in range(4):
        hand(i).wait_send()

    @pl.when(e == n - 1)
    def _():
        def one(j, carry):
            for i in range(3):
                deal(i, j).wait_send()
            return carry

        lax.fori_loop(0, n - 1, one, 0)


def tail(n, x, x1, cot, sums, q, k, v, o, prob, wq, wk, wv, wo, gain1, gain2, cosine, sine, cnt, length, logits, routes, scores, pay):
    nz = 4
    m = {16: 2, 64: 4}[n]
    rows, width = x.shape
    half = width // 2
    block = blocked(2 * half, n)
    vmem = pl.BlockSpec(memory_space=pltpu.VMEM)
    hbm = pl.BlockSpec(memory_space=pl.ANY)
    f32, b16 = jnp.float32, jnp.bfloat16
    out = jax.ShapeDtypeStruct
    dma = pltpu.SemaphoreType.DMA
    wide = pltpu.VMEM((rows, width), b16)
    return pl.pallas_call(
        functools.partial(tail_kernel, n),
        out_shape=(
            out((rows, width), b16), out((rows, width), b16), out(logits.shape, f32), out((8, width), f32),
            out((n, block, width), b16), out((n, block, width), b16),
            out((n, 3, pay.shape[2], width), b16),
        ),
        in_specs=[vmem] * 9 + [hbm] * 4 + [vmem] * 5 + [pl.BlockSpec(memory_space=pltpu.SMEM)] + [vmem] * 3 + [hbm],
        out_specs=(vmem,) * 4 + (hbm,) * 3,
        scratch_shapes=[
            pltpu.VMEM((rows, width), f32), wide, wide, wide, wide, wide,
            pltpu.VMEM((4, half, width), b16), pltpu.VMEM((4, half, width), b16),
            pltpu.VMEM((n, block, width), b16), pltpu.VMEM((n, block, width), b16),
            pltpu.VMEM((2, m - 1, nz, m, block, width), b16), pltpu.VMEM((2, m - 1, nz, block, width), b16),
            pltpu.VMEM((2, nz - 1, block, width), b16),
            pltpu.VMEM((2, 8, width), f32), pltpu.VMEM((m, 8, width), f32), pltpu.VMEM((m, 8, width), f32), pltpu.VMEM((nz, 8, width), f32),
            pltpu.VMEM((2, width, width), b16), dma((2,)), pltpu.VMEM((128, rows), f32), pltpu.VMEM((3, pay.shape[2], width), b16),
            dma((3, 160)), dma((3, 2, n)), dma((2, n)), dma((2, m - 1, nz, m)), dma((2, m - 1, nz)), dma((2, nz - 1)),
            dma((4,)), dma((4,)), dma((4, max(nz, m))), dma((4, max(nz, m, 2))), dma((3, n)), dma((3,)), dma((3,)),
        ],
        compiler_params=pltpu.CompilerParams(collective_id=2, has_side_effects=True, vmem_limit_bytes=62 * 2**20),
    )(x, x1, cot, sums, q, k, v, o, prob, wq, wk, wv, wo, gain1, gain2, cosine, sine, cnt, length, logits, routes, scores, pay)


def blocked(count, n):
    return -(-count // (16 * n)) * 16


def from_blocks(blocks, count):
    return blocks.reshape(-1, blocks.shape[2])[:count].astype(jnp.float32)


def rotary_rows(seq_len):
    position = np.arange(seq_len).astype(np.float32)
    inverse_freq = (rotary_base ** (-2.0 * np.arange(HD // 2).astype(np.float32) / HD)).astype(np.float32)
    angle = position[:, None] * inverse_freq[None, :]
    cosine, sine = np.cos(angle), np.sin(angle)
    return np.concatenate([cosine, cosine], axis=1), np.concatenate([-sine, sine], axis=1)


def on_device(
    tokens, norm_one, w_query, w_key, w_value, w_out, norm_two, r_gate, r_up, r_down, s_gate, s_up, s_down,
    logits, routes, lengths, cotangent,
):
    rows, width = tokens.shape
    n = lax.axis_size("exp")
    hidden = s_gate.shape[1]
    cosine, sine = (jnp.asarray(table) for table in rotary_rows(rows))
    gain1, gain2 = norm_one[None], norm_two[None]
    logits, routes = logits.T, routes.T
    attn_w = (w_query, w_key, w_value, w_out)
    routed_w = (r_gate[0].T, r_up[0].T, r_down[0])
    shared_w = (s_gate.T, s_up.T, s_down)
    (
        all_dy, all_h, fq, fk, fv, fo, fg, fu, fd, mixed, queries, keys_all, values_all, attended, prob, gates, counts,
    ) = front(
        n, tokens, cotangent, gain1, gain2, cosine, sine, lengths, logits, routes,
        attn_w, routed_w, shared_w,
    )
    scores, sums, tg, tu, td, payload = experts(
        all_h, all_dy, gates, routed_w, shared_w, (fg, fu, fd)
    )[:6]
    full = (width, width)
    output, grad_tokens, grad_logits, small_sums, sum0, sum1, sum_s = tail(
        n, tokens, mixed, cotangent, sums, queries, keys_all, values_all, attended, prob,
        fq.reshape(full), fk.reshape(full), fv.reshape(full), fo.reshape(full),
        gain1, gain2, cosine, sine, counts, lengths, logits, routes, scores,
        payload.reshape(3, n, -1, width),
    )
    half = width // 2
    wout_value = from_blocks(sum0, width)
    key_query = from_blocks(sum1, width)
    holds_shared = lax.axis_index("exp") == n - 1
    tg, tu, td = (jnp.where(holds_shared, 0.0, grad) for grad in (tg, tu, td))
    sg, su, sd = (from_blocks(sum_s[:, i], hidden) for i in range(3))
    return (
        output, grad_tokens, small_sums[0],
        key_query[half:], key_query[:half], wout_value[half:], wout_value[:half],
        small_sums[1], tg.T[None], tu.T[None], td[None], sg.T, su.T, sd,
        grad_logits.T, small_sums[2, :n].astype(jnp.int32),
    )


def solution(mesh):
    in_specs = (
        P(("exp", "hid"), None),
        P(),
        P("hid", None),
        P("hid", None),
        P("hid", None),
        P("hid", None),
        P(),
        P("exp", None, "hid"),
        P("exp", None, "hid"),
        P("exp", "hid", None),
        P(None, "hid"),
        P(None, "hid"),
        P("hid", None),
        P(("exp", "hid"), None),
        P(("exp", "hid"), None),
        P(("exp", "hid")),
        P(("exp", "hid"), None),
    )
    out_specs = (
        P(("exp", "hid"), None),
        P(("exp", "hid"), None),
        P(),
        P("hid", None),
        P("hid", None),
        P("hid", None),
        P("hid", None),
        P(),
        P("exp", None, "hid"),
        P("exp", None, "hid"),
        P("exp", "hid", None),
        P(None, "hid"),
        P(None, "hid"),
        P("hid", None),
        P(("exp", "hid"), None),
        P(),
    )
    return jax.shard_map(
        on_device, mesh=mesh, in_specs=in_specs, out_specs=out_specs, check_vma=False
    )
```

```python
import functools

import jax
import jax.numpy as jnp
import numpy as np
from jax import lax
from jax.experimental import pallas as pl
from jax.experimental.pallas import tpu as pltpu
from jax.sharding import PartitionSpec as P

HEADS = 10
HD = 128
MESH = pl.DeviceIdType.MESH


norm_eps = 1e-06
rotary_base = 10000.0
contract_rows = (((0,), (0,)), ((), ()))
contract_cols = (((1,), (1,)), ((), ()))


def matmul(left_side, right_side):
    return jnp.dot(left_side, right_side, preferred_element_type=jnp.float32)


def outer_rows(left_side, right_side):
    return lax.dot_general(left_side, right_side, contract_rows, preferred_element_type=jnp.float32)


def inner_cols(left_side, right_side):
    return lax.dot_general(left_side, right_side, contract_cols, preferred_element_type=jnp.float32)


class Place:
    def __init__(self, n):
        self.n = n; self.nz = 4; self.m = {16: 2, 64: 4}[n]; m = self.m
        self.e = lax.axis_index("exp"); self.c = lax.axis_index("hid"); c = self.c; e = self.e
        self.s1 = m * m; self.s2 = 1 + c * (m - 1); self.s3 = m - c * (m - 1)
        self.x = e % m; self.y = (e // m) % m
        self.c1 = e // self.s1; self.c2 = (e // self.s2) % m; self.c3 = (e // self.s3) % m
    def chip(self, z, y, x): return z * self.s1 + y * self.m + x
    def block(self, z, y): return z * self.m + y
    def others(self):
        far = [((self.c1 + i) % self.nz, (self.y + j) % self.m) for i in range(self.nz) for j in range(self.m)]
        return far[1:]
    def blk(self, a, b, d): return a * self.s1 + b * self.s2 + d * self.s3
    def o2(self): return [(self.c2 + j) % self.m for j in range(1, self.m)]
    def o3(self): return [(self.c3 + j) % self.m for j in range(1, self.m)]
    def greet_all(self):
        barrier = pltpu.get_barrier_semaphore()

        def greet(j, carry):
            pl.semaphore_signal(barrier, inc=1, device_id=((self.e + j) % self.n, self.c), device_id_type=MESH)
            return carry

        lax.fori_loop(1, self.n, greet, 0)
        pl.semaphore_signal(barrier, inc=1, device_id=(self.e, 1 - self.c), device_id_type=MESH)
        pl.semaphore_wait(barrier, self.n)


class Gather:
    def __init__(self, pc, src, dst, ssem, rsem, split, base=0):
        self.pc, self.src, self.dst, self.ssem, self.rsem = pc, src, dst, ssem, rsem
        self.split = split; self.sends = []; self.base = base
    def view(self, ref, part):
        R = self.src.shape[0]
        return ref.at[pl.ds(0, self.split)] if part == 0 else ref.at[pl.ds(self.split, R - self.split)]
    def send(self, part, own, b, to, cond=None):
        i = self.base + len(self.sends)
        src = self.view(self.src if own else self.dst.at[b], part)
        cp = pltpu.make_async_remote_copy(src_ref=src, dst_ref=self.view(self.dst.at[b], part), send_sem=self.ssem.at[i], recv_sem=self.rsem.at[part, b], device_id=(to, self.pc.c), device_id_type=MESH)
        self.sends.append((cond, cp))
        if cond is None: cp.start()
        else: pl.when(cond)(cp.start)
    def wait(self, part, b):
        v = self.view(self.dst.at[b], part)
        to = self.pc.blk(self.pc.c1, self.pc.c2, self.pc.o3()[0])
        pltpu.make_async_remote_copy(src_ref=v, dst_ref=v, send_sem=self.ssem.at[0], recv_sem=self.rsem.at[part, b], device_id=(to, self.pc.c), device_id_type=MESH).wait_recv()
    def updown(self, part, own, b):
        pc = self.pc
        self.send(part, own, b, pc.blk(pc.c1 + 1, pc.c2, pc.c3), pc.c1 < pc.nz - 1)
        self.send(part, own, b, pc.blk(pc.c1 - 1, pc.c2, pc.c3), pc.c1 > 0)
    def to2(self, part, own, b):
        pc = self.pc
        for j in pc.o2(): self.send(part, own, b, pc.blk(pc.c1, j, pc.c3))
    def to3(self, part, own, b):
        pc = self.pc
        for j in pc.o3(): self.send(part, own, b, pc.blk(pc.c1, pc.c2, j))
    def start(self):
        e = self.pc.e
        self.to3(0, True, e); self.to2(0, True, e); self.updown(0, True, e)
        if self.split < self.src.shape[0]:
            self.to3(1, True, e); self.to2(1, True, e); self.updown(1, True, e)
    def zarr(self, part, s, up, k2, k3, more):
        pc = self.pc
        a = pc.c1 - s if up else pc.c1 + s
        cond = (pc.c1 >= s) if up else (pc.c1 < pc.nz - s)
        b = pc.blk(a, k2, k3)
        pl.when(cond)(lambda: self.wait(part, b))
        if s < pc.nz - 1:
            if up: self.send(part, False, b, pc.blk(pc.c1 + 1, pc.c2, pc.c3), (pc.c1 >= s) & (pc.c1 < pc.nz - 1))
            else: self.send(part, False, b, pc.blk(pc.c1 - 1, pc.c2, pc.c3), (pc.c1 < pc.nz - s) & (pc.c1 > 0))
        if more:
            for j in pc.o2(): self.send(part, False, b, pc.blk(pc.c1, j, pc.c3), cond)
            for j in pc.o3(): self.send(part, False, b, pc.blk(pc.c1, pc.c2, j), cond)
    def events(self):
        pc = self.pc; ev = []
        def a2(s):
            def go():
                for j in pc.o2():
                    for sg in ((1, -1) if s else (1,)):
                        a = pc.c1 + sg * s
                        cond = None if s == 0 else ((a >= 0) & (a < pc.nz))
                        b = pc.blk(a, j, pc.c3)
                        if cond is None: self.wait(0, b)
                        else: pl.when(cond)(lambda b=b: self.wait(0, b))
                        for k in pc.o3(): self.send(0, False, b, pc.blk(pc.c1, pc.c2, k), cond)
            return go
        def az(s):
            def go():
                self.zarr(0, s, True, pc.c2, pc.c3, True); self.zarr(0, s, False, pc.c2, pc.c3, True)
            return go
        B = self.split < self.src.shape[0]
        def f1():
            for j in pc.o2():
                b = pc.blk(pc.c1, j, pc.c3); self.wait(1, b); self.to3(1, False, b); self.updown(1, False, b)
        def f2():
            for k in pc.o3():
                b = pc.blk(pc.c1, pc.c2, k); self.wait(1, b); self.updown(1, False, b)
        def f3():
            for j in pc.o2():
                for k in pc.o3():
                    b = pc.blk(pc.c1, j, k); self.wait(1, b); self.updown(1, False, b)
        def fz(s):
            def go():
                for k2 in range(pc.m):
                    for k3 in range(pc.m):
                        self.zarr(1, s, True, k2, k3, False); self.zarr(1, s, False, k2, k3, False)
            return go
        ev += [az(1), a2(0)]
        if B: ev += [f1, f2, f3]
        ev += [az(2), a2(1)]
        if B: ev += [fz(1)]
        ev += [az(3), a2(2)]
        if B: ev += [fz(2)]
        ev += [a2(3)]
        if B: ev += [fz(3)]
        def last():
            for a in range(pc.nz):
                for j in range(pc.m):
                    for k in pc.o3(): self.wait(0, pc.blk(a, j, k))
        ev += [last]
        return ev
    def finish(self):
        for cond, cp in self.sends:
            if cond is None: cp.wait_send()
            else: pl.when(cond)(cp.wait_send)


class Lines:
    def __init__(self, pc, src, dst, ssem, rsem):
        self.pc, self.src, self.dst, self.ssem, self.rsem = pc, src, dst, ssem, rsem
        self.places = [(0, way, 0) for way in (1, -1)] + [(0, 0, j) for j in range(1, pc.m)]
        for s in range(1, pc.nz):
            for way in (1, -1):
                self.places += [(s, way, j) for j in range(0 if s < pc.nz - 1 else 1, pc.m)]

    def send(self, place):
        pc = self.pc
        s, way, j = place
        a = pc.c1 - way * s
        b = pc.block(a, pc.y)
        on = pc.c1 + way
        to = pc.chip(on, pc.y, pc.x) if j == 0 else pc.chip(pc.c1, (pc.y + j) % pc.m, pc.x)
        cond = (a >= 0) & (a < pc.nz)
        if j == 0:
            cond = cond & (on >= 0) & (on < pc.nz)
        copy = pltpu.make_async_remote_copy(
            src_ref=self.src if s == 0 else self.dst.at[b], dst_ref=self.dst.at[b],
            send_sem=self.ssem.at[self.places.index(place)], recv_sem=self.rsem.at[b],
            device_id=(to, pc.c), device_id_type=MESH,
        )
        return cond, copy

    def wait(self, b):
        pc = self.pc
        pltpu.make_async_remote_copy(
            src_ref=self.dst.at[b], dst_ref=self.dst.at[b], send_sem=self.ssem.at[0], recv_sem=self.rsem.at[b],
            device_id=(pc.chip(pc.c1, (pc.y + 1) % pc.m, pc.x), pc.c), device_id_type=MESH,
        ).wait_recv()

    def pass_on(self, s):
        for place in self.places:
            if place[0] == s:
                cond, copy = self.send(place)
                pl.when(cond)(copy.start)

    def start(self):
        self.pass_on(0)

    def line(self, s):
        self.wait_line(s)
        self.pass_on(s)

    def wait_line(self, s):
        pc = self.pc
        for way in (1, -1):
            a = pc.c1 - way * s
            pl.when((a >= 0) & (a < pc.nz))(functools.partial(self.wait, pc.block(a, pc.y)))

    def wait_far(self):
        pc = self.pc
        for a in range(pc.nz):
            for j in range(1, pc.m):
                self.wait(pc.block(a, (pc.y + j) % pc.m))

    def finish(self, distances):
        for place in self.places:
            if place[0] in distances:
                cond, copy = self.send(place)
                pl.when(cond)(copy.wait_send)


def run_staggered(first, second, lag):
    for i in range(max(len(first), len(second) + lag)):
        if i < len(first):
            first[i]()
        if lag <= i < len(second) + lag:
            second[i - lag]()


def part_rows(rows):
    return rows - rows // 80 * 16


def front_kernel(
    n,
    x_ref, cot_ref, gain1, gain2, cos_ref, sin_ref, len_ref, logit_ref, route_ref,
    wq, wk, wv, wo, rg, ru, rd, sg, su, sd,
    all_dy, h_all, fq, fk, fv, fo, fg, fu, fd, pg, pu, pd,
    x1_ref, q_ref, k_ref, v_ref, o_ref, p_ref, gates_in, cnt_ref,
    wbuf, h_ref, rows_out, turn_ref,
    gs, gr, hs, hr, ls, ws, wr, wl, es, er, gss, grs, ps, pr, qs, qr,
):
    pc = Place(n)
    e, c = pc.e, pc.c
    rows, width = x_ref.shape
    half = width // 2
    pc.greet_all()
    x, y, m = pc.x, pc.y, pc.m
    me = pc.block(pc.c1, y)
    gather_dy = Lines(pc, cot_ref, all_dy, gs, gr)
    gather_h = Lines(pc, h_ref, h_all, hs, hr)
    own_dy = pltpu.make_async_copy(cot_ref, all_dy.at[me], ls.at[0])
    own_h = pltpu.make_async_copy(h_ref, h_all.at[me], ls.at[1])
    own_dy.start()
    partner = (e, 1 - c)
    halves = (wq, wk, wv, wo)
    fulls = (fq, fk, fv, fo)

    def swap(i):
        return pltpu.make_async_remote_copy(
            src_ref=halves[i], dst_ref=wbuf.at[i, c], send_sem=ws.at[i], recv_sem=wr.at[i],
            device_id=partner, device_id_type=MESH,
        )

    def own(i):
        return pltpu.make_async_copy(halves[i], wbuf.at[i, c], wl.at[0, i])

    def keep(i):
        return pltpu.make_async_copy(wbuf.at[i], fulls[i], wl.at[1, i])

    experts_other = (fg, fu, fd)

    def expert_swap(i, src):
        return pltpu.make_async_remote_copy(
            src_ref=src, dst_ref=experts_other[i], send_sem=es.at[i], recv_sem=er.at[i],
            device_id=partner, device_id_type=MESH,
        )

    beside = (pg, pu, pd)

    def half_send(i, j, src):
        return pltpu.make_async_remote_copy(
            src_ref=src, dst_ref=beside[i].at[m - j - 1, c], send_sem=ps.at[i, j - 1], recv_sem=pr.at[i, m - j - 1],
            device_id=(pc.chip(pc.c1, y, (x + j) % m), c), device_id_type=MESH,
        )

    def half_on(i, k):
        return pltpu.make_async_remote_copy(
            src_ref=beside[i].at[k, c], dst_ref=beside[i].at[k, c], send_sem=qs.at[i, k], recv_sem=qr.at[i, k],
            device_id=partner, device_id_type=MESH,
        )

    for i in range(4):
        swap(i).start()
        own(i).start()
    for i, (routed, shared) in enumerate(((rg, sg), (ru, su), (rd, sd))):
        @pl.when(e == n - 1)
        def _():
            expert_swap(i, shared).start()
            for j in range(1, m):
                half_send(i, j, shared).start()

        @pl.when(e != n - 1)
        def _():
            expert_swap(i, routed).start()
            for j in range(1, m):
                half_send(i, j, routed).start()

    gather_dy.start()

    lane = lax.broadcasted_iota(jnp.int32, (rows, 128), 1)
    row = lax.broadcasted_iota(jnp.int32, (rows, 128), 0)
    valid = (row < len_ref[0]).astype(jnp.float32)
    soft, routes = route_columns(logit_ref, route_ref, turn_ref)
    dense = jnp.zeros((rows, 128), jnp.float32)
    named = jnp.zeros((rows, 128), jnp.float32)
    for i in range(route_ref.shape[0]):
        hit = lane == routes[:, i : i + 1]
        dense = dense + jnp.where(hit, soft[:, i : i + 1], 0.0)
        named = named + jnp.where(hit, 1.0, 0.0)
    dense = jnp.where(lane == n - 1, 1.0, dense * valid)
    cnt_ref[...] = jnp.zeros_like(cnt_ref)
    cnt_ref[:, 0:128] = jnp.sum(named * valid, axis=0, keepdims=True)
    turned = dense.T
    for i in range(n):
        rows_out[i] = turned[i : i + 1, :]
    for i in range(m):
        gates_in[me * m + i] = rows_out[me * m + i]

    def gate_send(a, b2):
        return pltpu.make_async_remote_copy(
            src_ref=rows_out.at[pl.ds(pc.block(a, b2) * m, m)], dst_ref=gates_in.at[pl.ds(me * m, m)],
            send_sem=gss.at[a, b2], recv_sem=grs.at[pc.c1, y],
            device_id=(pc.chip(a, b2, x), c), device_id_type=MESH,
        )

    def gate_wait(a, b2):
        at = pl.ds(pc.block(a, b2) * m, m)
        pltpu.make_async_remote_copy(
            src_ref=rows_out.at[at], dst_ref=gates_in.at[at], send_sem=gss.at[a, b2], recv_sem=grs.at[a, b2],
            device_id=(pc.chip(a, b2, x), c), device_id_type=MESH,
        ).wait_recv()

    for a, b2 in pc.others():
        gate_send(a, b2).start()

    xv = x_ref[...].astype(jnp.float32)
    a = (xv * lax.rsqrt(jnp.mean(xv * xv, axis=-1, keepdims=True) + norm_eps) * gain1[...]).astype(jnp.bfloat16)
    cosine, sine = cos_ref[...], sin_ref[...]

    def project(values, i):
        own(i).wait()
        swap(i).wait_recv()
        keep(i).start()
        return matmul(values[:, :half], wbuf[i, 0]) + matmul(values[:, half:], wbuf[i, 1])

    for i, ref in ((0, q_ref), (1, k_ref)):
        flat = project(a, i)
        for hd in range(HEADS):
            part = flat[:, hd * HD : (hd + 1) * HD]
            ref[:, hd * HD : (hd + 1) * HD] = (part * cosine + swap_halves(part) * sine).astype(jnp.bfloat16)
    v_ref[...] = project(a, 2).astype(jnp.bfloat16)
    gather_dy.line(1)
    scale = HD ** (-0.5)
    row_pos = lax.broadcasted_iota(jnp.int32, (rows, rows), 0)
    col_pos = lax.broadcasted_iota(jnp.int32, (rows, rows), 1)
    allowed = (col_pos <= row_pos) & (col_pos < len_ref[0])

    def one_head(hd, carry):
        at = pl.ds(pl.multiple_of(hd * HD, HD), HD)
        scores = jnp.where(allowed, inner_cols(q_ref[:, at], k_ref[:, at]) * scale, -1e30)
        up = jnp.exp(scores - jnp.max(scores, axis=-1, keepdims=True))
        prob = up / jnp.sum(up, axis=-1, keepdims=True)
        p_ref[hd] = prob
        o_ref[:, at] = matmul(prob.astype(jnp.bfloat16), v_ref[:, at]).astype(jnp.bfloat16)
        return carry

    lax.fori_loop(0, HEADS, one_head, 0)
    gather_dy.line(2)
    x1 = xv + project(o_ref[...], 3)
    x1_ref[...] = x1
    h_ref[...] = (x1 * lax.rsqrt(jnp.mean(x1 * x1, axis=-1, keepdims=True) + norm_eps) * gain2[...]).astype(jnp.bfloat16)
    gather_h.start()
    own_h.start()
    for i in range(3, pc.nz):
        gather_dy.line(i)
    for k in range(m - 1):
        for i in range(3):
            half_send(i, m - k - 1, sd).wait_recv()
            half_on(i, k).start()
    gather_dy.wait_far()
    for a, b2 in pc.others():
        gate_wait(a, b2)
        gate_send(a, b2).wait_send()
    gather_h.wait_line(1)
    for j in range(1, m):
        gather_h.wait(pc.block(pc.c1, (y + j) % m))
    gather_dy.finish(range(pc.nz))
    gather_h.finish((0,))
    own_dy.wait()
    own_h.wait()
    for i in range(4):
        swap(i).wait_send()
        keep(i).wait()
    for i, shared in enumerate((sg, su, sd)):
        expert_swap(i, shared).wait()
        for k in range(m - 1):
            half_send(i, k + 1, shared).wait_send()
            half_on(i, k).wait_send()
            other = pltpu.make_async_remote_copy(
                src_ref=beside[i].at[k, 1 - c], dst_ref=beside[i].at[k, 1 - c], send_sem=qs.at[i, k], recv_sem=qr.at[i, k],
                device_id=partner, device_id_type=MESH,
            )
            other.wait_recv()


def front(n, x, cot, gain1, gain2, cosine, sine, length, logits, routes, attn_w, routed_w, shared_w):
    rows, width = x.shape
    hidden = shared_w[0].shape[0]
    vmem = pl.BlockSpec(memory_space=pltpu.VMEM)
    hbm = pl.BlockSpec(memory_space=pl.ANY)
    f32, b16 = jnp.float32, jnp.bfloat16
    out = jax.ShapeDtypeStruct
    dma = pltpu.SemaphoreType.DMA
    wide = out((rows, width), b16)
    full = out((2, width // 2, width), b16)
    nz = 4
    m = {16: 2, 64: 4}[n]
    beside = out((m - 1, 2, hidden, width), b16)
    return pl.pallas_call(
        functools.partial(front_kernel, n),
        out_shape=(
            out((nz * m, rows, width), b16), out((nz * m, rows, width), b16), full, full, full, full,
            out((hidden, width), b16), out((hidden, width), b16), out((hidden, width), b16), beside, beside, beside,
            out((rows, width), f32), wide, wide, wide, wide, out((HEADS, rows, rows), f32),
            out((n, 1, rows), f32), out((1, width), f32),
        ),
        in_specs=[vmem] * 6 + [pl.BlockSpec(memory_space=pltpu.SMEM)] + [vmem] * 2 + [hbm] * 10,
        out_specs=(hbm,) * 12 + (vmem,) * 8,
        scratch_shapes=[
            pltpu.VMEM((4, 2, width // 2, width), b16), pltpu.VMEM((rows, width), b16), pltpu.VMEM((n, 1, rows), f32), pltpu.VMEM((128, rows), f32),
            dma((64,)), dma((nz * m,)), dma((64,)), dma((nz * m,)), dma((2,)), dma((4,)), dma((4,)), dma((2, 4)), dma((3,)), dma((3,)),
            dma((nz, m)), dma((nz, m)), dma((3, m - 1)), dma((3, m - 1)), dma((3, m - 1)), dma((3, m - 1)),
        ],
        compiler_params=pltpu.CompilerParams(collective_id=0, has_side_effects=True, vmem_limit_bytes=56 * 2**20),
    )(x, cot, gain1, gain2, cosine, sine, length, logits, routes, *attn_w, *routed_w, *shared_w)


def experts_kernel(
    n, slots,
    h_in, dy_hbm, gates_in, rg, ru, rd, shg, shu, shd, xg, xu, xd, pg, pu, pd,
    scores_in, du_hbm, tg_hbm, tu_hbm, td_hbm, pay_hbm, y_hbm, far_hbm, h_all, part_hbm, xt_hbm, r3_hbm, r1_hbm,
    wbuf, og, ou, od, total_ref, hbuf, dbuf, act, dg, dup, stage, pbuf, rbuf, give, take, keep,
    gate_ref, s_ref, turn_ref, rows_out,
    gs, gr, lsem, ssem, r3sem, r1sem, bsem, wsem, partsem, pbsem, ysem,
    xssem, xrsem, gsend, grecv, osem, psem, scs, scr, room,
):
    pc = Place(n)
    nz, m = pc.nz, pc.m
    c1, e, c, x, y = pc.c1, pc.e, pc.c, pc.x, pc.y
    blocks = nz * m
    me = pc.block(c1, y)
    toward = 1 - 2 * (c1 // (nz // 2))
    together = nz // 2
    grads = (og, ou, od)
    own_half = ((rg, shg), (ru, shu), (rd, shd))
    other_half = (xg, xu, xd)
    shared_half = (pg, pu, pd)

    def weight(p, i, half, src):
        return pltpu.make_async_copy(src, wbuf.at[p % 2, i, half], wsem.at[p % 2, i, half])

    def weights_start(p):
        for i in range(3):
            if p < m - 1:
                for half in range(2):
                    weight(p, i, half, shared_half[i].at[p, half]).start()
            else:
                routed, shared = own_half[i]
                pl.when(e == n - 1)(weight(p, i, c, shared).start)
                pl.when(e != n - 1)(weight(p, i, c, routed).start)
                weight(p, i, 1 - c, other_half[i]).start()

    weights_start(0)
    weights_start(1)
    first_h = pltpu.make_async_copy(h_all.at[me], hbuf.at[0], lsem.at[0, 0])
    first_dy = pltpu.make_async_copy(dy_hbm.at[me], dbuf.at[0], lsem.at[1, 0])
    first_h.start()
    first_dy.start()
    pc.greet_all()
    gather = Lines(pc, None, h_all, gs, gr)
    gather.pass_on(1)
    turn_ref[...] = jnp.zeros_like(turn_ref)
    for i in range(n):
        turn_ref[i : i + 1, :] = gates_in[i]
    gate_ref[...] = turn_ref[...].T
    for total in grads:
        total[...] = jnp.zeros_like(total)
    s_ref[...] = jnp.zeros_like(s_ref)

    def dest(step):
        p, t = step // blocks, step % blocks
        last = (p + 1) // m
        return (c1 + toward * (t // m + last) + nz) % nz, (y + t % m + last) % m

    def load(step, i):
        b = pc.block(*dest(step))
        return (
            pltpu.make_async_copy(h_all.at[b], hbuf.at[i], lsem.at[0, i]),
            pltpu.make_async_copy(dy_hbm.at[b], dbuf.at[i], lsem.at[1, i]),
        )

    def part_load(step, i):
        return pltpu.make_async_copy(part_hbm.at[pc.block(*dest(step))], pbuf.at[i], pbsem.at[i])

    def part_store(slot, b):
        return pltpu.make_async_copy(stage.at[slot], part_hbm.at[b], partsem.at[slot])

    def y_store(slot, a, b2):
        return pltpu.make_async_copy(stage.at[slot, 0], y_hbm.at[a, b2], ysem.at[slot])

    def pair_send(slot, to, dst, sem):
        return pltpu.make_async_remote_copy(
            src_ref=stage.at[slot], dst_ref=dst, send_sem=ssem.at[slot], recv_sem=sem,
            device_id=(to, c), device_id_type=MESH,
        )

    def du_send(slot, to, dst, sem):
        return pltpu.make_async_remote_copy(
            src_ref=stage.at[slot, 1], dst_ref=dst, send_sem=ssem.at[slot], recv_sem=sem,
            device_id=(to, c), device_id_type=MESH,
        )

    def collect(slot, received):
        def fetch(i):
            return pltpu.make_async_copy(received[i][0], rbuf.at[i % 2], bsem.at[i % 2])

        def begin(i):
            src, sem, landed = received[i]
            pltpu.make_async_remote_copy(
                src_ref=landed, dst_ref=landed, send_sem=ssem.at[slot], recv_sem=sem,
                device_id=(e, 1 - c), device_id_type=MESH,
            ).wait_recv()
            fetch(i).start()

        begin(0)
        total_ref[...] = stage[slot, 1].astype(jnp.float32)
        for i in range(len(received)):
            if i + 1 < len(received):
                begin(i + 1)
            fetch(i).wait()
            total_ref[...] += rbuf[i % 2].astype(jnp.float32)

    def from_y(a, whole):
        if whole:
            return [(far_hbm.at[j, a, 1], r3sem.at[j, a], far_hbm.at[j, a]) for j in range(m - 1)]
        return [(r3_hbm.at[j, a], r3sem.at[j, a], r3_hbm.at[j, a]) for j in range(m - 1)]

    def from_z():
        return [(r1_hbm.at[(c1 + j) % nz], r1sem.at[(c1 + j) % nz], r1_hbm.at[(c1 + j) % nz]) for j in range(1, nz)]

    def swaps():
        return [
            pltpu.make_async_remote_copy(
                src_ref=give.at[i], dst_ref=take.at[i], send_sem=xssem.at[i], recv_sem=xrsem.at[i],
                device_id=(e, 1 - c), device_id_type=MESH,
            )
            for i in range(3)
        ]

    def grad_send(p):
        return pltpu.make_async_remote_copy(
            src_ref=keep, dst_ref=xt_hbm.at[x], send_sem=gsend, recv_sem=grecv.at[x],
            device_id=(pc.chip(c1, y, (x + p + 1) % m), c), device_id_type=MESH,
        )

    def totals():
        return [
            pltpu.make_async_copy(src.at[c], dst, osem.at[i])
            for i, (src, dst) in enumerate(((og, tg_hbm), (ou, tu_hbm), (od, td_hbm)))
        ]

    def payload():
        return [pltpu.make_async_copy(give.at[i], pay_hbm.at[i, pl.ds(0, give.shape[1])], psem.at[i]) for i in range(3)]

    first_h.wait()
    first_dy.wait()

    def body(step, carry):
        i = step % 2
        slot = step % slots
        p, t = step // blocks, step % blocks
        last = (p + 1) // m
        a, b2 = dest(step)
        b = pc.block(a, b2)
        column = b * m + (x + p + 1) % m
        for at in range(m):
            @pl.when(step == at * blocks)
            def _():
                for k in range(3):
                    for half in range(2):
                        weight(at, k, half, other_half[k]).wait()
                if at >= 1 and at + 1 < m:
                    weights_start(at + 1)

        @pl.when(step > 0)
        def _():
            for copy in load(step, i):
                copy.wait()

        wg, wu, wd = (wbuf.at[p % 2, k] for k in range(3))
        lane = lax.broadcasted_iota(jnp.int32, gate_ref.shape, 1)
        gate = jnp.sum(jnp.where(lane == column, gate_ref[...], 0.0), axis=1, keepdims=True)
        h = hbuf[i]
        dy = dbuf[i].astype(jnp.float32)
        z = (gate * dy).astype(jnp.bfloat16)
        for half in range(2):
            g = inner_cols(h, wg[half])
            u = inner_cols(h, wu[half])
            da = inner_cols(z, wd[half])
            sg = jax.nn.sigmoid(g)
            si = g * sg
            act[half] = (si * u).astype(jnp.bfloat16)
            dup[half] = (da * si).astype(jnp.bfloat16)
            dg[half] = (da * u * sg * (1.0 + g * (1.0 - sg))).astype(jnp.bfloat16)

        before = step - slots
        before_last = ((before + slots * blocks) // blocks - slots + 1) // m

        @pl.when((before >= 0) & (before_last < 1))
        def _():
            part_store(slot, b).wait()

        before_t = (before + slots * blocks) % blocks

        @pl.when((before >= 0) & (before_last >= 1) & (before_t < together * m) & (before_t % m < m - 1))
        def _():
            pair_send(slot, e, far_hbm.at[0, 0], r3sem.at[0, 0]).wait_send()

        @pl.when((before >= 0) & (before_last >= 1) & ((before_t >= together * m) | (before_t % m == m - 1)))
        def _():
            y_store(slot, a, b2).wait()
            du_send(slot, e, r1_hbm.at[0], r1sem.at[0]).wait_send()

        yv = (matmul(act[0], wd[0]) + matmul(act[1], wd[1])).astype(jnp.bfloat16).astype(jnp.float32)
        s = jnp.sum(yv * dy, axis=1, keepdims=True)
        s_ref[...] = jnp.where(lane == column, s, s_ref[...])
        yv = gate * yv
        du = (
            matmul(dg[0], wg[0]) + matmul(dg[1], wg[1]) + matmul(dup[0], wu[0]) + matmul(dup[1], wu[1])
        ).astype(jnp.bfloat16)

        @pl.when(p == 0)
        def _():
            stage[slot, 0] = yv.astype(jnp.bfloat16)
            stage[slot, 1] = du

        @pl.when(p > 0)
        def _():
            part_load(step, i).wait()
            stage[slot, 0] = (yv + pbuf[i, 0].astype(jnp.float32)).astype(jnp.bfloat16)
            stage[slot, 1] = (du.astype(jnp.float32) + pbuf[i, 1].astype(jnp.float32)).astype(jnp.bfloat16)

        @pl.when(last == 0)
        def _():
            part_store(slot, b).start()

        @pl.when((last == 1) & ((t >= together * m) | (t % m == m - 1)))
        def _():
            y_store(slot, a, b2).start()

        for j in range(1, m):
            @pl.when((last == 1) & (t < together * m) & (b2 == (y + j) % m))
            def _():
                pair_send(slot, pc.chip(c1, b2, x), far_hbm.at[m - j - 1, a], r3sem.at[m - j - 1, a]).start()

            @pl.when((last == 1) & (t >= together * m) & (b2 == (y + j) % m))
            def _():
                du_send(slot, pc.chip(c1, b2, x), r3_hbm.at[m - j - 1, a], r3sem.at[m - j - 1, a]).start()

        for k in range(2, nz):
            pl.when(step == (k - 1) * m - 1)(functools.partial(gather.line, k))

        @pl.when(step < m * blocks - 1)
        def _():
            after = step + 1
            next_a, next_b = dest(after)

            @pl.when((after < blocks) & (next_b != y) & (next_a != c1))
            def _():
                gather.wait(pc.block(next_a, next_b))

            for copy in load(after, 1 - i):
                copy.start()

            @pl.when(after >= blocks)
            def _():
                part_load(after, 1 - i).start()

        for half in range(2):
            og[half] += outer_rows(dg[half], h)
            ou[half] += outer_rows(dup[half], h)
            od[half] += outer_rows(act[half], z)

        for at in range(m - 1):
            @pl.when(step == (at + 1) * blocks - 1)
            def _():
                if at >= 1:
                    grad_send(at - 1).wait_send()
                    pl.semaphore_wait(room, 1)
                for k, total in enumerate(grads):
                    give[k] = total[1 - c].astype(jnp.bfloat16)
                    keep[k] = total[c].astype(jnp.bfloat16)
                    total[...] = jnp.zeros_like(total)
                for copy in swaps():
                    copy.start()

            @pl.when(step == (at + 1) * blocks)
            def _():
                for copy in swaps():
                    copy.wait()
                for k in range(3):
                    keep[k] = (keep[k].astype(jnp.float32) + take[k].astype(jnp.float32)).astype(jnp.bfloat16)
                pl.semaphore_signal(room, inc=1, device_id=(e, 1 - c), device_id_type=MESH)
                grad_send(at).start()

        for k in range(1, nz):
            @pl.when((last == 1) & (t == k * m))
            def _():
                at = (step - 1) % slots
                a1 = (c1 + toward * k + nz) % nz
                collect(at, from_y(a1, k - 1 < together))
                stage[at, 1] = total_ref[...].astype(jnp.bfloat16)
                du_send(at, pc.chip(a1, y, x), r1_hbm.at[c1], r1sem.at[c1]).start()

        return carry

    lax.fori_loop(0, m * blocks, body, 0)
    for i, total in enumerate(grads):
        give[i] = total[1 - c].astype(jnp.bfloat16)
    pl.semaphore_wait(room, 1)
    for copy in swaps():
        copy.start()
    turned = s_ref[...].T
    for i in range(n):
        rows_out[i] = turned[i : i + 1, :]
    for i in range(m):
        scores_in[me * m + i] = rows_out[me * m + i]

    def score_send(a, b2):
        return pltpu.make_async_remote_copy(
            src_ref=rows_out.at[pl.ds(pc.block(a, b2) * m, m)], dst_ref=scores_in.at[pl.ds(me * m, m)],
            send_sem=scs.at[a, b2], recv_sem=scr.at[c1, y],
            device_id=(pc.chip(a, b2, x), c), device_id_type=MESH,
        )

    def score_wait(a, b2):
        at = pl.ds(pc.block(a, b2) * m, m)
        pltpu.make_async_remote_copy(
            src_ref=rows_out.at[at], dst_ref=scores_in.at[at], send_sem=scs.at[a, b2], recv_sem=scr.at[a, b2],
            device_id=(pc.chip(a, b2, x), c), device_id_type=MESH,
        ).wait_recv()

    for a, b2 in pc.others():
        score_send(a, b2).start()
    for copy in swaps():
        copy.wait()
    for i, total in enumerate(grads):
        total[c] += take[i].astype(jnp.float32)
    grad_send(m - 2).wait_send()
    for j in range(1, m):
        at = (x + j) % m
        pltpu.make_async_remote_copy(
            src_ref=keep, dst_ref=xt_hbm.at[at], send_sem=gsend, recv_sem=grecv.at[at],
            device_id=(pc.chip(c1, y, at), c), device_id_type=MESH,
        ).wait_recv()
        back = pltpu.make_async_copy(xt_hbm.at[at], take, bsem.at[0])
        back.start()
        back.wait()
        for i, total in enumerate(grads):
            total[c] += take[i].astype(jnp.float32)
    for i, total in enumerate(grads):
        give[i] = total[c].astype(jnp.bfloat16)
    for copy in totals() + payload():
        copy.start()
    collect((m * blocks - 1) % slots, from_y(c1, nz - 1 < together) + from_z())
    final = pltpu.make_async_copy(total_ref, du_hbm, bsem.at[0])
    final.start()
    final.wait()
    for step in range(m * blocks - slots, m * blocks):
        t = step % blocks
        if t < together * m and t % m < m - 1:
            pair_send(step % slots, e, far_hbm.at[0, 0], r3sem.at[0, 0]).wait_send()
            continue
        y_store(step % slots, c1, y).wait()
        if step < m * blocks - 1:
            du_send(step % slots, e, r1_hbm.at[0], r1sem.at[0]).wait_send()
    for a, b2 in pc.others():
        score_wait(a, b2)
        score_send(a, b2).wait_send()
    gather.finish(range(1, nz))
    for copy in totals() + payload():
        copy.wait()


def experts(h, dy, gates, routed_w, shared_w, other_w, partner_w):
    blocks, rows, width = dy.shape
    n = gates.shape[0]
    hidden = shared_w[0].shape[0]
    nz = 4
    m = {16: 2, 64: 4}[n]
    slots = 4
    vmem = pl.BlockSpec(memory_space=pltpu.VMEM)
    hbm = pl.BlockSpec(memory_space=pl.ANY)
    f32, b16 = jnp.float32, jnp.bfloat16
    out = jax.ShapeDtypeStruct
    dma = pltpu.SemaphoreType.DMA
    grad = pltpu.VMEM((2, hidden, width), f32)
    pair = pltpu.VMEM((2, rows, width), b16)
    narrow = pltpu.VMEM((2, rows, hidden), b16)
    three = pltpu.VMEM((3, hidden, width), b16)
    return pl.pallas_call(
        functools.partial(experts_kernel, n, slots),
        out_shape=(
            out((n, 1, rows), f32), out((rows, width), f32),
            out((hidden, width), f32), out((hidden, width), f32), out((hidden, width), f32),
            out((3, n * blocked(hidden, n), width), b16), out((nz, m, rows, width), b16), out((m - 1, nz, 2, rows, width), b16),
            out((blocks, rows, width), b16), out((blocks, 2, rows, width), b16), out((m, 3, hidden, width), b16),
            out((m - 1, nz, rows, width), b16), out((nz, rows, width), b16),
        ),
        in_specs=[hbm, hbm, vmem] + [hbm] * 12,
        out_specs=(vmem,) + (hbm,) * 12,
        input_output_aliases={0: 8},
        scratch_shapes=[
            pltpu.VMEM((2, 3, 2, hidden, width), b16), grad, grad, grad,
            pltpu.VMEM((rows, width), f32), pair, pair, narrow, narrow, narrow,
            pltpu.VMEM((slots, 2, rows, width), b16), pltpu.VMEM((2, 2, rows, width), b16), pair, three, three, three,
            pltpu.VMEM((rows, 128), f32), pltpu.VMEM((rows, 128), f32), pltpu.VMEM((128, rows), f32), pltpu.VMEM((n, 1, rows), f32),
            dma((64,)), dma((blocks,)), dma((2, 2)), dma((slots,)), dma((m - 1, nz)), dma((nz,)), dma((2,)),
            dma((2, 3, 2)), dma((slots,)), dma((2,)), dma((slots,)),
            dma((3,)), dma((3,)), dma, dma((m,)), dma((3,)), dma((3,)), dma((nz, m)), dma((nz, m)),
            pltpu.SemaphoreType.REGULAR,
        ],
        compiler_params=pltpu.CompilerParams(collective_id=1, has_side_effects=True, vmem_limit_bytes=62 * 2**20),
    )(h, dy, gates, *routed_w, *shared_w, *other_w, *partner_w)


def swap_halves(values):
    return pltpu.roll(values, HD // 2, axis=1)


def route_columns(logit_ref, route_ref, turn_ref):
    count = logit_ref.shape[0]
    logits = logit_ref[...]
    raised = jnp.exp(logits - jnp.max(logits, axis=0, keepdims=True))
    turn_ref[...] = jnp.zeros_like(turn_ref)
    turn_ref[0:count, :] = raised / jnp.sum(raised, axis=0, keepdims=True)
    soft = turn_ref[...].T
    turn_ref[0:count, :] = route_ref[...].astype(jnp.float32)
    return soft, turn_ref[...].T.astype(jnp.int32)


class Scatter:
    def __init__(self, pc, stack, r3, r2, r1, sems):
        self.pc, self.stack, self.r3, self.r2, self.r1 = pc, stack, r3, r2, r1
        self.ssem, self.s3, self.s2, self.s1 = sems

    def copy(self, b, dst, sem, to):
        return pltpu.make_async_remote_copy(
            src_ref=self.stack.at[b], dst_ref=dst, send_sem=self.ssem.at[b], recv_sem=sem,
            device_id=(to, self.pc.c), device_id_type=MESH,
        )

    def add(self, total, src, sem):
        self.copy(self.pc.e, src, sem, self.pc.blk(self.pc.c1, self.pc.c2, self.pc.o3()[0])).wait_recv()
        return total + src[...].astype(jnp.float32)

    def start(self):
        pc = self.pc
        for i in range(pc.nz):
            a = (pc.c1 + i + 1) % pc.nz
            for k in range(1, pc.m):
                for b2 in pc.o2() + [pc.c2]:
                    b3 = (pc.c3 + k) % pc.m
                    self.copy(pc.blk(a, b2, b3), self.r3.at[pc.m - k - 1, a, b2], self.s3.at[pc.m - k - 1, a, b2], pc.blk(pc.c1, pc.c2, b3)).start()

    def collect(self, a, b2, level):
        pc = self.pc
        total = self.stack[pc.blk(a, b2, pc.c3)].astype(jnp.float32)
        for k in range(pc.m - 1):
            total = self.add(total, self.r3.at[k, a, b2], self.s3.at[k, a, b2])
        if level >= 2:
            for k in range(pc.m - 1):
                total = self.add(total, self.r2.at[k, a], self.s2.at[k, a])
        if level >= 3:
            for k in range(pc.nz - 1):
                total = self.add(total, self.r1.at[k], self.s1.at[k])
        self.stack[pc.blk(a, b2, pc.c3)] = total.astype(jnp.bfloat16)

    def second(self, i):
        pc = self.pc
        a = (pc.c1 + i + 1) % pc.nz
        for k in range(1, pc.m):
            b2 = (pc.c2 + k) % pc.m
            self.collect(a, b2, 1)
            self.copy(pc.blk(a, b2, pc.c3), self.r2.at[pc.m - k - 1, a], self.s2.at[pc.m - k - 1, a], pc.blk(pc.c1, b2, pc.c3)).start()

    def third(self, i):
        pc = self.pc
        a = (pc.c1 + i + 1) % pc.nz
        self.collect(a, pc.c2, 2)
        self.copy(pc.blk(a, pc.c2, pc.c3), self.r1.at[pc.nz - i - 2], self.s1.at[pc.nz - i - 2], pc.blk(a, pc.c2, pc.c3)).start()

    def last(self):
        self.collect(self.pc.c1, self.pc.c2, 3)

    def steps(self):
        nz = self.pc.nz
        found = [functools.partial(self.second, 0)]
        for i in range(1, nz):
            found += [functools.partial(self.second, i), functools.partial(self.third, i - 1)]
        return found + [self.last]

    def finish(self):
        pc = self.pc
        for j in range(1, pc.n):
            self.copy((pc.e + j) % pc.n, self.r1.at[0], self.s1.at[0], (pc.e + j) % pc.n).wait_send()


def tail_kernel(
    n,
    x_ref, x1_ref, cot_ref, dh_ref, q_ref, k_ref, v_ref, o_ref, p_ref, wq, wk, wv, wo,
    gain1, gain2, cos_ref, sin_ref, cnt_ref, len_ref, logit_ref, route_ref, scores_in, pay_hbm, y_hbm, far_hbm,
    out_ref, gtok_ref, glog_ref, small_ref, ag0, ag1, ags, y3_hbm, y1_hbm,
    dx_ref, dq_ref, dk_ref, dv_ref, a_ref, give, take, stack0, stack1, r3, r2, r1,
    sm_core, sm_d3, sm_d2, sm_z,
    wbuf, wsem, turn_ref, own_pay, ybuf, ytmp,
    gs, gr, ss, s3, s2, s1, xs, xr, cs, cr, scs, scr, locs, yl, yt, ys3, ys1, y3s, y1s,
):
    pc = Place(n)
    c1, c2, c3, e, c, nz, m = pc.c1, pc.c2, pc.c3, pc.e, pc.c, pc.nz, pc.m
    rows, width = x_ref.shape
    half = width // 2
    pc.greet_all()

    x, y = pc.x, pc.y

    def y_far(a, j):
        return pltpu.make_async_remote_copy(
            src_ref=y_hbm.at[a, (y + j) % m], dst_ref=y3_hbm.at[m - j - 1, a], send_sem=ys3.at[j - 1, a], recv_sem=y3s.at[m - j - 1, a],
            device_id=(pc.chip(c1, (y + j) % m, x), c), device_id_type=MESH,
        )

    def y_along(a):
        return pltpu.make_async_remote_copy(
            src_ref=ybuf.at[a], dst_ref=y1_hbm.at[c1], send_sem=ys1.at[a], recv_sem=y1s.at[c1],
            device_id=(pc.chip(a, y, x), c), device_id_type=MESH,
        )

    toward = 1 - 2 * (c1 // (nz // 2))
    together = nz // 2

    def plane(i):
        return (c1 + toward * (i + 1) + nz) % nz

    for i in range(together, nz):
        for j in range(1, m):
            y_far(plane(i), j).start()
    y_own = [pltpu.make_async_copy(y_hbm.at[a, y], ybuf.at[a], yl.at[a]) for a in range(nz)]
    for copy in y_own:
        copy.start()

    def y_sum(a, received):
        def fetched(i):
            return pltpu.make_async_copy(received[i][0], ytmp.at[i % 2], yt.at[i % 2])

        def begin(i):
            src, sem = received[i]
            if sem is not None:
                pltpu.make_async_remote_copy(
                    src_ref=src, dst_ref=src, send_sem=ys1.at[0], recv_sem=sem, device_id=(e, 1 - c), device_id_type=MESH,
                ).wait_recv()
            fetched(i).start()

        begin(0)
        total = ybuf[a].astype(jnp.float32)
        for i in range(len(received)):
            if i + 1 < len(received):
                begin(i + 1)
            fetched(i).wait()
            total = total + ytmp[i % 2].astype(jnp.float32)
        return total

    def y_from3(i):
        a = plane(i)
        if i < together:
            return [(far_hbm.at[k, a, 0], None) for k in range(m - 1)]
        return [(y3_hbm.at[k, a], y3s.at[k, a]) for k in range(m - 1)]

    def y_third(i):
        a = plane(i)
        ybuf[a] = y_sum(a, y_from3(i)).astype(jnp.bfloat16)
        y_along(a).start()

    def y_last():
        along = [(y1_hbm.at[(c1 + j) % nz], y1s.at[(c1 + j) % nz]) for j in range(1, nz)]
        out_ref[...] = (x1_ref[...] + y_sum(c1, y_from3(nz - 1) + along)).astype(jnp.bfloat16)

    def y_finish():
        for i in range(nz - 1):
            y_along(plane(i)).wait_send()
        for i in range(together, nz):
            for j in range(1, m):
                y_far(plane(i), j).wait_send()


    def deal(i, to):
        return pltpu.make_async_remote_copy(
            src_ref=pay_hbm.at[i, to], dst_ref=own_pay.at[i], send_sem=scs.at[i, to], recv_sem=scr.at[i],
            device_id=(to, c), device_id_type=MESH,
        )

    def keep(i):
        return pltpu.make_async_copy(pay_hbm.at[i, n - 1], own_pay.at[i], scs.at[i, n - 1])

    @pl.when(e == n - 1)
    def _():
        def one(j, carry):
            for i in range(3):
                deal(i, n - 2 - j).start()
            return carry

        lax.fori_loop(0, n - 1, one, 0)
        for i in range(3):
            keep(i).start()

    gather_s = Gather(pc, own_pay, ags, gs.at[2], gr.at[2], 3)
    loc_s = pltpu.make_async_copy(own_pay, ags.at[e], locs.at[2])

    def shared_start():
        @pl.when(e == n - 1)
        def _():
            for i in range(3):
                keep(i).wait()

        @pl.when(e != n - 1)
        def _():
            for i in range(3):
                pltpu.make_async_remote_copy(
                    src_ref=own_pay.at[i], dst_ref=own_pay.at[i], send_sem=scs.at[i, 0], recv_sem=scr.at[i],
                    device_id=(n - 1, c), device_id_type=MESH,
                ).wait_recv()

        gather_s.start()
        loc_s.start()

    def fetch(src, i):
        return pltpu.make_async_copy(src, wbuf.at[i], wsem.at[i])

    fetch(wo, 0).start()
    fetch(wv, 1).start()

    x1 = x1_ref[...]
    up = cot_ref[...].astype(jnp.float32)
    dh = dh_ref[...]
    r_two = lax.rsqrt(jnp.mean(x1 * x1, axis=-1, keepdims=True) + norm_eps)
    n_two = x1 * r_two
    scaled = dh * gain2[...]
    grad_two = jnp.sum(dh * n_two, axis=0, keepdims=True)
    dx = up + r_two * (scaled - n_two * jnp.mean(scaled * n_two, axis=-1, keepdims=True))
    dx_ref[...] = dx
    dx_low = dx.astype(jnp.bfloat16)

    def columns(ref, which):
        return ref[:, pl.ds(pl.multiple_of(which * half, 128), half)]

    def hand(i):
        return pltpu.make_async_remote_copy(
            src_ref=give.at[i], dst_ref=take.at[i], send_sem=xs.at[i], recv_sem=xr.at[i],
            device_id=(e, 1 - c), device_id_type=MESH,
        )

    def to_partner(i, left, right):
        give[i] = outer_rows(columns(left, 1 - c), right).astype(jnp.bfloat16)
        hand(i).start()

    def own_part(i, left, right, stack, at):
        block = stack.shape[1]
        part = outer_rows(columns(left, c), right)
        hand(i).wait_recv()
        total = (part + take[i].astype(jnp.float32)).astype(jnp.bfloat16)
        stack[pl.ds(at * (half // block), half // block)] = total.reshape(half // block, block, width)

    to_partner(0, o_ref, dx_low)
    fetch(wo, 0).wait()
    dq_ref[...] = inner_cols(dx_low, wbuf[0]).astype(jnp.bfloat16)
    fetch(wk, 0).start()
    cosine, sine = cos_ref[...], sin_ref[...]
    scale = HD ** (-0.5)

    def one_head(hd, carry):
        at = pl.ds(pl.multiple_of(hd * HD, HD), HD)
        prob = p_ref[hd]
        d_o, val, que, key = dq_ref[:, at], v_ref[:, at], q_ref[:, at], k_ref[:, at]
        dv_ref[:, at] = outer_rows(prob.astype(jnp.bfloat16), d_o).astype(jnp.bfloat16)
        d_prob = inner_cols(d_o, val)
        inner = jnp.sum(prob * d_prob, axis=-1, keepdims=True)
        d_score = (prob * (d_prob - inner)).astype(jnp.bfloat16)
        d_q = matmul(d_score, key) * scale
        d_k = outer_rows(d_score, que) * scale
        dq_ref[:, at] = (d_q * cosine - swap_halves(d_q) * sine).astype(jnp.bfloat16)
        dk_ref[:, at] = (d_k * cosine - swap_halves(d_k) * sine).astype(jnp.bfloat16)
        return carry

    lax.fori_loop(0, HEADS, one_head, 0)
    for copy in y_own:
        copy.wait()
    for i in range(nz - 1):
        y_third(i)
    xv = x_ref[...].astype(jnp.float32)
    r_one = lax.rsqrt(jnp.mean(xv * xv, axis=-1, keepdims=True) + norm_eps)
    n_one = xv * r_one
    a_ref[...] = (n_one * gain1[...]).astype(jnp.bfloat16)
    to_partner(1, a_ref, dv_ref[...])
    to_partner(2, a_ref, dk_ref[...])
    to_partner(3, a_ref, dq_ref[...])
    if n * stack0.shape[1] > 2 * half:
        stack0[...] = jnp.zeros_like(stack0)
        stack1[...] = jnp.zeros_like(stack1)
    own_part(0, o_ref, dx_low, stack0, 0)
    own_part(1, a_ref, dv_ref[...], stack0, 1)
    first = Scatter(pc, stack0, r3.at[0], r2.at[0], r1.at[0], (ss.at[0], s3.at[0], s2.at[0], s1.at[0]))
    second = Scatter(pc, stack1, r3.at[1], r2.at[1], r1.at[1], (ss.at[1], s3.at[1], s2.at[1], s1.at[1]))
    first.start()
    own_part(2, a_ref, dk_ref[...], stack1, 0)
    own_part(3, a_ref, dq_ref[...], stack1, 1)
    second.start()
    shared_start()
    shared_events = gather_s.events()
    fetch(wv, 1).wait()
    da = inner_cols(dv_ref[...], wbuf[1])
    fetch(wq, 1).start()
    fetch(wk, 0).wait()
    da = da + inner_cols(dk_ref[...], wbuf[0])
    fetch(wq, 1).wait()
    da = da + inner_cols(dq_ref[...], wbuf[1])
    scaled_one = da * gain1[...]
    grad_one = jnp.sum(da * n_one, axis=0, keepdims=True)
    back = r_one * (scaled_one - n_one * jnp.mean(scaled_one * n_one, axis=-1, keepdims=True))
    gtok_ref[...] = (dx_ref[...] + back).astype(jnp.bfloat16)

    def exchange(ref, own, level, peers, value):
        ref[own] = value
        copies = [
            pltpu.make_async_remote_copy(
                src_ref=ref.at[own], dst_ref=ref.at[own], send_sem=cs.at[level, i], recv_sem=cr.at[level, own],
                device_id=to, device_id_type=MESH,
            )
            for i, (to, at) in enumerate(peers)
        ]
        for copy in copies:
            copy.start()

        def done():
            for i, (to, at) in enumerate(peers):
                pltpu.make_async_remote_copy(
                    src_ref=ref.at[own], dst_ref=ref.at[at], send_sem=cs.at[level, i], recv_sem=cr.at[level, at],
                    device_id=to, device_id_type=MESH,
                ).wait_recv()
            for copy in copies:
                copy.wait_send()
            total = ref[0]
            for i in range(1, ref.shape[0]):
                total = total + ref[i]
            return total

        return done

    turn_ref[...] = jnp.zeros_like(turn_ref)
    for i in range(n):
        turn_ref[i : i + 1, :] = scores_in[i]
    scores = turn_ref[...].T
    lane = lax.broadcasted_iota(jnp.int32, (rows, 128), 1)
    row = lax.broadcasted_iota(jnp.int32, (rows, 128), 0)
    scores = jnp.where(row < len_ref[0], scores, 0.0)
    soft, routes = route_columns(logit_ref, route_ref, turn_ref)
    share = jnp.zeros((rows, 128), jnp.float32)
    for i in range(route_ref.shape[0]):
        picked = jnp.sum(jnp.where(lane == routes[:, i : i + 1], scores, 0.0), axis=-1, keepdims=True)
        share = jnp.where(lane == i, picked, share)
    grad_logits = soft * (share - jnp.sum(soft * share, axis=-1, keepdims=True))
    glog_ref[...] = grad_logits.T[0 : route_ref.shape[0], :]

    small = jnp.concatenate([grad_one, grad_two, cnt_ref[...], jnp.zeros((5, width), jnp.float32)], axis=0)
    level0 = exchange(sm_core, c, 0, [((e, 1 - c), 1 - c)], small)
    steps0, steps1 = first.steps(), second.steps()
    steps0[0]()
    steps0[1]()
    shared_events[0]()
    level1 = exchange(sm_d3, c3, 1, [((pc.blk(c1, c2, j), c), j) for j in pc.o3()], level0())
    steps0[2]()
    steps1[0]()
    steps0[3]()
    steps1[1]()
    steps0[4]()
    shared_events[1]()
    level2 = exchange(sm_d2, c2, 2, [((pc.blk(c1, j, c3), c), j) for j in pc.o2()], level1())
    steps1[2]()
    for step in steps0[5:-1]:
        step()
    level3 = exchange(sm_z, c1, 3, [((pc.blk((c1 + j) % nz, c2, c3), c), (c1 + j) % nz) for j in range(1, nz)], level2())
    for step in steps1[3:-1]:
        step()
    shared_events[2]()
    shared_events[3]()
    small_ref[...] = level3()
    steps0[-1]()
    g0 = Gather(pc, stack0.at[e], ag0, gs.at[0], gr.at[0], stack0.shape[1])
    g0.start()
    loc0 = pltpu.make_async_copy(stack0.at[e], ag0.at[e], locs.at[0])
    loc0.start()
    shared_events[4]()
    steps1[-1]()
    g1 = Gather(pc, stack1.at[e], ag1, gs.at[1], gr.at[1], stack1.shape[1])
    g1.start()
    loc1 = pltpu.make_async_copy(stack1.at[e], ag1.at[e], locs.at[1])
    loc1.start()
    y_last()
    for event in shared_events[5:-1]:
        event()
    run_staggered(g0.events(), g1.events(), 1)
    shared_events[-1]()
    for g in (gather_s, g0, g1):
        g.finish()
    first.finish()
    second.finish()
    loc_s.wait()
    loc0.wait()
    loc1.wait()
    y_finish()
    for i in range(4):
        hand(i).wait_send()

    @pl.when(e == n - 1)
    def _():
        def one(j, carry):
            for i in range(3):
                deal(i, j).wait_send()
            return carry

        lax.fori_loop(0, n - 1, one, 0)


def tail(n, x, x1, cot, dh, q, k, v, o, prob, wq, wk, wv, wo, gain1, gain2, cosine, sine, cnt, length, logits, routes, scores, pay, y, far):
    nz = 4
    m = {16: 2, 64: 4}[n]
    rows, width = x.shape
    half = width // 2
    block = blocked(2 * half, n)
    vmem = pl.BlockSpec(memory_space=pltpu.VMEM)
    hbm = pl.BlockSpec(memory_space=pl.ANY)
    f32, b16 = jnp.float32, jnp.bfloat16
    out = jax.ShapeDtypeStruct
    dma = pltpu.SemaphoreType.DMA
    wide = pltpu.VMEM((rows, width), b16)
    return pl.pallas_call(
        functools.partial(tail_kernel, n),
        out_shape=(
            out((rows, width), b16), out((rows, width), b16), out(logits.shape, f32), out((8, width), f32),
            out((n, block, width), b16), out((n, block, width), b16),
            out((n, 3, pay.shape[2], width), b16),
            out((m - 1, nz, rows, width), b16), out((nz, rows, width), b16),
        ),
        in_specs=[vmem] * 9 + [hbm] * 4 + [vmem] * 5 + [pl.BlockSpec(memory_space=pltpu.SMEM)] + [vmem] * 3 + [hbm] * 3,
        out_specs=(vmem,) * 4 + (hbm,) * 5,
        scratch_shapes=[
            pltpu.VMEM((rows, width), f32), wide, wide, wide, wide,
            pltpu.VMEM((4, half, width), b16), pltpu.VMEM((4, half, width), b16),
            pltpu.VMEM((n, block, width), b16), pltpu.VMEM((n, block, width), b16),
            pltpu.VMEM((2, m - 1, nz, m, block, width), b16), pltpu.VMEM((2, m - 1, nz, block, width), b16),
            pltpu.VMEM((2, nz - 1, block, width), b16),
            pltpu.VMEM((2, 8, width), f32), pltpu.VMEM((m, 8, width), f32), pltpu.VMEM((m, 8, width), f32), pltpu.VMEM((nz, 8, width), f32),
            pltpu.VMEM((2, width, width), b16), dma((2,)), pltpu.VMEM((128, rows), f32), pltpu.VMEM((3, pay.shape[2], width), b16),
            pltpu.VMEM((nz, rows, width), b16), pltpu.VMEM((2, rows, width), b16),
            dma((3, 160)), dma((3, 2, n)), dma((2, n)), dma((2, m - 1, nz, m)), dma((2, m - 1, nz)), dma((2, nz - 1)),
            dma((4,)), dma((4,)), dma((4, max(nz, m))), dma((4, max(nz, m, 2))), dma((3, n)), dma((3,)), dma((3,)),
            dma((nz,)), dma((2,)), dma((m - 1, nz)), dma((nz,)), dma((m - 1, nz)), dma((nz,)),
        ],
        compiler_params=pltpu.CompilerParams(collective_id=2, has_side_effects=True, vmem_limit_bytes=63 * 2**20),
    )(x, x1, cot, dh, q, k, v, o, prob, wq, wk, wv, wo, gain1, gain2, cosine, sine, cnt, length, logits, routes, scores, pay, y, far)


def blocked(count, n):
    return -(-count // (16 * n)) * 16


def from_blocks(blocks, count):
    return blocks.reshape(-1, blocks.shape[2])[:count].astype(jnp.float32)


def rotary_rows(seq_len):
    position = np.arange(seq_len).astype(np.float32)
    inverse_freq = (rotary_base ** (-2.0 * np.arange(HD // 2).astype(np.float32) / HD)).astype(np.float32)
    angle = position[:, None] * inverse_freq[None, :]
    cosine, sine = np.cos(angle), np.sin(angle)
    return np.concatenate([cosine, cosine], axis=1), np.concatenate([-sine, sine], axis=1)


def on_device(
    tokens, norm_one, w_query, w_key, w_value, w_out, norm_two, r_gate, r_up, r_down, s_gate, s_up, s_down,
    logits, routes, lengths, cotangent,
):
    rows, width = tokens.shape
    n = lax.axis_size("exp")
    hidden = s_gate.shape[1]
    cosine, sine = (jnp.asarray(table) for table in rotary_rows(rows))
    gain1, gain2 = norm_one[None], norm_two[None]
    logits, routes = logits.T, routes.T
    attn_w = (w_query, w_key, w_value, w_out)
    routed_w = (r_gate[0].T, r_up[0].T, r_down[0])
    shared_w = (s_gate.T, s_up.T, s_down)
    (
        all_dy, all_h, fq, fk, fv, fo, fg, fu, fd, pg, pu, pd, mixed, queries, keys_all, values_all, attended, prob, gates, counts,
    ) = front(
        n, tokens, cotangent, gain1, gain2, cosine, sine, lengths, logits, routes,
        attn_w, routed_w, shared_w,
    )
    scores, grad_hidden, tg, tu, td, payload, outs, far_outs = experts(
        all_h, all_dy, gates, routed_w, shared_w, (fg, fu, fd), (pg, pu, pd)
    )[:8]
    full = (width, width)
    output, grad_tokens, grad_logits, small_sums, sum0, sum1, sum_s = tail(
        n, tokens, mixed, cotangent, grad_hidden, queries, keys_all, values_all, attended, prob,
        fq.reshape(full), fk.reshape(full), fv.reshape(full), fo.reshape(full),
        gain1, gain2, cosine, sine, counts, lengths, logits, routes, scores,
        payload.reshape(3, n, -1, width), outs, far_outs,
    )[:7]
    half = width // 2
    wout_value = from_blocks(sum0, width)
    key_query = from_blocks(sum1, width)
    holds_shared = lax.axis_index("exp") == n - 1
    tg, tu, td = (jnp.where(holds_shared, 0.0, grad) for grad in (tg, tu, td))
    sg, su, sd = (from_blocks(sum_s[:, i], hidden) for i in range(3))
    return (
        output, grad_tokens, small_sums[0],
        key_query[half:], key_query[:half], wout_value[half:], wout_value[:half],
        small_sums[1], tg.T[None], tu.T[None], td[None], sg.T, su.T, sd,
        grad_logits.T, small_sums[2, :n].astype(jnp.int32),
    )


def solution(mesh):
    in_specs = (
        P(("exp", "hid"), None),
        P(),
        P("hid", None),
        P("hid", None),
        P("hid", None),
        P("hid", None),
        P(),
        P("exp", None, "hid"),
        P("exp", None, "hid"),
        P("exp", "hid", None),
        P(None, "hid"),
        P(None, "hid"),
        P("hid", None),
        P(("exp", "hid"), None),
        P(("exp", "hid"), None),
        P(("exp", "hid")),
        P(("exp", "hid"), None),
    )
    out_specs = (
        P(("exp", "hid"), None),
        P(("exp", "hid"), None),
        P(),
        P("hid", None),
        P("hid", None),
        P("hid", None),
        P("hid", None),
        P(),
        P("exp", None, "hid"),
        P("exp", None, "hid"),
        P("exp", "hid", None),
        P(None, "hid"),
        P(None, "hid"),
        P("hid", None),
        P(("exp", "hid"), None),
        P(),
    )
    return jax.shard_map(
        on_device, mesh=mesh, in_specs=in_specs, out_specs=out_specs, check_vma=False
    )
```

```python
import functools

import jax
import jax.numpy as jnp
import numpy as np
from jax import lax
from jax.experimental import pallas as pl
from jax.experimental.pallas import tpu as pltpu
from jax.sharding import PartitionSpec as P

HEADS = 10
HD = 128
MESH = pl.DeviceIdType.MESH


norm_eps = 1e-06
rotary_base = 10000.0
contract_rows = (((0,), (0,)), ((), ()))
contract_cols = (((1,), (1,)), ((), ()))


def matmul(left_side, right_side):
    return jnp.dot(left_side, right_side, preferred_element_type=jnp.float32)


def outer_rows(left_side, right_side):
    return lax.dot_general(left_side, right_side, contract_rows, preferred_element_type=jnp.float32)


def inner_cols(left_side, right_side):
    return lax.dot_general(left_side, right_side, contract_cols, preferred_element_type=jnp.float32)


class Place:
    def __init__(self, n):
        self.n = n; self.nz = 4; self.m = {16: 2, 64: 4}[n]; m = self.m
        self.e = lax.axis_index("exp"); self.c = lax.axis_index("hid"); c = self.c; e = self.e
        self.s1 = m * m; self.s2 = 1 + c * (m - 1); self.s3 = m - c * (m - 1)
        self.x = e % m; self.y = (e // m) % m
        self.c1 = e // self.s1; self.c2 = (e // self.s2) % m; self.c3 = (e // self.s3) % m
    def chip(self, z, y, x): return z * self.s1 + y * self.m + x
    def block(self, z, y): return z * self.m + y
    def others(self):
        far = [((self.c1 + i) % self.nz, (self.y + j) % self.m) for i in range(self.nz) for j in range(self.m)]
        return far[1:]
    def blk(self, a, b, d): return a * self.s1 + b * self.s2 + d * self.s3
    def o2(self): return [(self.c2 + j) % self.m for j in range(1, self.m)]
    def o3(self): return [(self.c3 + j) % self.m for j in range(1, self.m)]
    def greet_all(self):
        barrier = pltpu.get_barrier_semaphore()

        def greet(j, carry):
            pl.semaphore_signal(barrier, inc=1, device_id=((self.e + j) % self.n, self.c), device_id_type=MESH)
            return carry

        lax.fori_loop(1, self.n, greet, 0)
        pl.semaphore_signal(barrier, inc=1, device_id=(self.e, 1 - self.c), device_id_type=MESH)
        pl.semaphore_wait(barrier, self.n)


class Gather:
    def __init__(self, pc, src, dst, ssem, rsem, split, base=0):
        self.pc, self.src, self.dst, self.ssem, self.rsem = pc, src, dst, ssem, rsem
        self.split = split; self.sends = []; self.base = base
    def view(self, ref, part):
        R = self.src.shape[0]
        return ref.at[pl.ds(0, self.split)] if part == 0 else ref.at[pl.ds(self.split, R - self.split)]
    def send(self, part, own, b, to, cond=None):
        i = self.base + len(self.sends)
        src = self.view(self.src if own else self.dst.at[b], part)
        cp = pltpu.make_async_remote_copy(src_ref=src, dst_ref=self.view(self.dst.at[b], part), send_sem=self.ssem.at[i], recv_sem=self.rsem.at[part, b], device_id=(to, self.pc.c), device_id_type=MESH)
        self.sends.append((cond, cp))
        if cond is None: cp.start()
        else: pl.when(cond)(cp.start)
    def wait(self, part, b):
        v = self.view(self.dst.at[b], part)
        to = self.pc.blk(self.pc.c1, self.pc.c2, self.pc.o3()[0])
        pltpu.make_async_remote_copy(src_ref=v, dst_ref=v, send_sem=self.ssem.at[0], recv_sem=self.rsem.at[part, b], device_id=(to, self.pc.c), device_id_type=MESH).wait_recv()
    def updown(self, part, own, b):
        pc = self.pc
        self.send(part, own, b, pc.blk(pc.c1 + 1, pc.c2, pc.c3), pc.c1 < pc.nz - 1)
        self.send(part, own, b, pc.blk(pc.c1 - 1, pc.c2, pc.c3), pc.c1 > 0)
    def to2(self, part, own, b):
        pc = self.pc
        for j in pc.o2(): self.send(part, own, b, pc.blk(pc.c1, j, pc.c3))
    def to3(self, part, own, b):
        pc = self.pc
        for j in pc.o3(): self.send(part, own, b, pc.blk(pc.c1, pc.c2, j))
    def start(self):
        e = self.pc.e
        self.to3(0, True, e); self.to2(0, True, e); self.updown(0, True, e)
        if self.split < self.src.shape[0]:
            self.to3(1, True, e); self.to2(1, True, e); self.updown(1, True, e)
    def zarr(self, part, s, up, k2, k3, more):
        pc = self.pc
        a = pc.c1 - s if up else pc.c1 + s
        cond = (pc.c1 >= s) if up else (pc.c1 < pc.nz - s)
        b = pc.blk(a, k2, k3)
        pl.when(cond)(lambda: self.wait(part, b))
        if s < pc.nz - 1:
            if up: self.send(part, False, b, pc.blk(pc.c1 + 1, pc.c2, pc.c3), (pc.c1 >= s) & (pc.c1 < pc.nz - 1))
            else: self.send(part, False, b, pc.blk(pc.c1 - 1, pc.c2, pc.c3), (pc.c1 < pc.nz - s) & (pc.c1 > 0))
        if more:
            for j in pc.o2(): self.send(part, False, b, pc.blk(pc.c1, j, pc.c3), cond)
            for j in pc.o3(): self.send(part, False, b, pc.blk(pc.c1, pc.c2, j), cond)
    def events(self):
        pc = self.pc; ev = []
        def a2(s):
            def go():
                for j in pc.o2():
                    for sg in ((1, -1) if s else (1,)):
                        a = pc.c1 + sg * s
                        cond = None if s == 0 else ((a >= 0) & (a < pc.nz))
                        b = pc.blk(a, j, pc.c3)
                        if cond is None: self.wait(0, b)
                        else: pl.when(cond)(lambda b=b: self.wait(0, b))
                        for k in pc.o3(): self.send(0, False, b, pc.blk(pc.c1, pc.c2, k), cond)
            return go
        def az(s):
            def go():
                self.zarr(0, s, True, pc.c2, pc.c3, True); self.zarr(0, s, False, pc.c2, pc.c3, True)
            return go
        B = self.split < self.src.shape[0]
        def f1():
            for j in pc.o2():
                b = pc.blk(pc.c1, j, pc.c3); self.wait(1, b); self.to3(1, False, b); self.updown(1, False, b)
        def f2():
            for k in pc.o3():
                b = pc.blk(pc.c1, pc.c2, k); self.wait(1, b); self.updown(1, False, b)
        def f3():
            for j in pc.o2():
                for k in pc.o3():
                    b = pc.blk(pc.c1, j, k); self.wait(1, b); self.updown(1, False, b)
        def fz(s):
            def go():
                for k2 in range(pc.m):
                    for k3 in range(pc.m):
                        self.zarr(1, s, True, k2, k3, False); self.zarr(1, s, False, k2, k3, False)
            return go
        ev += [az(1), a2(0)]
        if B: ev += [f1, f2, f3]
        ev += [az(2), a2(1)]
        if B: ev += [fz(1)]
        ev += [az(3), a2(2)]
        if B: ev += [fz(2)]
        ev += [a2(3)]
        if B: ev += [fz(3)]
        def last():
            for a in range(pc.nz):
                for j in range(pc.m):
                    for k in pc.o3(): self.wait(0, pc.blk(a, j, k))
        ev += [last]
        return ev
    def finish(self):
        for cond, cp in self.sends:
            if cond is None: cp.wait_send()
            else: pl.when(cond)(cp.wait_send)


class Lines:
    def __init__(self, pc, src, dst, ssem, rsem):
        self.pc, self.src, self.dst, self.ssem, self.rsem = pc, src, dst, ssem, rsem
        self.places = [(0, way, 0) for way in (1, -1)] + [(0, 0, j) for j in range(1, pc.m)]
        for s in range(1, pc.nz):
            for way in (1, -1):
                self.places += [(s, way, j) for j in range(0 if s < pc.nz - 1 else 1, pc.m)]

    def send(self, place):
        pc = self.pc
        s, way, j = place
        a = pc.c1 - way * s
        b = pc.block(a, pc.y)
        on = pc.c1 + way
        to = pc.chip(on, pc.y, pc.x) if j == 0 else pc.chip(pc.c1, (pc.y + j) % pc.m, pc.x)
        cond = (a >= 0) & (a < pc.nz)
        if j == 0:
            cond = cond & (on >= 0) & (on < pc.nz)
        copy = pltpu.make_async_remote_copy(
            src_ref=self.src if s == 0 else self.dst.at[b], dst_ref=self.dst.at[b],
            send_sem=self.ssem.at[self.places.index(place)], recv_sem=self.rsem.at[b],
            device_id=(to, pc.c), device_id_type=MESH,
        )
        return cond, copy

    def wait(self, b):
        pc = self.pc
        pltpu.make_async_remote_copy(
            src_ref=self.dst.at[b], dst_ref=self.dst.at[b], send_sem=self.ssem.at[0], recv_sem=self.rsem.at[b],
            device_id=(pc.chip(pc.c1, (pc.y + 1) % pc.m, pc.x), pc.c), device_id_type=MESH,
        ).wait_recv()

    def pass_on(self, s):
        for place in self.places:
            if place[0] == s:
                cond, copy = self.send(place)
                pl.when(cond)(copy.start)

    def start(self):
        self.pass_on(0)

    def line(self, s):
        self.wait_line(s)
        self.pass_on(s)

    def wait_line(self, s):
        pc = self.pc
        for way in (1, -1):
            a = pc.c1 - way * s
            pl.when((a >= 0) & (a < pc.nz))(functools.partial(self.wait, pc.block(a, pc.y)))

    def wait_far(self):
        pc = self.pc
        for a in range(pc.nz):
            for j in range(1, pc.m):
                self.wait(pc.block(a, (pc.y + j) % pc.m))

    def finish(self, distances):
        for place in self.places:
            if place[0] in distances:
                cond, copy = self.send(place)
                pl.when(cond)(copy.wait_send)


def run_staggered(first, second, lag):
    for i in range(max(len(first), len(second) + lag)):
        if i < len(first):
            first[i]()
        if lag <= i < len(second) + lag:
            second[i - lag]()


def part_rows(rows):
    return rows - rows // 80 * 16


def front_kernel(
    n,
    x_ref, cot_ref, gain1, gain2, cos_ref, sin_ref, len_ref, logit_ref, route_ref,
    wq, wk, wv, wo, rg, ru, rd, sg, su, sd,
    all_dy, h_all, fq, fk, fv, fo, fg, fu, fd, pg, pu, pd,
    x1_ref, q_ref, k_ref, v_ref, o_ref, p_ref, gates_in, cnt_ref, base_ref, dus_ref, shared_ref,
    wbuf, h_ref, rows_out, turn_ref, shw, act, dg, dup, give, take,
    gs, gr, hs, hr, ls, ws, wr, wl, es, er, gss, grs, ps, pr, qs, qr, us, ur, ul, xs, xr,
):
    pc = Place(n)
    e, c = pc.e, pc.c
    rows, width = x_ref.shape
    half = width // 2
    pc.greet_all()
    x, y, m = pc.x, pc.y, pc.m
    me = pc.block(pc.c1, y)
    gather_dy = Lines(pc, cot_ref, all_dy, gs, gr)
    gather_h = Lines(pc, h_ref, h_all, hs, hr)
    own_dy = pltpu.make_async_copy(cot_ref, all_dy.at[me], ls.at[0])
    own_h = pltpu.make_async_copy(h_ref, h_all.at[me], ls.at[1])
    own_dy.start()
    partner = (e, 1 - c)
    halves = (wq, wk, wv, wo)
    fulls = (fq, fk, fv, fo)

    def swap(i):
        return pltpu.make_async_remote_copy(
            src_ref=halves[i], dst_ref=wbuf.at[i, c], send_sem=ws.at[i], recv_sem=wr.at[i],
            device_id=partner, device_id_type=MESH,
        )

    def own(i):
        return pltpu.make_async_copy(halves[i], wbuf.at[i, c], wl.at[0, i])

    def keep(i):
        return pltpu.make_async_copy(wbuf.at[i], fulls[i], wl.at[1, i])

    experts_other = (fg, fu, fd)

    def expert_swap(i, src):
        return pltpu.make_async_remote_copy(
            src_ref=src, dst_ref=experts_other[i], send_sem=es.at[i], recv_sem=er.at[i],
            device_id=partner, device_id_type=MESH,
        )

    beside = (pg, pu, pd)

    def half_send(i, j, src):
        return pltpu.make_async_remote_copy(
            src_ref=src, dst_ref=beside[i].at[m - j - 1, c], send_sem=ps.at[i, j - 1], recv_sem=pr.at[i, m - j - 1],
            device_id=(pc.chip(pc.c1, y, (x + j) % m), c), device_id_type=MESH,
        )

    def half_on(i, k):
        return pltpu.make_async_remote_copy(
            src_ref=beside[i].at[k, c], dst_ref=beside[i].at[k, c], send_sem=qs.at[i, k], recv_sem=qr.at[i, k],
            device_id=partner, device_id_type=MESH,
        )

    for i in range(4):
        swap(i).start()
        own(i).start()
    shared_halves = (sg, su, sd)

    def shared_swap(i):
        return pltpu.make_async_remote_copy(
            src_ref=shared_halves[i], dst_ref=shw.at[i, c], send_sem=us.at[i], recv_sem=ur.at[i],
            device_id=partner, device_id_type=MESH,
        )

    def shared_own(i):
        return pltpu.make_async_copy(shared_halves[i], shw.at[i, c], ul.at[i])

    for i, routed in enumerate((rg, ru, rd)):
        for j in range(1, m):
            half_send(i, j, routed).start()
    gather_dy.start()
    for i, routed in enumerate((rg, ru, rd)):
        expert_swap(i, routed).start()
        shared_swap(i).start()
        shared_own(i).start()

    lane = lax.broadcasted_iota(jnp.int32, (rows, 128), 1)
    row = lax.broadcasted_iota(jnp.int32, (rows, 128), 0)
    valid = (row < len_ref[0]).astype(jnp.float32)
    soft, routes = route_columns(logit_ref, route_ref, turn_ref)
    dense = jnp.zeros((rows, 128), jnp.float32)
    named = jnp.zeros((rows, 128), jnp.float32)
    for i in range(route_ref.shape[0]):
        hit = lane == routes[:, i : i + 1]
        dense = dense + jnp.where(hit, soft[:, i : i + 1], 0.0)
        named = named + jnp.where(hit, 1.0, 0.0)
    dense = dense * valid
    cnt_ref[...] = jnp.zeros_like(cnt_ref)
    cnt_ref[:, 0:128] = jnp.sum(named * valid, axis=0, keepdims=True)
    turned = dense.T
    for i in range(n):
        rows_out[i] = turned[i : i + 1, :]
    for i in range(m):
        gates_in[me * m + i] = rows_out[me * m + i]

    def gate_send(a, b2):
        return pltpu.make_async_remote_copy(
            src_ref=rows_out.at[pl.ds(pc.block(a, b2) * m, m)], dst_ref=gates_in.at[pl.ds(me * m, m)],
            send_sem=gss.at[a, b2], recv_sem=grs.at[pc.c1, y],
            device_id=(pc.chip(a, b2, x), c), device_id_type=MESH,
        )

    def gate_wait(a, b2):
        at = pl.ds(pc.block(a, b2) * m, m)
        pltpu.make_async_remote_copy(
            src_ref=rows_out.at[at], dst_ref=gates_in.at[at], send_sem=gss.at[a, b2], recv_sem=grs.at[a, b2],
            device_id=(pc.chip(a, b2, x), c), device_id_type=MESH,
        ).wait_recv()

    for a, b2 in pc.others():
        gate_send(a, b2).start()

    xv = x_ref[...].astype(jnp.float32)
    a = (xv * lax.rsqrt(jnp.mean(xv * xv, axis=-1, keepdims=True) + norm_eps) * gain1[...]).astype(jnp.bfloat16)
    cosine, sine = cos_ref[...], sin_ref[...]

    def project(values, i):
        own(i).wait()
        swap(i).wait_recv()
        keep(i).start()
        return matmul(values[:, :half], wbuf[i, 0]) + matmul(values[:, half:], wbuf[i, 1])

    for i, ref in ((0, q_ref), (1, k_ref)):
        flat = project(a, i)
        for hd in range(HEADS):
            part = flat[:, hd * HD : (hd + 1) * HD]
            ref[:, hd * HD : (hd + 1) * HD] = (part * cosine + swap_halves(part) * sine).astype(jnp.bfloat16)
    v_ref[...] = project(a, 2).astype(jnp.bfloat16)
    gather_dy.line(1)
    scale = HD ** (-0.5)
    row_pos = lax.broadcasted_iota(jnp.int32, (rows, rows), 0)
    col_pos = lax.broadcasted_iota(jnp.int32, (rows, rows), 1)
    allowed = (col_pos <= row_pos) & (col_pos < len_ref[0])

    def one_head(hd, carry):
        at = pl.ds(pl.multiple_of(hd * HD, HD), HD)
        scores = jnp.where(allowed, inner_cols(q_ref[:, at], k_ref[:, at]) * scale, -1e30)
        up = jnp.exp(scores - jnp.max(scores, axis=-1, keepdims=True))
        prob = up / jnp.sum(up, axis=-1, keepdims=True)
        p_ref[hd] = prob
        o_ref[:, at] = matmul(prob.astype(jnp.bfloat16), v_ref[:, at]).astype(jnp.bfloat16)
        return carry

    lax.fori_loop(0, HEADS, one_head, 0)
    gather_dy.line(2)
    x1 = xv + project(o_ref[...], 3)
    x1_ref[...] = x1
    h_ref[...] = (x1 * lax.rsqrt(jnp.mean(x1 * x1, axis=-1, keepdims=True) + norm_eps) * gain2[...]).astype(jnp.bfloat16)
    gather_h.start()
    own_h.start()
    for i in range(3, pc.nz):
        gather_dy.line(i)

    for i in range(3):
        shared_own(i).wait()
        shared_swap(i).wait_recv()
    wg, wu, wd = (shw.at[i] for i in range(3))
    h, z = h_ref[...], cot_ref[...]
    for half in range(2):
        g = inner_cols(h, wg[half])
        u = inner_cols(h, wu[half])
        da = inner_cols(z, wd[half])
        sig = jax.nn.sigmoid(g)
        si = g * sig
        act[half] = (si * u).astype(jnp.bfloat16)
        dup[half] = (da * si).astype(jnp.bfloat16)
        dg[half] = (da * u * sig * (1.0 + g * (1.0 - sig))).astype(jnp.bfloat16)

    def grad_swap(i):
        return pltpu.make_async_remote_copy(
            src_ref=give.at[i], dst_ref=take.at[i], send_sem=xs.at[i], recv_sem=xr.at[i],
            device_id=partner, device_id_type=MESH,
        )

    sides = ((dg, h), (dup, h), (act, z))
    for i, (left, right) in enumerate(sides):
        give[i] = outer_rows(left[1 - c], right).astype(jnp.bfloat16)
        grad_swap(i).start()
    base_ref[...] = x1_ref[...] + matmul(act[0], wd[0]) + matmul(act[1], wd[1])
    dus_ref[...] = matmul(dg[0], wg[0]) + matmul(dg[1], wg[1]) + matmul(dup[0], wu[0]) + matmul(dup[1], wu[1])
    hidden = give.shape[1]
    shared_ref[pl.ds(3 * hidden, shared_ref.shape[0] - 3 * hidden)] = jnp.zeros(
        (shared_ref.shape[0] - 3 * hidden, width), jnp.bfloat16
    )
    for i, (left, right) in enumerate(sides):
        part = outer_rows(left[c], right)
        grad_swap(i).wait()
        shared_ref[pl.ds(i * hidden, hidden)] = (part + take[i].astype(jnp.float32)).astype(jnp.bfloat16)
    for k in range(m - 1):
        for i in range(3):
            half_send(i, m - k - 1, sd).wait_recv()
            half_on(i, k).start()
    gather_dy.wait_far()
    for a, b2 in pc.others():
        gate_wait(a, b2)
        gate_send(a, b2).wait_send()
    gather_h.wait_line(1)
    for j in range(1, m):
        gather_h.wait(pc.block(pc.c1, (y + j) % m))
    gather_dy.finish(range(pc.nz))
    gather_h.finish((0,))
    own_dy.wait()
    own_h.wait()
    for i in range(4):
        swap(i).wait_send()
        keep(i).wait()
    for i, shared in enumerate((sg, su, sd)):
        expert_swap(i, shared).wait()
        shared_swap(i).wait_send()
        for k in range(m - 1):
            half_send(i, k + 1, shared).wait_send()
            half_on(i, k).wait_send()
            other = pltpu.make_async_remote_copy(
                src_ref=beside[i].at[k, 1 - c], dst_ref=beside[i].at[k, 1 - c], send_sem=qs.at[i, k], recv_sem=qr.at[i, k],
                device_id=partner, device_id_type=MESH,
            )
            other.wait_recv()


def front(n, x, cot, gain1, gain2, cosine, sine, length, logits, routes, attn_w, routed_w, shared_w):
    rows, width = x.shape
    hidden = shared_w[0].shape[0]
    vmem = pl.BlockSpec(memory_space=pltpu.VMEM)
    hbm = pl.BlockSpec(memory_space=pl.ANY)
    f32, b16 = jnp.float32, jnp.bfloat16
    out = jax.ShapeDtypeStruct
    dma = pltpu.SemaphoreType.DMA
    wide = out((rows, width), b16)
    full = out((2, width // 2, width), b16)
    nz = 4
    m = {16: 2, 64: 4}[n]
    beside = out((m - 1, 2, hidden, width), b16)
    narrow = pltpu.VMEM((2, rows, hidden), b16)
    three = pltpu.VMEM((3, hidden, width), b16)
    return pl.pallas_call(
        functools.partial(front_kernel, n),
        out_shape=(
            out((nz * m, rows, width), b16), out((nz * m, rows, width), b16), full, full, full, full,
            out((hidden, width), b16), out((hidden, width), b16), out((hidden, width), b16), beside, beside, beside,
            out((rows, width), f32), wide, wide, wide, wide, out((HEADS, rows, rows), f32),
            out((n, 1, rows), f32), out((1, width), f32),
            out((rows, width), f32), out((rows, width), f32), out((n * blocked(3 * hidden, n), width), b16),
        ),
        in_specs=[vmem] * 6 + [pl.BlockSpec(memory_space=pltpu.SMEM)] + [vmem] * 2 + [hbm] * 10,
        out_specs=(hbm,) * 12 + (vmem,) * 11,
        scratch_shapes=[
            pltpu.VMEM((4, 2, width // 2, width), b16), pltpu.VMEM((rows, width), b16), pltpu.VMEM((n, 1, rows), f32), pltpu.VMEM((128, rows), f32),
            pltpu.VMEM((3, 2, hidden, width), b16), narrow, narrow, narrow, three, three,
            dma((64,)), dma((nz * m,)), dma((64,)), dma((nz * m,)), dma((2,)), dma((4,)), dma((4,)), dma((2, 4)), dma((3,)), dma((3,)),
            dma((nz, m)), dma((nz, m)), dma((3, m - 1)), dma((3, m - 1)), dma((3, m - 1)), dma((3, m - 1)),
            dma((3,)), dma((3,)), dma((3,)), dma((3,)), dma((3,)),
        ],
        compiler_params=pltpu.CompilerParams(collective_id=0, has_side_effects=True, vmem_limit_bytes=56 * 2**20),
    )(x, cot, gain1, gain2, cosine, sine, length, logits, routes, *attn_w, *routed_w, *shared_w)


def experts_kernel(
    n, slots,
    h_in, dy_hbm, gates_in, rg, ru, rd, xg, xu, xd, pg, pu, pd, shared_hbm,
    scores_in, du_hbm, tg_hbm, tu_hbm, td_hbm, sum_hbm, y_hbm, far_hbm, h_all, part_hbm, xt_hbm, r3_hbm, r1_hbm,
    wbuf, og, ou, od, total_ref, hbuf, dbuf, act, dg, dup, stage, pbuf, rbuf, give, take, keep,
    gate_ref, s_ref, turn_ref, rows_out,
    gs, gr, lsem, ssem, r3sem, r1sem, bsem, wsem, partsem, pbsem, ysem,
    xssem, xrsem, gsend, grecv, osem, psem, scs, scr, room, vs, va, vb, vc,
):
    pc = Place(n)
    nz, m = pc.nz, pc.m
    c1, e, c, x, y = pc.c1, pc.e, pc.c, pc.x, pc.y
    blocks = nz * m
    me = pc.block(c1, y)
    toward = 1 - 2 * (c1 // (nz // 2))
    together = nz - 1
    grads = (og, ou, od)
    own_half = (rg, ru, rd)
    other_half = (xg, xu, xd)
    shared_half = (pg, pu, pd)

    def weight(p, i, half, src):
        return pltpu.make_async_copy(src, wbuf.at[p % 2, i, half], wsem.at[p % 2, i, half])

    def weights_start(p):
        for i in range(3):
            if p < m - 1:
                for half in range(2):
                    weight(p, i, half, shared_half[i].at[p, half]).start()
            else:
                weight(p, i, c, own_half[i]).start()
                weight(p, i, 1 - c, other_half[i]).start()

    weights_start(0)
    weights_start(1)
    hidden = give.shape[1]
    part_rows = keep.shape[0] // n
    fetch_shared = pltpu.make_async_copy(shared_hbm, keep, psem.at[0])
    fetch_shared.start()
    first_h = pltpu.make_async_copy(h_all.at[me], hbuf.at[0], lsem.at[0, 0])
    first_dy = pltpu.make_async_copy(dy_hbm.at[me], dbuf.at[0], lsem.at[1, 0])
    first_h.start()
    first_dy.start()
    pc.greet_all()
    gather = Lines(pc, None, h_all, gs, gr)
    gather.pass_on(1)

    def rows_of(ref, i):
        return ref.at[pl.ds(pl.multiple_of(i * part_rows, 16), part_rows)]

    from_b = (m - 1) * m * nz
    from_c = from_b + (nz - 1) * m
    shared_sum = Scatter(
        pc, ((m, x, 1), (nz, c1, m * m), (m, y, m)), functools.partial(rows_of, keep),
        lambda i, c_at, b_at: rows_of(take, (i * m + c_at) * nz + b_at),
        lambda i, c_at: rows_of(take, from_b + i * m + c_at),
        lambda i: rows_of(take, from_c + i), (vs, va, vb, vc),
    )
    fetch_shared.wait()
    shared_sum.start_plane(0)
    shared_steps = shared_sum.steps()
    sum_store = pltpu.make_async_copy(rows_of(keep, e), sum_hbm, psem.at[0])

    def shared_done():
        sum_store.start()
        shared_sum.finish()
        pl.semaphore_signal(room, inc=1, device_id=(e, 1 - c), device_id_type=MESH)
        sum_store.wait()

    shared_steps = shared_steps + [shared_done]

    def third(ref, i):
        return ref.at[pl.ds(i * hidden, hidden)]
    turn_ref[...] = jnp.zeros_like(turn_ref)
    for i in range(n):
        turn_ref[i : i + 1, :] = gates_in[i]
    gate_ref[...] = turn_ref[...].T
    for total in grads:
        total[...] = jnp.zeros_like(total)
    s_ref[...] = jnp.zeros_like(s_ref)

    def dest(step):
        p, t = step // blocks, step % blocks
        last = (p + 1) // m
        return (c1 + toward * (t // m + last) + nz) % nz, (y + t % m + last) % m

    def load(step, i):
        b = pc.block(*dest(step))
        return (
            pltpu.make_async_copy(h_all.at[b], hbuf.at[i], lsem.at[0, i]),
            pltpu.make_async_copy(dy_hbm.at[b], dbuf.at[i], lsem.at[1, i]),
        )

    def part_load(step, i):
        return pltpu.make_async_copy(part_hbm.at[pc.block(*dest(step))], pbuf.at[i], pbsem.at[i])

    def part_store(slot, b):
        return pltpu.make_async_copy(stage.at[slot], part_hbm.at[b], partsem.at[slot])

    def y_store(slot, a, b2):
        return pltpu.make_async_copy(stage.at[slot, 0], y_hbm.at[a, b2], ysem.at[slot])

    def pair_send(slot, to, dst, sem):
        return pltpu.make_async_remote_copy(
            src_ref=stage.at[slot], dst_ref=dst, send_sem=ssem.at[slot], recv_sem=sem,
            device_id=(to, c), device_id_type=MESH,
        )

    def du_send(slot, to, dst, sem):
        return pltpu.make_async_remote_copy(
            src_ref=stage.at[slot, 1], dst_ref=dst, send_sem=ssem.at[slot], recv_sem=sem,
            device_id=(to, c), device_id_type=MESH,
        )

    def collect(slot, received):
        def fetch(i):
            return pltpu.make_async_copy(received[i][0], rbuf.at[i % 2], bsem.at[i % 2])

        def begin(i):
            src, sem, landed = received[i]
            pltpu.make_async_remote_copy(
                src_ref=landed, dst_ref=landed, send_sem=ssem.at[slot], recv_sem=sem,
                device_id=(e, 1 - c), device_id_type=MESH,
            ).wait_recv()
            fetch(i).start()

        begin(0)
        total_ref[...] = stage[slot, 1].astype(jnp.float32)
        for i in range(len(received)):
            if i + 1 < len(received):
                begin(i + 1)
            fetch(i).wait()
            total_ref[...] += rbuf[i % 2].astype(jnp.float32)

    def from_y(a, whole):
        if whole:
            return [(far_hbm.at[j, a, 1], r3sem.at[j, a], far_hbm.at[j, a]) for j in range(m - 1)]
        return [(r3_hbm.at[j, a], r3sem.at[j, a], r3_hbm.at[j, a]) for j in range(m - 1)]

    def from_z():
        return [(r1_hbm.at[(c1 + j) % nz], r1sem.at[(c1 + j) % nz], r1_hbm.at[(c1 + j) % nz]) for j in range(1, nz)]

    def swaps():
        return [
            pltpu.make_async_remote_copy(
                src_ref=give.at[i], dst_ref=third(take, i), send_sem=xssem.at[i], recv_sem=xrsem.at[i],
                device_id=(e, 1 - c), device_id_type=MESH,
            )
            for i in range(3)
        ]

    def grad_send(p):
        return pltpu.make_async_remote_copy(
            src_ref=keep.at[pl.ds(0, 3 * hidden)], dst_ref=xt_hbm.at[x], send_sem=gsend, recv_sem=grecv.at[x],
            device_id=(pc.chip(c1, y, (x + p + 1) % m), c), device_id_type=MESH,
        )

    def totals():
        return [
            pltpu.make_async_copy(src.at[c], dst, osem.at[i])
            for i, (src, dst) in enumerate(((og, tg_hbm), (ou, tu_hbm), (od, td_hbm)))
        ]

    first_h.wait()
    first_dy.wait()

    def body(step, carry):
        i = step % 2
        slot = step % slots
        p, t = step // blocks, step % blocks
        last = (p + 1) // m
        a, b2 = dest(step)
        b = pc.block(a, b2)
        column = b * m + (x + p + 1) % m
        for at in range(m):
            @pl.when(step == at * blocks)
            def _():
                for k in range(3):
                    for half in range(2):
                        weight(at, k, half, other_half[k]).wait()
                if at >= 1 and at + 1 < m:
                    weights_start(at + 1)

        @pl.when(step > 0)
        def _():
            for copy in load(step, i):
                copy.wait()

        wg, wu, wd = (wbuf.at[p % 2, k] for k in range(3))
        lane = lax.broadcasted_iota(jnp.int32, gate_ref.shape, 1)
        gate = jnp.sum(jnp.where(lane == column, gate_ref[...], 0.0), axis=1, keepdims=True)
        h = hbuf[i]
        dy = dbuf[i].astype(jnp.float32)
        z = (gate * dy).astype(jnp.bfloat16)
        for half in range(2):
            g = inner_cols(h, wg[half])
            u = inner_cols(h, wu[half])
            da = inner_cols(z, wd[half])
            sg = jax.nn.sigmoid(g)
            si = g * sg
            act[half] = (si * u).astype(jnp.bfloat16)
            dup[half] = (da * si).astype(jnp.bfloat16)
            dg[half] = (da * u * sg * (1.0 + g * (1.0 - sg))).astype(jnp.bfloat16)

        before = step - slots
        before_last = ((before + slots * blocks) // blocks - slots + 1) // m

        @pl.when((before >= 0) & (before_last < 1))
        def _():
            part_store(slot, b).wait()

        before_t = (before + slots * blocks) % blocks

        @pl.when((before >= 0) & (before_last >= 1) & (before_t < together * m) & (before_t % m < m - 1))
        def _():
            pair_send(slot, e, far_hbm.at[0, 0], r3sem.at[0, 0]).wait_send()

        @pl.when((before >= 0) & (before_last >= 1) & ((before_t >= together * m) | (before_t % m == m - 1)))
        def _():
            y_store(slot, a, b2).wait()
            du_send(slot, e, r1_hbm.at[0], r1sem.at[0]).wait_send()

        yv = (matmul(act[0], wd[0]) + matmul(act[1], wd[1])).astype(jnp.bfloat16).astype(jnp.float32)
        s = jnp.sum(yv * dy, axis=1, keepdims=True)
        s_ref[...] = jnp.where(lane == column, s, s_ref[...])
        yv = gate * yv
        du = (
            matmul(dg[0], wg[0]) + matmul(dg[1], wg[1]) + matmul(dup[0], wu[0]) + matmul(dup[1], wu[1])
        ).astype(jnp.bfloat16)

        @pl.when(p == 0)
        def _():
            stage[slot, 0] = yv.astype(jnp.bfloat16)
            stage[slot, 1] = du

        @pl.when(p > 0)
        def _():
            part_load(step, i).wait()
            stage[slot, 0] = (yv + pbuf[i, 0].astype(jnp.float32)).astype(jnp.bfloat16)
            stage[slot, 1] = (du.astype(jnp.float32) + pbuf[i, 1].astype(jnp.float32)).astype(jnp.bfloat16)

        @pl.when(last == 0)
        def _():
            part_store(slot, b).start()

        @pl.when((last == 1) & ((t >= together * m) | (t % m == m - 1)))
        def _():
            y_store(slot, a, b2).start()

        for j in range(1, m):
            @pl.when((last == 1) & (t < together * m) & (b2 == (y + j) % m))
            def _():
                pair_send(slot, pc.chip(c1, b2, x), far_hbm.at[m - j - 1, a], r3sem.at[m - j - 1, a]).start()

            @pl.when((last == 1) & (t >= together * m) & (b2 == (y + j) % m))
            def _():
                du_send(slot, pc.chip(c1, b2, x), r3_hbm.at[m - j - 1, a], r3sem.at[m - j - 1, a]).start()

        for k in range(2, nz):
            pl.when(step == (k - 1) * m - 1)(functools.partial(gather.line, k))

        @pl.when(step < m * blocks - 1)
        def _():
            after = step + 1
            next_a, next_b = dest(after)

            @pl.when((after < blocks) & (next_b != y) & (next_a != c1))
            def _():
                gather.wait(pc.block(next_a, next_b))

            for copy in load(after, 1 - i):
                copy.start()

            @pl.when(after >= blocks)
            def _():
                part_load(after, 1 - i).start()

        for half in range(2):
            og[half] += outer_rows(dg[half], h)
            ou[half] += outer_rows(dup[half], h)
            od[half] += outer_rows(act[half], z)

        for k in range(1, m):
            pl.when(step == k - 1)(functools.partial(shared_sum.start_plane, k))
        spread = [(1 + i, i) for i in range(2 * m - 1)] + [(blocks - 2, 2 * m - 1), (blocks - 1, 2 * m)]
        for at, k in spread:
            pl.when(step == at)(shared_steps[k])

        for at in range(m - 1):
            @pl.when(step == (at + 1) * blocks - 1)
            def _():
                if at >= 1:
                    grad_send(at - 1).wait_send()
                for k, total in enumerate(grads):
                    give[k] = total[1 - c].astype(jnp.bfloat16)
                    third(keep, k)[...] = total[c].astype(jnp.bfloat16)
                    total[...] = jnp.zeros_like(total)
                pl.semaphore_wait(room, 1)
                for copy in swaps():
                    copy.start()

            @pl.when(step == (at + 1) * blocks)
            def _():
                for copy in swaps():
                    copy.wait()
                for k in range(3):
                    third(keep, k)[...] = (
                        third(keep, k)[...].astype(jnp.float32) + third(take, k)[...].astype(jnp.float32)
                    ).astype(jnp.bfloat16)
                pl.semaphore_signal(room, inc=1, device_id=(e, 1 - c), device_id_type=MESH)
                grad_send(at).start()

        for k in range(1, nz):
            @pl.when((last == 1) & (t == k * m))
            def _():
                at = (step - 1) % slots
                a1 = (c1 + toward * k + nz) % nz
                collect(at, from_y(a1, k - 1 < together))
                stage[at, 1] = total_ref[...].astype(jnp.bfloat16)
                du_send(at, pc.chip(a1, y, x), r1_hbm.at[c1], r1sem.at[c1]).start()

        return carry

    lax.fori_loop(0, m * blocks, body, 0)
    for i, total in enumerate(grads):
        give[i] = total[1 - c].astype(jnp.bfloat16)
    pl.semaphore_wait(room, 1)
    for copy in swaps():
        copy.start()
    turned = s_ref[...].T
    for i in range(n):
        rows_out[i] = turned[i : i + 1, :]
    for i in range(m):
        scores_in[me * m + i] = rows_out[me * m + i]

    def score_send(a, b2):
        return pltpu.make_async_remote_copy(
            src_ref=rows_out.at[pl.ds(pc.block(a, b2) * m, m)], dst_ref=scores_in.at[pl.ds(me * m, m)],
            send_sem=scs.at[a, b2], recv_sem=scr.at[c1, y],
            device_id=(pc.chip(a, b2, x), c), device_id_type=MESH,
        )

    def score_wait(a, b2):
        at = pl.ds(pc.block(a, b2) * m, m)
        pltpu.make_async_remote_copy(
            src_ref=rows_out.at[at], dst_ref=scores_in.at[at], send_sem=scs.at[a, b2], recv_sem=scr.at[a, b2],
            device_id=(pc.chip(a, b2, x), c), device_id_type=MESH,
        ).wait_recv()

    for a, b2 in pc.others():
        score_send(a, b2).start()
    for copy in swaps():
        copy.wait()
    for i, total in enumerate(grads):
        total[c] += third(take, i)[...].astype(jnp.float32)
    grad_send(m - 2).wait_send()
    for j in range(1, m):
        at = (x + j) % m
        pltpu.make_async_remote_copy(
            src_ref=xt_hbm.at[at], dst_ref=xt_hbm.at[at], send_sem=gsend, recv_sem=grecv.at[at],
            device_id=(pc.chip(c1, y, at), c), device_id_type=MESH,
        ).wait_recv()
        back = pltpu.make_async_copy(xt_hbm.at[at], take.at[pl.ds(0, 3 * hidden)], bsem.at[0])
        back.start()
        back.wait()
        for i, total in enumerate(grads):
            total[c] += third(take, i)[...].astype(jnp.float32)
    for copy in totals():
        copy.start()
    collect((m * blocks - 1) % slots, from_y(c1, nz - 1 < together) + from_z())
    final = pltpu.make_async_copy(total_ref, du_hbm, bsem.at[0])
    final.start()
    final.wait()
    for step in range(m * blocks - slots, m * blocks):
        t = step % blocks
        if t < together * m and t % m < m - 1:
            pair_send(step % slots, e, far_hbm.at[0, 0], r3sem.at[0, 0]).wait_send()
            continue
        y_store(step % slots, c1, y).wait()
        if step < m * blocks - 1:
            du_send(step % slots, e, r1_hbm.at[0], r1sem.at[0]).wait_send()
    for a, b2 in pc.others():
        score_wait(a, b2)
        score_send(a, b2).wait_send()
    gather.finish(range(1, nz))
    for copy in totals():
        copy.wait()


def experts(h, dy, gates, routed_w, other_w, partner_w, shared):
    blocks, rows, width = dy.shape
    n = gates.shape[0]
    hidden = routed_w[0].shape[0]
    nz = 4
    m = {16: 2, 64: 4}[n]
    slots = 4
    vmem = pl.BlockSpec(memory_space=pltpu.VMEM)
    hbm = pl.BlockSpec(memory_space=pl.ANY)
    f32, b16 = jnp.float32, jnp.bfloat16
    out = jax.ShapeDtypeStruct
    dma = pltpu.SemaphoreType.DMA
    grad = pltpu.VMEM((2, hidden, width), f32)
    pair = pltpu.VMEM((2, rows, width), b16)
    narrow = pltpu.VMEM((2, rows, hidden), b16)
    three = pltpu.VMEM((3, hidden, width), b16)
    return pl.pallas_call(
        functools.partial(experts_kernel, n, slots),
        out_shape=(
            out((n, 1, rows), f32), out((rows, width), f32),
            out((hidden, width), f32), out((hidden, width), f32), out((hidden, width), f32),
            out((shared.shape[0] // n, width), b16), out((nz, m, rows, width), b16), out((m - 1, nz, 2, rows, width), b16),
            out((blocks, rows, width), b16), out((blocks, 2, rows, width), b16), out((m, 3 * hidden, width), b16),
            out((m - 1, nz, rows, width), b16), out((nz, rows, width), b16),
        ),
        in_specs=[hbm, hbm, vmem] + [hbm] * 10,
        out_specs=(vmem,) + (hbm,) * 12,
        input_output_aliases={0: 8},
        scratch_shapes=[
            pltpu.VMEM((2, 3, 2, hidden, width), b16), grad, grad, grad,
            pltpu.VMEM((rows, width), f32), pair, pair, narrow, narrow, narrow,
            pltpu.VMEM((slots, 2, rows, width), b16), pltpu.VMEM((2, 2, rows, width), b16), pair, three,
            pltpu.VMEM((max(3 * hidden, shared.shape[0] // n * (n - 1)), width), b16), pltpu.VMEM(shared.shape, b16),
            pltpu.VMEM((rows, 128), f32), pltpu.VMEM((rows, 128), f32), pltpu.VMEM((128, rows), f32), pltpu.VMEM((n, 1, rows), f32),
            dma((64,)), dma((blocks,)), dma((2, 2)), dma((slots,)), dma((m - 1, nz)), dma((nz,)), dma((2,)),
            dma((2, 3, 2)), dma((slots,)), dma((2,)), dma((slots,)),
            dma((3,)), dma((3,)), dma, dma((m,)), dma((3,)), dma((3,)), dma((nz, m)), dma((nz, m)),
            pltpu.SemaphoreType.REGULAR, dma((n,)), dma((m - 1, m, nz)), dma((nz - 1, m)), dma((m - 1,)),
        ],
        compiler_params=pltpu.CompilerParams(collective_id=1, has_side_effects=True, vmem_limit_bytes=62 * 2**20),
    )(h, dy, gates, *routed_w, *other_w, *partner_w, shared)


def swap_halves(values):
    return pltpu.roll(values, HD // 2, axis=1)


def route_columns(logit_ref, route_ref, turn_ref):
    count = logit_ref.shape[0]
    logits = logit_ref[...]
    raised = jnp.exp(logits - jnp.max(logits, axis=0, keepdims=True))
    turn_ref[...] = jnp.zeros_like(turn_ref)
    turn_ref[0:count, :] = raised / jnp.sum(raised, axis=0, keepdims=True)
    soft = turn_ref[...].T
    turn_ref[0:count, :] = route_ref[...].astype(jnp.float32)
    return soft, turn_ref[...].T.astype(jnp.int32)


class Scatter:
    def __init__(self, pc, axes, block, ra, rb, rc, sems):
        self.pc, self.block, self.ra, self.rb, self.rc = pc, block, ra, rb, rc
        (self.na, self.a, self.sa), (self.nb, self.b, self.sb), (self.nc, self.c, self.sc) = axes
        self.ssem, self.sema, self.semb, self.semc = sems

    def at(self, i, j, k):
        a, b, c = (self.a + i) % self.na, (self.b + j) % self.nb, (self.c + k) % self.nc
        return a * self.sa + b * self.sb + c * self.sc

    def copy(self, b, dst, sem, to):
        return pltpu.make_async_remote_copy(
            src_ref=self.block(b), dst_ref=dst, send_sem=self.ssem.at[b], recv_sem=sem,
            device_id=(to, self.pc.c), device_id_type=MESH,
        )

    def add(self, total, src, sem):
        self.copy(self.pc.e, src, sem, self.at(1, 0, 0)).wait_recv()
        return total + src[...].astype(jnp.float32)

    def place_b(self, j):
        return (self.b + j) % self.nb

    def place_c(self, k):
        return (self.c + k) % self.nc

    def start(self):
        for k in range(self.nc):
            self.start_plane(k)

    def start_plane(self, p):
        k = (p + 1) % self.nc
        for i in range(1, self.na):
            for j in list(range(1, self.nb)) + [0]:
                b, c = self.place_b(j), self.place_c(k)
                slot = self.na - i - 1
                self.copy(self.at(i, j, k), self.ra(slot, c, b), self.sema.at[slot, c, b], self.at(i, 0, 0)).start()

    def collect(self, j, k, level):
        block = self.block(self.at(0, j, k))
        b, c = self.place_b(j), self.place_c(k)
        total = block[...].astype(jnp.float32)
        for i in range(self.na - 1):
            total = self.add(total, self.ra(i, c, b), self.sema.at[i, c, b])
        if level >= 2:
            for i in range(self.nb - 1):
                total = self.add(total, self.rb(i, c), self.semb.at[i, c])
        if level >= 3:
            for i in range(self.nc - 1):
                total = self.add(total, self.rc(i), self.semc.at[i])
        block[...] = total.astype(jnp.bfloat16)

    def second(self, p):
        k = (p + 1) % self.nc
        for j in range(1, self.nb):
            self.collect(j, k, 1)
            slot = self.nb - j - 1
            self.copy(self.at(0, j, k), self.rb(slot, self.place_c(k)), self.semb.at[slot, self.place_c(k)], self.at(0, j, 0)).start()

    def third(self, p):
        k = p + 1
        self.collect(0, k, 2)
        slot = self.nc - k - 1
        self.copy(self.at(0, 0, k), self.rc(slot), self.semc.at[slot], self.at(0, 0, k)).start()

    def last(self):
        self.collect(0, 0, 3)

    def steps(self):
        found = [functools.partial(self.second, 0)]
        for p in range(1, self.nc):
            found += [functools.partial(self.second, p), functools.partial(self.third, p - 1)]
        return found + [self.last]

    def finish(self):
        n = self.pc.n

        def one(j, carry):
            to = (self.pc.e + j) % n
            self.copy(to, self.rc(0), self.semc.at[0], to).wait_send()
            return carry

        lax.fori_loop(1, n, one, 0)


def tail_kernel(
    n,
    x_ref, x1_ref, cot_ref, dh_ref, dus_hbm, base_hbm, own_ref, q_ref, k_ref, v_ref, o_ref, p_ref, wq, wk, wv, wo,
    gain1, gain2, cos_ref, sin_ref, cnt_ref, len_ref, logit_ref, route_ref, scores_in, y_hbm, far_hbm,
    out_ref, gtok_ref, glog_ref, small_ref, ag0, ag1, ags, y3_hbm, y1_hbm,
    dx_ref, dq_ref, dk_ref, dv_ref, a_ref, give, take, stack0, stack1, r3, r2, r1,
    sm_core, sm_d3, sm_d2, sm_z,
    wbuf, wsem, turn_ref, ybuf, ytmp,
    gs, gr, ss, s3, s2, s1, xs, xr, cs, cr, locs, yl, yt, ys3, ys1, y3s, y1s,
):
    pc = Place(n)
    c1, c2, c3, e, c, nz, m = pc.c1, pc.c2, pc.c3, pc.e, pc.c, pc.nz, pc.m
    rows, width = x_ref.shape
    half = width // 2
    pc.greet_all()

    x, y = pc.x, pc.y

    def y_far(a, j):
        return pltpu.make_async_remote_copy(
            src_ref=y_hbm.at[a, (y + j) % m], dst_ref=y3_hbm.at[m - j - 1, a], send_sem=ys3.at[j - 1, a], recv_sem=y3s.at[m - j - 1, a],
            device_id=(pc.chip(c1, (y + j) % m, x), c), device_id_type=MESH,
        )

    def y_along(a):
        return pltpu.make_async_remote_copy(
            src_ref=ybuf.at[a], dst_ref=y1_hbm.at[c1], send_sem=ys1.at[a], recv_sem=y1s.at[c1],
            device_id=(pc.chip(a, y, x), c), device_id_type=MESH,
        )

    toward = 1 - 2 * (c1 // (nz // 2))
    together = nz - 1

    def plane(i):
        return (c1 + toward * (i + 1) + nz) % nz

    for i in range(together, nz):
        for j in range(1, m):
            y_far(plane(i), j).start()
    y_own = [pltpu.make_async_copy(y_hbm.at[a, y], ybuf.at[a], yl.at[a]) for a in range(nz)]
    for copy in y_own:
        copy.start()

    def y_sum(a, received):
        def fetched(i):
            return pltpu.make_async_copy(received[i][0], ytmp.at[i % 2], yt.at[i % 2])

        def begin(i):
            src, sem = received[i]
            if sem is not None:
                pltpu.make_async_remote_copy(
                    src_ref=src, dst_ref=src, send_sem=ys1.at[0], recv_sem=sem, device_id=(e, 1 - c), device_id_type=MESH,
                ).wait_recv()
            fetched(i).start()

        begin(0)
        total = ybuf[a].astype(jnp.float32)
        for i in range(len(received)):
            if i + 1 < len(received):
                begin(i + 1)
            fetched(i).wait()
            total = total + ytmp[i % 2].astype(jnp.float32)
        return total

    def y_from3(i):
        a = plane(i)
        if i < together:
            return [(far_hbm.at[k, a, 0], None) for k in range(m - 1)]
        return [(y3_hbm.at[k, a], y3s.at[k, a]) for k in range(m - 1)]

    def y_third(i):
        a = plane(i)
        ybuf[a] = y_sum(a, y_from3(i)).astype(jnp.bfloat16)
        y_along(a).start()

    def y_last():
        along = [(y1_hbm.at[(c1 + j) % nz], y1s.at[(c1 + j) % nz]) for j in range(1, nz)]
        out_ref[...] = (dx_ref[...] + y_sum(c1, y_from3(nz - 1) + along)).astype(jnp.bfloat16)

    def y_finish():
        for i in range(nz - 1):
            y_along(plane(i)).wait_send()
        for i in range(together, nz):
            for j in range(1, m):
                y_far(plane(i), j).wait_send()

    gather_s = Gather(pc, own_ref, ags, gs.at[2], gr.at[2], own_ref.shape[0])
    loc_s = pltpu.make_async_copy(own_ref, ags.at[e], locs.at[2])
    gather_s.start()
    loc_s.start()
    shared_events = gather_s.events()

    def fetch(src, i):
        return pltpu.make_async_copy(src, wbuf.at[i], wsem.at[i])

    get_dus = pltpu.make_async_copy(dus_hbm, dx_ref, locs.at[0])
    get_dus.start()
    fetch(wo, 0).start()
    fetch(wv, 1).start()

    x1 = x1_ref[...]
    up = cot_ref[...].astype(jnp.float32)
    get_dus.wait()
    dh = dh_ref[...] + dx_ref[...]
    r_two = lax.rsqrt(jnp.mean(x1 * x1, axis=-1, keepdims=True) + norm_eps)
    n_two = x1 * r_two
    scaled = dh * gain2[...]
    grad_two = jnp.sum(dh * n_two, axis=0, keepdims=True)
    dx = up + r_two * (scaled - n_two * jnp.mean(scaled * n_two, axis=-1, keepdims=True))
    dx_ref[...] = dx
    dx_low = dx.astype(jnp.bfloat16)

    def columns(ref, which):
        return ref[:, pl.ds(pl.multiple_of(which * half, 128), half)]

    def hand(i):
        return pltpu.make_async_remote_copy(
            src_ref=give.at[i], dst_ref=take.at[i], send_sem=xs.at[i], recv_sem=xr.at[i],
            device_id=(e, 1 - c), device_id_type=MESH,
        )

    def to_partner(i, left, right):
        give[i] = outer_rows(columns(left, 1 - c), right).astype(jnp.bfloat16)
        hand(i).start()

    def own_part(i, left, right, stack, at):
        block = stack.shape[1]
        part = outer_rows(columns(left, c), right)
        hand(i).wait_recv()
        total = (part + take[i].astype(jnp.float32)).astype(jnp.bfloat16)
        stack[pl.ds(at * (half // block), half // block)] = total.reshape(half // block, block, width)

    to_partner(0, o_ref, dx_low)
    shared_events[0]()
    fetch(wo, 0).wait()
    dq_ref[...] = inner_cols(dx_low, wbuf[0]).astype(jnp.bfloat16)
    fetch(wk, 0).start()
    cosine, sine = cos_ref[...], sin_ref[...]
    scale = HD ** (-0.5)

    def one_head(hd, carry):
        at = pl.ds(pl.multiple_of(hd * HD, HD), HD)
        prob = p_ref[hd]
        d_o, val, que, key = dq_ref[:, at], v_ref[:, at], q_ref[:, at], k_ref[:, at]
        dv_ref[:, at] = outer_rows(prob.astype(jnp.bfloat16), d_o).astype(jnp.bfloat16)
        d_prob = inner_cols(d_o, val)
        inner = jnp.sum(prob * d_prob, axis=-1, keepdims=True)
        d_score = (prob * (d_prob - inner)).astype(jnp.bfloat16)
        d_q = matmul(d_score, key) * scale
        d_k = outer_rows(d_score, que) * scale
        dq_ref[:, at] = (d_q * cosine - swap_halves(d_q) * sine).astype(jnp.bfloat16)
        dk_ref[:, at] = (d_k * cosine - swap_halves(d_k) * sine).astype(jnp.bfloat16)
        return carry

    lax.fori_loop(0, HEADS, one_head, 0)
    for copy in y_own:
        copy.wait()
    for i in range(nz - 1):
        y_third(i)
    xv = x_ref[...].astype(jnp.float32)
    r_one = lax.rsqrt(jnp.mean(xv * xv, axis=-1, keepdims=True) + norm_eps)
    n_one = xv * r_one
    a_ref[...] = (n_one * gain1[...]).astype(jnp.bfloat16)
    shared_events[1]()
    to_partner(1, a_ref, dv_ref[...])
    to_partner(2, a_ref, dk_ref[...])
    to_partner(3, a_ref, dq_ref[...])
    if n * stack0.shape[1] > 2 * half:
        stack0[...] = jnp.zeros_like(stack0)
        stack1[...] = jnp.zeros_like(stack1)
    own_part(0, o_ref, dx_low, stack0, 0)
    own_part(1, a_ref, dv_ref[...], stack0, 1)
    first, second = (
        Scatter(
            pc, ((m, c3, pc.s3), (m, c2, pc.s2), (nz, c1, pc.s1)), lambda b, stack=stack: stack.at[b], lambda k, a, b2, i=i: r3.at[i, k, a, b2], lambda k, a, i=i: r2.at[i, k, a],
            lambda k, i=i: r1.at[i, k], (ss.at[i], s3.at[i], s2.at[i], s1.at[i]),
        )
        for i, stack in enumerate((stack0, stack1))
    )
    first.start()
    shared_events[2]()
    shared_events[3]()
    own_part(2, a_ref, dk_ref[...], stack1, 0)
    own_part(3, a_ref, dq_ref[...], stack1, 1)
    second.start()
    fetch(wv, 1).wait()
    da = inner_cols(dv_ref[...], wbuf[1])
    fetch(wq, 1).start()
    fetch(wk, 0).wait()
    da = da + inner_cols(dk_ref[...], wbuf[0])
    fetch(wq, 1).wait()
    da = da + inner_cols(dq_ref[...], wbuf[1])
    scaled_one = da * gain1[...]
    grad_one = jnp.sum(da * n_one, axis=0, keepdims=True)
    back = r_one * (scaled_one - n_one * jnp.mean(scaled_one * n_one, axis=-1, keepdims=True))
    gtok_ref[...] = (dx_ref[...] + back).astype(jnp.bfloat16)
    get_base = pltpu.make_async_copy(base_hbm, dx_ref, wsem.at[0])
    get_base.start()

    def exchange(ref, own, level, peers, value):
        ref[own] = value
        copies = [
            pltpu.make_async_remote_copy(
                src_ref=ref.at[own], dst_ref=ref.at[own], send_sem=cs.at[level, i], recv_sem=cr.at[level, own],
                device_id=to, device_id_type=MESH,
            )
            for i, (to, at) in enumerate(peers)
        ]
        for copy in copies:
            copy.start()

        def done():
            for i, (to, at) in enumerate(peers):
                pltpu.make_async_remote_copy(
                    src_ref=ref.at[own], dst_ref=ref.at[at], send_sem=cs.at[level, i], recv_sem=cr.at[level, at],
                    device_id=to, device_id_type=MESH,
                ).wait_recv()
            for copy in copies:
                copy.wait_send()
            total = ref[0]
            for i in range(1, ref.shape[0]):
                total = total + ref[i]
            return total

        return done

    turn_ref[...] = jnp.zeros_like(turn_ref)
    for i in range(n):
        turn_ref[i : i + 1, :] = scores_in[i]
    scores = turn_ref[...].T
    lane = lax.broadcasted_iota(jnp.int32, (rows, 128), 1)
    row = lax.broadcasted_iota(jnp.int32, (rows, 128), 0)
    scores = jnp.where(row < len_ref[0], scores, 0.0)
    soft, routes = route_columns(logit_ref, route_ref, turn_ref)
    share = jnp.zeros((rows, 128), jnp.float32)
    for i in range(route_ref.shape[0]):
        picked = jnp.sum(jnp.where(lane == routes[:, i : i + 1], scores, 0.0), axis=-1, keepdims=True)
        share = jnp.where(lane == i, picked, share)
    grad_logits = soft * (share - jnp.sum(soft * share, axis=-1, keepdims=True))
    glog_ref[...] = grad_logits.T[0 : route_ref.shape[0], :]

    small = jnp.concatenate([grad_one, grad_two, cnt_ref[...], jnp.zeros((5, width), jnp.float32)], axis=0)
    level0 = exchange(sm_core, c, 0, [((e, 1 - c), 1 - c)], small)
    steps0, steps1 = first.steps(), second.steps()
    steps0[0]()
    steps0[1]()
    shared_events[4]()
    level1 = exchange(sm_d3, c3, 1, [((pc.blk(c1, c2, j), c), j) for j in pc.o3()], level0())
    steps0[2]()
    steps1[0]()
    steps0[3]()
    steps1[1]()
    steps0[4]()
    for event in shared_events[5:-1]:
        event()
    level2 = exchange(sm_d2, c2, 2, [((pc.blk(c1, j, c3), c), j) for j in pc.o2()], level1())
    steps1[2]()
    for step in steps0[5:-1]:
        step()
    level3 = exchange(sm_z, c1, 3, [((pc.blk((c1 + j) % nz, c2, c3), c), (c1 + j) % nz) for j in range(1, nz)], level2())
    for step in steps1[3:-1]:
        step()
    small_ref[...] = level3()
    steps0[-1]()
    g0 = Gather(pc, stack0.at[e], ag0, gs.at[0], gr.at[0], stack0.shape[1])
    g0.start()
    loc0 = pltpu.make_async_copy(stack0.at[e], ag0.at[e], locs.at[0])
    loc0.start()
    steps1[-1]()
    g1 = Gather(pc, stack1.at[e], ag1, gs.at[1], gr.at[1], stack1.shape[1])
    g1.start()
    loc1 = pltpu.make_async_copy(stack1.at[e], ag1.at[e], locs.at[1])
    loc1.start()
    get_base.wait()
    y_last()
    run_staggered(g0.events(), g1.events(), 1)
    shared_events[-1]()
    for g in (gather_s, g0, g1):
        g.finish()
    first.finish()
    second.finish()
    loc_s.wait()
    loc0.wait()
    loc1.wait()
    y_finish()
    for i in range(4):
        hand(i).wait_send()


def tail(n, x, x1, cot, dh, dus, base, own, q, k, v, o, prob, wq, wk, wv, wo, gain1, gain2, cosine, sine, cnt, length, logits, routes, scores, y, far):
    nz = 4
    m = {16: 2, 64: 4}[n]
    rows, width = x.shape
    half = width // 2
    block = blocked(2 * half, n)
    vmem = pl.BlockSpec(memory_space=pltpu.VMEM)
    hbm = pl.BlockSpec(memory_space=pl.ANY)
    f32, b16 = jnp.float32, jnp.bfloat16
    out = jax.ShapeDtypeStruct
    dma = pltpu.SemaphoreType.DMA
    wide = pltpu.VMEM((rows, width), b16)
    return pl.pallas_call(
        functools.partial(tail_kernel, n),
        out_shape=(
            out((rows, width), b16), out((rows, width), b16), out(logits.shape, f32), out((8, width), f32),
            out((n, block, width), b16), out((n, block, width), b16),
            out((n,) + own.shape, b16),
            out((m - 1, nz, rows, width), b16), out((nz, rows, width), b16),
        ),
        in_specs=[vmem] * 4 + [hbm] * 2 + [vmem] * 6 + [hbm] * 4 + [vmem] * 5 + [pl.BlockSpec(memory_space=pltpu.SMEM)] + [vmem] * 3 + [hbm] * 2,
        out_specs=(vmem,) * 4 + (hbm,) * 5,
        scratch_shapes=[
            pltpu.VMEM((rows, width), f32), wide, wide, wide, wide,
            pltpu.VMEM((4, half, width), b16), pltpu.VMEM((4, half, width), b16),
            pltpu.VMEM((n, block, width), b16), pltpu.VMEM((n, block, width), b16),
            pltpu.VMEM((2, m - 1, nz, m, block, width), b16), pltpu.VMEM((2, m - 1, nz, block, width), b16),
            pltpu.VMEM((2, nz - 1, block, width), b16),
            pltpu.VMEM((2, 8, width), f32), pltpu.VMEM((m, 8, width), f32), pltpu.VMEM((m, 8, width), f32), pltpu.VMEM((nz, 8, width), f32),
            pltpu.VMEM((2, width, width), b16), dma((2,)), pltpu.VMEM((128, rows), f32),
            pltpu.VMEM((nz, rows, width), b16), pltpu.VMEM((2, rows, width), b16),
            dma((3, 160)), dma((3, 2, n)), dma((2, n)), dma((2, m - 1, nz, m)), dma((2, m - 1, nz)), dma((2, nz - 1)),
            dma((4,)), dma((4,)), dma((4, max(nz, m))), dma((4, max(nz, m, 2))), dma((3,)),
            dma((nz,)), dma((2,)), dma((m - 1, nz)), dma((nz,)), dma((m - 1, nz)), dma((nz,)),
        ],
        compiler_params=pltpu.CompilerParams(collective_id=2, has_side_effects=True, vmem_limit_bytes=63 * 2**20),
    )(x, x1, cot, dh, dus, base, own, q, k, v, o, prob, wq, wk, wv, wo, gain1, gain2, cosine, sine, cnt, length, logits, routes, scores, y, far)


def blocked(count, n):
    return -(-count // (16 * n)) * 16


def from_blocks(blocks, count):
    return blocks.reshape(-1, blocks.shape[2])[:count].astype(jnp.float32)


def rotary_rows(seq_len):
    position = np.arange(seq_len).astype(np.float32)
    inverse_freq = (rotary_base ** (-2.0 * np.arange(HD // 2).astype(np.float32) / HD)).astype(np.float32)
    angle = position[:, None] * inverse_freq[None, :]
    cosine, sine = np.cos(angle), np.sin(angle)
    return np.concatenate([cosine, cosine], axis=1), np.concatenate([-sine, sine], axis=1)


def on_device(
    tokens, norm_one, w_query, w_key, w_value, w_out, norm_two, r_gate, r_up, r_down, s_gate, s_up, s_down,
    logits, routes, lengths, cotangent,
):
    rows, width = tokens.shape
    n = lax.axis_size("exp")
    hidden = s_gate.shape[1]
    cosine, sine = (jnp.asarray(table) for table in rotary_rows(rows))
    gain1, gain2 = norm_one[None], norm_two[None]
    logits, routes = logits.T, routes.T
    attn_w = (w_query, w_key, w_value, w_out)
    routed_w = (r_gate[0].T, r_up[0].T, r_down[0])
    shared_w = (s_gate.T, s_up.T, s_down)
    (
        all_dy, all_h, fq, fk, fv, fo, fg, fu, fd, pg, pu, pd, mixed, queries, keys_all, values_all, attended, prob, gates, counts,
        base, shared_back, shared_grads,
    ) = front(
        n, tokens, cotangent, gain1, gain2, cosine, sine, lengths, logits, routes,
        attn_w, routed_w, shared_w,
    )
    scores, grad_hidden, tg, tu, td, shared_sum, outs, far_outs = experts(
        all_h, all_dy, gates, routed_w, (fg, fu, fd), (pg, pu, pd), shared_grads
    )[:8]
    full = (width, width)
    output, grad_tokens, grad_logits, small_sums, sum0, sum1, sum_s = tail(
        n, tokens, mixed, cotangent, grad_hidden, shared_back, base, shared_sum, queries, keys_all, values_all, attended, prob,
        fq.reshape(full), fk.reshape(full), fv.reshape(full), fo.reshape(full),
        gain1, gain2, cosine, sine, counts, lengths, logits, routes, scores,
        outs, far_outs,
    )[:7]
    half = width // 2
    wout_value = from_blocks(sum0, width)
    key_query = from_blocks(sum1, width)
    shared = from_blocks(sum_s, 3 * hidden)
    sg, su, sd = (shared[i * hidden : (i + 1) * hidden] for i in range(3))
    return (
        output, grad_tokens, small_sums[0],
        key_query[half:], key_query[:half], wout_value[half:], wout_value[:half],
        small_sums[1], tg.T[None], tu.T[None], td[None], sg.T, su.T, sd,
        grad_logits.T, small_sums[2, :n].astype(jnp.int32),
    )


def solution(mesh):
    in_specs = (
        P(("exp", "hid"), None),
        P(),
        P("hid", None),
        P("hid", None),
        P("hid", None),
        P("hid", None),
        P(),
        P("exp", None, "hid"),
        P("exp", None, "hid"),
        P("exp", "hid", None),
        P(None, "hid"),
        P(None, "hid"),
        P("hid", None),
        P(("exp", "hid"), None),
        P(("exp", "hid"), None),
        P(("exp", "hid")),
        P(("exp", "hid"), None),
    )
    out_specs = (
        P(("exp", "hid"), None),
        P(("exp", "hid"), None),
        P(),
        P("hid", None),
        P("hid", None),
        P("hid", None),
        P("hid", None),
        P(),
        P("exp", None, "hid"),
        P("exp", None, "hid"),
        P("exp", "hid", None),
        P(None, "hid"),
        P(None, "hid"),
        P("hid", None),
        P(("exp", "hid"), None),
        P(),
    )
    return jax.shard_map(
        on_device, mesh=mesh, in_specs=in_specs, out_specs=out_specs, check_vma=False
    )
```

```python
import functools

import jax
import jax.numpy as jnp
import numpy as np
from jax import lax
from jax.experimental import pallas as pl
from jax.experimental.pallas import tpu as pltpu
from jax.sharding import PartitionSpec as P

HEADS = 10
HD = 128
MESH = pl.DeviceIdType.MESH


norm_eps = 1e-06
rotary_base = 10000.0
contract_rows = (((0,), (0,)), ((), ()))
contract_cols = (((1,), (1,)), ((), ()))


def matmul(left_side, right_side):
    return jnp.dot(left_side, right_side, preferred_element_type=jnp.float32)


def outer_rows(left_side, right_side):
    return lax.dot_general(left_side, right_side, contract_rows, preferred_element_type=jnp.float32)


def inner_cols(left_side, right_side):
    return lax.dot_general(left_side, right_side, contract_cols, preferred_element_type=jnp.float32)


class Place:
    def __init__(self, n):
        self.n = n; self.nz = 4; self.m = {16: 2, 64: 4}[n]; m = self.m
        self.e = lax.axis_index("exp"); self.c = lax.axis_index("hid"); c = self.c; e = self.e
        self.s1 = m * m; self.s2 = 1 + c * (m - 1); self.s3 = m - c * (m - 1)
        self.x = e % m; self.y = (e // m) % m
        self.c1 = e // self.s1; self.c2 = (e // self.s2) % m; self.c3 = (e // self.s3) % m
    def chip(self, z, y, x): return z * self.s1 + y * self.m + x
    def block(self, z, y): return z * self.m + y
    def others(self):
        far = [((self.c1 + i) % self.nz, (self.y + j) % self.m) for i in range(self.nz) for j in range(self.m)]
        return far[1:]
    def blk(self, a, b, d): return a * self.s1 + b * self.s2 + d * self.s3
    def o2(self): return [(self.c2 + j) % self.m for j in range(1, self.m)]
    def o3(self): return [(self.c3 + j) % self.m for j in range(1, self.m)]
    def greet_all(self):
        barrier = pltpu.get_barrier_semaphore()

        def greet(j, carry):
            pl.semaphore_signal(barrier, inc=1, device_id=((self.e + j) % self.n, self.c), device_id_type=MESH)
            return carry

        lax.fori_loop(1, self.n, greet, 0)
        pl.semaphore_signal(barrier, inc=1, device_id=(self.e, 1 - self.c), device_id_type=MESH)
        pl.semaphore_wait(barrier, self.n)


class Gather:
    def __init__(self, pc, src, dst, ssem, rsem, split, base=0):
        self.pc, self.src, self.dst, self.ssem, self.rsem = pc, src, dst, ssem, rsem
        self.split = split; self.sends = []; self.base = base
    def view(self, ref, part):
        R = self.src.shape[0]
        return ref.at[pl.ds(0, self.split)] if part == 0 else ref.at[pl.ds(self.split, R - self.split)]
    def send(self, part, own, b, to, cond=None):
        i = self.base + len(self.sends)
        src = self.view(self.src if own else self.dst.at[b], part)
        cp = pltpu.make_async_remote_copy(src_ref=src, dst_ref=self.view(self.dst.at[b], part), send_sem=self.ssem.at[i], recv_sem=self.rsem.at[part, b], device_id=(to, self.pc.c), device_id_type=MESH)
        self.sends.append((cond, cp))
        if cond is None: cp.start()
        else: pl.when(cond)(cp.start)
    def wait(self, part, b):
        v = self.view(self.dst.at[b], part)
        to = self.pc.blk(self.pc.c1, self.pc.c2, self.pc.o3()[0])
        pltpu.make_async_remote_copy(src_ref=v, dst_ref=v, send_sem=self.ssem.at[0], recv_sem=self.rsem.at[part, b], device_id=(to, self.pc.c), device_id_type=MESH).wait_recv()
    def updown(self, part, own, b):
        pc = self.pc
        self.send(part, own, b, pc.blk(pc.c1 + 1, pc.c2, pc.c3), pc.c1 < pc.nz - 1)
        self.send(part, own, b, pc.blk(pc.c1 - 1, pc.c2, pc.c3), pc.c1 > 0)
    def to2(self, part, own, b):
        pc = self.pc
        for j in pc.o2(): self.send(part, own, b, pc.blk(pc.c1, j, pc.c3))
    def to3(self, part, own, b):
        pc = self.pc
        for j in pc.o3(): self.send(part, own, b, pc.blk(pc.c1, pc.c2, j))
    def start(self):
        e = self.pc.e
        self.to3(0, True, e); self.to2(0, True, e); self.updown(0, True, e)
        if self.split < self.src.shape[0]:
            self.to3(1, True, e); self.to2(1, True, e); self.updown(1, True, e)
    def zarr(self, part, s, up, k2, k3, more):
        pc = self.pc
        a = pc.c1 - s if up else pc.c1 + s
        cond = (pc.c1 >= s) if up else (pc.c1 < pc.nz - s)
        b = pc.blk(a, k2, k3)
        pl.when(cond)(lambda: self.wait(part, b))
        if s < pc.nz - 1:
            if up: self.send(part, False, b, pc.blk(pc.c1 + 1, pc.c2, pc.c3), (pc.c1 >= s) & (pc.c1 < pc.nz - 1))
            else: self.send(part, False, b, pc.blk(pc.c1 - 1, pc.c2, pc.c3), (pc.c1 < pc.nz - s) & (pc.c1 > 0))
        if more:
            for j in pc.o2(): self.send(part, False, b, pc.blk(pc.c1, j, pc.c3), cond)
            for j in pc.o3(): self.send(part, False, b, pc.blk(pc.c1, pc.c2, j), cond)
    def events(self):
        pc = self.pc; ev = []
        def a2(s):
            def go():
                for j in pc.o2():
                    for sg in ((1, -1) if s else (1,)):
                        a = pc.c1 + sg * s
                        cond = None if s == 0 else ((a >= 0) & (a < pc.nz))
                        b = pc.blk(a, j, pc.c3)
                        if cond is None: self.wait(0, b)
                        else: pl.when(cond)(lambda b=b: self.wait(0, b))
                        for k in pc.o3(): self.send(0, False, b, pc.blk(pc.c1, pc.c2, k), cond)
            return go
        def az(s):
            def go():
                self.zarr(0, s, True, pc.c2, pc.c3, True); self.zarr(0, s, False, pc.c2, pc.c3, True)
            return go
        B = self.split < self.src.shape[0]
        def f1():
            for j in pc.o2():
                b = pc.blk(pc.c1, j, pc.c3); self.wait(1, b); self.to3(1, False, b); self.updown(1, False, b)
        def f2():
            for k in pc.o3():
                b = pc.blk(pc.c1, pc.c2, k); self.wait(1, b); self.updown(1, False, b)
        def f3():
            for j in pc.o2():
                for k in pc.o3():
                    b = pc.blk(pc.c1, j, k); self.wait(1, b); self.updown(1, False, b)
        def fz(s):
            def go():
                for k2 in range(pc.m):
                    for k3 in range(pc.m):
                        self.zarr(1, s, True, k2, k3, False); self.zarr(1, s, False, k2, k3, False)
            return go
        ev += [az(1), a2(0)]
        if B: ev += [f1, f2, f3]
        ev += [az(2), a2(1)]
        if B: ev += [fz(1)]
        ev += [az(3), a2(2)]
        if B: ev += [fz(2)]
        ev += [a2(3)]
        if B: ev += [fz(3)]
        def last():
            for a in range(pc.nz):
                for j in range(pc.m):
                    for k in pc.o3(): self.wait(0, pc.blk(a, j, k))
        ev += [last]
        return ev
    def finish(self):
        for cond, cp in self.sends:
            if cond is None: cp.wait_send()
            else: pl.when(cond)(cp.wait_send)


class Lines:
    def __init__(self, pc, src, dst, ssem, rsem):
        self.pc, self.src, self.dst, self.ssem, self.rsem = pc, src, dst, ssem, rsem
        self.places = [(0, way, 0) for way in (1, -1)] + [(0, 0, j) for j in range(1, pc.m)]
        for s in range(1, pc.nz):
            for way in (1, -1):
                self.places += [(s, way, j) for j in range(0 if s < pc.nz - 1 else 1, pc.m)]

    def send(self, place):
        pc = self.pc
        s, way, j = place
        a = pc.c1 - way * s
        b = pc.block(a, pc.y)
        on = pc.c1 + way
        to = pc.chip(on, pc.y, pc.x) if j == 0 else pc.chip(pc.c1, (pc.y + j) % pc.m, pc.x)
        cond = (a >= 0) & (a < pc.nz)
        if j == 0:
            cond = cond & (on >= 0) & (on < pc.nz)
        copy = pltpu.make_async_remote_copy(
            src_ref=self.src if s == 0 else self.dst.at[b], dst_ref=self.dst.at[b],
            send_sem=self.ssem.at[self.places.index(place)], recv_sem=self.rsem.at[b],
            device_id=(to, pc.c), device_id_type=MESH,
        )
        return cond, copy

    def wait(self, b):
        pc = self.pc
        pltpu.make_async_remote_copy(
            src_ref=self.dst.at[b], dst_ref=self.dst.at[b], send_sem=self.ssem.at[0], recv_sem=self.rsem.at[b],
            device_id=(pc.chip(pc.c1, (pc.y + 1) % pc.m, pc.x), pc.c), device_id_type=MESH,
        ).wait_recv()

    def pass_on(self, s):
        for place in self.places:
            if place[0] == s:
                cond, copy = self.send(place)
                pl.when(cond)(copy.start)

    def start(self):
        self.pass_on(0)

    def line(self, s):
        self.wait_line(s)
        self.pass_on(s)

    def wait_line(self, s):
        pc = self.pc
        for way in (1, -1):
            a = pc.c1 - way * s
            pl.when((a >= 0) & (a < pc.nz))(functools.partial(self.wait, pc.block(a, pc.y)))

    def wait_far(self):
        pc = self.pc
        for a in range(pc.nz):
            for j in range(1, pc.m):
                self.wait(pc.block(a, (pc.y + j) % pc.m))

    def finish(self, distances):
        for place in self.places:
            if place[0] in distances:
                cond, copy = self.send(place)
                pl.when(cond)(copy.wait_send)


def run_staggered(first, second, lag):
    for i in range(max(len(first), len(second) + lag)):
        if i < len(first):
            first[i]()
        if lag <= i < len(second) + lag:
            second[i - lag]()


def part_rows(rows):
    return rows - rows // 80 * 16


def front_kernel(
    n,
    x_ref, cot_ref, gain1, gain2, cos_ref, sin_ref, len_ref, logit_ref, route_ref,
    wq, wk, wv, wo, rg, ru, rd, sg, su, sd,
    all_dy, h_all, fq, fk, fv, fo, fg, fu, fd, pg, pu, pd,
    x1_ref, q_ref, k_ref, v_ref, o_ref, p_ref, gates_in, cnt_ref, base_ref, dus_ref, shared_ref,
    wbuf, h_ref, rows_out, turn_ref, shw, act, dg, dup, give, take,
    gs, gr, hs, hr, ls, ws, wr, wl, es, er, gss, grs, ps, pr, qs, qr, us, ur, ul, xs, xr,
):
    pc = Place(n)
    e, c = pc.e, pc.c
    rows, width = x_ref.shape
    half = width // 2
    pc.greet_all()
    x, y, m = pc.x, pc.y, pc.m
    me = pc.block(pc.c1, y)
    gather_dy = Lines(pc, cot_ref, all_dy, gs, gr)
    gather_h = Lines(pc, h_ref, h_all, hs, hr)
    own_dy = pltpu.make_async_copy(cot_ref, all_dy.at[me], ls.at[0])
    own_h = pltpu.make_async_copy(h_ref, h_all.at[me], ls.at[1])
    own_dy.start()
    partner = (e, 1 - c)
    halves = (wq, wk, wv, wo)
    fulls = (fq, fk, fv, fo)

    def swap(i):
        return pltpu.make_async_remote_copy(
            src_ref=halves[i], dst_ref=wbuf.at[i, c], send_sem=ws.at[i], recv_sem=wr.at[i],
            device_id=partner, device_id_type=MESH,
        )

    def own(i):
        return pltpu.make_async_copy(halves[i], wbuf.at[i, c], wl.at[0, i])

    def keep(i):
        return pltpu.make_async_copy(wbuf.at[i], fulls[i], wl.at[1, i])

    experts_other = (fg, fu, fd)

    def expert_swap(i, src):
        return pltpu.make_async_remote_copy(
            src_ref=src, dst_ref=experts_other[i], send_sem=es.at[i], recv_sem=er.at[i],
            device_id=partner, device_id_type=MESH,
        )

    beside = (pg, pu, pd)

    def half_send(i, j, src):
        return pltpu.make_async_remote_copy(
            src_ref=src, dst_ref=beside[i].at[m - j - 1, c], send_sem=ps.at[i, j - 1], recv_sem=pr.at[i, m - j - 1],
            device_id=(pc.chip(pc.c1, y, (x + j) % m), c), device_id_type=MESH,
        )

    def half_on(i, k):
        return pltpu.make_async_remote_copy(
            src_ref=beside[i].at[k, c], dst_ref=beside[i].at[k, c], send_sem=qs.at[i, k], recv_sem=qr.at[i, k],
            device_id=partner, device_id_type=MESH,
        )

    for i in range(4):
        swap(i).start()
        own(i).start()
    shared_halves = (sg, su, sd)

    def shared_swap(i):
        return pltpu.make_async_remote_copy(
            src_ref=shared_halves[i], dst_ref=shw.at[i, c], send_sem=us.at[i], recv_sem=ur.at[i],
            device_id=partner, device_id_type=MESH,
        )

    def shared_own(i):
        return pltpu.make_async_copy(shared_halves[i], shw.at[i, c], ul.at[i])

    for i, routed in enumerate((rg, ru, rd)):
        for j in range(1, m):
            half_send(i, j, routed).start()
    gather_dy.start()
    for i, routed in enumerate((rg, ru, rd)):
        expert_swap(i, routed).start()
        shared_swap(i).start()
        shared_own(i).start()

    lane = lax.broadcasted_iota(jnp.int32, (rows, 128), 1)
    row = lax.broadcasted_iota(jnp.int32, (rows, 128), 0)
    valid = (row < len_ref[0]).astype(jnp.float32)
    soft, routes = route_columns(logit_ref, route_ref, turn_ref)
    dense = jnp.zeros((rows, 128), jnp.float32)
    named = jnp.zeros((rows, 128), jnp.float32)
    for i in range(route_ref.shape[0]):
        hit = lane == routes[:, i : i + 1]
        dense = dense + jnp.where(hit, soft[:, i : i + 1], 0.0)
        named = named + jnp.where(hit, 1.0, 0.0)
    dense = dense * valid
    cnt_ref[...] = jnp.zeros_like(cnt_ref)
    cnt_ref[:, 0:128] = jnp.sum(named * valid, axis=0, keepdims=True)
    turned = dense.T
    for i in range(n):
        rows_out[i] = turned[i : i + 1, :]
    for i in range(m):
        gates_in[me * m + i] = rows_out[me * m + i]

    def gate_send(a, b2):
        return pltpu.make_async_remote_copy(
            src_ref=rows_out.at[pl.ds(pc.block(a, b2) * m, m)], dst_ref=gates_in.at[pl.ds(me * m, m)],
            send_sem=gss.at[a, b2], recv_sem=grs.at[pc.c1, y],
            device_id=(pc.chip(a, b2, x), c), device_id_type=MESH,
        )

    def gate_wait(a, b2):
        at = pl.ds(pc.block(a, b2) * m, m)
        pltpu.make_async_remote_copy(
            src_ref=rows_out.at[at], dst_ref=gates_in.at[at], send_sem=gss.at[a, b2], recv_sem=grs.at[a, b2],
            device_id=(pc.chip(a, b2, x), c), device_id_type=MESH,
        ).wait_recv()

    for a, b2 in pc.others():
        gate_send(a, b2).start()

    xv = x_ref[...].astype(jnp.float32)
    a = (xv * lax.rsqrt(jnp.mean(xv * xv, axis=-1, keepdims=True) + norm_eps) * gain1[...]).astype(jnp.bfloat16)
    cosine, sine = cos_ref[...], sin_ref[...]

    def project(values, i):
        own(i).wait()
        swap(i).wait_recv()
        keep(i).start()
        return matmul(values[:, :half], wbuf[i, 0]) + matmul(values[:, half:], wbuf[i, 1])

    for i, ref in ((0, q_ref), (1, k_ref)):
        flat = project(a, i)
        for hd in range(HEADS):
            part = flat[:, hd * HD : (hd + 1) * HD]
            ref[:, hd * HD : (hd + 1) * HD] = (part * cosine + swap_halves(part) * sine).astype(jnp.bfloat16)
    v_ref[...] = project(a, 2).astype(jnp.bfloat16)
    gather_dy.line(1)
    scale = HD ** (-0.5)
    row_pos = lax.broadcasted_iota(jnp.int32, (rows, rows), 0)
    col_pos = lax.broadcasted_iota(jnp.int32, (rows, rows), 1)
    allowed = (col_pos <= row_pos) & (col_pos < len_ref[0])

    def one_head(hd, carry):
        at = pl.ds(pl.multiple_of(hd * HD, HD), HD)
        scores = jnp.where(allowed, inner_cols(q_ref[:, at], k_ref[:, at]) * scale, -1e30)
        up = jnp.exp(scores - jnp.max(scores, axis=-1, keepdims=True))
        prob = up / jnp.sum(up, axis=-1, keepdims=True)
        p_ref[hd] = prob
        o_ref[:, at] = matmul(prob.astype(jnp.bfloat16), v_ref[:, at]).astype(jnp.bfloat16)
        return carry

    lax.fori_loop(0, HEADS, one_head, 0)
    gather_dy.line(2)
    x1 = xv + project(o_ref[...], 3)
    x1_ref[...] = x1
    h_ref[...] = (x1 * lax.rsqrt(jnp.mean(x1 * x1, axis=-1, keepdims=True) + norm_eps) * gain2[...]).astype(jnp.bfloat16)
    gather_h.start()
    own_h.start()
    for i in range(3, pc.nz):
        gather_dy.line(i)

    for i in range(3):
        shared_own(i).wait()
        shared_swap(i).wait_recv()
    wg, wu, wd = (shw.at[i] for i in range(3))
    h, z = h_ref[...], cot_ref[...]
    for half in range(2):
        g = inner_cols(h, wg[half])
        u = inner_cols(h, wu[half])
        da = inner_cols(z, wd[half])
        sig = jax.nn.sigmoid(g)
        si = g * sig
        act[half] = (si * u).astype(jnp.bfloat16)
        dup[half] = (da * si).astype(jnp.bfloat16)
        dg[half] = (da * u * sig * (1.0 + g * (1.0 - sig))).astype(jnp.bfloat16)

    def grad_swap(i):
        return pltpu.make_async_remote_copy(
            src_ref=give.at[i], dst_ref=take.at[i], send_sem=xs.at[i], recv_sem=xr.at[i],
            device_id=partner, device_id_type=MESH,
        )

    sides = ((dg, h), (dup, h), (act, z))
    for i, (left, right) in enumerate(sides):
        give[i] = outer_rows(left[1 - c], right).astype(jnp.bfloat16)
        grad_swap(i).start()
    base_ref[...] = x1_ref[...] + matmul(act[0], wd[0]) + matmul(act[1], wd[1])
    dus_ref[...] = matmul(dg[0], wg[0]) + matmul(dg[1], wg[1]) + matmul(dup[0], wu[0]) + matmul(dup[1], wu[1])
    hidden = give.shape[1]
    shared_ref[pl.ds(3 * hidden, shared_ref.shape[0] - 3 * hidden)] = jnp.zeros(
        (shared_ref.shape[0] - 3 * hidden, width), jnp.bfloat16
    )
    for i, (left, right) in enumerate(sides):
        part = outer_rows(left[c], right)
        grad_swap(i).wait()
        shared_ref[pl.ds(i * hidden, hidden)] = (part + take[i].astype(jnp.float32)).astype(jnp.bfloat16)
    for k in range(m - 1):
        for i in range(3):
            half_send(i, m - k - 1, sd).wait_recv()
            half_on(i, k).start()
    gather_dy.wait_far()
    for a, b2 in pc.others():
        gate_wait(a, b2)
        gate_send(a, b2).wait_send()
    gather_h.wait_line(1)
    for j in range(1, m):
        gather_h.wait(pc.block(pc.c1, (y + j) % m))
    gather_dy.finish(range(pc.nz))
    gather_h.finish((0,))
    own_dy.wait()
    own_h.wait()
    for i in range(4):
        swap(i).wait_send()
        keep(i).wait()
    for i, shared in enumerate((sg, su, sd)):
        expert_swap(i, shared).wait()
        shared_swap(i).wait_send()
        for k in range(m - 1):
            half_send(i, k + 1, shared).wait_send()
            half_on(i, k).wait_send()
            other = pltpu.make_async_remote_copy(
                src_ref=beside[i].at[k, 1 - c], dst_ref=beside[i].at[k, 1 - c], send_sem=qs.at[i, k], recv_sem=qr.at[i, k],
                device_id=partner, device_id_type=MESH,
            )
            other.wait_recv()


def front(n, x, cot, gain1, gain2, cosine, sine, length, logits, routes, attn_w, routed_w, shared_w):
    rows, width = x.shape
    hidden = shared_w[0].shape[0]
    vmem = pl.BlockSpec(memory_space=pltpu.VMEM)
    hbm = pl.BlockSpec(memory_space=pl.ANY)
    f32, b16 = jnp.float32, jnp.bfloat16
    out = jax.ShapeDtypeStruct
    dma = pltpu.SemaphoreType.DMA
    wide = out((rows, width), b16)
    full = out((2, width // 2, width), b16)
    nz = 4
    m = {16: 2, 64: 4}[n]
    beside = out((m - 1, 2, hidden, width), b16)
    narrow = pltpu.VMEM((2, rows, hidden), b16)
    three = pltpu.VMEM((3, hidden, width), b16)
    return pl.pallas_call(
        functools.partial(front_kernel, n),
        out_shape=(
            out((nz * m, rows, width), b16), out((nz * m, rows, width), b16), full, full, full, full,
            out((hidden, width), b16), out((hidden, width), b16), out((hidden, width), b16), beside, beside, beside,
            out((rows, width), f32), wide, wide, wide, wide, out((HEADS, rows, rows), f32),
            out((n, 1, rows), f32), out((1, width), f32),
            out((rows, width), f32), out((rows, width), f32), out((n * blocked(3 * hidden, n), width), b16),
        ),
        in_specs=[vmem] * 6 + [pl.BlockSpec(memory_space=pltpu.SMEM)] + [vmem] * 2 + [hbm] * 10,
        out_specs=(hbm,) * 12 + (vmem,) * 11,
        scratch_shapes=[
            pltpu.VMEM((4, 2, width // 2, width), b16), pltpu.VMEM((rows, width), b16), pltpu.VMEM((n, 1, rows), f32), pltpu.VMEM((128, rows), f32),
            pltpu.VMEM((3, 2, hidden, width), b16), narrow, narrow, narrow, three, three,
            dma((64,)), dma((nz * m,)), dma((64,)), dma((nz * m,)), dma((2,)), dma((4,)), dma((4,)), dma((2, 4)), dma((3,)), dma((3,)),
            dma((nz, m)), dma((nz, m)), dma((3, m - 1)), dma((3, m - 1)), dma((3, m - 1)), dma((3, m - 1)),
            dma((3,)), dma((3,)), dma((3,)), dma((3,)), dma((3,)),
        ],
        compiler_params=pltpu.CompilerParams(collective_id=0, has_side_effects=True, vmem_limit_bytes=56 * 2**20),
    )(x, cot, gain1, gain2, cosine, sine, length, logits, routes, *attn_w, *routed_w, *shared_w)


def experts_kernel(
    n, slots,
    h_in, dy_hbm, gates_in, rg, ru, rd, xg, xu, xd, pg, pu, pd, shared_hbm,
    scores_in, du_hbm, tg_hbm, tu_hbm, td_hbm, sum_hbm, y_hbm, far_hbm, h_all, part_hbm, xt_hbm, r3_hbm, r1_hbm,
    wbuf, og, ou, od, total_ref, hbuf, dbuf, act, dg, dup, stage, pbuf, rbuf, give, take, keep,
    gate_ref, s_ref, turn_ref, rows_out,
    gs, gr, lsem, ssem, r3sem, r1sem, bsem, wsem, partsem, pbsem, ysem,
    xssem, xrsem, gsend, grecv, osem, psem, scs, scr, room, vs, va, vb, vc,
):
    pc = Place(n)
    nz, m = pc.nz, pc.m
    c1, e, c, x, y = pc.c1, pc.e, pc.c, pc.x, pc.y
    blocks = nz * m
    me = pc.block(c1, y)
    toward = 1 - 2 * (c1 // (nz // 2))
    together = nz - 1
    grads = (og, ou, od)
    own_half = (rg, ru, rd)
    other_half = (xg, xu, xd)
    shared_half = (pg, pu, pd)

    def weight(p, i, half, src):
        return pltpu.make_async_copy(src, wbuf.at[p % 2, i, half], wsem.at[p % 2, i, half])

    def weights_start(p):
        for i in range(3):
            if p < m - 1:
                for half in range(2):
                    weight(p, i, half, shared_half[i].at[p, half]).start()
            else:
                weight(p, i, c, own_half[i]).start()
                weight(p, i, 1 - c, other_half[i]).start()

    weights_start(0)
    weights_start(1)
    hidden = give.shape[1]
    part_rows = keep.shape[0] // n
    fetch_shared = pltpu.make_async_copy(shared_hbm, keep, psem.at[0])
    fetch_shared.start()
    first_h = pltpu.make_async_copy(h_all.at[me], hbuf.at[0], lsem.at[0, 0])
    first_dy = pltpu.make_async_copy(dy_hbm.at[me], dbuf.at[0], lsem.at[1, 0])
    first_h.start()
    first_dy.start()
    pc.greet_all()
    gather = Lines(pc, None, h_all, gs, gr)
    gather.pass_on(1)

    def rows_of(ref, i):
        return ref.at[pl.ds(pl.multiple_of(i * part_rows, 16), part_rows)]

    from_b = (m - 1) * m * nz
    from_c = from_b + (nz - 1) * m
    shared_sum = Scatter(
        pc, ((m, x, 1), (nz, c1, m * m), (m, y, m)), functools.partial(rows_of, keep),
        lambda i, c_at, b_at: rows_of(take, (i * m + c_at) * nz + b_at),
        lambda i, c_at: rows_of(take, from_b + i * m + c_at),
        lambda i: rows_of(take, from_c + i), (vs, va, vb, vc),
    )
    fetch_shared.wait()
    shared_sum.start_plane(0)
    shared_steps = shared_sum.steps()
    sum_store = pltpu.make_async_copy(rows_of(keep, e), sum_hbm, psem.at[0])

    def shared_done():
        sum_store.start()
        shared_sum.finish()
        pl.semaphore_signal(room, inc=1, device_id=(e, 1 - c), device_id_type=MESH)
        sum_store.wait()

    shared_steps = shared_steps + [shared_done]

    def third(ref, i):
        return ref.at[pl.ds(i * hidden, hidden)]
    turn_ref[...] = jnp.zeros_like(turn_ref)
    for i in range(n):
        turn_ref[i : i + 1, :] = gates_in[i]
    gate_ref[...] = turn_ref[...].T
    for total in grads:
        total[...] = jnp.zeros_like(total)
    s_ref[...] = jnp.zeros_like(s_ref)

    def dest(step):
        p, t = step // blocks, step % blocks
        last = (p + 1) // m
        return (c1 + toward * (t // m + last) + nz) % nz, (y + t % m + last) % m

    def load(step, i):
        b = pc.block(*dest(step))
        return (
            pltpu.make_async_copy(h_all.at[b], hbuf.at[i], lsem.at[0, i]),
            pltpu.make_async_copy(dy_hbm.at[b], dbuf.at[i], lsem.at[1, i]),
        )

    def part_load(step, i):
        return pltpu.make_async_copy(part_hbm.at[pc.block(*dest(step))], pbuf.at[i], pbsem.at[i])

    def part_store(slot, b):
        return pltpu.make_async_copy(stage.at[slot], part_hbm.at[b], partsem.at[slot])

    def y_store(slot, a, b2):
        return pltpu.make_async_copy(stage.at[slot, 0], y_hbm.at[a, b2], ysem.at[slot])

    def pair_send(slot, to, dst, sem):
        return pltpu.make_async_remote_copy(
            src_ref=stage.at[slot], dst_ref=dst, send_sem=ssem.at[slot], recv_sem=sem,
            device_id=(to, c), device_id_type=MESH,
        )

    def du_send(slot, to, dst, sem):
        return pltpu.make_async_remote_copy(
            src_ref=stage.at[slot, 1], dst_ref=dst, send_sem=ssem.at[slot], recv_sem=sem,
            device_id=(to, c), device_id_type=MESH,
        )

    def collect(slot, received):
        def fetch(i):
            return pltpu.make_async_copy(received[i][0], rbuf.at[i % 2], bsem.at[i % 2])

        def begin(i):
            src, sem, landed = received[i]
            pltpu.make_async_remote_copy(
                src_ref=landed, dst_ref=landed, send_sem=ssem.at[slot], recv_sem=sem,
                device_id=(e, 1 - c), device_id_type=MESH,
            ).wait_recv()
            fetch(i).start()

        begin(0)
        total_ref[...] = stage[slot, 1].astype(jnp.float32)
        for i in range(len(received)):
            if i + 1 < len(received):
                begin(i + 1)
            fetch(i).wait()
            total_ref[...] += rbuf[i % 2].astype(jnp.float32)

    def from_y(a, whole):
        if whole:
            return [(far_hbm.at[j, a, 1], r3sem.at[j, a], far_hbm.at[j, a]) for j in range(m - 1)]
        return [(r3_hbm.at[j, a], r3sem.at[j, a], r3_hbm.at[j, a]) for j in range(m - 1)]

    def from_z():
        return [(r1_hbm.at[(c1 + j) % nz], r1sem.at[(c1 + j) % nz], r1_hbm.at[(c1 + j) % nz]) for j in range(1, nz)]

    def swaps():
        return [
            pltpu.make_async_remote_copy(
                src_ref=give.at[i], dst_ref=third(take, i), send_sem=xssem.at[i], recv_sem=xrsem.at[i],
                device_id=(e, 1 - c), device_id_type=MESH,
            )
            for i in range(3)
        ]

    def grad_send(p):
        return pltpu.make_async_remote_copy(
            src_ref=keep.at[pl.ds(0, 3 * hidden)], dst_ref=xt_hbm.at[x], send_sem=gsend, recv_sem=grecv.at[x],
            device_id=(pc.chip(c1, y, (x + p + 1) % m), c), device_id_type=MESH,
        )

    def totals():
        return [
            pltpu.make_async_copy(src.at[c], dst, osem.at[i])
            for i, (src, dst) in enumerate(((og, tg_hbm), (ou, tu_hbm), (od, td_hbm)))
        ]

    first_h.wait()
    first_dy.wait()

    def body(step, carry):
        i = step % 2
        slot = step % slots
        p, t = step // blocks, step % blocks
        last = (p + 1) // m
        a, b2 = dest(step)
        b = pc.block(a, b2)
        column = b * m + (x + p + 1) % m
        for at in range(m):
            @pl.when(step == at * blocks)
            def _():
                for k in range(3):
                    for half in range(2):
                        weight(at, k, half, other_half[k]).wait()
                if at >= 1 and at + 1 < m:
                    weights_start(at + 1)

        @pl.when(step > 0)
        def _():
            for copy in load(step, i):
                copy.wait()

        wg, wu, wd = (wbuf.at[p % 2, k] for k in range(3))
        lane = lax.broadcasted_iota(jnp.int32, gate_ref.shape, 1)
        gate = jnp.sum(jnp.where(lane == column, gate_ref[...], 0.0), axis=1, keepdims=True)
        h = hbuf[i]
        dy = dbuf[i].astype(jnp.float32)
        z = (gate * dy).astype(jnp.bfloat16)
        for half in range(2):
            g = inner_cols(h, wg[half])
            u = inner_cols(h, wu[half])
            da = inner_cols(z, wd[half])
            sg = jax.nn.sigmoid(g)
            si = g * sg
            act[half] = (si * u).astype(jnp.bfloat16)
            dup[half] = (da * si).astype(jnp.bfloat16)
            dg[half] = (da * u * sg * (1.0 + g * (1.0 - sg))).astype(jnp.bfloat16)

        before = step - slots
        before_last = ((before + slots * blocks) // blocks - slots + 1) // m

        @pl.when((before >= 0) & (before_last < 1))
        def _():
            part_store(slot, b).wait()

        before_t = (before + slots * blocks) % blocks

        @pl.when((before >= 0) & (before_last >= 1) & (before_t < together * m) & (before_t % m < m - 1))
        def _():
            pair_send(slot, e, far_hbm.at[0, 0], r3sem.at[0, 0]).wait_send()

        @pl.when((before >= 0) & (before_last >= 1) & ((before_t >= together * m) | (before_t % m == m - 1)))
        def _():
            y_store(slot, a, b2).wait()
            du_send(slot, e, r1_hbm.at[0], r1sem.at[0]).wait_send()

        yv = (matmul(act[0], wd[0]) + matmul(act[1], wd[1])).astype(jnp.bfloat16).astype(jnp.float32)
        s = jnp.sum(yv * dy, axis=1, keepdims=True)
        s_ref[...] = jnp.where(lane == column, s, s_ref[...])
        yv = gate * yv
        du = (
            matmul(dg[0], wg[0]) + matmul(dg[1], wg[1]) + matmul(dup[0], wu[0]) + matmul(dup[1], wu[1])
        ).astype(jnp.bfloat16)

        @pl.when(p == 0)
        def _():
            stage[slot, 0] = yv.astype(jnp.bfloat16)
            stage[slot, 1] = du

        @pl.when(p > 0)
        def _():
            part_load(step, i).wait()
            stage[slot, 0] = (yv + pbuf[i, 0].astype(jnp.float32)).astype(jnp.bfloat16)
            stage[slot, 1] = (du.astype(jnp.float32) + pbuf[i, 1].astype(jnp.float32)).astype(jnp.bfloat16)

        @pl.when(last == 0)
        def _():
            part_store(slot, b).start()

        @pl.when((last == 1) & ((t >= together * m) | (t % m == m - 1)))
        def _():
            y_store(slot, a, b2).start()

        for j in range(1, m):
            @pl.when((last == 1) & (t < together * m) & (b2 == (y + j) % m))
            def _():
                pair_send(slot, pc.chip(c1, b2, x), far_hbm.at[m - j - 1, a], r3sem.at[m - j - 1, a]).start()

            @pl.when((last == 1) & (t >= together * m) & (b2 == (y + j) % m))
            def _():
                du_send(slot, pc.chip(c1, b2, x), r3_hbm.at[m - j - 1, a], r3sem.at[m - j - 1, a]).start()

        for k in range(2, nz):
            pl.when(step == (k - 1) * m - 1)(functools.partial(gather.line, k))

        @pl.when(step < m * blocks - 1)
        def _():
            after = step + 1
            next_a, next_b = dest(after)

            @pl.when((after < blocks) & (next_b != y) & (next_a != c1))
            def _():
                gather.wait(pc.block(next_a, next_b))

            for copy in load(after, 1 - i):
                copy.start()

            @pl.when(after >= blocks)
            def _():
                part_load(after, 1 - i).start()

        for half in range(2):
            og[half] += outer_rows(dg[half], h)
            ou[half] += outer_rows(dup[half], h)
            od[half] += outer_rows(act[half], z)

        for k in range(1, m):
            pl.when(step == k - 1)(functools.partial(shared_sum.start_plane, k))
        spread = [(1 + i, i) for i in range(2 * m - 1)] + [(blocks - 2, 2 * m - 1), (blocks - 1, 2 * m)]
        for at, k in spread:
            pl.when(step == at)(shared_steps[k])

        for at in range(m - 1):
            @pl.when(step == (at + 1) * blocks - 1)
            def _():
                if at >= 1:
                    grad_send(at - 1).wait_send()
                for k, total in enumerate(grads):
                    give[k] = total[1 - c].astype(jnp.bfloat16)
                    third(keep, k)[...] = total[c].astype(jnp.bfloat16)
                    total[...] = jnp.zeros_like(total)
                pl.semaphore_wait(room, 1)
                for copy in swaps():
                    copy.start()

            @pl.when(step == (at + 1) * blocks)
            def _():
                for copy in swaps():
                    copy.wait()
                for k in range(3):
                    third(keep, k)[...] = (
                        third(keep, k)[...].astype(jnp.float32) + third(take, k)[...].astype(jnp.float32)
                    ).astype(jnp.bfloat16)
                pl.semaphore_signal(room, inc=1, device_id=(e, 1 - c), device_id_type=MESH)
                grad_send(at).start()

        for k in range(1, nz):
            @pl.when((last == 1) & (t == k * m))
            def _():
                at = (step - 1) % slots
                a1 = (c1 + toward * k + nz) % nz
                collect(at, from_y(a1, k - 1 < together))
                stage[at, 1] = total_ref[...].astype(jnp.bfloat16)
                du_send(at, pc.chip(a1, y, x), r1_hbm.at[c1], r1sem.at[c1]).start()

        return carry

    lax.fori_loop(0, m * blocks, body, 0)
    for i, total in enumerate(grads):
        give[i] = total[1 - c].astype(jnp.bfloat16)
    pl.semaphore_wait(room, 1)
    for copy in swaps():
        copy.start()
    turned = s_ref[...].T
    for i in range(n):
        rows_out[i] = turned[i : i + 1, :]
    for i in range(m):
        scores_in[me * m + i] = rows_out[me * m + i]

    def score_send(a, b2):
        return pltpu.make_async_remote_copy(
            src_ref=rows_out.at[pl.ds(pc.block(a, b2) * m, m)], dst_ref=scores_in.at[pl.ds(me * m, m)],
            send_sem=scs.at[a, b2], recv_sem=scr.at[c1, y],
            device_id=(pc.chip(a, b2, x), c), device_id_type=MESH,
        )

    def score_wait(a, b2):
        at = pl.ds(pc.block(a, b2) * m, m)
        pltpu.make_async_remote_copy(
            src_ref=rows_out.at[at], dst_ref=scores_in.at[at], send_sem=scs.at[a, b2], recv_sem=scr.at[a, b2],
            device_id=(pc.chip(a, b2, x), c), device_id_type=MESH,
        ).wait_recv()

    for a, b2 in pc.others():
        score_send(a, b2).start()
    for copy in swaps():
        copy.wait()
    for i, total in enumerate(grads):
        total[c] += third(take, i)[...].astype(jnp.float32)
    grad_send(m - 2).wait_send()
    for j in range(1, m):
        at = (x + j) % m
        pltpu.make_async_remote_copy(
            src_ref=xt_hbm.at[at], dst_ref=xt_hbm.at[at], send_sem=gsend, recv_sem=grecv.at[at],
            device_id=(pc.chip(c1, y, at), c), device_id_type=MESH,
        ).wait_recv()
        back = pltpu.make_async_copy(xt_hbm.at[at], take.at[pl.ds(0, 3 * hidden)], bsem.at[0])
        back.start()
        back.wait()
        for i, total in enumerate(grads):
            total[c] += third(take, i)[...].astype(jnp.float32)
    for copy in totals():
        copy.start()
    collect((m * blocks - 1) % slots, from_y(c1, nz - 1 < together) + from_z())
    final = pltpu.make_async_copy(total_ref, du_hbm, bsem.at[0])
    final.start()
    final.wait()
    for step in range(m * blocks - slots, m * blocks):
        t = step % blocks
        if t < together * m and t % m < m - 1:
            pair_send(step % slots, e, far_hbm.at[0, 0], r3sem.at[0, 0]).wait_send()
            continue
        y_store(step % slots, c1, y).wait()
        if step < m * blocks - 1:
            du_send(step % slots, e, r1_hbm.at[0], r1sem.at[0]).wait_send()
    for a, b2 in pc.others():
        score_wait(a, b2)
        score_send(a, b2).wait_send()
    gather.finish(range(1, nz))
    for copy in totals():
        copy.wait()


def experts(h, dy, gates, routed_w, other_w, partner_w, shared):
    blocks, rows, width = dy.shape
    n = gates.shape[0]
    hidden = routed_w[0].shape[0]
    nz = 4
    m = {16: 2, 64: 4}[n]
    slots = 4
    vmem = pl.BlockSpec(memory_space=pltpu.VMEM)
    hbm = pl.BlockSpec(memory_space=pl.ANY)
    f32, b16 = jnp.float32, jnp.bfloat16
    out = jax.ShapeDtypeStruct
    dma = pltpu.SemaphoreType.DMA
    grad = pltpu.VMEM((2, hidden, width), f32)
    pair = pltpu.VMEM((2, rows, width), b16)
    narrow = pltpu.VMEM((2, rows, hidden), b16)
    three = pltpu.VMEM((3, hidden, width), b16)
    return pl.pallas_call(
        functools.partial(experts_kernel, n, slots),
        out_shape=(
            out((n, 1, rows), f32), out((rows, width), f32),
            out((hidden, width), f32), out((hidden, width), f32), out((hidden, width), f32),
            out((shared.shape[0] // n, width), b16), out((nz, m, rows, width), b16), out((m - 1, nz, 2, rows, width), b16),
            out((blocks, rows, width), b16), out((blocks, 2, rows, width), b16), out((m, 3 * hidden, width), b16),
            out((m - 1, nz, rows, width), b16), out((nz, rows, width), b16),
        ),
        in_specs=[hbm, hbm, vmem] + [hbm] * 10,
        out_specs=(vmem,) + (hbm,) * 12,
        input_output_aliases={0: 8},
        scratch_shapes=[
            pltpu.VMEM((2, 3, 2, hidden, width), b16), grad, grad, grad,
            pltpu.VMEM((rows, width), f32), pair, pair, narrow, narrow, narrow,
            pltpu.VMEM((slots, 2, rows, width), b16), pltpu.VMEM((2, 2, rows, width), b16), pair, three,
            pltpu.VMEM((max(3 * hidden, shared.shape[0] // n * (n - 1)), width), b16), pltpu.VMEM(shared.shape, b16),
            pltpu.VMEM((rows, 128), f32), pltpu.VMEM((rows, 128), f32), pltpu.VMEM((128, rows), f32), pltpu.VMEM((n, 1, rows), f32),
            dma((64,)), dma((blocks,)), dma((2, 2)), dma((slots,)), dma((m - 1, nz)), dma((nz,)), dma((2,)),
            dma((2, 3, 2)), dma((slots,)), dma((2,)), dma((slots,)),
            dma((3,)), dma((3,)), dma, dma((m,)), dma((3,)), dma((3,)), dma((nz, m)), dma((nz, m)),
            pltpu.SemaphoreType.REGULAR, dma((n,)), dma((m - 1, m, nz)), dma((nz - 1, m)), dma((m - 1,)),
        ],
        compiler_params=pltpu.CompilerParams(collective_id=1, has_side_effects=True, vmem_limit_bytes=62 * 2**20),
    )(h, dy, gates, *routed_w, *other_w, *partner_w, shared)


def swap_halves(values):
    return pltpu.roll(values, HD // 2, axis=1)


def route_columns(logit_ref, route_ref, turn_ref):
    count = logit_ref.shape[0]
    logits = logit_ref[...]
    raised = jnp.exp(logits - jnp.max(logits, axis=0, keepdims=True))
    turn_ref[...] = jnp.zeros_like(turn_ref)
    turn_ref[0:count, :] = raised / jnp.sum(raised, axis=0, keepdims=True)
    soft = turn_ref[...].T
    turn_ref[0:count, :] = route_ref[...].astype(jnp.float32)
    return soft, turn_ref[...].T.astype(jnp.int32)


class Scatter:
    def __init__(self, pc, axes, block, ra, rb, rc, sems):
        self.pc, self.block, self.ra, self.rb, self.rc = pc, block, ra, rb, rc
        (self.na, self.a, self.sa), (self.nb, self.b, self.sb), (self.nc, self.c, self.sc) = axes
        self.ssem, self.sema, self.semb, self.semc = sems

    def at(self, i, j, k):
        a, b, c = (self.a + i) % self.na, (self.b + j) % self.nb, (self.c + k) % self.nc
        return a * self.sa + b * self.sb + c * self.sc

    def copy(self, b, dst, sem, to):
        return pltpu.make_async_remote_copy(
            src_ref=self.block(b), dst_ref=dst, send_sem=self.ssem.at[b], recv_sem=sem,
            device_id=(to, self.pc.c), device_id_type=MESH,
        )

    def add(self, total, src, sem):
        self.copy(self.pc.e, src, sem, self.at(1, 0, 0)).wait_recv()
        return total + src[...].astype(jnp.float32)

    def place_b(self, j):
        return (self.b + j) % self.nb

    def place_c(self, k):
        return (self.c + k) % self.nc

    def start(self):
        for k in range(self.nc):
            self.start_plane(k)

    def start_plane(self, p):
        k = (p + 1) % self.nc
        for i in range(1, self.na):
            for j in list(range(1, self.nb)) + [0]:
                b, c = self.place_b(j), self.place_c(k)
                slot = self.na - i - 1
                self.copy(self.at(i, j, k), self.ra(slot, c, b), self.sema.at[slot, c, b], self.at(i, 0, 0)).start()

    def collect(self, j, k, level):
        block = self.block(self.at(0, j, k))
        b, c = self.place_b(j), self.place_c(k)
        total = block[...].astype(jnp.float32)
        for i in range(self.na - 1):
            total = self.add(total, self.ra(i, c, b), self.sema.at[i, c, b])
        if level >= 2:
            for i in range(self.nb - 1):
                total = self.add(total, self.rb(i, c), self.semb.at[i, c])
        if level >= 3:
            for i in range(self.nc - 1):
                total = self.add(total, self.rc(i), self.semc.at[i])
        block[...] = total.astype(jnp.bfloat16)

    def second(self, p):
        k = (p + 1) % self.nc
        for j in range(1, self.nb):
            self.collect(j, k, 1)
            slot = self.nb - j - 1
            self.copy(self.at(0, j, k), self.rb(slot, self.place_c(k)), self.semb.at[slot, self.place_c(k)], self.at(0, j, 0)).start()

    def third(self, p):
        k = p + 1
        self.collect(0, k, 2)
        slot = self.nc - k - 1
        self.copy(self.at(0, 0, k), self.rc(slot), self.semc.at[slot], self.at(0, 0, k)).start()

    def last(self):
        self.collect(0, 0, 3)

    def steps(self):
        found = [functools.partial(self.second, 0)]
        for p in range(1, self.nc):
            found += [functools.partial(self.second, p), functools.partial(self.third, p - 1)]
        return found + [self.last]

    def finish(self):
        n = self.pc.n

        def one(j, carry):
            to = (self.pc.e + j) % n
            self.copy(to, self.rc(0), self.semc.at[0], to).wait_send()
            return carry

        lax.fori_loop(1, n, one, 0)


def tail_kernel(
    n,
    x_ref, x1_ref, cot_ref, dh_ref, dus_hbm, base_hbm, own_ref, q_ref, k_ref, v_ref, o_ref, p_ref, wq, wk, wv, wo,
    gain1, gain2, cos_ref, sin_ref, cnt_ref, len_ref, logit_ref, route_ref, scores_in, y_hbm, far_hbm,
    out_ref, gtok_ref, glog_ref, small_ref, ag0, ag1, ags, y3_hbm, y1_hbm,
    dx_ref, dq_ref, dk_ref, dv_ref, a_ref, give, take, stack0, stack1, r3, r2, r1,
    sm_core, sm_d3, sm_d2, sm_z,
    wbuf, wsem, turn_ref, ybuf, ytmp,
    gs, gr, ss, s3, s2, s1, xs, xr, cs, cr, locs, yl, yt, ys3, ys1, y3s, y1s,
):
    pc = Place(n)
    c1, c2, c3, e, c, nz, m = pc.c1, pc.c2, pc.c3, pc.e, pc.c, pc.nz, pc.m
    rows, width = x_ref.shape
    half = width // 2
    pc.greet_all()

    x, y = pc.x, pc.y

    def y_far(a, j):
        return pltpu.make_async_remote_copy(
            src_ref=y_hbm.at[a, (y + j) % m], dst_ref=y3_hbm.at[m - j - 1, a], send_sem=ys3.at[j - 1, a], recv_sem=y3s.at[m - j - 1, a],
            device_id=(pc.chip(c1, (y + j) % m, x), c), device_id_type=MESH,
        )

    def y_along(a):
        return pltpu.make_async_remote_copy(
            src_ref=ybuf.at[a], dst_ref=y1_hbm.at[c1], send_sem=ys1.at[a], recv_sem=y1s.at[c1],
            device_id=(pc.chip(a, y, x), c), device_id_type=MESH,
        )

    toward = 1 - 2 * (c1 // (nz // 2))
    together = nz - 1

    def plane(i):
        return (c1 + toward * (i + 1) + nz) % nz

    for i in range(together, nz):
        for j in range(1, m):
            y_far(plane(i), j).start()
    y_own = [pltpu.make_async_copy(y_hbm.at[a, y], ybuf.at[a], yl.at[a]) for a in range(nz)]
    for copy in y_own:
        copy.start()

    def y_sum(a, received):
        def fetched(i):
            return pltpu.make_async_copy(received[i][0], ytmp.at[i % 2], yt.at[i % 2])

        def begin(i):
            src, sem = received[i]
            if sem is not None:
                pltpu.make_async_remote_copy(
                    src_ref=src, dst_ref=src, send_sem=ys1.at[0], recv_sem=sem, device_id=(e, 1 - c), device_id_type=MESH,
                ).wait_recv()
            fetched(i).start()

        begin(0)
        total = ybuf[a].astype(jnp.float32)
        for i in range(len(received)):
            if i + 1 < len(received):
                begin(i + 1)
            fetched(i).wait()
            total = total + ytmp[i % 2].astype(jnp.float32)
        return total

    def y_from3(i):
        a = plane(i)
        if i < together:
            return [(far_hbm.at[k, a, 0], None) for k in range(m - 1)]
        return [(y3_hbm.at[k, a], y3s.at[k, a]) for k in range(m - 1)]

    def y_third(i):
        a = plane(i)
        ybuf[a] = y_sum(a, y_from3(i)).astype(jnp.bfloat16)
        y_along(a).start()

    def y_last():
        along = [(y1_hbm.at[(c1 + j) % nz], y1s.at[(c1 + j) % nz]) for j in range(1, nz)]
        out_ref[...] = (dx_ref[...] + y_sum(c1, y_from3(nz - 1) + along)).astype(jnp.bfloat16)

    def y_finish():
        for i in range(nz - 1):
            y_along(plane(i)).wait_send()
        for i in range(together, nz):
            for j in range(1, m):
                y_far(plane(i), j).wait_send()

    gather_s = Gather(pc, own_ref, ags, gs.at[2], gr.at[2], own_ref.shape[0])
    loc_s = pltpu.make_async_copy(own_ref, ags.at[e], locs.at[2])
    gather_s.start()
    loc_s.start()
    shared_events = gather_s.events()

    def fetch(src, i):
        return pltpu.make_async_copy(src, wbuf.at[i], wsem.at[i])

    get_dus = pltpu.make_async_copy(dus_hbm, dx_ref, locs.at[0])
    get_dus.start()
    fetch(wo, 0).start()
    fetch(wv, 1).start()

    x1 = x1_ref[...]
    up = cot_ref[...].astype(jnp.float32)
    get_dus.wait()
    dh = dh_ref[...] + dx_ref[...]
    r_two = lax.rsqrt(jnp.mean(x1 * x1, axis=-1, keepdims=True) + norm_eps)
    n_two = x1 * r_two
    scaled = dh * gain2[...]
    grad_two = jnp.sum(dh * n_two, axis=0, keepdims=True)
    dx = up + r_two * (scaled - n_two * jnp.mean(scaled * n_two, axis=-1, keepdims=True))
    dx_ref[...] = dx
    dx_low = dx.astype(jnp.bfloat16)

    def columns(ref, which):
        return ref[:, pl.ds(pl.multiple_of(which * half, 128), half)]

    def hand(i):
        return pltpu.make_async_remote_copy(
            src_ref=give.at[i], dst_ref=take.at[i], send_sem=xs.at[i], recv_sem=xr.at[i],
            device_id=(e, 1 - c), device_id_type=MESH,
        )

    def to_partner(i, left, right):
        give[i] = outer_rows(columns(left, 1 - c), right).astype(jnp.bfloat16)
        hand(i).start()

    def own_part(i, left, right, stack, at):
        block = stack.shape[1]
        part = outer_rows(columns(left, c), right)
        hand(i).wait_recv()
        total = (part + take[i].astype(jnp.float32)).astype(jnp.bfloat16)
        stack[pl.ds(at * (half // block), half // block)] = total.reshape(half // block, block, width)

    to_partner(0, o_ref, dx_low)
    shared_events[0]()
    fetch(wo, 0).wait()
    dq_ref[...] = inner_cols(dx_low, wbuf[0]).astype(jnp.bfloat16)
    fetch(wk, 0).start()
    cosine, sine = cos_ref[...], sin_ref[...]
    scale = HD ** (-0.5)

    def one_head(hd, carry):
        at = pl.ds(pl.multiple_of(hd * HD, HD), HD)
        prob = p_ref[hd]
        d_o, val, que, key = dq_ref[:, at], v_ref[:, at], q_ref[:, at], k_ref[:, at]
        dv_ref[:, at] = outer_rows(prob.astype(jnp.bfloat16), d_o).astype(jnp.bfloat16)
        d_prob = inner_cols(d_o, val)
        inner = jnp.sum(prob * d_prob, axis=-1, keepdims=True)
        d_score = (prob * (d_prob - inner)).astype(jnp.bfloat16)
        d_q = matmul(d_score, key) * scale
        d_k = outer_rows(d_score, que) * scale
        dq_ref[:, at] = (d_q * cosine - swap_halves(d_q) * sine).astype(jnp.bfloat16)
        dk_ref[:, at] = (d_k * cosine - swap_halves(d_k) * sine).astype(jnp.bfloat16)
        return carry

    lax.fori_loop(0, HEADS, one_head, 0)
    for copy in y_own:
        copy.wait()
    for i in range(nz - 1):
        y_third(i)
    xv = x_ref[...].astype(jnp.float32)
    r_one = lax.rsqrt(jnp.mean(xv * xv, axis=-1, keepdims=True) + norm_eps)
    n_one = xv * r_one
    a_ref[...] = (n_one * gain1[...]).astype(jnp.bfloat16)
    shared_events[1]()
    to_partner(1, a_ref, dv_ref[...])
    to_partner(2, a_ref, dk_ref[...])
    to_partner(3, a_ref, dq_ref[...])
    if n * stack0.shape[1] > 2 * half:
        stack0[...] = jnp.zeros_like(stack0)
        stack1[...] = jnp.zeros_like(stack1)
    own_part(0, o_ref, dx_low, stack0, 0)
    own_part(1, a_ref, dv_ref[...], stack0, 1)
    first, second = (
        Scatter(
            pc, ((m, c3, pc.s3), (m, c2, pc.s2), (nz, c1, pc.s1)), lambda b, stack=stack: stack.at[b], lambda k, a, b2, i=i: r3.at[i, k, a, b2], lambda k, a, i=i: r2.at[i, k, a],
            lambda k, i=i: r1.at[i, k], (ss.at[i], s3.at[i], s2.at[i], s1.at[i]),
        )
        for i, stack in enumerate((stack0, stack1))
    )
    first.start_plane(0)
    first.start_plane(1)
    shared_events[2]()
    own_part(2, a_ref, dk_ref[...], stack1, 0)
    for p in range(2, nz):
        first.start_plane(p)
    own_part(3, a_ref, dq_ref[...], stack1, 1)
    second.start_plane(0)
    second.start_plane(1)
    shared_events[3]()
    fetch(wv, 1).wait()
    da = inner_cols(dv_ref[...], wbuf[1])
    fetch(wq, 1).start()
    fetch(wk, 0).wait()
    da = da + inner_cols(dk_ref[...], wbuf[0])
    fetch(wq, 1).wait()
    da = da + inner_cols(dq_ref[...], wbuf[1])
    for p in range(2, nz):
        second.start_plane(p)
    scaled_one = da * gain1[...]
    grad_one = jnp.sum(da * n_one, axis=0, keepdims=True)
    back = r_one * (scaled_one - n_one * jnp.mean(scaled_one * n_one, axis=-1, keepdims=True))
    gtok_ref[...] = (dx_ref[...] + back).astype(jnp.bfloat16)
    get_base = pltpu.make_async_copy(base_hbm, dx_ref, wsem.at[0])
    get_base.start()

    def exchange(ref, own, level, peers, value):
        ref[own] = value
        copies = [
            pltpu.make_async_remote_copy(
                src_ref=ref.at[own], dst_ref=ref.at[own], send_sem=cs.at[level, i], recv_sem=cr.at[level, own],
                device_id=to, device_id_type=MESH,
            )
            for i, (to, at) in enumerate(peers)
        ]
        for copy in copies:
            copy.start()

        def done():
            for i, (to, at) in enumerate(peers):
                pltpu.make_async_remote_copy(
                    src_ref=ref.at[own], dst_ref=ref.at[at], send_sem=cs.at[level, i], recv_sem=cr.at[level, at],
                    device_id=to, device_id_type=MESH,
                ).wait_recv()
            for copy in copies:
                copy.wait_send()
            total = ref[0]
            for i in range(1, ref.shape[0]):
                total = total + ref[i]
            return total

        return done

    turn_ref[...] = jnp.zeros_like(turn_ref)
    for i in range(n):
        turn_ref[i : i + 1, :] = scores_in[i]
    scores = turn_ref[...].T
    lane = lax.broadcasted_iota(jnp.int32, (rows, 128), 1)
    row = lax.broadcasted_iota(jnp.int32, (rows, 128), 0)
    scores = jnp.where(row < len_ref[0], scores, 0.0)
    soft, routes = route_columns(logit_ref, route_ref, turn_ref)
    share = jnp.zeros((rows, 128), jnp.float32)
    for i in range(route_ref.shape[0]):
        picked = jnp.sum(jnp.where(lane == routes[:, i : i + 1], scores, 0.0), axis=-1, keepdims=True)
        share = jnp.where(lane == i, picked, share)
    grad_logits = soft * (share - jnp.sum(soft * share, axis=-1, keepdims=True))
    glog_ref[...] = grad_logits.T[0 : route_ref.shape[0], :]

    small = jnp.concatenate([grad_one, grad_two, cnt_ref[...], jnp.zeros((5, width), jnp.float32)], axis=0)
    level0 = exchange(sm_core, c, 0, [((e, 1 - c), 1 - c)], small)
    steps0, steps1 = first.steps(), second.steps()
    steps0[0]()
    steps0[1]()
    shared_events[4]()
    level1 = exchange(sm_d3, c3, 1, [((pc.blk(c1, c2, j), c), j) for j in pc.o3()], level0())
    steps0[2]()
    steps1[0]()
    steps0[3]()
    steps1[1]()
    steps0[4]()
    for event in shared_events[5:-1]:
        event()
    level2 = exchange(sm_d2, c2, 2, [((pc.blk(c1, j, c3), c), j) for j in pc.o2()], level1())
    steps1[2]()
    for step in steps0[5:-1]:
        step()
    level3 = exchange(sm_z, c1, 3, [((pc.blk((c1 + j) % nz, c2, c3), c), (c1 + j) % nz) for j in range(1, nz)], level2())
    for step in steps1[3:-1]:
        step()
    small_ref[...] = level3()
    steps0[-1]()
    g0 = Gather(pc, stack0.at[e], ag0, gs.at[0], gr.at[0], stack0.shape[1])
    g0.start()
    loc0 = pltpu.make_async_copy(stack0.at[e], ag0.at[e], locs.at[0])
    loc0.start()
    steps1[-1]()
    g1 = Gather(pc, stack1.at[e], ag1, gs.at[1], gr.at[1], stack1.shape[1])
    g1.start()
    loc1 = pltpu.make_async_copy(stack1.at[e], ag1.at[e], locs.at[1])
    loc1.start()
    get_base.wait()
    y_last()
    run_staggered(g0.events(), g1.events(), 1)
    shared_events[-1]()
    for g in (gather_s, g0, g1):
        g.finish()
    first.finish()
    second.finish()
    loc_s.wait()
    loc0.wait()
    loc1.wait()
    y_finish()
    for i in range(4):
        hand(i).wait_send()


def tail(n, x, x1, cot, dh, dus, base, own, q, k, v, o, prob, wq, wk, wv, wo, gain1, gain2, cosine, sine, cnt, length, logits, routes, scores, y, far):
    nz = 4
    m = {16: 2, 64: 4}[n]
    rows, width = x.shape
    half = width // 2
    block = blocked(2 * half, n)
    vmem = pl.BlockSpec(memory_space=pltpu.VMEM)
    hbm = pl.BlockSpec(memory_space=pl.ANY)
    f32, b16 = jnp.float32, jnp.bfloat16
    out = jax.ShapeDtypeStruct
    dma = pltpu.SemaphoreType.DMA
    wide = pltpu.VMEM((rows, width), b16)
    return pl.pallas_call(
        functools.partial(tail_kernel, n),
        out_shape=(
            out((rows, width), b16), out((rows, width), b16), out(logits.shape, f32), out((8, width), f32),
            out((n, block, width), b16), out((n, block, width), b16),
            out((n,) + own.shape, b16),
            out((m - 1, nz, rows, width), b16), out((nz, rows, width), b16),
        ),
        in_specs=[vmem] * 4 + [hbm] * 2 + [vmem] * 6 + [hbm] * 4 + [vmem] * 5 + [pl.BlockSpec(memory_space=pltpu.SMEM)] + [vmem] * 3 + [hbm] * 2,
        out_specs=(vmem,) * 4 + (hbm,) * 5,
        scratch_shapes=[
            pltpu.VMEM((rows, width), f32), wide, wide, wide, wide,
            pltpu.VMEM((4, half, width), b16), pltpu.VMEM((4, half, width), b16),
            pltpu.VMEM((n, block, width), b16), pltpu.VMEM((n, block, width), b16),
            pltpu.VMEM((2, m - 1, nz, m, block, width), b16), pltpu.VMEM((2, m - 1, nz, block, width), b16),
            pltpu.VMEM((2, nz - 1, block, width), b16),
            pltpu.VMEM((2, 8, width), f32), pltpu.VMEM((m, 8, width), f32), pltpu.VMEM((m, 8, width), f32), pltpu.VMEM((nz, 8, width), f32),
            pltpu.VMEM((2, width, width), b16), dma((2,)), pltpu.VMEM((128, rows), f32),
            pltpu.VMEM((nz, rows, width), b16), pltpu.VMEM((2, rows, width), b16),
            dma((3, 160)), dma((3, 2, n)), dma((2, n)), dma((2, m - 1, nz, m)), dma((2, m - 1, nz)), dma((2, nz - 1)),
            dma((4,)), dma((4,)), dma((4, max(nz, m))), dma((4, max(nz, m, 2))), dma((3,)),
            dma((nz,)), dma((2,)), dma((m - 1, nz)), dma((nz,)), dma((m - 1, nz)), dma((nz,)),
        ],
        compiler_params=pltpu.CompilerParams(collective_id=2, has_side_effects=True, vmem_limit_bytes=63 * 2**20),
    )(x, x1, cot, dh, dus, base, own, q, k, v, o, prob, wq, wk, wv, wo, gain1, gain2, cosine, sine, cnt, length, logits, routes, scores, y, far)


def blocked(count, n):
    return -(-count // (16 * n)) * 16


def from_blocks(blocks, count):
    return blocks.reshape(-1, blocks.shape[2])[:count].astype(jnp.float32)


def rotary_rows(seq_len):
    position = np.arange(seq_len).astype(np.float32)
    inverse_freq = (rotary_base ** (-2.0 * np.arange(HD // 2).astype(np.float32) / HD)).astype(np.float32)
    angle = position[:, None] * inverse_freq[None, :]
    cosine, sine = np.cos(angle), np.sin(angle)
    return np.concatenate([cosine, cosine], axis=1), np.concatenate([-sine, sine], axis=1)


def on_device(
    tokens, norm_one, w_query, w_key, w_value, w_out, norm_two, r_gate, r_up, r_down, s_gate, s_up, s_down,
    logits, routes, lengths, cotangent,
):
    rows, width = tokens.shape
    n = lax.axis_size("exp")
    hidden = s_gate.shape[1]
    cosine, sine = (jnp.asarray(table) for table in rotary_rows(rows))
    gain1, gain2 = norm_one, norm_two
    logits, routes = logits.T, routes.T
    attn_w = (w_query, w_key, w_value, w_out)
    routed_w = (r_gate[0].T, r_up[0].T, r_down[0])
    shared_w = (s_gate.T, s_up.T, s_down)
    (
        all_dy, all_h, fq, fk, fv, fo, fg, fu, fd, pg, pu, pd, mixed, queries, keys_all, values_all, attended, prob, gates, counts,
        base, shared_back, shared_grads,
    ) = front(
        n, tokens, cotangent, gain1, gain2, cosine, sine, lengths, logits, routes,
        attn_w, routed_w, shared_w,
    )
    scores, grad_hidden, tg, tu, td, shared_sum, outs, far_outs = experts(
        all_h, all_dy, gates, routed_w, (fg, fu, fd), (pg, pu, pd), shared_grads
    )[:8]
    full = (width, width)
    output, grad_tokens, grad_logits, small_sums, sum0, sum1, sum_s = tail(
        n, tokens, mixed, cotangent, grad_hidden, shared_back, base, shared_sum, queries, keys_all, values_all, attended, prob,
        fq.reshape(full), fk.reshape(full), fv.reshape(full), fo.reshape(full),
        gain1, gain2, cosine, sine, counts, lengths, logits, routes, scores,
        outs, far_outs,
    )[:7]
    half = width // 2
    wout_value = from_blocks(sum0, width)
    key_query = from_blocks(sum1, width)
    shared = from_blocks(sum_s, 3 * hidden)
    sg, su, sd = (shared[i * hidden : (i + 1) * hidden] for i in range(3))
    return (
        output, grad_tokens, small_sums[0],
        key_query[half:], key_query[:half], wout_value[half:], wout_value[:half],
        small_sums[1], tg.T[None], tu.T[None], td[None], sg.T, su.T, sd,
        grad_logits.T, small_sums[2, :n].astype(jnp.int32),
    )


def solution(mesh):
    in_specs = (
        P(("exp", "hid"), None),
        P(),
        P("hid", None),
        P("hid", None),
        P("hid", None),
        P("hid", None),
        P(),
        P("exp", None, "hid"),
        P("exp", None, "hid"),
        P("exp", "hid", None),
        P(None, "hid"),
        P(None, "hid"),
        P("hid", None),
        P(("exp", "hid"), None),
        P(("exp", "hid"), None),
        P(("exp", "hid")),
        P(("exp", "hid"), None),
    )
    out_specs = (
        P(("exp", "hid"), None),
        P(("exp", "hid"), None),
        P(),
        P("hid", None),
        P("hid", None),
        P("hid", None),
        P("hid", None),
        P(),
        P("exp", None, "hid"),
        P("exp", None, "hid"),
        P("exp", "hid", None),
        P(None, "hid"),
        P(None, "hid"),
        P("hid", None),
        P(("exp", "hid"), None),
        P(),
    )
    return jax.shard_map(
        on_device, mesh=mesh, in_specs=in_specs, out_specs=out_specs, check_vma=False
    )
```

```python
import functools

import jax
import jax.numpy as jnp
import numpy as np
from jax import lax
from jax.experimental import pallas as pl
from jax.experimental.pallas import tpu as pltpu
from jax.sharding import PartitionSpec as P

HEADS = 10
HD = 128
MESH = pl.DeviceIdType.MESH


norm_eps = 1e-06
rotary_base = 10000.0
contract_rows = (((0,), (0,)), ((), ()))
contract_cols = (((1,), (1,)), ((), ()))


def matmul(left_side, right_side):
    return jnp.dot(left_side, right_side, preferred_element_type=jnp.float32)


def outer_rows(left_side, right_side):
    return lax.dot_general(left_side, right_side, contract_rows, preferred_element_type=jnp.float32)


def inner_cols(left_side, right_side):
    return lax.dot_general(left_side, right_side, contract_cols, preferred_element_type=jnp.float32)


class Place:
    def __init__(self, n):
        self.n = n; self.nz = 4; self.m = {16: 2, 64: 4}[n]; m = self.m
        self.e = lax.axis_index("exp"); self.c = lax.axis_index("hid"); c = self.c; e = self.e
        self.s1 = m * m; self.s2 = 1 + c * (m - 1); self.s3 = m - c * (m - 1)
        self.x = e % m; self.y = (e // m) % m
        self.c1 = e // self.s1; self.c2 = (e // self.s2) % m; self.c3 = (e // self.s3) % m
    def chip(self, z, y, x): return z * self.s1 + y * self.m + x
    def block(self, z, y): return z * self.m + y
    def others(self):
        far = [((self.c1 + i) % self.nz, (self.y + j) % self.m) for i in range(self.nz) for j in range(self.m)]
        return far[1:]
    def blk(self, a, b, d): return a * self.s1 + b * self.s2 + d * self.s3
    def o2(self): return [(self.c2 + j) % self.m for j in range(1, self.m)]
    def o3(self): return [(self.c3 + j) % self.m for j in range(1, self.m)]
    def greet_all(self):
        barrier = pltpu.get_barrier_semaphore()

        def greet(j, carry):
            pl.semaphore_signal(barrier, inc=1, device_id=((self.e + j) % self.n, self.c), device_id_type=MESH)
            return carry

        lax.fori_loop(1, self.n, greet, 0)
        pl.semaphore_signal(barrier, inc=1, device_id=(self.e, 1 - self.c), device_id_type=MESH)
        pl.semaphore_wait(barrier, self.n)


class Gather:
    def __init__(self, pc, src, dst, ssem, rsem, split, base=0):
        self.pc, self.src, self.dst, self.ssem, self.rsem = pc, src, dst, ssem, rsem
        self.split = split; self.sends = []; self.base = base
    def view(self, ref, part):
        R = self.src.shape[0]
        return ref.at[pl.ds(0, self.split)] if part == 0 else ref.at[pl.ds(self.split, R - self.split)]
    def send(self, part, own, b, to, cond=None):
        i = self.base + len(self.sends)
        src = self.view(self.src if own else self.dst.at[b], part)
        cp = pltpu.make_async_remote_copy(src_ref=src, dst_ref=self.view(self.dst.at[b], part), send_sem=self.ssem.at[i], recv_sem=self.rsem.at[part, b], device_id=(to, self.pc.c), device_id_type=MESH)
        self.sends.append((cond, cp))
        if cond is None: cp.start()
        else: pl.when(cond)(cp.start)
    def wait(self, part, b):
        v = self.view(self.dst.at[b], part)
        to = self.pc.blk(self.pc.c1, self.pc.c2, self.pc.o3()[0])
        pltpu.make_async_remote_copy(src_ref=v, dst_ref=v, send_sem=self.ssem.at[0], recv_sem=self.rsem.at[part, b], device_id=(to, self.pc.c), device_id_type=MESH).wait_recv()
    def updown(self, part, own, b):
        pc = self.pc
        self.send(part, own, b, pc.blk(pc.c1 + 1, pc.c2, pc.c3), pc.c1 < pc.nz - 1)
        self.send(part, own, b, pc.blk(pc.c1 - 1, pc.c2, pc.c3), pc.c1 > 0)
    def to2(self, part, own, b):
        pc = self.pc
        for j in pc.o2(): self.send(part, own, b, pc.blk(pc.c1, j, pc.c3))
    def to3(self, part, own, b):
        pc = self.pc
        for j in pc.o3(): self.send(part, own, b, pc.blk(pc.c1, pc.c2, j))
    def start(self):
        e = self.pc.e
        self.to3(0, True, e); self.to2(0, True, e); self.updown(0, True, e)
        if self.split < self.src.shape[0]:
            self.to3(1, True, e); self.to2(1, True, e); self.updown(1, True, e)
    def zarr(self, part, s, up, k2, k3, more):
        pc = self.pc
        a = pc.c1 - s if up else pc.c1 + s
        cond = (pc.c1 >= s) if up else (pc.c1 < pc.nz - s)
        b = pc.blk(a, k2, k3)
        pl.when(cond)(lambda: self.wait(part, b))
        if s < pc.nz - 1:
            if up: self.send(part, False, b, pc.blk(pc.c1 + 1, pc.c2, pc.c3), (pc.c1 >= s) & (pc.c1 < pc.nz - 1))
            else: self.send(part, False, b, pc.blk(pc.c1 - 1, pc.c2, pc.c3), (pc.c1 < pc.nz - s) & (pc.c1 > 0))
        if more:
            for j in pc.o2(): self.send(part, False, b, pc.blk(pc.c1, j, pc.c3), cond)
            for j in pc.o3(): self.send(part, False, b, pc.blk(pc.c1, pc.c2, j), cond)
    def events(self):
        pc = self.pc; ev = []
        def a2(s):
            def go():
                for j in pc.o2():
                    for sg in ((1, -1) if s else (1,)):
                        a = pc.c1 + sg * s
                        cond = None if s == 0 else ((a >= 0) & (a < pc.nz))
                        b = pc.blk(a, j, pc.c3)
                        if cond is None: self.wait(0, b)
                        else: pl.when(cond)(lambda b=b: self.wait(0, b))
                        for k in pc.o3(): self.send(0, False, b, pc.blk(pc.c1, pc.c2, k), cond)
            return go
        def az(s):
            def go():
                self.zarr(0, s, True, pc.c2, pc.c3, True); self.zarr(0, s, False, pc.c2, pc.c3, True)
            return go
        B = self.split < self.src.shape[0]
        def f1():
            for j in pc.o2():
                b = pc.blk(pc.c1, j, pc.c3); self.wait(1, b); self.to3(1, False, b); self.updown(1, False, b)
        def f2():
            for k in pc.o3():
                b = pc.blk(pc.c1, pc.c2, k); self.wait(1, b); self.updown(1, False, b)
        def f3():
            for j in pc.o2():
                for k in pc.o3():
                    b = pc.blk(pc.c1, j, k); self.wait(1, b); self.updown(1, False, b)
        def fz(s):
            def go():
                for k2 in range(pc.m):
                    for k3 in range(pc.m):
                        self.zarr(1, s, True, k2, k3, False); self.zarr(1, s, False, k2, k3, False)
            return go
        ev += [az(1), a2(0)]
        if B: ev += [f1, f2, f3]
        ev += [az(2), a2(1)]
        if B: ev += [fz(1)]
        ev += [az(3), a2(2)]
        if B: ev += [fz(2)]
        ev += [a2(3)]
        if B: ev += [fz(3)]
        def last():
            for a in range(pc.nz):
                for j in range(pc.m):
                    for k in pc.o3(): self.wait(0, pc.blk(a, j, k))
        ev += [last]
        return ev
    def finish(self):
        for cond, cp in self.sends:
            if cond is None: cp.wait_send()
            else: pl.when(cond)(cp.wait_send)


class Lines:
    def __init__(self, pc, src, dst, ssem, rsem):
        self.pc, self.src, self.dst, self.ssem, self.rsem = pc, src, dst, ssem, rsem
        self.places = [(0, way, 0) for way in (1, -1)] + [(0, 0, j) for j in range(1, pc.m)]
        for s in range(1, pc.nz):
            for way in (1, -1):
                self.places += [(s, way, j) for j in range(0 if s < pc.nz - 1 else 1, pc.m)]

    def send(self, place):
        pc = self.pc
        s, way, j = place
        a = pc.c1 - way * s
        b = pc.block(a, pc.y)
        on = pc.c1 + way
        to = pc.chip(on, pc.y, pc.x) if j == 0 else pc.chip(pc.c1, (pc.y + j) % pc.m, pc.x)
        cond = (a >= 0) & (a < pc.nz)
        if j == 0:
            cond = cond & (on >= 0) & (on < pc.nz)
        copy = pltpu.make_async_remote_copy(
            src_ref=self.src if s == 0 else self.dst.at[b], dst_ref=self.dst.at[b],
            send_sem=self.ssem.at[self.places.index(place)], recv_sem=self.rsem.at[b],
            device_id=(to, pc.c), device_id_type=MESH,
        )
        return cond, copy

    def wait(self, b):
        pc = self.pc
        pltpu.make_async_remote_copy(
            src_ref=self.dst.at[b], dst_ref=self.dst.at[b], send_sem=self.ssem.at[0], recv_sem=self.rsem.at[b],
            device_id=(pc.chip(pc.c1, (pc.y + 1) % pc.m, pc.x), pc.c), device_id_type=MESH,
        ).wait_recv()

    def pass_on(self, s):
        for place in self.places:
            if place[0] == s:
                cond, copy = self.send(place)
                pl.when(cond)(copy.start)

    def start(self):
        self.pass_on(0)

    def line(self, s):
        self.wait_line(s)
        self.pass_on(s)

    def wait_line(self, s):
        pc = self.pc
        for way in (1, -1):
            a = pc.c1 - way * s
            pl.when((a >= 0) & (a < pc.nz))(functools.partial(self.wait, pc.block(a, pc.y)))

    def wait_far(self):
        pc = self.pc
        for a in range(pc.nz):
            for j in range(1, pc.m):
                self.wait(pc.block(a, (pc.y + j) % pc.m))

    def finish(self, distances):
        for place in self.places:
            if place[0] in distances:
                cond, copy = self.send(place)
                pl.when(cond)(copy.wait_send)


def run_staggered(first, second, lag):
    for i in range(max(len(first), len(second) + lag)):
        if i < len(first):
            first[i]()
        if lag <= i < len(second) + lag:
            second[i - lag]()


def part_rows(rows):
    return rows - rows // 80 * 16


def front_kernel(
    n,
    x_ref, cot_ref, gain1, gain2, cos_ref, sin_ref, len_ref, logit_ref, route_ref,
    wq, wk, wv, wo, rg, ru, rd, sg, su, sd,
    all_dy, h_all, fq, fk, fv, fo, fg, fu, fd, pg, pu, pd,
    x1_ref, q_ref, k_ref, v_ref, o_ref, p_ref, gates_in, cnt_ref, base_ref, dus_ref, shared_ref,
    wbuf, h_ref, rows_out, turn_ref, shw, act, dg, dup, give, take,
    gs, gr, hs, hr, ls, ws, wr, wl, es, er, gss, grs, ps, pr, qs, qr, us, ur, ul, xs, xr,
):
    pc = Place(n)
    e, c = pc.e, pc.c
    rows, width = x_ref.shape
    half = width // 2
    pc.greet_all()
    x, y, m = pc.x, pc.y, pc.m
    me = pc.block(pc.c1, y)
    gather_dy = Lines(pc, cot_ref, all_dy, gs, gr)
    gather_h = Lines(pc, h_ref, h_all, hs, hr)
    own_dy = pltpu.make_async_copy(cot_ref, all_dy.at[me], ls.at[0])
    own_h = pltpu.make_async_copy(h_ref, h_all.at[me], ls.at[1])
    own_dy.start()
    partner = (e, 1 - c)
    halves = (wq, wk, wv, wo)
    fulls = (fq, fk, fv, fo)

    def swap(i):
        return pltpu.make_async_remote_copy(
            src_ref=halves[i], dst_ref=wbuf.at[i, c], send_sem=ws.at[i], recv_sem=wr.at[i],
            device_id=partner, device_id_type=MESH,
        )

    def own(i):
        return pltpu.make_async_copy(halves[i], wbuf.at[i, c], wl.at[0, i])

    def keep(i):
        return pltpu.make_async_copy(wbuf.at[i], fulls[i], wl.at[1, i])

    experts_other = (fg, fu, fd)

    def expert_swap(i, src):
        return pltpu.make_async_remote_copy(
            src_ref=src, dst_ref=experts_other[i], send_sem=es.at[i], recv_sem=er.at[i],
            device_id=partner, device_id_type=MESH,
        )

    beside = (pg, pu, pd)

    def half_send(i, j, src):
        return pltpu.make_async_remote_copy(
            src_ref=src, dst_ref=beside[i].at[m - j - 1, c], send_sem=ps.at[i, j - 1], recv_sem=pr.at[i, m - j - 1],
            device_id=(pc.chip(pc.c1, y, (x + j) % m), c), device_id_type=MESH,
        )

    def half_on(i, k):
        return pltpu.make_async_remote_copy(
            src_ref=beside[i].at[k, c], dst_ref=beside[i].at[k, c], send_sem=qs.at[i, k], recv_sem=qr.at[i, k],
            device_id=partner, device_id_type=MESH,
        )

    for i in range(4):
        swap(i).start()
        own(i).start()
    shared_halves = (sg, su, sd)

    def shared_swap(i):
        return pltpu.make_async_remote_copy(
            src_ref=shared_halves[i], dst_ref=shw.at[i, c], send_sem=us.at[i], recv_sem=ur.at[i],
            device_id=partner, device_id_type=MESH,
        )

    def shared_own(i):
        return pltpu.make_async_copy(shared_halves[i], shw.at[i, c], ul.at[i])

    for i, routed in enumerate((rg, ru, rd)):
        for j in range(1, m):
            half_send(i, j, routed).start()
    gather_dy.start()
    for i, routed in enumerate((rg, ru, rd)):
        expert_swap(i, routed).start()
        shared_swap(i).start()
        shared_own(i).start()

    lane = lax.broadcasted_iota(jnp.int32, (rows, 128), 1)
    row = lax.broadcasted_iota(jnp.int32, (rows, 128), 0)
    valid = (row < len_ref[0]).astype(jnp.float32)
    soft, routes = route_columns(logit_ref, route_ref, turn_ref)
    dense = jnp.zeros((rows, 128), jnp.float32)
    named = jnp.zeros((rows, 128), jnp.float32)
    for i in range(route_ref.shape[0]):
        hit = lane == routes[:, i : i + 1]
        dense = dense + jnp.where(hit, soft[:, i : i + 1], 0.0)
        named = named + jnp.where(hit, 1.0, 0.0)
    dense = dense * valid
    cnt_ref[...] = jnp.zeros_like(cnt_ref)
    cnt_ref[:, 0:128] = jnp.sum(named * valid, axis=0, keepdims=True)
    turned = dense.T
    for i in range(n):
        rows_out[i] = turned[i : i + 1, :]
    for i in range(m):
        gates_in[me * m + i] = rows_out[me * m + i]

    def gate_send(a, b2):
        return pltpu.make_async_remote_copy(
            src_ref=rows_out.at[pl.ds(pc.block(a, b2) * m, m)], dst_ref=gates_in.at[pl.ds(me * m, m)],
            send_sem=gss.at[a, b2], recv_sem=grs.at[pc.c1, y],
            device_id=(pc.chip(a, b2, x), c), device_id_type=MESH,
        )

    def gate_wait(a, b2):
        at = pl.ds(pc.block(a, b2) * m, m)
        pltpu.make_async_remote_copy(
            src_ref=rows_out.at[at], dst_ref=gates_in.at[at], send_sem=gss.at[a, b2], recv_sem=grs.at[a, b2],
            device_id=(pc.chip(a, b2, x), c), device_id_type=MESH,
        ).wait_recv()

    for a, b2 in pc.others():
        gate_send(a, b2).start()

    xv = x_ref[...].astype(jnp.float32)
    a = (xv * lax.rsqrt(jnp.mean(xv * xv, axis=-1, keepdims=True) + norm_eps) * gain1[...]).astype(jnp.bfloat16)
    cosine, sine = cos_ref[...], sin_ref[...]

    def project(values, i):
        own(i).wait()
        swap(i).wait_recv()
        keep(i).start()
        return matmul(values[:, :half], wbuf[i, 0]) + matmul(values[:, half:], wbuf[i, 1])

    for i, ref in ((0, q_ref), (1, k_ref)):
        flat = project(a, i)
        for hd in range(HEADS):
            part = flat[:, hd * HD : (hd + 1) * HD]
            ref[:, hd * HD : (hd + 1) * HD] = (part * cosine + swap_halves(part) * sine).astype(jnp.bfloat16)
    v_ref[...] = project(a, 2).astype(jnp.bfloat16)
    gather_dy.line(1)
    scale = HD ** (-0.5)
    row_pos = lax.broadcasted_iota(jnp.int32, (rows, rows), 0)
    col_pos = lax.broadcasted_iota(jnp.int32, (rows, rows), 1)
    allowed = (col_pos <= row_pos) & (col_pos < len_ref[0])

    def one_head(hd, carry):
        at = pl.ds(pl.multiple_of(hd * HD, HD), HD)
        scores = jnp.where(allowed, inner_cols(q_ref[:, at], k_ref[:, at]) * scale, -1e30)
        up = jnp.exp(scores - jnp.max(scores, axis=-1, keepdims=True))
        prob = up / jnp.sum(up, axis=-1, keepdims=True)
        p_ref[hd] = prob
        o_ref[:, at] = matmul(prob.astype(jnp.bfloat16), v_ref[:, at]).astype(jnp.bfloat16)
        return carry

    lax.fori_loop(0, HEADS, one_head, 0)
    gather_dy.line(2)
    x1 = xv + project(o_ref[...], 3)
    x1_ref[...] = x1
    h_ref[...] = (x1 * lax.rsqrt(jnp.mean(x1 * x1, axis=-1, keepdims=True) + norm_eps) * gain2[...]).astype(jnp.bfloat16)
    gather_h.start()
    own_h.start()
    for i in range(3, pc.nz):
        gather_dy.line(i)

    for i in range(3):
        shared_own(i).wait()
        shared_swap(i).wait_recv()
    wg, wu, wd = (shw.at[i] for i in range(3))
    h, z = h_ref[...], cot_ref[...]
    for half in range(2):
        g = inner_cols(h, wg[half])
        u = inner_cols(h, wu[half])
        da = inner_cols(z, wd[half])
        sig = jax.nn.sigmoid(g)
        si = g * sig
        act[half] = (si * u).astype(jnp.bfloat16)
        dup[half] = (da * si).astype(jnp.bfloat16)
        dg[half] = (da * u * sig * (1.0 + g * (1.0 - sig))).astype(jnp.bfloat16)

    def grad_swap(i):
        return pltpu.make_async_remote_copy(
            src_ref=give.at[i], dst_ref=take.at[i], send_sem=xs.at[i], recv_sem=xr.at[i],
            device_id=partner, device_id_type=MESH,
        )

    sides = ((dg, h), (dup, h), (act, z))
    for i, (left, right) in enumerate(sides):
        give[i] = outer_rows(left[1 - c], right).astype(jnp.bfloat16)
        grad_swap(i).start()
    base_ref[...] = x1_ref[...] + matmul(act[0], wd[0]) + matmul(act[1], wd[1])
    dus_ref[...] = matmul(dg[0], wg[0]) + matmul(dg[1], wg[1]) + matmul(dup[0], wu[0]) + matmul(dup[1], wu[1])
    hidden = give.shape[1]
    shared_ref[pl.ds(3 * hidden, shared_ref.shape[0] - 3 * hidden)] = jnp.zeros(
        (shared_ref.shape[0] - 3 * hidden, width), jnp.bfloat16
    )
    for i, (left, right) in enumerate(sides):
        part = outer_rows(left[c], right)
        grad_swap(i).wait()
        shared_ref[pl.ds(i * hidden, hidden)] = (part + take[i].astype(jnp.float32)).astype(jnp.bfloat16)
    for k in range(m - 1):
        for i in range(3):
            half_send(i, m - k - 1, sd).wait_recv()
            half_on(i, k).start()
    gather_dy.wait_far()
    for a, b2 in pc.others():
        gate_wait(a, b2)
        gate_send(a, b2).wait_send()
    gather_h.wait_line(1)
    for j in range(1, m):
        gather_h.wait(pc.block(pc.c1, (y + j) % m))
    gather_dy.finish(range(pc.nz))
    gather_h.finish((0,))
    own_dy.wait()
    own_h.wait()
    for i in range(4):
        swap(i).wait_send()
        keep(i).wait()
    for i, shared in enumerate((sg, su, sd)):
        expert_swap(i, shared).wait()
        shared_swap(i).wait_send()
        for k in range(m - 1):
            half_send(i, k + 1, shared).wait_send()
            half_on(i, k).wait_send()
            other = pltpu.make_async_remote_copy(
                src_ref=beside[i].at[k, 1 - c], dst_ref=beside[i].at[k, 1 - c], send_sem=qs.at[i, k], recv_sem=qr.at[i, k],
                device_id=partner, device_id_type=MESH,
            )
            other.wait_recv()


def front(n, x, cot, gain1, gain2, cosine, sine, length, logits, routes, attn_w, routed_w, shared_w):
    rows, width = x.shape
    hidden = shared_w[0].shape[0]
    vmem = pl.BlockSpec(memory_space=pltpu.VMEM)
    hbm = pl.BlockSpec(memory_space=pl.ANY)
    f32, b16 = jnp.float32, jnp.bfloat16
    out = jax.ShapeDtypeStruct
    dma = pltpu.SemaphoreType.DMA
    wide = out((rows, width), b16)
    full = out((2, width // 2, width), b16)
    nz = 4
    m = {16: 2, 64: 4}[n]
    beside = out((m - 1, 2, hidden, width), b16)
    narrow = pltpu.VMEM((2, rows, hidden), b16)
    three = pltpu.VMEM((3, hidden, width), b16)
    return pl.pallas_call(
        functools.partial(front_kernel, n),
        out_shape=(
            out((nz * m, rows, width), b16), out((nz * m, rows, width), b16), full, full, full, full,
            out((hidden, width), b16), out((hidden, width), b16), out((hidden, width), b16), beside, beside, beside,
            out((rows, width), f32), wide, wide, wide, wide, out((HEADS, rows, rows), f32),
            out((n, 1, rows), f32), out((1, width), f32),
            out((rows, width), f32), out((rows, width), f32), out((n * blocked(3 * hidden, n), width), b16),
        ),
        in_specs=[vmem] * 6 + [pl.BlockSpec(memory_space=pltpu.SMEM)] + [vmem] * 2 + [hbm] * 10,
        out_specs=(hbm,) * 12 + (vmem,) * 11,
        scratch_shapes=[
            pltpu.VMEM((4, 2, width // 2, width), b16), pltpu.VMEM((rows, width), b16), pltpu.VMEM((n, 1, rows), f32), pltpu.VMEM((128, rows), f32),
            pltpu.VMEM((3, 2, hidden, width), b16), narrow, narrow, narrow, three, three,
            dma((64,)), dma((nz * m,)), dma((64,)), dma((nz * m,)), dma((2,)), dma((4,)), dma((4,)), dma((2, 4)), dma((3,)), dma((3,)),
            dma((nz, m)), dma((nz, m)), dma((3, m - 1)), dma((3, m - 1)), dma((3, m - 1)), dma((3, m - 1)),
            dma((3,)), dma((3,)), dma((3,)), dma((3,)), dma((3,)),
        ],
        compiler_params=pltpu.CompilerParams(collective_id=0, has_side_effects=True, vmem_limit_bytes=56 * 2**20),
    )(x, cot, gain1, gain2, cosine, sine, length, logits, routes, *attn_w, *routed_w, *shared_w)


def experts_kernel(
    n, slots,
    h_in, dy_hbm, gates_in, rg, ru, rd, xg, xu, xd, pg, pu, pd, shared_hbm,
    scores_in, du_hbm, tg_hbm, tu_hbm, td_hbm, sum_hbm, y_hbm, far_hbm, h_all, part_hbm, xt_hbm, r3_hbm, r1_hbm,
    wbuf, og, ou, od, total_ref, hbuf, dbuf, act, dg, dup, stage, pbuf, rbuf, give, take, keep,
    gate_ref, s_ref, turn_ref, rows_out,
    gs, gr, lsem, ssem, r3sem, r1sem, bsem, wsem, partsem, pbsem, ysem,
    xssem, xrsem, gsend, grecv, osem, psem, scs, scr, room, vs, va, vb, vc,
):
    pc = Place(n)
    nz, m = pc.nz, pc.m
    c1, e, c, x, y = pc.c1, pc.e, pc.c, pc.x, pc.y
    blocks = nz * m
    me = pc.block(c1, y)
    toward = 1 - 2 * (c1 // (nz // 2))
    together = nz - 1
    grads = (og, ou, od)
    own_half = (rg, ru, rd)
    other_half = (xg, xu, xd)
    shared_half = (pg, pu, pd)

    def weight(p, i, half, src):
        return pltpu.make_async_copy(src, wbuf.at[p % 2, i, half], wsem.at[p % 2, i, half])

    def weights_start(p):
        for i in range(3):
            if p < m - 1:
                for half in range(2):
                    weight(p, i, half, shared_half[i].at[p, half]).start()
            else:
                weight(p, i, c, own_half[i]).start()
                weight(p, i, 1 - c, other_half[i]).start()

    weights_start(0)
    weights_start(1)
    hidden = give.shape[1]
    part_rows = keep.shape[0] // n
    fetch_shared = pltpu.make_async_copy(shared_hbm, keep, psem.at[0])
    fetch_shared.start()
    first_h = pltpu.make_async_copy(h_all.at[me], hbuf.at[0], lsem.at[0, 0])
    first_dy = pltpu.make_async_copy(dy_hbm.at[me], dbuf.at[0], lsem.at[1, 0])
    first_h.start()
    first_dy.start()
    pc.greet_all()
    gather = Lines(pc, None, h_all, gs, gr)
    gather.pass_on(1)

    def rows_of(ref, i):
        return ref.at[pl.ds(pl.multiple_of(i * part_rows, 16), part_rows)]

    from_b = (m - 1) * m * nz
    from_c = from_b + (nz - 1) * m
    shared_sum = Scatter(
        pc, ((m, x, 1), (nz, c1, m * m), (m, y, m)), functools.partial(rows_of, keep),
        lambda i, c_at, b_at: rows_of(take, (i * m + c_at) * nz + b_at),
        lambda i, c_at: rows_of(take, from_b + i * m + c_at),
        lambda i: rows_of(take, from_c + i), (vs, va, vb, vc),
    )
    fetch_shared.wait()
    shared_sum.start_plane(0)
    shared_steps = shared_sum.steps()
    sum_store = pltpu.make_async_copy(rows_of(keep, e), sum_hbm, psem.at[0])

    def shared_done():
        sum_store.start()
        shared_sum.finish()
        pl.semaphore_signal(room, inc=1, device_id=(e, 1 - c), device_id_type=MESH)
        sum_store.wait()

    shared_steps = shared_steps + [shared_done]

    def third(ref, i):
        return ref.at[pl.ds(i * hidden, hidden)]
    turn_ref[...] = jnp.zeros_like(turn_ref)
    for i in range(n):
        turn_ref[i : i + 1, :] = gates_in[i]
    gate_ref[...] = turn_ref[...].T
    for total in grads:
        total[...] = jnp.zeros_like(total)
    s_ref[...] = jnp.zeros_like(s_ref)

    def dest(step):
        p, t = step // blocks, step % blocks
        last = (p + 1) // m
        return (c1 + toward * (t // m + last) + nz) % nz, (y + t % m + last) % m

    def load(step, i):
        b = pc.block(*dest(step))
        return (
            pltpu.make_async_copy(h_all.at[b], hbuf.at[i], lsem.at[0, i]),
            pltpu.make_async_copy(dy_hbm.at[b], dbuf.at[i], lsem.at[1, i]),
        )

    def part_load(step, i):
        return pltpu.make_async_copy(part_hbm.at[pc.block(*dest(step))], pbuf.at[i], pbsem.at[i])

    def part_store(slot, b):
        return pltpu.make_async_copy(stage.at[slot], part_hbm.at[b], partsem.at[slot])

    def y_store(slot, a, b2):
        return pltpu.make_async_copy(stage.at[slot, 0], y_hbm.at[a, b2], ysem.at[slot])

    def pair_send(slot, to, dst, sem):
        return pltpu.make_async_remote_copy(
            src_ref=stage.at[slot], dst_ref=dst, send_sem=ssem.at[slot], recv_sem=sem,
            device_id=(to, c), device_id_type=MESH,
        )

    def du_send(slot, to, dst, sem):
        return pltpu.make_async_remote_copy(
            src_ref=stage.at[slot, 1], dst_ref=dst, send_sem=ssem.at[slot], recv_sem=sem,
            device_id=(to, c), device_id_type=MESH,
        )

    def collect(slot, received):
        def fetch(i):
            return pltpu.make_async_copy(received[i][0], rbuf.at[i % 2], bsem.at[i % 2])

        def begin(i):
            src, sem, landed = received[i]
            pltpu.make_async_remote_copy(
                src_ref=landed, dst_ref=landed, send_sem=ssem.at[slot], recv_sem=sem,
                device_id=(e, 1 - c), device_id_type=MESH,
            ).wait_recv()
            fetch(i).start()

        begin(0)
        total_ref[...] = stage[slot, 1].astype(jnp.float32)
        for i in range(len(received)):
            if i + 1 < len(received):
                begin(i + 1)
            fetch(i).wait()
            total_ref[...] += rbuf[i % 2].astype(jnp.float32)

    def from_y(a, whole):
        if whole:
            return [(far_hbm.at[j, a, 1], r3sem.at[j, a], far_hbm.at[j, a]) for j in range(m - 1)]
        return [(r3_hbm.at[j, a], r3sem.at[j, a], r3_hbm.at[j, a]) for j in range(m - 1)]

    def from_z():
        return [(r1_hbm.at[(c1 + j) % nz], r1sem.at[(c1 + j) % nz], r1_hbm.at[(c1 + j) % nz]) for j in range(1, nz)]

    def swaps():
        return [
            pltpu.make_async_remote_copy(
                src_ref=give.at[i], dst_ref=third(take, i), send_sem=xssem.at[i], recv_sem=xrsem.at[i],
                device_id=(e, 1 - c), device_id_type=MESH,
            )
            for i in range(3)
        ]

    def grad_send(p):
        return pltpu.make_async_remote_copy(
            src_ref=keep.at[pl.ds(0, 3 * hidden)], dst_ref=xt_hbm.at[x], send_sem=gsend, recv_sem=grecv.at[x],
            device_id=(pc.chip(c1, y, (x + p + 1) % m), c), device_id_type=MESH,
        )

    def totals():
        return [
            pltpu.make_async_copy(src.at[c], dst, osem.at[i])
            for i, (src, dst) in enumerate(((og, tg_hbm), (ou, tu_hbm), (od, td_hbm)))
        ]

    first_h.wait()
    first_dy.wait()

    def body(step, carry):
        i = step % 2
        slot = step % slots
        p, t = step // blocks, step % blocks
        last = (p + 1) // m
        a, b2 = dest(step)
        b = pc.block(a, b2)
        column = b * m + (x + p + 1) % m
        for at in range(m):
            @pl.when(step == at * blocks)
            def _():
                for k in range(3):
                    for half in range(2):
                        weight(at, k, half, other_half[k]).wait()
                if at >= 1 and at + 1 < m:
                    weights_start(at + 1)

        @pl.when(step > 0)
        def _():
            for copy in load(step, i):
                copy.wait()

        wg, wu, wd = (wbuf.at[p % 2, k] for k in range(3))
        lane = lax.broadcasted_iota(jnp.int32, gate_ref.shape, 1)
        gate = jnp.sum(jnp.where(lane == column, gate_ref[...], 0.0), axis=1, keepdims=True)
        h = hbuf[i]
        dy = dbuf[i].astype(jnp.float32)
        z = (gate * dy).astype(jnp.bfloat16)
        for half in range(2):
            g = inner_cols(h, wg[half])
            u = inner_cols(h, wu[half])
            da = inner_cols(z, wd[half])
            sg = jax.nn.sigmoid(g)
            si = g * sg
            act[half] = (si * u).astype(jnp.bfloat16)
            dup[half] = (da * si).astype(jnp.bfloat16)
            dg[half] = (da * u * sg * (1.0 + g * (1.0 - sg))).astype(jnp.bfloat16)

        before = step - slots
        before_last = ((before + slots * blocks) // blocks - slots + 1) // m

        @pl.when((before >= 0) & (before_last < 1))
        def _():
            part_store(slot, b).wait()

        before_t = (before + slots * blocks) % blocks

        @pl.when((before >= 0) & (before_last >= 1) & (before_t < together * m) & (before_t % m < m - 1))
        def _():
            pair_send(slot, e, far_hbm.at[0, 0], r3sem.at[0, 0]).wait_send()

        @pl.when((before >= 0) & (before_last >= 1) & ((before_t >= together * m) | (before_t % m == m - 1)))
        def _():
            y_store(slot, a, b2).wait()
            du_send(slot, e, r1_hbm.at[0], r1sem.at[0]).wait_send()

        yv = (matmul(act[0], wd[0]) + matmul(act[1], wd[1])).astype(jnp.bfloat16).astype(jnp.float32)
        s = jnp.sum(yv * dy, axis=1, keepdims=True)
        s_ref[...] = jnp.where(lane == column, s, s_ref[...])
        yv = gate * yv
        du = (
            matmul(dg[0], wg[0]) + matmul(dg[1], wg[1]) + matmul(dup[0], wu[0]) + matmul(dup[1], wu[1])
        ).astype(jnp.bfloat16)

        @pl.when(p == 0)
        def _():
            stage[slot, 0] = yv.astype(jnp.bfloat16)
            stage[slot, 1] = du

        @pl.when(p > 0)
        def _():
            part_load(step, i).wait()
            stage[slot, 0] = (yv + pbuf[i, 0].astype(jnp.float32)).astype(jnp.bfloat16)
            stage[slot, 1] = (du.astype(jnp.float32) + pbuf[i, 1].astype(jnp.float32)).astype(jnp.bfloat16)

        @pl.when(last == 0)
        def _():
            part_store(slot, b).start()

        @pl.when((last == 1) & ((t >= together * m) | (t % m == m - 1)))
        def _():
            y_store(slot, a, b2).start()

        for j in range(1, m):
            @pl.when((last == 1) & (t < together * m) & (b2 == (y + j) % m))
            def _():
                pair_send(slot, pc.chip(c1, b2, x), far_hbm.at[m - j - 1, a], r3sem.at[m - j - 1, a]).start()

            @pl.when((last == 1) & (t >= together * m) & (b2 == (y + j) % m))
            def _():
                du_send(slot, pc.chip(c1, b2, x), r3_hbm.at[m - j - 1, a], r3sem.at[m - j - 1, a]).start()

        for k in range(2, nz):
            pl.when(step == (k - 1) * m - 1)(functools.partial(gather.line, k))

        @pl.when(step < m * blocks - 1)
        def _():
            after = step + 1
            next_a, next_b = dest(after)

            @pl.when((after < blocks) & (next_b != y) & (next_a != c1))
            def _():
                gather.wait(pc.block(next_a, next_b))

            for copy in load(after, 1 - i):
                copy.start()

            @pl.when(after >= blocks)
            def _():
                part_load(after, 1 - i).start()

        for half in range(2):
            og[half] += outer_rows(dg[half], h)
            ou[half] += outer_rows(dup[half], h)
            od[half] += outer_rows(act[half], z)

        for k in range(1, m):
            pl.when(step == k - 1)(functools.partial(shared_sum.start_plane, k))
        spread = [(1 + i, i) for i in range(2 * m - 1)] + [(blocks - 2, 2 * m - 1), (blocks - 1, 2 * m)]
        for at, k in spread:
            pl.when(step == at)(shared_steps[k])

        for at in range(m - 1):
            @pl.when(step == (at + 1) * blocks - 1)
            def _():
                if at >= 1:
                    grad_send(at - 1).wait_send()
                for k, total in enumerate(grads):
                    give[k] = total[1 - c].astype(jnp.bfloat16)
                    third(keep, k)[...] = total[c].astype(jnp.bfloat16)
                    total[...] = jnp.zeros_like(total)
                pl.semaphore_wait(room, 1)
                for copy in swaps():
                    copy.start()

            @pl.when(step == (at + 1) * blocks)
            def _():
                for copy in swaps():
                    copy.wait()
                for k in range(3):
                    third(keep, k)[...] = (
                        third(keep, k)[...].astype(jnp.float32) + third(take, k)[...].astype(jnp.float32)
                    ).astype(jnp.bfloat16)
                pl.semaphore_signal(room, inc=1, device_id=(e, 1 - c), device_id_type=MESH)
                grad_send(at).start()

        for k in range(1, nz):
            @pl.when((last == 1) & (t == k * m))
            def _():
                at = (step - 1) % slots
                a1 = (c1 + toward * k + nz) % nz
                collect(at, from_y(a1, k - 1 < together))
                stage[at, 1] = total_ref[...].astype(jnp.bfloat16)
                du_send(at, pc.chip(a1, y, x), r1_hbm.at[c1], r1sem.at[c1]).start()

        return carry

    lax.fori_loop(0, m * blocks, body, 0)
    for i, total in enumerate(grads):
        give[i] = total[1 - c].astype(jnp.bfloat16)
    pl.semaphore_wait(room, 1)
    for copy in swaps():
        copy.start()
    turned = s_ref[...].T
    for i in range(n):
        rows_out[i] = turned[i : i + 1, :]
    for i in range(m):
        scores_in[me * m + i] = rows_out[me * m + i]

    def score_send(a, b2):
        return pltpu.make_async_remote_copy(
            src_ref=rows_out.at[pl.ds(pc.block(a, b2) * m, m)], dst_ref=scores_in.at[pl.ds(me * m, m)],
            send_sem=scs.at[a, b2], recv_sem=scr.at[c1, y],
            device_id=(pc.chip(a, b2, x), c), device_id_type=MESH,
        )

    def score_wait(a, b2):
        at = pl.ds(pc.block(a, b2) * m, m)
        pltpu.make_async_remote_copy(
            src_ref=rows_out.at[at], dst_ref=scores_in.at[at], send_sem=scs.at[a, b2], recv_sem=scr.at[a, b2],
            device_id=(pc.chip(a, b2, x), c), device_id_type=MESH,
        ).wait_recv()

    for a, b2 in pc.others():
        score_send(a, b2).start()
    for copy in swaps():
        copy.wait()
    for i, total in enumerate(grads):
        total[c] += third(take, i)[...].astype(jnp.float32)
    grad_send(m - 2).wait_send()
    for j in range(1, m):
        at = (x + j) % m
        pltpu.make_async_remote_copy(
            src_ref=xt_hbm.at[at], dst_ref=xt_hbm.at[at], send_sem=gsend, recv_sem=grecv.at[at],
            device_id=(pc.chip(c1, y, at), c), device_id_type=MESH,
        ).wait_recv()
        back = pltpu.make_async_copy(xt_hbm.at[at], take.at[pl.ds(0, 3 * hidden)], bsem.at[0])
        back.start()
        back.wait()
        for i, total in enumerate(grads):
            total[c] += third(take, i)[...].astype(jnp.float32)
    for copy in totals():
        copy.start()
    collect((m * blocks - 1) % slots, from_y(c1, nz - 1 < together) + from_z())
    final = pltpu.make_async_copy(total_ref, du_hbm, bsem.at[0])
    final.start()
    final.wait()
    for step in range(m * blocks - slots, m * blocks):
        t = step % blocks
        if t < together * m and t % m < m - 1:
            pair_send(step % slots, e, far_hbm.at[0, 0], r3sem.at[0, 0]).wait_send()
            continue
        y_store(step % slots, c1, y).wait()
        if step < m * blocks - 1:
            du_send(step % slots, e, r1_hbm.at[0], r1sem.at[0]).wait_send()
    for a, b2 in pc.others():
        score_wait(a, b2)
        score_send(a, b2).wait_send()
    gather.finish(range(1, nz))
    for copy in totals():
        copy.wait()


def experts(h, dy, gates, routed_w, other_w, partner_w, shared):
    blocks, rows, width = dy.shape
    n = gates.shape[0]
    hidden = routed_w[0].shape[0]
    nz = 4
    m = {16: 2, 64: 4}[n]
    slots = 4
    vmem = pl.BlockSpec(memory_space=pltpu.VMEM)
    hbm = pl.BlockSpec(memory_space=pl.ANY)
    f32, b16 = jnp.float32, jnp.bfloat16
    out = jax.ShapeDtypeStruct
    dma = pltpu.SemaphoreType.DMA
    grad = pltpu.VMEM((2, hidden, width), f32)
    pair = pltpu.VMEM((2, rows, width), b16)
    narrow = pltpu.VMEM((2, rows, hidden), b16)
    three = pltpu.VMEM((3, hidden, width), b16)
    return pl.pallas_call(
        functools.partial(experts_kernel, n, slots),
        out_shape=(
            out((n, 1, rows), f32), out((rows, width), f32),
            out((hidden, width), f32), out((hidden, width), f32), out((hidden, width), f32),
            out((shared.shape[0] // n, width), b16), out((nz, m, rows, width), b16), out((m - 1, nz, 2, rows, width), b16),
            out((blocks, rows, width), b16), out((blocks, 2, rows, width), b16), out((m, 3 * hidden, width), b16),
            out((m - 1, nz, rows, width), b16), out((nz, rows, width), b16),
        ),
        in_specs=[hbm, hbm, vmem] + [hbm] * 10,
        out_specs=(vmem,) + (hbm,) * 12,
        input_output_aliases={0: 8},
        scratch_shapes=[
            pltpu.VMEM((2, 3, 2, hidden, width), b16), grad, grad, grad,
            pltpu.VMEM((rows, width), f32), pair, pair, narrow, narrow, narrow,
            pltpu.VMEM((slots, 2, rows, width), b16), pltpu.VMEM((2, 2, rows, width), b16), pair, three,
            pltpu.VMEM((max(3 * hidden, shared.shape[0] // n * (n - 1)), width), b16), pltpu.VMEM(shared.shape, b16),
            pltpu.VMEM((rows, 128), f32), pltpu.VMEM((rows, 128), f32), pltpu.VMEM((128, rows), f32), pltpu.VMEM((n, 1, rows), f32),
            dma((64,)), dma((blocks,)), dma((2, 2)), dma((slots,)), dma((m - 1, nz)), dma((nz,)), dma((2,)),
            dma((2, 3, 2)), dma((slots,)), dma((2,)), dma((slots,)),
            dma((3,)), dma((3,)), dma, dma((m,)), dma((3,)), dma((3,)), dma((nz, m)), dma((nz, m)),
            pltpu.SemaphoreType.REGULAR, dma((n,)), dma((m - 1, m, nz)), dma((nz - 1, m)), dma((m - 1,)),
        ],
        compiler_params=pltpu.CompilerParams(collective_id=1, has_side_effects=True, vmem_limit_bytes=62 * 2**20),
    )(h, dy, gates, *routed_w, *other_w, *partner_w, shared)


def swap_halves(values):
    return pltpu.roll(values, HD // 2, axis=1)


def route_columns(logit_ref, route_ref, turn_ref):
    count = logit_ref.shape[0]
    logits = logit_ref[...]
    raised = jnp.exp(logits - jnp.max(logits, axis=0, keepdims=True))
    turn_ref[...] = jnp.zeros_like(turn_ref)
    turn_ref[0:count, :] = raised / jnp.sum(raised, axis=0, keepdims=True)
    soft = turn_ref[...].T
    turn_ref[0:count, :] = route_ref[...].astype(jnp.float32)
    return soft, turn_ref[...].T.astype(jnp.int32)


class Scatter:
    def __init__(self, pc, axes, block, ra, rb, rc, sems):
        self.pc, self.block, self.ra, self.rb, self.rc = pc, block, ra, rb, rc
        (self.na, self.a, self.sa), (self.nb, self.b, self.sb), (self.nc, self.c, self.sc) = axes
        self.ssem, self.sema, self.semb, self.semc = sems

    def at(self, i, j, k):
        a, b, c = (self.a + i) % self.na, (self.b + j) % self.nb, (self.c + k) % self.nc
        return a * self.sa + b * self.sb + c * self.sc

    def copy(self, b, dst, sem, to):
        return pltpu.make_async_remote_copy(
            src_ref=self.block(b), dst_ref=dst, send_sem=self.ssem.at[b], recv_sem=sem,
            device_id=(to, self.pc.c), device_id_type=MESH,
        )

    def add(self, total, src, sem):
        self.copy(self.pc.e, src, sem, self.at(1, 0, 0)).wait_recv()
        return total + src[...].astype(jnp.float32)

    def place_b(self, j):
        return (self.b + j) % self.nb

    def place_c(self, k):
        return (self.c + k) % self.nc

    def start(self):
        for k in range(self.nc):
            self.start_plane(k)

    def start_plane(self, p):
        k = (p + 1) % self.nc
        for i in range(1, self.na):
            for j in list(range(1, self.nb)) + [0]:
                b, c = self.place_b(j), self.place_c(k)
                slot = self.na - i - 1
                self.copy(self.at(i, j, k), self.ra(slot, c, b), self.sema.at[slot, c, b], self.at(i, 0, 0)).start()

    def collect(self, j, k, level):
        block = self.block(self.at(0, j, k))
        b, c = self.place_b(j), self.place_c(k)
        total = block[...].astype(jnp.float32)
        for i in range(self.na - 1):
            total = self.add(total, self.ra(i, c, b), self.sema.at[i, c, b])
        if level >= 2:
            for i in range(self.nb - 1):
                total = self.add(total, self.rb(i, c), self.semb.at[i, c])
        if level >= 3:
            for i in range(self.nc - 1):
                total = self.add(total, self.rc(i), self.semc.at[i])
        block[...] = total.astype(jnp.bfloat16)

    def second(self, p):
        k = (p + 1) % self.nc
        for j in range(1, self.nb):
            self.collect(j, k, 1)
            slot = self.nb - j - 1
            self.copy(self.at(0, j, k), self.rb(slot, self.place_c(k)), self.semb.at[slot, self.place_c(k)], self.at(0, j, 0)).start()

    def third(self, p):
        k = p + 1
        self.collect(0, k, 2)
        slot = self.nc - k - 1
        self.copy(self.at(0, 0, k), self.rc(slot), self.semc.at[slot], self.at(0, 0, k)).start()

    def last(self):
        self.collect(0, 0, 3)

    def steps(self):
        found = [functools.partial(self.second, 0)]
        for p in range(1, self.nc):
            found += [functools.partial(self.second, p), functools.partial(self.third, p - 1)]
        return found + [self.last]

    def finish(self):
        n = self.pc.n

        def one(j, carry):
            to = (self.pc.e + j) % n
            self.copy(to, self.rc(0), self.semc.at[0], to).wait_send()
            return carry

        lax.fori_loop(1, n, one, 0)


def tail_kernel(
    n,
    x_ref, x1_ref, cot_ref, dh_ref, dus_hbm, base_hbm, own_ref, q_ref, k_ref, v_ref, o_ref, p_ref, wq, wk, wv, wo,
    gain1, gain2, cos_ref, sin_ref, cnt_ref, len_ref, logit_ref, route_ref, scores_in, y_hbm, far_hbm,
    out_ref, gtok_ref, glog_ref, small_ref, ag0, ag1, ags, y3_hbm, y1_hbm,
    dx_ref, dq_ref, dk_ref, dv_ref, a_ref, give, take, stack0, stack1, r3, r2, r1,
    sm_core, sm_d3, sm_d2, sm_z,
    wbuf, wsem, turn_ref, ybuf, ytmp,
    gs, gr, ss, s3, s2, s1, xs, xr, cs, cr, locs, yl, yt, ys3, ys1, y3s, y1s,
):
    pc = Place(n)
    c1, c2, c3, e, c, nz, m = pc.c1, pc.c2, pc.c3, pc.e, pc.c, pc.nz, pc.m
    rows, width = x_ref.shape
    half = width // 2
    pc.greet_all()

    x, y = pc.x, pc.y

    def y_far(a, j):
        return pltpu.make_async_remote_copy(
            src_ref=y_hbm.at[a, (y + j) % m], dst_ref=y3_hbm.at[m - j - 1, a], send_sem=ys3.at[j - 1, a], recv_sem=y3s.at[m - j - 1, a],
            device_id=(pc.chip(c1, (y + j) % m, x), c), device_id_type=MESH,
        )

    def y_along(a):
        return pltpu.make_async_remote_copy(
            src_ref=ybuf.at[a], dst_ref=y1_hbm.at[c1], send_sem=ys1.at[a], recv_sem=y1s.at[c1],
            device_id=(pc.chip(a, y, x), c), device_id_type=MESH,
        )

    toward = 1 - 2 * (c1 // (nz // 2))
    together = nz - 1

    def plane(i):
        return (c1 + toward * (i + 1) + nz) % nz

    for i in range(together, nz):
        for j in range(1, m):
            y_far(plane(i), j).start()
    y_own = [pltpu.make_async_copy(y_hbm.at[a, y], ybuf.at[a], yl.at[a]) for a in range(nz)]
    for copy in y_own:
        copy.start()

    def y_sum(a, received):
        def fetched(i):
            return pltpu.make_async_copy(received[i][0], ytmp.at[i % 2], yt.at[i % 2])

        def begin(i):
            src, sem = received[i]
            if sem is not None:
                pltpu.make_async_remote_copy(
                    src_ref=src, dst_ref=src, send_sem=ys1.at[0], recv_sem=sem, device_id=(e, 1 - c), device_id_type=MESH,
                ).wait_recv()
            fetched(i).start()

        begin(0)
        total = ybuf[a].astype(jnp.float32)
        for i in range(len(received)):
            if i + 1 < len(received):
                begin(i + 1)
            fetched(i).wait()
            total = total + ytmp[i % 2].astype(jnp.float32)
        return total

    def y_from3(i):
        a = plane(i)
        if i < together:
            return [(far_hbm.at[k, a, 0], None) for k in range(m - 1)]
        return [(y3_hbm.at[k, a], y3s.at[k, a]) for k in range(m - 1)]

    def y_third(i):
        a = plane(i)
        ybuf[a] = y_sum(a, y_from3(i)).astype(jnp.bfloat16)
        y_along(a).start()

    def y_last():
        along = [(y1_hbm.at[(c1 + j) % nz], y1s.at[(c1 + j) % nz]) for j in range(1, nz)]
        out_ref[...] = (dx_ref[...] + y_sum(c1, y_from3(nz - 1) + along)).astype(jnp.bfloat16)

    def y_finish():
        for i in range(nz - 1):
            y_along(plane(i)).wait_send()
        for i in range(together, nz):
            for j in range(1, m):
                y_far(plane(i), j).wait_send()

    gather_s = Gather(pc, own_ref, ags, gs.at[2], gr.at[2], own_ref.shape[0])
    loc_s = pltpu.make_async_copy(own_ref, ags.at[e], locs.at[2])
    gather_s.start()
    loc_s.start()
    shared_events = gather_s.events()

    def fetch(src, i):
        return pltpu.make_async_copy(src, wbuf.at[i], wsem.at[i])

    get_dus = pltpu.make_async_copy(dus_hbm, dx_ref, locs.at[0])
    get_dus.start()
    fetch(wo, 0).start()
    fetch(wv, 1).start()

    x1 = x1_ref[...]
    up = cot_ref[...].astype(jnp.float32)
    get_dus.wait()
    dh = dh_ref[...] + dx_ref[...]
    r_two = lax.rsqrt(jnp.mean(x1 * x1, axis=-1, keepdims=True) + norm_eps)
    n_two = x1 * r_two
    scaled = dh * gain2[...]
    grad_two = jnp.sum(dh * n_two, axis=0, keepdims=True)
    dx = up + r_two * (scaled - n_two * jnp.mean(scaled * n_two, axis=-1, keepdims=True))
    dx_ref[...] = dx
    dx_low = dx.astype(jnp.bfloat16)

    def columns(ref, which):
        return ref[:, pl.ds(pl.multiple_of(which * half, 128), half)]

    def hand(i):
        return pltpu.make_async_remote_copy(
            src_ref=give.at[i], dst_ref=take.at[i], send_sem=xs.at[i], recv_sem=xr.at[i],
            device_id=(e, 1 - c), device_id_type=MESH,
        )

    def to_partner(i, left, right):
        give[i] = outer_rows(columns(left, 1 - c), right).astype(jnp.bfloat16)
        hand(i).start()

    def own_part(i, left, right, stack, at):
        block = stack.shape[1]
        part = outer_rows(columns(left, c), right)
        hand(i).wait_recv()
        total = (part + take[i].astype(jnp.float32)).astype(jnp.bfloat16)
        stack[pl.ds(at * (half // block), half // block)] = total.reshape(half // block, block, width)

    to_partner(0, o_ref, dx_low)
    shared_events[0]()
    fetch(wo, 0).wait()
    dq_ref[...] = inner_cols(dx_low, wbuf[0]).astype(jnp.bfloat16)
    fetch(wk, 0).start()
    cosine, sine = cos_ref[...], sin_ref[...]
    scale = HD ** (-0.5)

    def one_head(hd, carry):
        at = pl.ds(pl.multiple_of(hd * HD, HD), HD)
        prob = p_ref[hd]
        d_o, val, que, key = dq_ref[:, at], v_ref[:, at], q_ref[:, at], k_ref[:, at]
        dv_ref[:, at] = outer_rows(prob.astype(jnp.bfloat16), d_o).astype(jnp.bfloat16)
        d_prob = inner_cols(d_o, val)
        inner = jnp.sum(prob * d_prob, axis=-1, keepdims=True)
        d_score = (prob * (d_prob - inner)).astype(jnp.bfloat16)
        d_q = matmul(d_score, key) * scale
        d_k = outer_rows(d_score, que) * scale
        dq_ref[:, at] = (d_q * cosine - swap_halves(d_q) * sine).astype(jnp.bfloat16)
        dk_ref[:, at] = (d_k * cosine - swap_halves(d_k) * sine).astype(jnp.bfloat16)
        return carry

    lax.fori_loop(0, HEADS, one_head, 0)
    for copy in y_own:
        copy.wait()
    for i in range(nz - 1):
        y_third(i)
    xv = x_ref[...].astype(jnp.float32)
    r_one = lax.rsqrt(jnp.mean(xv * xv, axis=-1, keepdims=True) + norm_eps)
    n_one = xv * r_one
    a_ref[...] = (n_one * gain1[...]).astype(jnp.bfloat16)
    shared_events[1]()
    to_partner(1, a_ref, dv_ref[...])
    to_partner(2, a_ref, dk_ref[...])
    to_partner(3, a_ref, dq_ref[...])
    if n * stack0.shape[1] > 2 * half:
        stack0[...] = jnp.zeros_like(stack0)
        stack1[...] = jnp.zeros_like(stack1)
    own_part(0, o_ref, dx_low, stack0, 0)
    own_part(1, a_ref, dv_ref[...], stack0, 1)
    first, second = (
        Scatter(
            pc, ((m, c3, pc.s3), (m, c2, pc.s2), (nz, c1, pc.s1)), lambda b, stack=stack: stack.at[b], lambda k, a, b2, i=i: r3.at[i, k, a, b2], lambda k, a, i=i: r2.at[i, k, a],
            lambda k, i=i: r1.at[i, k], (ss.at[i], s3.at[i], s2.at[i], s1.at[i]),
        )
        for i, stack in enumerate((stack0, stack1))
    )
    first.start_plane(0)
    first.start_plane(1)
    shared_events[2]()
    own_part(2, a_ref, dk_ref[...], stack1, 0)
    for p in range(2, nz):
        first.start_plane(p)
    own_part(3, a_ref, dq_ref[...], stack1, 1)
    second.start_plane(0)
    second.start_plane(1)
    shared_events[3]()
    fetch(wv, 1).wait()
    da = inner_cols(dv_ref[...], wbuf[1])
    fetch(wq, 1).start()
    fetch(wk, 0).wait()
    da = da + inner_cols(dk_ref[...], wbuf[0])
    fetch(wq, 1).wait()
    da = da + inner_cols(dq_ref[...], wbuf[1])
    for p in range(2, nz):
        second.start_plane(p)
    scaled_one = da * gain1[...]
    grad_one = jnp.sum(da * n_one, axis=0, keepdims=True)
    back = r_one * (scaled_one - n_one * jnp.mean(scaled_one * n_one, axis=-1, keepdims=True))
    gtok_ref[...] = (dx_ref[...] + back).astype(jnp.bfloat16)
    get_base = pltpu.make_async_copy(base_hbm, dx_ref, wsem.at[0])
    get_base.start()

    def exchange(ref, own, level, peers, value):
        ref[own] = value
        copies = [
            pltpu.make_async_remote_copy(
                src_ref=ref.at[own], dst_ref=ref.at[own], send_sem=cs.at[level, i], recv_sem=cr.at[level, own],
                device_id=to, device_id_type=MESH,
            )
            for i, (to, at) in enumerate(peers)
        ]
        for copy in copies:
            copy.start()

        def done():
            for i, (to, at) in enumerate(peers):
                pltpu.make_async_remote_copy(
                    src_ref=ref.at[own], dst_ref=ref.at[at], send_sem=cs.at[level, i], recv_sem=cr.at[level, at],
                    device_id=to, device_id_type=MESH,
                ).wait_recv()
            for copy in copies:
                copy.wait_send()
            total = ref[0]
            for i in range(1, ref.shape[0]):
                total = total + ref[i]
            return total

        return done

    turn_ref[...] = jnp.zeros_like(turn_ref)
    for i in range(n):
        turn_ref[i : i + 1, :] = scores_in[i]
    scores = turn_ref[...].T
    lane = lax.broadcasted_iota(jnp.int32, (rows, 128), 1)
    row = lax.broadcasted_iota(jnp.int32, (rows, 128), 0)
    scores = jnp.where(row < len_ref[0], scores, 0.0)
    soft, routes = route_columns(logit_ref, route_ref, turn_ref)
    share = jnp.zeros((rows, 128), jnp.float32)
    for i in range(route_ref.shape[0]):
        picked = jnp.sum(jnp.where(lane == routes[:, i : i + 1], scores, 0.0), axis=-1, keepdims=True)
        share = jnp.where(lane == i, picked, share)
    grad_logits = soft * (share - jnp.sum(soft * share, axis=-1, keepdims=True))
    glog_ref[...] = grad_logits.T[0 : route_ref.shape[0], :]

    small = jnp.concatenate([grad_one, grad_two, cnt_ref[...], jnp.zeros((5, width), jnp.float32)], axis=0)
    level0 = exchange(sm_core, c, 0, [((e, 1 - c), 1 - c)], small)
    steps0, steps1 = first.steps(), second.steps()
    steps0[0]()
    steps0[1]()
    shared_events[4]()
    level1 = exchange(sm_d3, c3, 1, [((pc.blk(c1, c2, j), c), j) for j in pc.o3()], level0())
    steps0[2]()
    steps1[0]()
    steps0[3]()
    steps1[1]()
    steps0[4]()
    for event in shared_events[5:-1]:
        event()
    level2 = exchange(sm_d2, c2, 2, [((pc.blk(c1, j, c3), c), j) for j in pc.o2()], level1())
    steps1[2]()
    for step in steps0[5:-1]:
        step()
    level3 = exchange(sm_z, c1, 3, [((pc.blk((c1 + j) % nz, c2, c3), c), (c1 + j) % nz) for j in range(1, nz)], level2())
    for step in steps1[3:-1]:
        step()
    small_ref[...] = level3()
    steps0[-1]()
    g0 = Gather(pc, stack0.at[e], ag0, gs.at[0], gr.at[0], stack0.shape[1])
    g0.start()
    loc0 = pltpu.make_async_copy(stack0.at[e], ag0.at[e], locs.at[0])
    loc0.start()
    steps1[-1]()
    g1 = Gather(pc, stack1.at[e], ag1, gs.at[1], gr.at[1], stack1.shape[1])
    g1.start()
    loc1 = pltpu.make_async_copy(stack1.at[e], ag1.at[e], locs.at[1])
    loc1.start()
    get_base.wait()
    y_last()
    run_staggered(g0.events(), g1.events(), 3)
    shared_events[-1]()
    for g in (gather_s, g0, g1):
        g.finish()
    first.finish()
    second.finish()
    loc_s.wait()
    loc0.wait()
    loc1.wait()
    y_finish()
    for i in range(4):
        hand(i).wait_send()


def tail(n, x, x1, cot, dh, dus, base, own, q, k, v, o, prob, wq, wk, wv, wo, gain1, gain2, cosine, sine, cnt, length, logits, routes, scores, y, far):
    nz = 4
    m = {16: 2, 64: 4}[n]
    rows, width = x.shape
    half = width // 2
    block = blocked(2 * half, n)
    vmem = pl.BlockSpec(memory_space=pltpu.VMEM)
    hbm = pl.BlockSpec(memory_space=pl.ANY)
    f32, b16 = jnp.float32, jnp.bfloat16
    out = jax.ShapeDtypeStruct
    dma = pltpu.SemaphoreType.DMA
    wide = pltpu.VMEM((rows, width), b16)
    return pl.pallas_call(
        functools.partial(tail_kernel, n),
        out_shape=(
            out((rows, width), b16), out((rows, width), b16), out(logits.shape, f32), out((8, width), f32),
            out((n, block, width), b16), out((n, block, width), b16),
            out((n,) + own.shape, b16),
            out((m - 1, nz, rows, width), b16), out((nz, rows, width), b16),
        ),
        in_specs=[vmem] * 4 + [hbm] * 2 + [vmem] * 6 + [hbm] * 4 + [vmem] * 5 + [pl.BlockSpec(memory_space=pltpu.SMEM)] + [vmem] * 3 + [hbm] * 2,
        out_specs=(vmem,) * 4 + (hbm,) * 5,
        scratch_shapes=[
            pltpu.VMEM((rows, width), f32), wide, wide, wide, wide,
            pltpu.VMEM((4, half, width), b16), pltpu.VMEM((4, half, width), b16),
            pltpu.VMEM((n, block, width), b16), pltpu.VMEM((n, block, width), b16),
            pltpu.VMEM((2, m - 1, nz, m, block, width), b16), pltpu.VMEM((2, m - 1, nz, block, width), b16),
            pltpu.VMEM((2, nz - 1, block, width), b16),
            pltpu.VMEM((2, 8, width), f32), pltpu.VMEM((m, 8, width), f32), pltpu.VMEM((m, 8, width), f32), pltpu.VMEM((nz, 8, width), f32),
            pltpu.VMEM((2, width, width), b16), dma((2,)), pltpu.VMEM((128, rows), f32),
            pltpu.VMEM((nz, rows, width), b16), pltpu.VMEM((2, rows, width), b16),
            dma((3, 160)), dma((3, 2, n)), dma((2, n)), dma((2, m - 1, nz, m)), dma((2, m - 1, nz)), dma((2, nz - 1)),
            dma((4,)), dma((4,)), dma((4, max(nz, m))), dma((4, max(nz, m, 2))), dma((3,)),
            dma((nz,)), dma((2,)), dma((m - 1, nz)), dma((nz,)), dma((m - 1, nz)), dma((nz,)),
        ],
        compiler_params=pltpu.CompilerParams(collective_id=2, has_side_effects=True, vmem_limit_bytes=63 * 2**20),
    )(x, x1, cot, dh, dus, base, own, q, k, v, o, prob, wq, wk, wv, wo, gain1, gain2, cosine, sine, cnt, length, logits, routes, scores, y, far)


def blocked(count, n):
    return -(-count // (16 * n)) * 16


def from_blocks(blocks, count):
    return blocks.reshape(-1, blocks.shape[2])[:count].astype(jnp.float32)


def rotary_rows(seq_len):
    position = np.arange(seq_len).astype(np.float32)
    inverse_freq = (rotary_base ** (-2.0 * np.arange(HD // 2).astype(np.float32) / HD)).astype(np.float32)
    angle = position[:, None] * inverse_freq[None, :]
    cosine, sine = np.cos(angle), np.sin(angle)
    return np.concatenate([cosine, cosine], axis=1), np.concatenate([-sine, sine], axis=1)


def on_device(
    tokens, norm_one, w_query, w_key, w_value, w_out, norm_two, r_gate, r_up, r_down, s_gate, s_up, s_down,
    logits, routes, lengths, cotangent,
):
    rows, width = tokens.shape
    n = lax.axis_size("exp")
    hidden = s_gate.shape[1]
    cosine, sine = (jnp.asarray(table) for table in rotary_rows(rows))
    gain1, gain2 = norm_one, norm_two
    logits, routes = logits.T, routes.T
    attn_w = (w_query, w_key, w_value, w_out)
    routed_w = (r_gate[0].T, r_up[0].T, r_down[0])
    shared_w = (s_gate.T, s_up.T, s_down)
    (
        all_dy, all_h, fq, fk, fv, fo, fg, fu, fd, pg, pu, pd, mixed, queries, keys_all, values_all, attended, prob, gates, counts,
        base, shared_back, shared_grads,
    ) = front(
        n, tokens, cotangent, gain1, gain2, cosine, sine, lengths, logits, routes,
        attn_w, routed_w, shared_w,
    )
    scores, grad_hidden, tg, tu, td, shared_sum, outs, far_outs = experts(
        all_h, all_dy, gates, routed_w, (fg, fu, fd), (pg, pu, pd), shared_grads
    )[:8]
    full = (width, width)
    output, grad_tokens, grad_logits, small_sums, sum0, sum1, sum_s = tail(
        n, tokens, mixed, cotangent, grad_hidden, shared_back, base, shared_sum, queries, keys_all, values_all, attended, prob,
        fq.reshape(full), fk.reshape(full), fv.reshape(full), fo.reshape(full),
        gain1, gain2, cosine, sine, counts, lengths, logits, routes, scores,
        outs, far_outs,
    )[:7]
    half = width // 2
    wout_value = from_blocks(sum0, width)
    key_query = from_blocks(sum1, width)
    shared = from_blocks(sum_s, 3 * hidden)
    sg, su, sd = (shared[i * hidden : (i + 1) * hidden] for i in range(3))
    return (
        output, grad_tokens, small_sums[0],
        key_query[half:], key_query[:half], wout_value[half:], wout_value[:half],
        small_sums[1], tg.T[None], tu.T[None], td[None], sg.T, su.T, sd,
        grad_logits.T, small_sums[2, :n].astype(jnp.int32),
    )


def solution(mesh):
    in_specs = (
        P(("exp", "hid"), None),
        P(),
        P("hid", None),
        P("hid", None),
        P("hid", None),
        P("hid", None),
        P(),
        P("exp", None, "hid"),
        P("exp", None, "hid"),
        P("exp", "hid", None),
        P(None, "hid"),
        P(None, "hid"),
        P("hid", None),
        P(("exp", "hid"), None),
        P(("exp", "hid"), None),
        P(("exp", "hid")),
        P(("exp", "hid"), None),
    )
    out_specs = (
        P(("exp", "hid"), None),
        P(("exp", "hid"), None),
        P(),
        P("hid", None),
        P("hid", None),
        P("hid", None),
        P("hid", None),
        P(),
        P("exp", None, "hid"),
        P("exp", None, "hid"),
        P("exp", "hid", None),
        P(None, "hid"),
        P(None, "hid"),
        P("hid", None),
        P(("exp", "hid"), None),
        P(),
    )
    return jax.shard_map(
        on_device, mesh=mesh, in_specs=in_specs, out_specs=out_specs, check_vma=False
    )
```
